32 devices in a mesh: groups: 2 (over y), dev: 8 (over z, x), sub: 2 (over core).
Axes of the slice: x: 2, y: 2, z: 4, core: 2. Of those that a mesh axis runs over, the one named last changes fastest.
Arguments:
- tokens: bfloat16 [2048, 2048], P(('groups', 'dev')), parts along dimension 0, may hold values from -6 to 6
- query_key_value: bfloat16 [2048, 3, 2048], P(('groups', 'dev'), None, 'sub'), parts along dimension 0, may hold values from -6 to 6
- out_weight: bfloat16 [2048, 2048], P('dev', 'sub'), may hold values from -0.125 to 0.125
- modulation: float32 [8, 2048], P('groups'), parts along dimension 0, may hold values from -3 to 3
- router_weight: bfloat16 [2048, 64], replicated, may hold values from -0.125 to 0.125
- expert_ids: int32 [2048, 4], P(('groups', 'dev')), parts along dimension 0, may hold values from 0 to 63, all different within a row; in each aligned block of 128 rows (0 to 127, 128 to 255, ...) at most 12 rows name the same one
- gate_up_weight: bfloat16 [128, 2, 2048, 384], P('dev', None, None, 'sub'), may hold values from -0.125 to 0.125
- down_weight: bfloat16 [128, 384, 2048], P('dev', None, 'sub'), may hold values from -0.21875 to 0.21875
Outputs:
- block_out: bfloat16 [2048, 2048], P(('groups', 'dev'), 'sub'), parts along dimension 0
The draws below stay inside these ranges and needn't reach their ends.
There are 2 independent parts, one for each index of `groups`. The reference program is written for one: setup_inputs(seed, part) draws one part's arguments, and reference() takes and returns one part's arrays. A program takes and returns all parts, laid end to end along the dimension named above; an argument that names none is the same for every part. Nothing has to cross between parts.
Inputs may be any that keep to these rules, and one draw needn't show every extreme that they name: `expert_ids`: each token names 4 different experts. Within each aligned block of 128 rows no expert is named by more than 12 rows, a bound that some block reaches.
All inputs are finite; a program needn't handle non-finite values.
Results may differ from the reference program's by a relative error of at most 0.008.
Values may be sent and summed in bfloat16 or wider, within the bound.
No kernel may reach another device: no remote copies, remote signals or barrier semaphores. Data moves between devices by JAX's collectives and lax.ppermute only.
A program may use at most 128 MiB of HBM per device.

```python
import math
import jax
import jax.numpy as jnp
import numpy as np
from jax import lax

D = 2048
HEADS = 16
HEAD = 128
FF = 768
EXPERTS = 64
TOPK = 4
TOK_DEV = 128
CAP = 12
TOKENS = 1024
N_DEV = 8


def draw_query_key_value(key, part):
    base_key = jax.random.fold_in(jax.random.fold_in(key, 7331), 0)
    width = HEADS * HEAD
    values = jnp.clip(jax.random.normal(base_key, (TOKENS, 3, width), jnp.float32), -6.0, 6.0)
    return values.astype(jnp.bfloat16)


def steps_of(stream_key, dims, cuts, smallest, top_value):
    def one(axis_at, blocks):
        heights = jax.random.uniform(jax.random.fold_in(jax.random.fold_in(stream_key, 6), axis_at), (blocks,), jnp.float32, smallest / len(cuts), top_value / len(cuts))
        return jnp.repeat(jnp.exp(heights), dims[axis_at] // blocks).reshape((-1,) + (1,) * (len(dims) - axis_at - 1))

    loudness = one(*cuts[0])
    for cut in cuts[1:]:
        loudness = loudness * one(*cut)
    return loudness


def routed_block(own_key, own, number, rows, amount, top, most, lean):
    ranking = jax.random.permutation(own_key, amount)
    crowded, ordinary = load_shares(amount, rows * top, most, lean, True), load_shares(amount, rows * top, most, lean, False)
    places = jnp.arange(amount)

    def named(tallies, turn):
        used = int((tallies > 0).sum())
        fixed = max(1, used // 4)
        shifted = fixed + (places - fixed + turn * (used - fixed)) % max(1, amount - fixed)
        return jnp.zeros((amount,), jnp.int32).at[ranking[jnp.where(places < fixed, places, shifted)]].set(jnp.asarray(tallies, jnp.int32))

    tallies = jnp.where(number % 4 == 0, named(crowded, number // 4), named(ordinary, number - number // 4 - 1))
    mixed = jax.random.permutation(jax.random.fold_in(own, 3), amount)
    giver, receiver = mixed[0:amount // 2 * 2:2], mixed[1:amount // 2 * 2:2]
    room = jnp.minimum(tallies[giver] - 1, most - tallies[receiver]) // 2
    room = jnp.where((giver == ranking[0]) | (receiver == ranking[0]) | (tallies[receiver] == 0), 0, jnp.maximum(room, 0))
    shifted = jax.random.randint(jax.random.fold_in(own, 4), (amount // 2,), 0, 1 << 20) % (room + 1)
    tallies = tallies.at[giver].add(-shifted).at[receiver].add(shifted)
    members = jnp.searchsorted(jnp.cumsum(tallies), jnp.arange(rows * top), side="right").astype(jnp.int32)
    listing = members.reshape(top, rows).T
    listing = listing[jax.random.permutation(jax.random.fold_in(own, 1), rows)]
    turn = jax.random.randint(jax.random.fold_in(own, 2), (rows, 1), 0, top)
    return jnp.take_along_axis(listing, (jnp.arange(top)[None, :] + turn) % top, axis=1)


def load_shares(number_of, total, most, slope, full):
    portions = [(1 << 20) // math.isqrt(rank ** slope) + 1 for rank in range(1, number_of + 1)]
    largest = most if full else min(most, max(-(-total // number_of), total * portions[0] // sum(portions)))
    least = 1 if total - largest >= number_of - 1 else 0
    given, rest = [largest] + [least] * (number_of - 1), total - largest - least * (number_of - 1)
    while rest > 0:
        candidates = [i for i in range(1, number_of) if given[i] < largest] or [i for i in range(1, number_of) if given[i] < most]
        whole, remaining = sum([portions[i] for i in candidates]), rest
        for i in candidates:
            more = min(most - given[i], max(1, remaining * portions[i] // whole), rest)
            given[i] = given[i] + more
            rest = rest - more
    return np.array(given)


def gaussian(stream_key, dims, deviation, limit, cuts=(), kind=jnp.bfloat16):
    entries = jax.random.normal(stream_key, dims, jnp.float32) * deviation
    if len(cuts) > 0:
        entries = steps_of(stream_key, dims, cuts, -0.22, 0.18) * entries
    return jnp.clip(entries, min=-limit, max=limit).astype(kind)


def setup_inputs(seed: int = 0, part: int = 0) -> dict:
    key_list = jax.random.split(jax.random.key(seed), 9)
    part_splits = jax.random.split(jax.random.fold_in(key_list[8], part), 9)
    tokens = gaussian(part_splits[0], (TOKENS, D), 1.0, 6.0, ((0, 8),))
    query_key_value = draw_query_key_value(jax.random.fold_in(jax.random.fold_in(key_list[8], part), 71), part)
    out_weight = gaussian(key_list[2], (D, HEADS * HEAD), (HEADS * HEAD) ** -0.5, 0.125, ((0, 8), (1, 2)))
    modulation = gaussian(part_splits[3], (4, D), 0.5, 3.0, (), jnp.float32)
    router_weight = gaussian(key_list[4], (D, EXPERTS), D ** -0.5, 0.125)
    expert_ids_keys = jax.random.split(jax.random.fold_in(part_splits[5], 1), TOKENS // TOK_DEV)
    expert_ids_turns = jax.random.permutation(jax.random.fold_in(part_splits[5], 3), TOKENS // TOK_DEV)
    expert_ids = jax.vmap(lambda own, number: routed_block(jax.random.fold_in(part_splits[5], 2), own, number, TOK_DEV, EXPERTS, TOPK, CAP, 1))(expert_ids_keys, expert_ids_turns).reshape((TOKENS, TOPK))
    gate_up_weight = gaussian(key_list[6], (2 * EXPERTS, 2, D, FF // 2), D ** -0.5, 0.125, ((0, 8), (3, 2)))
    down_weight = gaussian(key_list[7], (2 * EXPERTS, FF // 2, D), FF ** -0.5, 0.21875, ((0, 8), (2, 2)))
    return {"tokens": tokens, "query_key_value": query_key_value, "out_weight": out_weight, "modulation": modulation, "router_weight": router_weight, "expert_ids": expert_ids, "gate_up_weight": gate_up_weight, "down_weight": down_weight}


EPS = 1e-06
NEG = -1e+30

def window_attention(query, keys, values, index, total):
    count = query.shape[0]
    rows = jnp.arange(count, dtype=jnp.int32)[:, None]
    cols = jnp.arange(3 * count, dtype=jnp.int32)[None, :] - count
    place = index * count + cols
    allowed = (jnp.abs(cols - rows) <= count) & (place >= 0) & (place < total)
    scores = jnp.einsum('qhd,khd->hqk', query.astype(jnp.float32), keys.astype(jnp.float32)) / math.sqrt(query.shape[2])
    scores = jnp.where(allowed[None], scores, NEG)
    top = lax.optimization_barrier(jnp.max(scores, -1, keepdims=True))
    weight = jnp.exp(scores - top)
    weight = (weight / lax.optimization_barrier(jnp.sum(weight, -1, keepdims=True))).astype(jnp.bfloat16)
    mixed = jnp.einsum('hqk,khd->qhd', weight.astype(jnp.float32), values.astype(jnp.float32))
    return mixed.astype(jnp.bfloat16)

def attend(query_key_value):
    blocks = TOKENS // TOK_DEV
    packed = query_key_value.reshape(blocks, TOK_DEV, 3, HEADS, HEAD)
    empty = jnp.zeros((1, TOK_DEV, 3, HEADS, HEAD), packed.dtype)
    padded = jnp.concatenate([empty, packed, empty], 0)

    def block(index):
        near = lax.dynamic_slice_in_dim(padded, index, 3, 0).reshape(3 * TOK_DEV, 3, HEADS, HEAD)
        query = lax.dynamic_index_in_dim(packed, index, 0, keepdims=False)[:, 0]
        return window_attention(query, near[:, 1], near[:, 2], index, TOKENS)
    result = lax.map(block, jnp.arange(blocks, dtype=jnp.int32))
    return result.reshape(TOKENS, HEADS * HEAD)

def normalize(state, modulation):
    scale = lax.rsqrt(lax.optimization_barrier(jnp.mean(state * state, -1, keepdims=True)) + EPS)
    return (state * scale * (1.0 + modulation[2]) + modulation[1]).astype(jnp.bfloat16)

def route(normed, router_weight, expert_ids):
    logits = jnp.dot(normed, router_weight, preferred_element_type=jnp.float32)
    experts = router_weight.shape[1]
    match = expert_ids[:, :, None] == jnp.arange(experts, dtype=jnp.int32)[None, None, :]
    picked = lax.optimization_barrier(jnp.sum(jnp.where(match, logits[:, None, :], 0.0), -1))
    lifted = jax.nn.sigmoid(picked)
    return lifted / lax.optimization_barrier(jnp.sum(lifted, -1, keepdims=True))

def experts_sum(normed, gates, expert_ids, gate_up_weight, down_weight):
    room = N_DEV * CAP

    def step(total, expert):
        match = expert_ids == expert
        chosen = jnp.any(match, 1)
        rows = jnp.nonzero(chosen, size=room, fill_value=0)[0].astype(jnp.int32)
        live = jnp.arange(room, dtype=jnp.int32) < jnp.sum(chosen.astype(jnp.int32))
        weight = lax.optimization_barrier(jnp.sum(jnp.where(match, gates, 0.0), 1))[rows]
        weight = jnp.where(live, weight, 0.0)
        pair = lax.dynamic_slice_in_dim(gate_up_weight, 2 * expert, 2, 0)
        down_pair = lax.dynamic_slice_in_dim(down_weight, 2 * expert, 2, 0)
        inputs = normed[rows]
        output = jnp.zeros((room, normed.shape[1]), jnp.float32)
        for half in range(2):
            gate = jnp.dot(inputs, pair[half, 0], preferred_element_type=jnp.float32)
            up = jnp.dot(inputs, pair[half, 1], preferred_element_type=jnp.float32)
            hidden = (jax.nn.silu(gate) * up).astype(jnp.bfloat16)
            piece = jnp.dot(hidden, down_pair[half], preferred_element_type=jnp.float32).astype(jnp.bfloat16)
            output = output + piece.astype(jnp.float32)
        return (total.at[rows].add(weight[:, None] * output), None)
    total = jnp.zeros((normed.shape[0], normed.shape[1]), jnp.float32)
    total, _ = lax.scan(step, total, jnp.arange(EXPERTS, dtype=jnp.int32))
    return total

def reference(tokens, query_key_value, out_weight, modulation, router_weight, expert_ids, gate_up_weight, down_weight):
    mixed = attend(query_key_value)
    proj = lax.dot_general(mixed, out_weight, (((1,), (1,)), ((), ())), preferred_element_type=jnp.float32)
    state = tokens.astype(jnp.float32) + (1.0 + modulation[0]) * proj
    normed = normalize(state, modulation)
    gates = route(normed, router_weight, expert_ids)
    routed = experts_sum(normed, gates, expert_ids, gate_up_weight, down_weight)
    return (state + (1.0 + modulation[3]) * routed).astype(jnp.bfloat16)
```

```python
import functools
import math

import jax
import jax.numpy as jnp
from jax import lax
from jax.experimental import pallas as pl
from jax.experimental.pallas import tpu as pltpu
from jax.sharding import PartitionSpec as P

HEAD = 128
CAP = 12
SLOTS = 16
TILE = 16

EPS = 1e-06
NEG = -1e30
F32 = jnp.float32
BF16 = jnp.bfloat16

NT = (((1,), (1,)), ((), ()))


def vmem(mib):
    return pltpu.CompilerParams(vmem_limit_bytes=mib * 2**20)


def whole():
    return pl.BlockSpec(memory_space=pltpu.VMEM)


def attention_kernel(q_ref, before_ref, own_ref, after_ref, mixed_ref):
    count, width = q_ref.shape
    place = lax.axis_index("dev")
    last = lax.axis_size("dev") - 1
    row = lax.broadcasted_iota(jnp.int32, (count, count), 0)
    col = lax.broadcasted_iota(jnp.int32, (count, count), 1)
    see_before = (col >= row) & (place > 0)
    see_after = (col <= row) & (place < last)
    scale = 1.0 / math.sqrt(HEAD)

    def scored(q, ref, lanes):
        return lax.dot_general(q, ref[:, lanes], NT, preferred_element_type=F32) * scale

    for head in range(width // HEAD):
        lanes = slice(head * HEAD, (head + 1) * HEAD)
        vlanes = slice(width + head * HEAD, width + (head + 1) * HEAD)
        q = q_ref[:, lanes]
        sb = jnp.where(see_before, scored(q, before_ref, lanes), NEG)
        so = scored(q, own_ref, lanes)
        sa = jnp.where(see_after, scored(q, after_ref, lanes), NEG)
        top = jnp.max(jnp.maximum(jnp.maximum(sb, so), sa), 1, keepdims=True)
        wb, wo, wa = jnp.exp(sb - top), jnp.exp(so - top), jnp.exp(sa - top)
        inv = 1.0 / jnp.sum(wb + wo + wa, 1, keepdims=True)
        out = jnp.dot((wo * inv).astype(BF16), own_ref[:, vlanes], preferred_element_type=F32)
        out += jnp.dot((wb * inv).astype(BF16), before_ref[:, vlanes], preferred_element_type=F32)
        out += jnp.dot((wa * inv).astype(BF16), after_ref[:, vlanes], preferred_element_type=F32)
        mixed_ref[:, lanes] = out.astype(BF16)


def projection_kernel(steps, pieces, *refs):
    mixed_ref, other_ref = refs[0], refs[1]
    weight_refs = refs[2 : 2 + len(pieces)]
    keep_ref, send_ref, both_ref = refs[2 + len(pieces) :]
    count = mixed_ref.shape[0]
    half = steps // 2
    chunk = keep_ref.shape[1] // half
    z = lax.axis_index("dev") // 2
    part = lax.axis_index("sub")
    group = lax.axis_index("groups")
    for (hop, side), w_ref in zip(pieces, weight_refs):
        rows = w_ref.shape[0]
        target = jnp.bitwise_xor(z, hop)
        away = jnp.where(target // half == part, 0, 1)
        lane = (target % half) * chunk
        if side is not None:
            lane += (group if side == 0 else 1 - group) * rows
        lane = pl.multiple_of(lane, 128)
        for block, ref in enumerate((mixed_ref, other_ref)):
            both_ref[away, block * count : (block + 1) * count, pl.ds(lane, rows)] = (
                lax.dot_general(ref[...], w_ref[...], NT, preferred_element_type=F32)
            )
    keep_ref[...] = both_ref[0]
    send_ref[...] = both_ref[1]


def state_kernel(keep_ref, got_ref, near_ref, far_ref, ids_ref, mod_ref, out_ref):
    count, lanes = near_ref.shape
    chunk = mod_ref.shape[1] // lax.axis_size("dev")
    side = lax.axis_index("dev") % 2
    part = lax.axis_index("sub")
    for i in range(lanes // chunk):
        at = pl.multiple_of(part * 2 * lanes + (2 * i + side) * chunk, 128)
        lift = 1.0 + mod_ref[0:1, pl.ds(at, chunk)]
        cols = slice(i * chunk, (i + 1) * chunk)
        for block, ref in enumerate((near_ref, far_ref)):
            rows = slice(block * count, (block + 1) * count)
            proj = keep_ref[rows, cols] + got_ref[rows, cols]
            out_ref[rows, cols] = (ref[:, cols].astype(F32) + lift * proj).astype(BF16)
    out_ref[2 * count :, :] = ids_ref[...]


def hidden_kernel(steps, local, topk, *refs):
    shard_refs = refs[: 4 * steps]
    mod_ref, router_ref, w_ref = refs[4 * steps : 4 * steps + 3]
    hidden_ref, state_ref, back_ref = refs[4 * steps + 3 : 4 * steps + 6]
    full_ref, rows_ref, gate_ref = refs[4 * steps + 6 :]
    step = pl.program_id(0)
    count, width = full_ref.shape
    lanes = shard_refs[0].shape[1]
    device = lax.axis_index("dev")
    side = device % 2
    part = lax.axis_index("sub")
    chunk = width // lax.axis_size("dev")
    experts = router_ref.shape[0]
    slots = local * SLOTS

    @pl.when(step == 0)
    def _():
        before = lax.broadcasted_iota(jnp.int32, (count, count), 0)
        after = lax.broadcasted_iota(jnp.int32, (count, count), 1)
        earlier = (before < after).astype(F32).astype(BF16)
        slot = lax.broadcasted_iota(jnp.int32, (slots, count), 0) % SLOTS
        mine = lax.broadcasted_iota(jnp.int32, (local, count), 0) + device * local
        every = lax.broadcasted_iota(jnp.int32, (experts, count), 0)
        for source in range(2 * steps):
            hop, cross = source // 2, source % 2
            for far_half in range(2):
                for far_side in range(2):
                    ref = shard_refs[4 * hop + 2 * far_half + far_side]
                    top = (cross ^ far_side) * count
                    half = part if far_half == 0 else 1 - part
                    parity = side if far_side == 0 else 1 - side
                    for i in range(lanes // chunk):
                        block = ref[top : top + count, i * chunk : (i + 1) * chunk]
                        at = (2 * i + parity) * chunk
                        full_ref[:, pl.ds(pl.multiple_of(half * 2 * lanes + at, 128), chunk)] = block
                        if source == 0 and far_half == 0:
                            state_ref[:, pl.ds(pl.multiple_of(at, 128), chunk)] = block
            state = full_ref[...].astype(F32)
            scale = lax.rsqrt(jnp.mean(state * state, 1, keepdims=True) + EPS)
            normed = state * scale * (1.0 + mod_ref[2:3, :]) + mod_ref[1:2, :]
            normed = normed.astype(BF16)
            ids = shard_refs[4 * hop + cross][2 * count : 2 * count + TILE, :]
            ids = ids.astype(F32)[0:1, :].astype(jnp.int32)
            named = [ids[:, k * count : (k + 1) * count] for k in range(topk)]
            hot = sum((mine == n).astype(F32) for n in named)
            rank = jnp.dot(hot.astype(BF16), earlier, preferred_element_type=F32)
            rank = jnp.where(hot > 0.0, rank, -1.0)
            rank = jnp.concatenate(
                [jnp.broadcast_to(rank[e : e + 1], (SLOTS, count)) for e in range(local)]
            )
            pick = rank == slot.astype(F32)
            chosen = jnp.dot(
                jnp.where(pick, 1.0, 0.0).astype(BF16), normed, preferred_element_type=F32
            ).astype(BF16)
            for e in range(local):
                rows_ref[e, source * SLOTS : (source + 1) * SLOTS, :] = chosen[
                    e * SLOTS : (e + 1) * SLOTS
                ]
            logits = lax.dot_general(router_ref[...], normed, NT, preferred_element_type=F32)
            lifted = sum(jnp.where(every == n, 1.0, 0.0) for n in named) * jax.nn.sigmoid(logits)
            gate_ref[...] = lifted / jnp.sum(lifted, 0, keepdims=True)
            here = gate_ref[pl.ds(pl.multiple_of(device * local, local), local), :]
            here = jnp.concatenate(
                [jnp.broadcast_to(here[e : e + 1], (SLOTS, count)) for e in range(local)]
            )
            back_ref[source] = jnp.where(pick, here, 0.0).T.astype(BF16)

    rows = rows_ref[step // 2]
    gate = jnp.dot(rows, w_ref[0, 0], preferred_element_type=F32)
    up = jnp.dot(rows, w_ref[0, 1], preferred_element_type=F32)
    hidden_ref[0] = (jax.nn.silu(gate) * up).astype(BF16)


def output_kernel(sources, near_ref, far_ref, w_ref, back_ref, *refs):
    out_refs, held_ref = refs[:sources], refs[sources]
    step = pl.program_id(0)
    part = lax.axis_index("sub")
    units = near_ref.shape[2]
    total = None
    for half in range(2):
        for ref, who in ((near_ref, part), (far_ref, 1 - part)):
            at = pl.multiple_of(who * units, 64)
            piece = jnp.dot(ref[half], w_ref[half, pl.ds(at, units), :], preferred_element_type=F32)
            total = piece if total is None else total + piece
    total = total.astype(BF16)
    row = pl.multiple_of(step * SLOTS, SLOTS)
    for source in range(sources):
        held_ref[source, pl.ds(row, SLOTS), :] = total[source * SLOTS : (source + 1) * SLOTS]

    @pl.when(step == pl.num_programs(0) - 1)
    def _():
        for source in range(sources):
            out_refs[source][...] = jnp.dot(
                back_ref[source], held_ref[source], preferred_element_type=F32
            ).astype(BF16)


def gathered_body(
    tokens,
    query_key_value,
    out_weight,
    modulation,
    router_weight,
    expert_ids,
    gate_up_weight,
    down_weight,
):
    count, width = tokens.shape
    devices = lax.axis_size("dev")
    groups = lax.axis_size("groups")
    steps = devices // 2
    side = lax.axis_index("dev") % 2
    part = lax.axis_index("sub")
    group = lax.axis_index("groups")
    local_width = query_key_value.shape[2]
    chunk = width // devices
    lanes = width // 4
    halves_here = gate_up_weight.shape[0]
    local = halves_here // 2
    experts = router_weight.shape[1]
    topk = expert_ids.shape[1]
    struct = jax.ShapeDtypeStruct

    def hop(x, flip):
        return lax.ppermute(x, "dev", [(i, i ^ flip) for i in range(devices)])

    def swap(x):
        return lax.ppermute(x, "sub", [(0, 1), (1, 0)])

    query = query_key_value[:, 0]
    pair = jnp.concatenate([query_key_value[:, 1], query_key_value[:, 2]], 1)
    before = lax.ppermute(pair, "dev", [(i, i + 1) for i in range(devices - 1)])
    after = lax.ppermute(pair, "dev", [(i + 1, i) for i in range(devices - 1)])

    cut = tokens.reshape(count, 2, devices // 4, 2, chunk)
    cut = lax.dynamic_index_in_dim(cut, part, 1, keepdims=False)
    near = lax.dynamic_index_in_dim(cut, side, 2, keepdims=False).reshape(count, lanes)
    far = lax.dynamic_index_in_dim(cut, 1 - side, 2, keepdims=False).reshape(count, lanes)
    far = hop(far, 1)

    pieces, weights = [(0, None)], [out_weight]
    if groups == 2:
        rows = out_weight.shape[0] // 2
        sent = lax.dynamic_slice_in_dim(out_weight, group * rows, rows, 0)
        for flip in range(1, steps):
            mine = hop(sent, 2 * flip)
            theirs = lax.ppermute(mine, "groups", [(0, 1), (1, 0)])
            pieces += [(flip, 0), (flip, 1)]
            weights += [mine, theirs]
    else:
        for flip in range(1, steps):
            pieces.append((flip, None))
            weights.append(hop(out_weight, 2 * flip))

    mixed = pl.pallas_call(
        attention_kernel,
        out_shape=struct((count, local_width), BF16),
        in_specs=[whole()] * 4,
        out_specs=whole(),
        compiler_params=vmem(32),
    )(query, before, pair, after)
    keep, send = pl.pallas_call(
        functools.partial(projection_kernel, steps, tuple(pieces)),
        out_shape=[struct((2 * count, lanes), F32)] * 2,
        in_specs=[whole()] * (2 + len(weights)),
        out_specs=[whole()] * 2,
        scratch_shapes=[pltpu.VMEM((2, 2 * count, lanes), F32)],
        compiler_params=vmem(32),
    )(mixed, hop(mixed, 1), *weights)
    ids = expert_ids.T.reshape(1, topk * count).astype(BF16)
    ids = jnp.pad(ids, ((0, TILE - 1), (0, lanes - topk * count)))
    shard = pl.pallas_call(
        state_kernel,
        out_shape=struct((2 * count + TILE, lanes), BF16),
        in_specs=[whole()] * 6,
        out_specs=whole(),
        compiler_params=vmem(32),
    )(keep, swap(send), near, far, ids, modulation)

    column = [shard] + [hop(shard, 2 * flip) for flip in range(1, steps)]
    shards = []
    for block in column:
        crossed = hop(block, 1)
        shards += [block, crossed, swap(block), swap(crossed)]

    sources = 2 * steps
    slots = local * SLOTS
    room = sources * SLOTS
    units = gate_up_weight.shape[3]
    hidden, state, back = pl.pallas_call(
        functools.partial(hidden_kernel, steps, local, topk),
        grid=(halves_here,),
        out_shape=[
            struct((halves_here, room, units), BF16),
            struct((count, 2 * lanes), BF16),
            struct((sources, count, slots), BF16),
        ],
        in_specs=[whole()] * (4 * steps + 2)
        + [pl.BlockSpec((1, 2, width, units), lambda i: (i, 0, 0, 0))],
        out_specs=[
            pl.BlockSpec((1, room, units), lambda i: (i, 0, 0)),
            whole(),
            whole(),
        ],
        scratch_shapes=[
            pltpu.VMEM((count, width), BF16),
            pltpu.VMEM((local, room, width), BF16),
            pltpu.VMEM((experts, count), F32),
        ],
        compiler_params=vmem(48),
    )(*shards, modulation, router_weight.T, gate_up_weight)

    share = pl.pallas_call(
        functools.partial(output_kernel, sources),
        grid=(local,),
        out_shape=[struct((count, 2 * lanes), BF16)] * sources,
        in_specs=[
            pl.BlockSpec((2, room, units), lambda i: (i, 0, 0)),
            pl.BlockSpec((2, room, units), lambda i: (i, 0, 0)),
            pl.BlockSpec((2, 2 * units, 2 * lanes), lambda i: (i, 0, 0)),
            whole(),
        ],
        out_specs=[whole()] * sources,
        scratch_shapes=[pltpu.VMEM((sources, slots, 2 * lanes), BF16)],
        compiler_params=vmem(32),
    )(hidden, swap(hidden), down_weight, back)

    routed = None
    for flip in range(steps - 1, -1, -1):
        mine = share[2 * flip].astype(F32) + hop(share[2 * flip + 1], 1).astype(F32)
        if flip:
            mine = hop(mine.astype(BF16), 2 * flip).astype(F32)
        routed = mine if routed is None else routed + mine
    lift = lax.dynamic_slice_in_dim(modulation[3], part * 2 * lanes, 2 * lanes, 0)
    return (state.astype(F32) + (1.0 + lift) * routed).astype(BF16)


def extended(cells, sides, width):
    for axis, dim in sides:
        count = lax.axis_size(axis)
        ends = count - 1
        head = lax.slice_in_dim(cells, 0, width, axis=dim)
        tail = lax.slice_in_dim(cells, cells.shape[dim] - width, cells.shape[dim], axis=dim)
        cells = jnp.concatenate(
            [
                lax.ppermute(tail, axis, [(i, (i + 1) % count) for i in range(ends)]),
                cells,
                lax.ppermute(head, axis, [((i + 1) % count, i) for i in range(ends)]),
            ],
            axis=dim,
        )
    return cells


def window_attention(query, keys, values, index, total):
    count = query.shape[0]
    rows = jnp.arange(count, dtype=jnp.int32)[:, None]
    cols = jnp.arange(3 * count, dtype=jnp.int32)[None, :] - count
    place = index * count + cols
    allowed = (jnp.abs(cols - rows) <= count) & (place >= 0) & (place < total)
    scores = jnp.einsum(
        "qhd,khd->hqk", query, keys, preferred_element_type=jnp.float32
    ) / math.sqrt(query.shape[2])
    scores = jnp.where(allowed[None], scores, NEG)
    top = jnp.max(scores, -1, keepdims=True)
    weight = jnp.exp(scores - top)
    weight = (weight / jnp.sum(weight, -1, keepdims=True)).astype(jnp.bfloat16)
    mixed = jnp.einsum("hqk,khd->qhd", weight, values, preferred_element_type=jnp.float32)
    return mixed.astype(jnp.bfloat16)


def normalize(state, modulation):
    scale = lax.rsqrt(jnp.mean(state * state, -1, keepdims=True) + EPS)
    return (state * scale * (1.0 + modulation[2]) + modulation[1]).astype(jnp.bfloat16)


def route(normed, router_weight, expert_ids):
    logits = jnp.dot(normed, router_weight, preferred_element_type=jnp.float32)
    experts = router_weight.shape[1]
    match = expert_ids[:, :, None] == jnp.arange(experts, dtype=jnp.int32)[None, None, :]
    picked = jnp.sum(jnp.where(match, logits[:, None, :], 0.0), -1)
    lifted = jax.nn.sigmoid(picked)
    return lifted / jnp.sum(lifted, -1, keepdims=True)


def exchanged_body(
    tokens,
    query_key_value,
    out_weight,
    modulation,
    router_weight,
    expert_ids,
    gate_up_weight,
    down_weight,
):
    count = tokens.shape[0]
    width = tokens.shape[1]
    parts = lax.axis_size("sub")
    part = lax.axis_index("sub")
    position = lax.axis_index("dev")
    devices = lax.axis_size("dev")
    total = count * devices
    local_width = query_key_value.shape[2]
    heads_here = local_width // HEAD
    query = query_key_value[:, 0].reshape(count, heads_here, HEAD)
    pair = query_key_value[:, 1:]
    near = extended(pair, (("dev", 0),), count)
    keys = near[:, 0].reshape(3 * count, heads_here, HEAD)
    values = near[:, 1].reshape(3 * count, heads_here, HEAD)
    mixed = window_attention(query, keys, values, position, total).reshape(count, local_width)
    partial_proj = lax.dot_general(
        mixed,
        lax.all_gather(out_weight, "dev", axis=0, tiled=True),
        (((1,), (1,)), ((), ())),
        preferred_element_type=jnp.float32,
    )
    proj = lax.psum(partial_proj, "sub")
    state = tokens.astype(jnp.float32) + (1.0 + modulation[0]) * proj
    normed = normalize(state, modulation)
    gates = route(normed, router_weight, expert_ids)
    experts = router_weight.shape[1]
    topk = expert_ids.shape[1]
    flat = expert_ids.reshape(-1)
    picks = flat.shape[0]
    onehot = (flat[:, None] == jnp.arange(experts, dtype=jnp.int32)[None, :]).astype(BF16)
    order = jnp.arange(picks, dtype=jnp.int32)
    earlier = (order[None, :] < order[:, None]).astype(BF16)
    ahead = jnp.dot(earlier, onehot, preferred_element_type=F32)
    rank = jnp.sum(ahead * onehot.astype(F32), 1).astype(jnp.int32)
    target = flat * CAP + rank
    hit = target[None, :] == jnp.arange(experts * CAP, dtype=jnp.int32)[:, None]
    owner = jnp.any(hit.reshape(experts * CAP, count, topk), 2).astype(BF16)
    slice_width = width // parts
    sent = lax.dynamic_slice_in_dim(normed, part * slice_width, slice_width, 1)
    sent_width = sent.shape[1]
    rows_out = jnp.dot(owner, sent, preferred_element_type=F32).astype(BF16)
    halves_here = gate_up_weight.shape[0]
    doubled = jnp.broadcast_to(
        rows_out.reshape(experts, 1, CAP, sent_width), (experts, 2, CAP, sent_width)
    )
    outgoing = doubled.reshape(devices, halves_here, CAP, sent_width)
    up_form = "sxcd,xgdf->sxcgf"
    down_form = "sxcf,xfd->sxcd"
    incoming = lax.all_to_all(outgoing, "dev", split_axis=0, concat_axis=0, tiled=True)
    both = jnp.einsum(
        up_form,
        lax.all_gather(incoming, "sub", axis=3, tiled=True),
        gate_up_weight,
        preferred_element_type=jnp.float32,
    )
    hidden = (jax.nn.silu(both[..., 0, :]) * both[..., 1, :]).astype(jnp.bfloat16)
    gathered = lax.all_gather(hidden, "sub", axis=hidden.ndim - 1, tiled=True)
    result = jnp.einsum(down_form, gathered, down_weight, preferred_element_type=jnp.float32)
    returned = lax.all_to_all(
        result.astype(jnp.bfloat16), "dev", split_axis=0, concat_axis=0, tiled=True
    )
    own_width = returned.shape[-1]
    arranged = returned.reshape(experts, 2, CAP, own_width)
    combined = arranged[:, 0].astype(F32) + arranged[:, 1].astype(F32)
    share = jnp.sum(
        jnp.where(hit.reshape(experts * CAP, count, topk), gates[None], 0.0), 2
    )
    routed = lax.dot_general(
        share,
        combined.reshape(experts * CAP, own_width),
        (((0,), (0,)), ((), ())),
        precision=lax.Precision.HIGHEST,
        preferred_element_type=F32,
    )
    own = lax.dynamic_slice_in_dim(state, part * slice_width, slice_width, 1)
    lift = lax.dynamic_slice_in_dim(modulation[3], part * slice_width, slice_width, 0)
    return (own + (1.0 + lift) * routed).astype(jnp.bfloat16)


def body(*arrays):
    tokens, router_weight, expert_ids, gate_up_weight = arrays[0], arrays[4], arrays[5], arrays[6]
    devices = lax.axis_size("dev")
    count, width = tokens.shape
    local = gate_up_weight.shape[0] // 2
    fits = (
        lax.axis_size("sub") == 2
        and devices >= 4
        and devices & (devices - 1) == 0
        and gate_up_weight.shape[0] % 2 == 0
        and width % (devices * 128) == 0
        and count % HEAD == 0
        and expert_ids.shape[1] * count <= width // 4
        and router_weight.shape[1] <= 256
    )
    if fits and count * devices <= 2 * local * devices * CAP:
        return gathered_body(*arrays)
    return exchanged_body(*arrays)


def solution(mesh):
    return jax.shard_map(
        body,
        mesh=mesh,
        in_specs=(
            P(("groups", "dev"), None),
            P(("groups", "dev"), None, "sub"),
            P("dev", "sub"),
            P("groups", None),
            P(),
            P(("groups", "dev"), None),
            P("dev", None, None, "sub"),
            P("dev", None, "sub"),
        ),
        out_specs=P(("groups", "dev"), "sub"),
        check_vma=False,
    )
```

```python
import functools
import math

import jax
import jax.numpy as jnp
from jax import lax
from jax.experimental import pallas as pl
from jax.experimental.pallas import tpu as pltpu
from jax.sharding import PartitionSpec as P

HEAD = 128
CAP = 12
SLOTS = 16
TILE = 16

EPS = 1e-06
NEG = -1e30
F32 = jnp.float32
BF16 = jnp.bfloat16

NT = (((1,), (1,)), ((), ()))


def vmem(mib):
    return pltpu.CompilerParams(vmem_limit_bytes=mib * 2**20)


def whole():
    return pl.BlockSpec(memory_space=pltpu.VMEM)


def cut_kernel(split, tokens_ref, weight_ref, ids_ref, near_ref, far_ref, sent_ref, row_ref):
    lanes = near_ref.shape[1]
    chunk = tokens_ref.shape[1] // lax.axis_size("dev")
    side = lax.axis_index("dev") % 2
    part = lax.axis_index("sub")
    for ref, parity in ((near_ref, side), (far_ref, 1 - side)):
        for i in range(lanes // chunk):
            at = pl.multiple_of(part * 2 * lanes + (2 * i + parity) * chunk, 128)
            ref[:, i * chunk : (i + 1) * chunk] = tokens_ref[:, pl.ds(at, chunk)]
    if split:
        rows = sent_ref.shape[0]
        at = pl.multiple_of(lax.axis_index("groups") * rows, TILE)
        sent_ref[...] = weight_ref[pl.ds(at, rows), :]
    else:
        sent_ref[...] = weight_ref[...]
    topk, count = ids_ref.shape
    row_ref[...] = jnp.zeros(row_ref.shape, BF16)
    for k in range(topk):
        named = jnp.broadcast_to(ids_ref[k : k + 1, :], (TILE, count))
        row_ref[:, k * count : (k + 1) * count] = named.astype(F32).astype(BF16)


def attention_kernel(own_ref, before_ref, after_ref, _, mixed_ref):
    count, width = mixed_ref.shape
    place = lax.axis_index("dev")
    last = lax.axis_size("dev") - 1
    row = lax.broadcasted_iota(jnp.int32, (count, count), 0)
    col = lax.broadcasted_iota(jnp.int32, (count, count), 1)
    see_before = (col >= row) & (place > 0)
    see_after = (col <= row) & (place < last)
    scale = 1.0 / math.sqrt(HEAD)

    def scored(q, k):
        return lax.dot_general(q, k, NT, preferred_element_type=F32) * scale

    for head in range(width // HEAD):
        lanes = slice(head * HEAD, (head + 1) * HEAD)
        q = own_ref[0, :, lanes]
        sb = jnp.where(see_before, scored(q, before_ref[0, :, lanes]), NEG)
        so = scored(q, own_ref[1, :, lanes])
        sa = jnp.where(see_after, scored(q, after_ref[0, :, lanes]), NEG)
        top = jnp.max(jnp.maximum(jnp.maximum(sb, so), sa), 1, keepdims=True)
        wb, wo, wa = jnp.exp(sb - top), jnp.exp(so - top), jnp.exp(sa - top)
        inv = 1.0 / jnp.sum(wb + wo + wa, 1, keepdims=True)
        out = 0.0
        for weight, value in (
            (wo, own_ref[2, :, lanes]),
            (wb, before_ref[1, :, lanes]),
            (wa, after_ref[1, :, lanes]),
        ):
            out += jnp.dot((weight * inv).astype(BF16), value, preferred_element_type=F32)
        mixed_ref[:, lanes] = out.astype(BF16)


def projection_kernel(steps, pieces, *refs):
    mixed_ref, other_ref = refs[0], refs[1]
    weight_refs = refs[2 : 2 + len(pieces)]
    keep_ref, send_ref, both_ref = refs[2 + len(pieces) :]
    count = mixed_ref.shape[0]
    half = steps // 2
    chunk = keep_ref.shape[1] // half
    z = lax.axis_index("dev") // 2
    part = lax.axis_index("sub")
    group = lax.axis_index("groups")
    for (hop, side), w_ref in zip(pieces, weight_refs):
        rows = w_ref.shape[0]
        target = jnp.bitwise_xor(z, hop)
        away = jnp.where(target // half == part, 0, 1)
        lane = (target % half) * chunk
        if side is not None:
            lane += (group if side == 0 else 1 - group) * rows
        lane = pl.multiple_of(lane, 128)
        for block, ref in enumerate((mixed_ref, other_ref)):
            both_ref[away, block * count : (block + 1) * count, pl.ds(lane, rows)] = (
                lax.dot_general(ref[...], w_ref[...], NT, preferred_element_type=F32)
            )
    keep_ref[...] = both_ref[0]
    send_ref[...] = both_ref[1]


def state_kernel(keep_ref, got_ref, near_ref, far_ref, ids_ref, mod_ref, out_ref):
    count, lanes = near_ref.shape
    chunk = mod_ref.shape[1] // lax.axis_size("dev")
    side = lax.axis_index("dev") % 2
    part = lax.axis_index("sub")
    for i in range(lanes // chunk):
        at = pl.multiple_of(part * 2 * lanes + (2 * i + side) * chunk, 128)
        lift = 1.0 + mod_ref[0:1, pl.ds(at, chunk)]
        cols = slice(i * chunk, (i + 1) * chunk)
        for block, ref in enumerate((near_ref, far_ref)):
            rows = slice(block * count, (block + 1) * count)
            proj = keep_ref[rows, cols] + got_ref[rows, cols]
            out_ref[rows, cols] = (ref[:, cols].astype(F32) + lift * proj).astype(BF16)
    out_ref[2 * count :, :] = ids_ref[...]


def select_kernel(local, topk, own, *refs):
    shard_refs, (mod_ref, router_ref, rows_ref, back_ref) = refs[:4], refs[4:8]
    state_ref = refs[8] if own else None
    full_ref, gate_ref = refs[-2:]
    count, width = full_ref.shape
    lanes = shard_refs[0].shape[1]
    device = lax.axis_index("dev")
    side = device % 2
    part = lax.axis_index("sub")
    chunk = width // lax.axis_size("dev")
    experts = router_ref.shape[0]
    slots = local * SLOTS
    before = lax.broadcasted_iota(jnp.int32, (count, count), 0)
    after = lax.broadcasted_iota(jnp.int32, (count, count), 1)
    earlier = (before < after).astype(F32).astype(BF16)
    slot = lax.broadcasted_iota(jnp.int32, (slots, count), 0) % SLOTS
    mine = lax.broadcasted_iota(jnp.int32, (local, count), 0) + device * local
    every = lax.broadcasted_iota(jnp.int32, (experts, count), 0)
    for cross in range(2):
        for far_half in range(2):
            for far_side in range(2):
                ref = shard_refs[2 * far_half + far_side]
                top = (cross ^ far_side) * count
                half = part if far_half == 0 else 1 - part
                parity = side if far_side == 0 else 1 - side
                for i in range(lanes // chunk):
                    block = ref[top : top + count, i * chunk : (i + 1) * chunk]
                    at = (2 * i + parity) * chunk
                    full_ref[:, pl.ds(pl.multiple_of(half * 2 * lanes + at, 128), chunk)] = block
                    if own and cross == 0 and far_half == 0:
                        state_ref[:, pl.ds(pl.multiple_of(at, 128), chunk)] = block
        state = full_ref[...].astype(F32)
        scale = lax.rsqrt(jnp.mean(state * state, 1, keepdims=True) + EPS)
        normed = state * scale * (1.0 + mod_ref[2:3, :]) + mod_ref[1:2, :]
        normed = normed.astype(BF16)
        ids = shard_refs[cross][2 * count : 2 * count + TILE, :]
        ids = ids.astype(F32)[0:1, :].astype(jnp.int32)
        named = [ids[:, k * count : (k + 1) * count] for k in range(topk)]
        hot = sum((mine == n).astype(F32) for n in named)
        rank = jnp.dot(hot.astype(BF16), earlier, preferred_element_type=F32)
        rank = jnp.where(hot > 0.0, rank, -1.0)
        rank = jnp.concatenate(
            [jnp.broadcast_to(rank[e : e + 1], (SLOTS, count)) for e in range(local)]
        )
        pick = rank == slot.astype(F32)
        chosen = jnp.dot(
            jnp.where(pick, 1.0, 0.0).astype(BF16), normed, preferred_element_type=F32
        ).astype(BF16)
        for e in range(local):
            rows_ref[e, cross * SLOTS : (cross + 1) * SLOTS, :] = chosen[
                e * SLOTS : (e + 1) * SLOTS
            ]
        logits = lax.dot_general(router_ref[...], normed, NT, preferred_element_type=F32)
        lifted = sum(jnp.where(every == n, 1.0, 0.0) for n in named) * jax.nn.sigmoid(logits)
        gate_ref[...] = lifted / jnp.sum(lifted, 0, keepdims=True)
        here = gate_ref[pl.ds(pl.multiple_of(device * local, local), local), :]
        here = jnp.concatenate(
            [jnp.broadcast_to(here[e : e + 1], (SLOTS, count)) for e in range(local)]
        )
        back_ref[cross] = jnp.where(pick, here, 0.0).T.astype(BF16)


def hidden_kernel(steps, *refs):
    rows_refs, (w_ref, hidden_ref) = refs[:steps], refs[steps:]

    def expert(e, _):
        rows = jnp.concatenate([ref[e] for ref in rows_refs])

        def product(member):
            weight = jnp.concatenate([w_ref[2 * e, member], w_ref[2 * e + 1, member]])
            return lax.dot_general(rows, weight, NT, preferred_element_type=F32)

        hidden_ref[e] = (jax.nn.silu(product(0)) * product(1)).astype(BF16)
        return 0

    lax.fori_loop(0, hidden_ref.shape[0], expert, 0, unroll=2)


def output_kernel(steps, near_ref, far_ref, w_ref, *refs):
    back_refs, out_refs, held_ref = refs[:steps], refs[steps : 3 * steps], refs[3 * steps]
    part = lax.axis_index("sub")
    units = near_ref.shape[2] // 2

    def expert(e, _):
        total = 0.0
        for ref, who in ((near_ref, part), (far_ref, 1 - part)):
            at = pl.multiple_of(who * units, 64)
            weight = jnp.concatenate([w_ref[2 * e + b, pl.ds(at, units), :] for b in range(2)])
            total += jnp.dot(ref[e], weight, preferred_element_type=F32)
        total = total.astype(BF16)
        row = pl.multiple_of(e * SLOTS, SLOTS)
        for source in range(2 * steps):
            held_ref[source, pl.ds(row, SLOTS), :] = total[source * SLOTS : (source + 1) * SLOTS]
        return 0

    lax.fori_loop(0, near_ref.shape[0], expert, 0, unroll=2)
    for source in range(2 * steps):
        out_refs[source][...] = jnp.dot(
            back_refs[source // 2][source % 2], held_ref[source], preferred_element_type=F32
        ).astype(BF16)


def gathered_body(
    tokens,
    query_key_value,
    out_weight,
    modulation,
    router_weight,
    expert_ids,
    gate_up_weight,
    down_weight,
):
    count, width = tokens.shape
    devices = lax.axis_size("dev")
    groups = lax.axis_size("groups")
    steps = devices // 2
    side = lax.axis_index("dev") % 2
    part = lax.axis_index("sub")
    group = lax.axis_index("groups")
    local_width = query_key_value.shape[2]
    chunk = width // devices
    lanes = width // 4
    halves_here = gate_up_weight.shape[0]
    local = halves_here // 2
    experts = router_weight.shape[1]
    topk = expert_ids.shape[1]
    struct = jax.ShapeDtypeStruct

    def hop(x, flip):
        return lax.ppermute(x, "dev", [(i, i ^ flip) for i in range(devices)])

    def swap(x):
        return lax.ppermute(x, "sub", [(0, 1), (1, 0)])

    stacked = query_key_value.transpose(1, 0, 2)
    pair = stacked[1:]
    before = lax.ppermute(pair, "dev", [(i, i + 1) for i in range(devices - 1)])
    after = lax.ppermute(pair, "dev", [(i + 1, i) for i in range(devices - 1)])

    split = groups == 2
    held = out_weight.shape[0] // (2 if split else 1)
    near, far, sent, ids = pl.pallas_call(
        functools.partial(cut_kernel, split),
        out_shape=[
            struct((count, lanes), BF16),
            struct((count, lanes), BF16),
            struct((held, local_width), BF16),
            struct((TILE, lanes), BF16),
        ],
        in_specs=[whole()] * 3,
        out_specs=[whole()] * 4,
        compiler_params=vmem(8),
    )(tokens, out_weight, expert_ids.T)
    far = hop(far, 1)

    pieces, weights = [(0, None)], [out_weight]
    for flip in range(1, steps):
        mine = hop(sent, 2 * flip)
        if split:
            theirs = lax.ppermute(mine, "groups", [(0, 1), (1, 0)])
            pieces += [(flip, 0), (flip, 1)]
            weights += [mine, theirs]
        else:
            pieces.append((flip, None))
            weights.append(mine)

    mixed = pl.pallas_call(
        attention_kernel,
        out_shape=struct((count, local_width), BF16),
        in_specs=[whole()] * 3 + [pl.BlockSpec(memory_space=pl.ANY)],
        out_specs=whole(),
        compiler_params=vmem(8),
    )(stacked, before, after, far)
    keep, send = pl.pallas_call(
        functools.partial(projection_kernel, steps, tuple(pieces)),
        out_shape=[struct((2 * count, lanes), F32)] * 2,
        in_specs=[whole()] * (2 + len(weights)),
        out_specs=[whole()] * 2,
        scratch_shapes=[pltpu.VMEM((2, 2 * count, lanes), F32)],
        compiler_params=vmem(10),
    )(mixed, hop(mixed, 1), *weights)
    shard = pl.pallas_call(
        state_kernel,
        out_shape=struct((2 * count + TILE, lanes), BF16),
        in_specs=[whole()] * 6,
        out_specs=whole(),
        compiler_params=vmem(10),
    )(keep, swap(send), near, far, ids, modulation)

    slots = local * SLOTS
    router = router_weight.T
    state = None
    picked, backs = [], []
    for flip in range(steps):
        block = shard if flip == 0 else hop(shard, 2 * flip)
        crossed = hop(block, 1)
        own = flip == 0
        results = pl.pallas_call(
            functools.partial(select_kernel, local, topk, own),
            out_shape=[
                struct((local, 2 * SLOTS, width), BF16),
                struct((2, count, slots), BF16),
            ]
            + ([struct((count, 2 * lanes), BF16)] if own else []),
            in_specs=[whole()] * 6,
            out_specs=[whole()] * (3 if own else 2),
            scratch_shapes=[pltpu.VMEM((count, width), BF16), pltpu.VMEM((experts, count), F32)],
            compiler_params=vmem(12),
        )(block, crossed, swap(block), swap(crossed), modulation, router)
        picked.append(results[0])
        backs.append(results[1])
        if own:
            state = results[2]

    sources = 2 * steps
    room = sources * SLOTS
    units = gate_up_weight.shape[3]
    hidden = pl.pallas_call(
        functools.partial(hidden_kernel, steps),
        out_shape=struct((local, room, 2 * units), BF16),
        in_specs=[whole()] * (steps + 1),
        out_specs=whole(),
        compiler_params=vmem(12),
    )(*picked, gate_up_weight.swapaxes(2, 3))
    share = pl.pallas_call(
        functools.partial(output_kernel, steps),
        out_shape=[struct((count, 2 * lanes), BF16)] * sources,
        in_specs=[whole()] * (3 + steps),
        out_specs=[whole()] * sources,
        scratch_shapes=[pltpu.VMEM((sources, slots, 2 * lanes), BF16)],
        compiler_params=vmem(8),
    )(hidden, swap(hidden), down_weight, *backs)

    routed = None
    for flip in range(steps - 1, -1, -1):
        mine = share[2 * flip].astype(F32) + hop(share[2 * flip + 1], 1).astype(F32)
        if flip:
            mine = hop(mine.astype(BF16), 2 * flip).astype(F32)
        routed = mine if routed is None else routed + mine
    lift = lax.dynamic_slice_in_dim(modulation[3], part * 2 * lanes, 2 * lanes, 0)
    return (state.astype(F32) + (1.0 + lift) * routed).astype(BF16)


def extended(cells, sides, width):
    for axis, dim in sides:
        count = lax.axis_size(axis)
        ends = count - 1
        head = lax.slice_in_dim(cells, 0, width, axis=dim)
        tail = lax.slice_in_dim(cells, cells.shape[dim] - width, cells.shape[dim], axis=dim)
        cells = jnp.concatenate(
            [
                lax.ppermute(tail, axis, [(i, (i + 1) % count) for i in range(ends)]),
                cells,
                lax.ppermute(head, axis, [((i + 1) % count, i) for i in range(ends)]),
            ],
            axis=dim,
        )
    return cells


def window_attention(query, keys, values, index, total):
    count = query.shape[0]
    rows = jnp.arange(count, dtype=jnp.int32)[:, None]
    cols = jnp.arange(3 * count, dtype=jnp.int32)[None, :] - count
    place = index * count + cols
    allowed = (jnp.abs(cols - rows) <= count) & (place >= 0) & (place < total)
    scores = jnp.einsum(
        "qhd,khd->hqk", query, keys, preferred_element_type=jnp.float32
    ) / math.sqrt(query.shape[2])
    scores = jnp.where(allowed[None], scores, NEG)
    top = jnp.max(scores, -1, keepdims=True)
    weight = jnp.exp(scores - top)
    weight = (weight / jnp.sum(weight, -1, keepdims=True)).astype(jnp.bfloat16)
    mixed = jnp.einsum("hqk,khd->qhd", weight, values, preferred_element_type=jnp.float32)
    return mixed.astype(jnp.bfloat16)


def normalize(state, modulation):
    scale = lax.rsqrt(jnp.mean(state * state, -1, keepdims=True) + EPS)
    return (state * scale * (1.0 + modulation[2]) + modulation[1]).astype(jnp.bfloat16)


def route(normed, router_weight, expert_ids):
    logits = jnp.dot(normed, router_weight, preferred_element_type=jnp.float32)
    experts = router_weight.shape[1]
    match = expert_ids[:, :, None] == jnp.arange(experts, dtype=jnp.int32)[None, None, :]
    picked = jnp.sum(jnp.where(match, logits[:, None, :], 0.0), -1)
    lifted = jax.nn.sigmoid(picked)
    return lifted / jnp.sum(lifted, -1, keepdims=True)


def exchanged_body(
    tokens,
    query_key_value,
    out_weight,
    modulation,
    router_weight,
    expert_ids,
    gate_up_weight,
    down_weight,
):
    count = tokens.shape[0]
    width = tokens.shape[1]
    parts = lax.axis_size("sub")
    part = lax.axis_index("sub")
    position = lax.axis_index("dev")
    devices = lax.axis_size("dev")
    total = count * devices
    local_width = query_key_value.shape[2]
    heads_here = local_width // HEAD
    query = query_key_value[:, 0].reshape(count, heads_here, HEAD)
    pair = query_key_value[:, 1:]
    near = extended(pair, (("dev", 0),), count)
    keys = near[:, 0].reshape(3 * count, heads_here, HEAD)
    values = near[:, 1].reshape(3 * count, heads_here, HEAD)
    mixed = window_attention(query, keys, values, position, total).reshape(count, local_width)
    partial_proj = lax.dot_general(
        mixed,
        lax.all_gather(out_weight, "dev", axis=0, tiled=True),
        (((1,), (1,)), ((), ())),
        preferred_element_type=jnp.float32,
    )
    proj = lax.psum(partial_proj, "sub")
    state = tokens.astype(jnp.float32) + (1.0 + modulation[0]) * proj
    normed = normalize(state, modulation)
    gates = route(normed, router_weight, expert_ids)
    experts = router_weight.shape[1]
    topk = expert_ids.shape[1]
    flat = expert_ids.reshape(-1)
    picks = flat.shape[0]
    onehot = (flat[:, None] == jnp.arange(experts, dtype=jnp.int32)[None, :]).astype(BF16)
    order = jnp.arange(picks, dtype=jnp.int32)
    earlier = (order[None, :] < order[:, None]).astype(BF16)
    ahead = jnp.dot(earlier, onehot, preferred_element_type=F32)
    rank = jnp.sum(ahead * onehot.astype(F32), 1).astype(jnp.int32)
    target = flat * CAP + rank
    hit = target[None, :] == jnp.arange(experts * CAP, dtype=jnp.int32)[:, None]
    owner = jnp.any(hit.reshape(experts * CAP, count, topk), 2).astype(BF16)
    slice_width = width // parts
    sent = lax.dynamic_slice_in_dim(normed, part * slice_width, slice_width, 1)
    sent_width = sent.shape[1]
    rows_out = jnp.dot(owner, sent, preferred_element_type=F32).astype(BF16)
    halves_here = gate_up_weight.shape[0]
    doubled = jnp.broadcast_to(
        rows_out.reshape(experts, 1, CAP, sent_width), (experts, 2, CAP, sent_width)
    )
    outgoing = doubled.reshape(devices, halves_here, CAP, sent_width)
    up_form = "sxcd,xgdf->sxcgf"
    down_form = "sxcf,xfd->sxcd"
    incoming = lax.all_to_all(outgoing, "dev", split_axis=0, concat_axis=0, tiled=True)
    both = jnp.einsum(
        up_form,
        lax.all_gather(incoming, "sub", axis=3, tiled=True),
        gate_up_weight,
        preferred_element_type=jnp.float32,
    )
    hidden = (jax.nn.silu(both[..., 0, :]) * both[..., 1, :]).astype(jnp.bfloat16)
    gathered = lax.all_gather(hidden, "sub", axis=hidden.ndim - 1, tiled=True)
    result = jnp.einsum(down_form, gathered, down_weight, preferred_element_type=jnp.float32)
    returned = lax.all_to_all(
        result.astype(jnp.bfloat16), "dev", split_axis=0, concat_axis=0, tiled=True
    )
    own_width = returned.shape[-1]
    arranged = returned.reshape(experts, 2, CAP, own_width)
    combined = arranged[:, 0].astype(F32) + arranged[:, 1].astype(F32)
    share = jnp.sum(
        jnp.where(hit.reshape(experts * CAP, count, topk), gates[None], 0.0), 2
    )
    routed = lax.dot_general(
        share,
        combined.reshape(experts * CAP, own_width),
        (((0,), (0,)), ((), ())),
        precision=lax.Precision.HIGHEST,
        preferred_element_type=F32,
    )
    own = lax.dynamic_slice_in_dim(state, part * slice_width, slice_width, 1)
    lift = lax.dynamic_slice_in_dim(modulation[3], part * slice_width, slice_width, 0)
    return (own + (1.0 + lift) * routed).astype(jnp.bfloat16)


def body(*arrays):
    tokens, router_weight, expert_ids, gate_up_weight = arrays[0], arrays[4], arrays[5], arrays[6]
    devices = lax.axis_size("dev")
    count, width = tokens.shape
    local = gate_up_weight.shape[0] // 2
    fits = (
        lax.axis_size("sub") == 2
        and devices >= 4
        and devices & (devices - 1) == 0
        and gate_up_weight.shape[0] % 2 == 0
        and width % (devices * 128) == 0
        and count % HEAD == 0
        and expert_ids.shape[1] * count <= width // 4
        and router_weight.shape[1] <= 256
    )
    if fits and count * devices <= 2 * local * devices * CAP:
        return gathered_body(*arrays)
    return exchanged_body(*arrays)


def solution(mesh):
    return jax.shard_map(
        body,
        mesh=mesh,
        in_specs=(
            P(("groups", "dev"), None),
            P(("groups", "dev"), None, "sub"),
            P("dev", "sub"),
            P("groups", None),
            P(),
            P(("groups", "dev"), None),
            P("dev", None, None, "sub"),
            P("dev", None, "sub"),
        ),
        out_specs=P(("groups", "dev"), "sub"),
        check_vma=False,
    )
```

```python
import functools
import math

import jax
import jax.numpy as jnp
from jax import lax
from jax.experimental import pallas as pl
from jax.experimental.pallas import tpu as pltpu
from jax.sharding import PartitionSpec as P

HEAD = 128
CAP = 12
SLOTS = 16
TILE = 16

EPS = 1e-06
NEG = -1e30
F32 = jnp.float32
BF16 = jnp.bfloat16

NT = (((1,), (1,)), ((), ()))


def vmem(mib):
    return pltpu.CompilerParams(vmem_limit_bytes=mib * 2**20)


def whole():
    return pl.BlockSpec(memory_space=pltpu.VMEM)


def cut_kernel(split, tokens_ref, pair_ref, weight_ref, ids_ref, near_ref, cross_ref, sent_ref, row_ref):
    count, lanes = near_ref.shape
    chunk = tokens_ref.shape[1] // lax.axis_size("dev")
    side = lax.axis_index("dev") % 2
    part = lax.axis_index("sub")
    half = count // 2
    cross_ref[: 2 * count] = pair_ref[...]
    for i in range(lanes // chunk):
        cols = slice(i * chunk, (i + 1) * chunk)
        at = pl.multiple_of(part * 2 * lanes + (2 * i + side) * chunk, 128)
        near_ref[:, cols] = tokens_ref[:, pl.ds(at, chunk)]
        at = pl.multiple_of(part * 2 * lanes + (2 * i + 1 - side) * chunk, 128)
        for j in range(2):
            cross_ref[2 * count :, j * lanes + i * chunk : j * lanes + (i + 1) * chunk] = (
                tokens_ref[j * half : (j + 1) * half, pl.ds(at, chunk)]
            )
    if split:
        rows = sent_ref.shape[0]
        at = pl.multiple_of(lax.axis_index("groups") * rows, TILE)
        sent_ref[...] = weight_ref[pl.ds(at, rows), :]
    else:
        sent_ref[...] = weight_ref[...]
    topk = ids_ref.shape[0]
    row_ref[...] = jnp.zeros(row_ref.shape, BF16)
    for k in range(topk):
        named = jnp.broadcast_to(ids_ref[k : k + 1, :], (TILE, count))
        row_ref[:, k * count : (k + 1) * count] = named.astype(F32).astype(BF16)


def attention_kernel(own_ref, cross_ref, next_ref, mixed_ref):
    count, width = mixed_ref.shape
    place = lax.axis_index("dev")
    even = place % 2 == 0
    row = lax.broadcasted_iota(jnp.int32, (count, count), 0)
    col = lax.broadcasted_iota(jnp.int32, (count, count), 1)
    alone = (place == 0) | (place == lax.axis_size("dev") - 1)
    see_cross = jnp.where(even, col - row, row - col) <= 0
    see_next = (jnp.where(even, row - col, col - row) <= 0) & jnp.logical_not(alone)
    scale = 1.0 / math.sqrt(HEAD)

    def scored(q, k):
        return lax.dot_general(q, k, NT, preferred_element_type=F32) * scale

    for head in range(width // HEAD):
        lanes = slice(head * HEAD, (head + 1) * HEAD)
        q = own_ref[0, :, lanes]
        sc = jnp.where(see_cross, scored(q, cross_ref[:count, lanes]), NEG)
        so = scored(q, own_ref[1, :, lanes])
        sn = jnp.where(see_next, scored(q, next_ref[:count, lanes]), NEG)
        top = jnp.max(jnp.maximum(jnp.maximum(sc, so), sn), 1, keepdims=True)
        wc, wo, wn = jnp.exp(sc - top), jnp.exp(so - top), jnp.exp(sn - top)
        inv = 1.0 / jnp.sum(wc + wo + wn, 1, keepdims=True)
        out = 0.0
        for weight, value in (
            (wo, own_ref[2, :, lanes]),
            (wc, cross_ref[count : 2 * count, lanes]),
            (wn, next_ref[count:, lanes]),
        ):
            out += jnp.dot((weight * inv).astype(BF16), value, preferred_element_type=F32)
        mixed_ref[:, lanes] = out.astype(BF16)


def projection_kernel(steps, pieces, *refs):
    mixed_ref, other_ref = refs[0], refs[1]
    weight_refs = refs[2 : 2 + len(pieces)]
    keep_ref, send_ref, both_ref = refs[2 + len(pieces) :]
    count = mixed_ref.shape[0]
    half = steps // 2
    chunk = keep_ref.shape[1] // half
    z = lax.axis_index("dev") // 2
    part = lax.axis_index("sub")
    group = lax.axis_index("groups")
    for (hop, side), w_ref in zip(pieces, weight_refs):
        rows = w_ref.shape[0]
        target = jnp.bitwise_xor(z, hop)
        away = jnp.where(target // half == part, 0, 1)
        lane = (target % half) * chunk
        if side is not None:
            lane += (group if side == 0 else 1 - group) * rows
        lane = pl.multiple_of(lane, 128)
        for block, ref in enumerate((mixed_ref, other_ref)):
            both_ref[away, block * count : (block + 1) * count, pl.ds(lane, rows)] = (
                lax.dot_general(ref[...], w_ref[...], NT, preferred_element_type=F32)
            )
    keep_ref[...] = both_ref[0]
    send_ref[...] = both_ref[1]


def state_kernel(keep_ref, got_ref, near_ref, cross_ref, ids_ref, mod_ref, out_ref):
    count, lanes = near_ref.shape
    half = count // 2
    chunk = mod_ref.shape[1] // lax.axis_size("dev")
    side = lax.axis_index("dev") % 2
    part = lax.axis_index("sub")
    for i in range(lanes // chunk):
        at = pl.multiple_of(part * 2 * lanes + (2 * i + side) * chunk, 128)
        lift = 1.0 + mod_ref[0:1, pl.ds(at, chunk)]
        cols = slice(i * chunk, (i + 1) * chunk)
        for j in range(4):
            rows = slice(j * half, (j + 1) * half)
            if j < 2:
                token = near_ref[rows, cols]
            else:
                left = (j - 2) * lanes + i * chunk
                token = cross_ref[2 * count :, left : left + chunk]
            proj = keep_ref[rows, cols] + got_ref[rows, cols]
            out_ref[rows, cols] = (token.astype(F32) + lift * proj).astype(BF16)
    out_ref[2 * count :, :] = ids_ref[...]


def select_kernel(local, topk, own, carried, *refs):
    shard_refs, (mod_ref, router_ref) = refs[:4], refs[4:6]
    rows_ref, back_ref = refs[6 + carried : 8 + carried]
    state_ref = refs[8 + carried] if own else None
    full_ref, gate_ref = refs[-2:]
    count, width = full_ref.shape
    lanes = shard_refs[0].shape[1]
    device = lax.axis_index("dev")
    side = device % 2
    part = lax.axis_index("sub")
    chunk = width // lax.axis_size("dev")
    experts = router_ref.shape[0]
    slots = local * SLOTS
    before = lax.broadcasted_iota(jnp.int32, (count, count), 0)
    after = lax.broadcasted_iota(jnp.int32, (count, count), 1)
    earlier = (before < after).astype(F32).astype(BF16)
    slot = lax.broadcasted_iota(jnp.int32, (slots, count), 0) % SLOTS
    mine = lax.broadcasted_iota(jnp.int32, (local, count), 0) + device * local
    every = lax.broadcasted_iota(jnp.int32, (experts, count), 0)
    for cross in range(2):
        for far_half in range(2):
            for far_side in range(2):
                ref = shard_refs[2 * far_half + far_side]
                top = (cross ^ far_side) * count
                half = part if far_half == 0 else 1 - part
                parity = side if far_side == 0 else 1 - side
                for i in range(lanes // chunk):
                    block = ref[top : top + count, i * chunk : (i + 1) * chunk]
                    at = (2 * i + parity) * chunk
                    full_ref[:, pl.ds(pl.multiple_of(half * 2 * lanes + at, 128), chunk)] = block
                    if own and cross == 0 and far_half == 0:
                        state_ref[:, pl.ds(pl.multiple_of(at, 128), chunk)] = block
        state = full_ref[...].astype(F32)
        scale = lax.rsqrt(jnp.mean(state * state, 1, keepdims=True) + EPS)
        normed = state * scale * (1.0 + mod_ref[2:3, :]) + mod_ref[1:2, :]
        normed = normed.astype(BF16)
        ids = shard_refs[cross][2 * count : 2 * count + TILE, :]
        ids = ids.astype(F32)[0:1, :].astype(jnp.int32)
        named = [ids[:, k * count : (k + 1) * count] for k in range(topk)]
        hot = sum((mine == n).astype(F32) for n in named)
        rank = jnp.dot(hot.astype(BF16), earlier, preferred_element_type=F32)
        rank = jnp.where(hot > 0.0, rank, -1.0)
        rank = jnp.concatenate(
            [jnp.broadcast_to(rank[e : e + 1], (SLOTS, count)) for e in range(local)]
        )
        pick = rank == slot.astype(F32)
        chosen = jnp.dot(
            jnp.where(pick, 1.0, 0.0).astype(BF16), normed, preferred_element_type=F32
        ).astype(BF16)
        for e in range(local):
            rows_ref[e, cross * SLOTS : (cross + 1) * SLOTS, :] = chosen[
                e * SLOTS : (e + 1) * SLOTS
            ]
        logits = lax.dot_general(router_ref[...], normed, NT, preferred_element_type=F32)
        lifted = sum(jnp.where(every == n, 1.0, 0.0) for n in named) * jax.nn.sigmoid(logits)
        gate_ref[...] = lifted / jnp.sum(lifted, 0, keepdims=True)
        here = gate_ref[pl.ds(pl.multiple_of(device * local, local), local), :]
        here = jnp.concatenate(
            [jnp.broadcast_to(here[e : e + 1], (SLOTS, count)) for e in range(local)]
        )
        back_ref[cross] = jnp.where(pick, here, 0.0).T.astype(BF16)


def hidden_kernel(steps, *refs):
    rows_refs, (w_ref, hidden_ref) = refs[:steps], refs[steps:]
    both = hidden_ref.shape[2]
    e = pl.program_id(0)
    rows = jnp.concatenate([ref[e] for ref in rows_refs])
    weight = jnp.concatenate([w_ref[b, g] for g in range(2) for b in range(2)])
    product = lax.dot_general(rows, weight, NT, preferred_element_type=F32)
    hidden_ref[0] = (jax.nn.silu(product[:, :both]) * product[:, both:]).astype(BF16)


def output_kernel(steps, near_ref, far_ref, w_ref, *refs):
    back_refs, out_refs, held_ref = refs[:steps], refs[steps : 3 * steps], refs[3 * steps]
    part = lax.axis_index("sub")
    units = near_ref.shape[2] // 2

    def expert(e, _):
        total = 0.0
        for ref, who in ((near_ref, part), (far_ref, 1 - part)):
            at = pl.multiple_of(who * units, 64)
            weight = jnp.concatenate([w_ref[2 * e + b, pl.ds(at, units), :] for b in range(2)])
            total += jnp.dot(ref[e], weight, preferred_element_type=F32)
        total = total.astype(BF16)
        row = pl.multiple_of(e * SLOTS, SLOTS)
        for source in range(2 * steps):
            held_ref[source, pl.ds(row, SLOTS), :] = total[source * SLOTS : (source + 1) * SLOTS]
        return 0

    lax.fori_loop(0, near_ref.shape[0], expert, 0, unroll=2)
    for source in range(2 * steps):
        out_refs[source][...] = jnp.dot(
            back_refs[source // 2][source % 2], held_ref[source], preferred_element_type=F32
        ).astype(BF16)


def gathered_body(
    tokens,
    query_key_value,
    out_weight,
    modulation,
    router_weight,
    expert_ids,
    gate_up_weight,
    down_weight,
):
    count, width = tokens.shape
    devices = lax.axis_size("dev")
    groups = lax.axis_size("groups")
    steps = devices // 2
    side = lax.axis_index("dev") % 2
    part = lax.axis_index("sub")
    group = lax.axis_index("groups")
    local_width = query_key_value.shape[2]
    chunk = width // devices
    lanes = width // 4
    halves_here = gate_up_weight.shape[0]
    local = halves_here // 2
    experts = router_weight.shape[1]
    topk = expert_ids.shape[1]
    struct = jax.ShapeDtypeStruct

    def hop(x, flip):
        return lax.ppermute(x, "dev", [(i, i ^ flip) for i in range(devices)])

    def swap(x):
        return lax.ppermute(x, "sub", [(0, 1), (1, 0)])

    stacked = query_key_value.transpose(1, 0, 2)
    pair = stacked[1:].reshape(2 * count, local_width)
    odd = [(i, i + 1) for i in range(1, devices - 1, 2)]
    after = lax.ppermute(pair, "dev", odd + [(j, i) for i, j in odd])
    split = groups == 2
    held = out_weight.shape[0] // (2 if split else 1)
    near, cross, sent, ids = pl.pallas_call(
        functools.partial(cut_kernel, split),
        out_shape=[
            struct((count, lanes), BF16),
            struct((2 * count + count // 2, local_width), BF16),
            struct((held, local_width), BF16),
            struct((TILE, lanes), BF16),
        ],
        in_specs=[whole()] * 4,
        out_specs=[whole()] * 4,
        compiler_params=vmem(8),
    )(tokens, pair, out_weight, expert_ids.T)
    cross = hop(cross, 1)

    pieces, weights = [(0, None), (1, None)], [out_weight, hop(out_weight, 2)]
    for flip in range(2, steps):
        mine = hop(sent, 2 * flip)
        if split:
            theirs = lax.ppermute(mine, "groups", [(0, 1), (1, 0)])
            pieces += [(flip, 0), (flip, 1)]
            weights += [mine, theirs]
        else:
            pieces.append((flip, None))
            weights.append(mine)

    gate_up = gate_up_weight.swapaxes(2, 3)
    mixed = pl.pallas_call(
        attention_kernel,
        out_shape=struct((count, local_width), BF16),
        in_specs=[whole()] * 3,
        out_specs=whole(),
        compiler_params=vmem(8),
    )(stacked, cross, after)
    keep, send = pl.pallas_call(
        functools.partial(projection_kernel, steps, tuple(pieces)),
        out_shape=[struct((2 * count, lanes), F32)] * 2,
        in_specs=[whole()] * (2 + len(weights)),
        out_specs=[whole()] * 2,
        scratch_shapes=[pltpu.VMEM((2, 2 * count, lanes), F32)],
        compiler_params=vmem(6),
    )(mixed, hop(mixed, 1), *weights)
    shard = pl.pallas_call(
        state_kernel,
        out_shape=struct((2 * count + TILE, lanes), BF16),
        in_specs=[whole()] * 6,
        out_specs=whole(),
        compiler_params=vmem(6),
    )(keep, swap(send), near, cross, ids, modulation)

    slots = local * SLOTS
    router = router_weight.T
    state = None
    picked, backs = [], []
    column = {0: shard}
    for flip in range(1, steps):
        low = flip & -flip
        column[flip] = hop(column[flip - low], 2 * low)
    for flip in range(steps):
        block = column[flip]
        crossed = hop(block, 1)
        own = flip == 0
        later = steps - 1 if flip == steps - 3 else None
        out_shape = [
            struct((local, 2 * SLOTS, width), BF16),
            struct((2, count, slots), BF16),
        ]
        out_specs = [whole()] * 2
        if own:
            out_shape.append(struct((count, 2 * lanes), BF16))
            out_specs.append(whole())
        inputs = [block, crossed, swap(block), swap(crossed), modulation, router]
        in_specs = [whole()] * 6
        aliases = {}
        if later is not None:
            inputs.append(column[later])
            in_specs.append(pl.BlockSpec(memory_space=pl.ANY))
            aliases = {6: len(out_shape)}
            out_shape.append(struct(shard.shape, BF16))
            out_specs.append(pl.BlockSpec(memory_space=pl.ANY))
        results = pl.pallas_call(
            functools.partial(select_kernel, local, topk, own, later is not None),
            out_shape=out_shape,
            in_specs=in_specs,
            out_specs=out_specs,
            scratch_shapes=[pltpu.VMEM((count, width), BF16), pltpu.VMEM((experts, count), F32)],
            input_output_aliases=aliases,
            compiler_params=vmem(6),
        )(*inputs)
        picked.append(results[0])
        backs.append(results[1])
        if own:
            state = results[2]
        if later is not None:
            column[later] = results[-1]

    sources = 2 * steps
    room = sources * SLOTS
    units = gate_up_weight.shape[3]
    hidden = pl.pallas_call(
        functools.partial(hidden_kernel, steps),
        grid=(local,),
        out_shape=struct((local, room, 2 * units), BF16),
        in_specs=[whole()] * steps
        + [pl.BlockSpec((2, 2, units, width), lambda e: (e, 0, 0, 0))],
        out_specs=pl.BlockSpec((1, room, 2 * units), lambda e: (e, 0, 0)),
        compiler_params=vmem(40),
    )(*picked, gate_up)
    share = pl.pallas_call(
        functools.partial(output_kernel, steps),
        out_shape=[struct((count, 2 * lanes), BF16)] * sources,
        in_specs=[whole()] * (3 + steps),
        out_specs=[whole()] * sources,
        scratch_shapes=[pltpu.VMEM((sources, slots, 2 * lanes), BF16)],
        compiler_params=vmem(8),
    )(hidden, swap(hidden), down_weight, *backs)

    routed = None
    for flip in range(steps - 1, -1, -1):
        mine = share[2 * flip].astype(F32) + hop(share[2 * flip + 1], 1).astype(F32)
        if flip:
            mine = hop(mine.astype(BF16), 2 * flip).astype(F32)
        routed = mine if routed is None else routed + mine
    lift = lax.dynamic_slice_in_dim(modulation[3], part * 2 * lanes, 2 * lanes, 0)
    return (state.astype(F32) + (1.0 + lift) * routed).astype(BF16)


def extended(cells, sides, width):
    for axis, dim in sides:
        count = lax.axis_size(axis)
        ends = count - 1
        head = lax.slice_in_dim(cells, 0, width, axis=dim)
        tail = lax.slice_in_dim(cells, cells.shape[dim] - width, cells.shape[dim], axis=dim)
        cells = jnp.concatenate(
            [
                lax.ppermute(tail, axis, [(i, (i + 1) % count) for i in range(ends)]),
                cells,
                lax.ppermute(head, axis, [((i + 1) % count, i) for i in range(ends)]),
            ],
            axis=dim,
        )
    return cells


def window_attention(query, keys, values, index, total):
    count = query.shape[0]
    rows = jnp.arange(count, dtype=jnp.int32)[:, None]
    cols = jnp.arange(3 * count, dtype=jnp.int32)[None, :] - count
    place = index * count + cols
    allowed = (jnp.abs(cols - rows) <= count) & (place >= 0) & (place < total)
    scores = jnp.einsum(
        "qhd,khd->hqk", query, keys, preferred_element_type=jnp.float32
    ) / math.sqrt(query.shape[2])
    scores = jnp.where(allowed[None], scores, NEG)
    top = jnp.max(scores, -1, keepdims=True)
    weight = jnp.exp(scores - top)
    weight = (weight / jnp.sum(weight, -1, keepdims=True)).astype(jnp.bfloat16)
    mixed = jnp.einsum("hqk,khd->qhd", weight, values, preferred_element_type=jnp.float32)
    return mixed.astype(jnp.bfloat16)


def normalize(state, modulation):
    scale = lax.rsqrt(jnp.mean(state * state, -1, keepdims=True) + EPS)
    return (state * scale * (1.0 + modulation[2]) + modulation[1]).astype(jnp.bfloat16)


def route(normed, router_weight, expert_ids):
    logits = jnp.dot(normed, router_weight, preferred_element_type=jnp.float32)
    experts = router_weight.shape[1]
    match = expert_ids[:, :, None] == jnp.arange(experts, dtype=jnp.int32)[None, None, :]
    picked = jnp.sum(jnp.where(match, logits[:, None, :], 0.0), -1)
    lifted = jax.nn.sigmoid(picked)
    return lifted / jnp.sum(lifted, -1, keepdims=True)


def exchanged_body(
    tokens,
    query_key_value,
    out_weight,
    modulation,
    router_weight,
    expert_ids,
    gate_up_weight,
    down_weight,
):
    count = tokens.shape[0]
    width = tokens.shape[1]
    parts = lax.axis_size("sub")
    part = lax.axis_index("sub")
    position = lax.axis_index("dev")
    devices = lax.axis_size("dev")
    total = count * devices
    local_width = query_key_value.shape[2]
    heads_here = local_width // HEAD
    query = query_key_value[:, 0].reshape(count, heads_here, HEAD)
    pair = query_key_value[:, 1:]
    near = extended(pair, (("dev", 0),), count)
    keys = near[:, 0].reshape(3 * count, heads_here, HEAD)
    values = near[:, 1].reshape(3 * count, heads_here, HEAD)
    mixed = window_attention(query, keys, values, position, total).reshape(count, local_width)
    partial_proj = lax.dot_general(
        mixed,
        lax.all_gather(out_weight, "dev", axis=0, tiled=True),
        (((1,), (1,)), ((), ())),
        preferred_element_type=jnp.float32,
    )
    proj = lax.psum(partial_proj, "sub")
    state = tokens.astype(jnp.float32) + (1.0 + modulation[0]) * proj
    normed = normalize(state, modulation)
    gates = route(normed, router_weight, expert_ids)
    experts = router_weight.shape[1]
    topk = expert_ids.shape[1]
    flat = expert_ids.reshape(-1)
    picks = flat.shape[0]
    onehot = (flat[:, None] == jnp.arange(experts, dtype=jnp.int32)[None, :]).astype(BF16)
    order = jnp.arange(picks, dtype=jnp.int32)
    earlier = (order[None, :] < order[:, None]).astype(BF16)
    ahead = jnp.dot(earlier, onehot, preferred_element_type=F32)
    rank = jnp.sum(ahead * onehot.astype(F32), 1).astype(jnp.int32)
    target = flat * CAP + rank
    hit = target[None, :] == jnp.arange(experts * CAP, dtype=jnp.int32)[:, None]
    owner = jnp.any(hit.reshape(experts * CAP, count, topk), 2).astype(BF16)
    slice_width = width // parts
    sent = lax.dynamic_slice_in_dim(normed, part * slice_width, slice_width, 1)
    sent_width = sent.shape[1]
    rows_out = jnp.dot(owner, sent, preferred_element_type=F32).astype(BF16)
    halves_here = gate_up_weight.shape[0]
    doubled = jnp.broadcast_to(
        rows_out.reshape(experts, 1, CAP, sent_width), (experts, 2, CAP, sent_width)
    )
    outgoing = doubled.reshape(devices, halves_here, CAP, sent_width)
    up_form = "sxcd,xgdf->sxcgf"
    down_form = "sxcf,xfd->sxcd"
    incoming = lax.all_to_all(outgoing, "dev", split_axis=0, concat_axis=0, tiled=True)
    both = jnp.einsum(
        up_form,
        lax.all_gather(incoming, "sub", axis=3, tiled=True),
        gate_up_weight,
        preferred_element_type=jnp.float32,
    )
    hidden = (jax.nn.silu(both[..., 0, :]) * both[..., 1, :]).astype(jnp.bfloat16)
    gathered = lax.all_gather(hidden, "sub", axis=hidden.ndim - 1, tiled=True)
    result = jnp.einsum(down_form, gathered, down_weight, preferred_element_type=jnp.float32)
    returned = lax.all_to_all(
        result.astype(jnp.bfloat16), "dev", split_axis=0, concat_axis=0, tiled=True
    )
    own_width = returned.shape[-1]
    arranged = returned.reshape(experts, 2, CAP, own_width)
    combined = arranged[:, 0].astype(F32) + arranged[:, 1].astype(F32)
    share = jnp.sum(
        jnp.where(hit.reshape(experts * CAP, count, topk), gates[None], 0.0), 2
    )
    routed = lax.dot_general(
        share,
        combined.reshape(experts * CAP, own_width),
        (((0,), (0,)), ((), ())),
        precision=lax.Precision.HIGHEST,
        preferred_element_type=F32,
    )
    own = lax.dynamic_slice_in_dim(state, part * slice_width, slice_width, 1)
    lift = lax.dynamic_slice_in_dim(modulation[3], part * slice_width, slice_width, 0)
    return (own + (1.0 + lift) * routed).astype(jnp.bfloat16)


def body(*arrays):
    tokens, router_weight, expert_ids, gate_up_weight = arrays[0], arrays[4], arrays[5], arrays[6]
    devices = lax.axis_size("dev")
    count, width = tokens.shape
    local = gate_up_weight.shape[0] // 2
    fits = (
        lax.axis_size("sub") == 2
        and devices >= 4
        and devices & (devices - 1) == 0
        and gate_up_weight.shape[0] % 2 == 0
        and width % (devices * 128) == 0
        and arrays[1].shape[2] * 2 == width
        and count % HEAD == 0
        and expert_ids.shape[1] * count <= width // 4
        and router_weight.shape[1] <= 256
    )
    if fits and count * devices <= 2 * local * devices * CAP:
        return gathered_body(*arrays)
    return exchanged_body(*arrays)


def solution(mesh):
    return jax.shard_map(
        body,
        mesh=mesh,
        in_specs=(
            P(("groups", "dev"), None),
            P(("groups", "dev"), None, "sub"),
            P("dev", "sub"),
            P("groups", None),
            P(),
            P(("groups", "dev"), None),
            P("dev", None, None, "sub"),
            P("dev", None, "sub"),
        ),
        out_specs=P(("groups", "dev"), "sub"),
        check_vma=False,
    )
```

```python
import functools
import math

import jax
import jax.numpy as jnp
from jax import lax
from jax.experimental import pallas as pl
from jax.experimental.pallas import tpu as pltpu
from jax.sharding import PartitionSpec as P

HEAD = 128
CAP = 12
SLOTS = 16
TILE = 16

EPS = 1e-06
NEG = -1e30
F32 = jnp.float32
BF16 = jnp.bfloat16

NT = (((1,), (1,)), ((), ()))


def vmem(mib):
    return pltpu.CompilerParams(vmem_limit_bytes=mib * 2**20)


def whole():
    return pl.BlockSpec(memory_space=pltpu.VMEM)


def cut_kernel(split, tokens_ref, qkv_ref, weight_ref, *refs):
    query_ref, pair_ref, near_ref, cross_ref, sent_ref, own_ref, sem_ref = refs
    count, lanes = near_ref.shape
    chunk = tokens_ref.shape[1] // lax.axis_size("dev")
    side = lax.axis_index("dev") % 2
    part = lax.axis_index("sub")
    half = count // 2
    moves = [
        (qkv_ref.at[1], pair_ref.at[:count]),
        (qkv_ref.at[2], pair_ref.at[count:]),
        (qkv_ref.at[1], cross_ref.at[:count]),
        (qkv_ref.at[2], cross_ref.at[count : 2 * count]),
    ]
    for i in range(lanes // chunk):
        at = pl.multiple_of(part * 2 * lanes + (2 * i + 1 - side) * chunk, 128)
        for j in range(2):
            left = j * lanes + i * chunk
            moves.append(
                (
                    tokens_ref.at[j * half : (j + 1) * half, pl.ds(at, chunk)],
                    cross_ref.at[2 * count :, left : left + chunk],
                )
            )
        at = pl.multiple_of(part * 2 * lanes + (2 * i + side) * chunk, 128)
        moves.append(
            (tokens_ref.at[:, pl.ds(at, chunk)], near_ref.at[:, i * chunk : (i + 1) * chunk])
        )
    rows = sent_ref.shape[0]
    at = pl.multiple_of(lax.axis_index("groups") * rows if split else 0, TILE)
    moves += [
        (weight_ref.at[pl.ds(at, rows)], sent_ref),
        (qkv_ref.at[0], query_ref),
        (weight_ref, own_ref),
    ]
    copies = [pltpu.make_async_copy(*move, sem_ref.at[n]) for n, move in enumerate(moves)]
    for copy in copies:
        copy.start()
    for copy in copies:
        copy.wait()


def small_kernel(ids_ref, mod_ref, router_ref, _, row_ref, mod_to_ref, router_to_ref):
    topk, count = ids_ref.shape
    row_ref[...] = jnp.zeros(row_ref.shape, BF16)
    for k in range(topk):
        named = jnp.broadcast_to(ids_ref[k : k + 1, :], (TILE, count))
        row_ref[:, k * count : (k + 1) * count] = named.astype(F32).astype(BF16)
    mod_to_ref[...] = mod_ref[...]
    router_to_ref[...] = router_ref[...]


def attention_kernel(query_ref, own_ref, cross_ref, next_ref, _, mixed_ref):
    count, width = mixed_ref.shape
    place = lax.axis_index("dev")
    even = place % 2 == 0
    row = lax.broadcasted_iota(jnp.int32, (count, count), 0)
    col = lax.broadcasted_iota(jnp.int32, (count, count), 1)
    alone = (place == 0) | (place == lax.axis_size("dev") - 1)
    see_cross = jnp.where(even, col - row, row - col) <= 0
    see_next = (jnp.where(even, row - col, col - row) <= 0) & jnp.logical_not(alone)
    scale = 1.0 / math.sqrt(HEAD)

    def scored(q, k):
        return lax.dot_general(q, k, NT, preferred_element_type=F32) * scale

    for head in range(width // HEAD):
        lanes = slice(head * HEAD, (head + 1) * HEAD)
        q = query_ref[:, lanes]
        sc = jnp.where(see_cross, scored(q, cross_ref[:count, lanes]), NEG)
        so = scored(q, own_ref[:count, lanes])
        sn = jnp.where(see_next, scored(q, next_ref[:count, lanes]), NEG)
        top = jnp.max(jnp.maximum(jnp.maximum(sc, so), sn), 1, keepdims=True)
        wc, wo, wn = jnp.exp(sc - top), jnp.exp(so - top), jnp.exp(sn - top)
        inv = 1.0 / jnp.sum(wc + wo + wn, 1, keepdims=True)
        out = 0.0
        for weight, value in (
            (wo, own_ref[count:, lanes]),
            (wc, cross_ref[count : 2 * count, lanes]),
            (wn, next_ref[count:, lanes]),
        ):
            out += jnp.dot((weight * inv).astype(BF16), value, preferred_element_type=F32)
        mixed_ref[:, lanes] = out.astype(BF16)


def projection_kernel(steps, pieces, *refs):
    mixed_ref, other_ref = refs[0], refs[1]
    weight_refs = refs[2 : 2 + len(pieces)]
    keep_ref, send_ref, both_ref = refs[2 + len(pieces) :]
    count = mixed_ref.shape[0]
    half = steps // 2
    chunk = keep_ref.shape[1] // half
    z = lax.axis_index("dev") // 2
    part = lax.axis_index("sub")
    group = lax.axis_index("groups")
    for (hop, side), w_ref in zip(pieces, weight_refs):
        rows = w_ref.shape[0]
        target = jnp.bitwise_xor(z, hop)
        away = jnp.where(target // half == part, 0, 1)
        lane = (target % half) * chunk
        if side is not None:
            lane += (group if side == 0 else 1 - group) * rows
        lane = pl.multiple_of(lane, 128)
        for block, ref in enumerate((mixed_ref, other_ref)):
            both_ref[away, block * count : (block + 1) * count, pl.ds(lane, rows)] = (
                lax.dot_general(ref[...], w_ref[...], NT, preferred_element_type=F32)
            )
    keep_ref[...] = both_ref[0]
    send_ref[...] = both_ref[1]


def state_kernel(keep_ref, got_ref, near_ref, cross_ref, ids_ref, mod_ref, out_ref):
    count, lanes = near_ref.shape
    half = count // 2
    chunk = mod_ref.shape[1] // lax.axis_size("dev")
    side = lax.axis_index("dev") % 2
    part = lax.axis_index("sub")
    for i in range(lanes // chunk):
        at = pl.multiple_of(part * 2 * lanes + (2 * i + side) * chunk, 128)
        lift = 1.0 + mod_ref[0:1, pl.ds(at, chunk)]
        cols = slice(i * chunk, (i + 1) * chunk)
        for j in range(4):
            rows = slice(j * half, (j + 1) * half)
            if j < 2:
                token = near_ref[rows, cols]
            else:
                left = (j - 2) * lanes + i * chunk
                token = cross_ref[2 * count :, left : left + chunk]
            proj = keep_ref[rows, cols] + got_ref[rows, cols]
            out_ref[rows, cols] = (token.astype(F32) + lift * proj).astype(BF16)
    out_ref[2 * count :, :] = ids_ref[...]


def tie_kernel(*refs):
    pass


def tie(array, *others):
    anywhere = pl.BlockSpec(memory_space=pl.ANY)
    return pl.pallas_call(
        tie_kernel,
        out_shape=jax.ShapeDtypeStruct(array.shape, array.dtype),
        in_specs=[anywhere] * (1 + len(others)),
        out_specs=anywhere,
        input_output_aliases={0: 0},
        compiler_params=vmem(1),
    )(array, *others)


def select_kernel(local, topk, own, carried, *refs):
    shard_refs, (mod_ref, router_ref) = refs[:4], refs[4:6]
    rows_ref, back_ref = refs[6 + carried : 8 + carried]
    state_ref = refs[8 + carried] if own else None
    full_ref, gate_ref = refs[-2:]
    count, width = full_ref.shape
    lanes = shard_refs[0].shape[1]
    device = lax.axis_index("dev")
    side = device % 2
    part = lax.axis_index("sub")
    chunk = width // lax.axis_size("dev")
    experts = router_ref.shape[0]
    slots = local * SLOTS
    before = lax.broadcasted_iota(jnp.int32, (count, count), 0)
    after = lax.broadcasted_iota(jnp.int32, (count, count), 1)
    earlier = (before < after).astype(F32).astype(BF16)
    slot = lax.broadcasted_iota(jnp.int32, (slots, count), 0) % SLOTS
    mine = lax.broadcasted_iota(jnp.int32, (local, count), 0) + device * local
    every = lax.broadcasted_iota(jnp.int32, (experts, count), 0)
    for cross in range(2):
        for far_half in range(2):
            for far_side in range(2):
                ref = shard_refs[2 * far_half + far_side]
                top = (cross ^ far_side) * count
                half = part if far_half == 0 else 1 - part
                parity = side if far_side == 0 else 1 - side
                for i in range(lanes // chunk):
                    block = ref[top : top + count, i * chunk : (i + 1) * chunk]
                    at = (2 * i + parity) * chunk
                    full_ref[:, pl.ds(pl.multiple_of(half * 2 * lanes + at, 128), chunk)] = block
                    if own and cross == 0 and far_half == 0:
                        state_ref[:, pl.ds(pl.multiple_of(at, 128), chunk)] = block
        state = full_ref[...].astype(F32)
        scale = lax.rsqrt(jnp.mean(state * state, 1, keepdims=True) + EPS)
        normed = state * scale * (1.0 + mod_ref[2:3, :]) + mod_ref[1:2, :]
        normed = normed.astype(BF16)
        ids = shard_refs[cross][2 * count : 2 * count + TILE, :]
        ids = ids.astype(F32)[0:1, :].astype(jnp.int32)
        named = [ids[:, k * count : (k + 1) * count] for k in range(topk)]
        hot = sum((mine == n).astype(F32) for n in named)
        rank = jnp.dot(hot.astype(BF16), earlier, preferred_element_type=F32)
        rank = jnp.where(hot > 0.0, rank, -1.0)
        rank = jnp.concatenate(
            [jnp.broadcast_to(rank[e : e + 1], (SLOTS, count)) for e in range(local)]
        )
        pick = rank == slot.astype(F32)
        chosen = jnp.dot(
            jnp.where(pick, 1.0, 0.0).astype(BF16), normed, preferred_element_type=F32
        ).astype(BF16)
        for e in range(local):
            rows_ref[e, cross * SLOTS : (cross + 1) * SLOTS, :] = chosen[
                e * SLOTS : (e + 1) * SLOTS
            ]
        logits = lax.dot_general(router_ref[...], normed, NT, preferred_element_type=F32)
        lifted = sum(jnp.where(every == n, 1.0, 0.0) for n in named) * jax.nn.sigmoid(logits)
        gate_ref[...] = lifted / jnp.sum(lifted, 0, keepdims=True)
        here = gate_ref[pl.ds(pl.multiple_of(device * local, local), local), :]
        here = jnp.concatenate(
            [jnp.broadcast_to(here[e : e + 1], (SLOTS, count)) for e in range(local)]
        )
        back_ref[cross] = jnp.where(pick, here, 0.0).T.astype(BF16)


def load_kernel(local, up_ref, down_ref, _, *refs):
    to_refs, done_ref, sem_ref = refs[: 2 * local], refs[2 * local], refs[2 * local + 1]
    copies = []
    for n, ref in enumerate(to_refs):
        e = n % local
        whole_ref = up_ref if n < local else down_ref
        copies.append(
            pltpu.make_async_copy(whole_ref.at[2 * e : 2 * e + 2], ref, sem_ref.at[n])
        )
    for copy in copies:
        copy.start()
    done_ref[...] = jnp.zeros(done_ref.shape, F32)
    for copy in copies:
        copy.wait()


def hidden_kernel(steps, *refs):
    rows_refs, w_refs, hidden_ref = refs[:steps], refs[steps:-1], refs[-1]
    both = hidden_ref.shape[2]
    for e, w_ref in enumerate(w_refs):
        rows = jnp.concatenate([ref[e] for ref in rows_refs])
        weight = jnp.concatenate([w_ref[b, g] for g in range(2) for b in range(2)])
        product = lax.dot_general(rows, weight, NT, preferred_element_type=F32)
        hidden_ref[e] = (jax.nn.silu(product[:, :both]) * product[:, both:]).astype(BF16)


def output_kernel(steps, local, near_ref, far_ref, *refs):
    w_refs, back_refs = refs[:local], refs[local : local + steps]
    out_refs, held_ref = refs[local + steps : local + 3 * steps], refs[-1]
    part = lax.axis_index("sub")
    units = near_ref.shape[2] // 2
    for e, w_ref in enumerate(w_refs):
        total = 0.0
        for ref, who in ((near_ref, part), (far_ref, 1 - part)):
            at = pl.multiple_of(who * units, 64)
            weight = jnp.concatenate([w_ref[b, pl.ds(at, units), :] for b in range(2)])
            total += jnp.dot(ref[e], weight, preferred_element_type=F32)
        total = total.astype(BF16)
        for source in range(2 * steps):
            held_ref[source, e * SLOTS : (e + 1) * SLOTS, :] = total[
                source * SLOTS : (source + 1) * SLOTS
            ]
    for source in range(2 * steps):
        out_refs[source][...] = jnp.dot(
            back_refs[source // 2][source % 2], held_ref[source], preferred_element_type=F32
        ).astype(BF16)


def final_kernel(state_ref, mod_ref, *refs):
    routed = sum(ref[...].astype(F32) for ref in refs[:-1])
    lanes = state_ref.shape[1]
    at = pl.multiple_of(lax.axis_index("sub") * lanes, 128)
    lift = 1.0 + mod_ref[3:4, pl.ds(at, lanes)]
    refs[-1][...] = (state_ref[...].astype(F32) + lift * routed).astype(BF16)


def gathered_body(
    tokens,
    query_key_value,
    out_weight,
    modulation,
    router_weight,
    expert_ids,
    gate_up_weight,
    down_weight,
):
    count, width = tokens.shape
    devices = lax.axis_size("dev")
    groups = lax.axis_size("groups")
    steps = devices // 2
    local_width = query_key_value.shape[2]
    chunk = width // devices
    lanes = width // 4
    halves_here = gate_up_weight.shape[0]
    local = halves_here // 2
    experts = router_weight.shape[1]
    topk = expert_ids.shape[1]
    struct = jax.ShapeDtypeStruct

    def hop(x, flip):
        return lax.ppermute(x, "dev", [(i, i ^ flip) for i in range(devices)])

    def swap(x):
        return lax.ppermute(x, "sub", [(0, 1), (1, 0)])

    split = groups == 2
    held = out_weight.shape[0] // (2 if split else 1)
    query, pair, near, cross, sent, own_weight = pl.pallas_call(
        functools.partial(cut_kernel, split),
        out_shape=[
            struct((count, local_width), BF16),
            struct((2 * count, local_width), BF16),
            struct((count, lanes), BF16),
            struct((2 * count + count // 2, local_width), BF16),
            struct((held, local_width), BF16),
            struct(out_weight.shape, BF16),
        ],
        in_specs=[pl.BlockSpec(memory_space=pl.ANY)] * 3,
        out_specs=[whole()] * 6,
        scratch_shapes=[pltpu.SemaphoreType.DMA((7 + 3 * (lanes // chunk),))],
        compiler_params=vmem(52),
    )(tokens, query_key_value.transpose(1, 0, 2), out_weight)
    ids, small, router = pl.pallas_call(
        small_kernel,
        out_shape=[
            struct((TILE, lanes), BF16),
            struct(modulation.shape, F32),
            struct((experts, width), BF16),
        ],
        in_specs=[whole()] * 3 + [pl.BlockSpec(memory_space=pl.ANY)],
        out_specs=[whole()] * 3,
        compiler_params=vmem(4),
    )(expert_ids.T, modulation, router_weight.T, query)
    odd = [(i, i + 1) for i in range(1, devices - 1, 2)]
    after = lax.ppermute(pair, "dev", odd + [(j, i) for i, j in odd])
    cross = hop(cross, 1)

    pieces, weights = [(0, None), (1, None)], [own_weight, hop(own_weight, 2)]
    mine = {0: sent}
    for flip in range(2, steps):
        low = flip & -flip
        if flip > 2 and flip - low > 0:
            mine[flip] = hop(mine[flip - low], 2 * low)
        else:
            mine[flip] = hop(sent, 2 * flip)
        if split:
            theirs = lax.ppermute(mine[flip], "groups", [(0, 1), (1, 0)])
            pieces += [(flip, 0), (flip, 1)]
            weights += [mine[flip], theirs]
        else:
            pieces.append((flip, None))
            weights.append(mine[flip])

    mixed = pl.pallas_call(
        attention_kernel,
        out_shape=struct((count, local_width), BF16),
        in_specs=[whole()] * 4 + [pl.BlockSpec(memory_space=pl.ANY)],
        out_specs=whole(),
        compiler_params=vmem(6),
    )(query, pair, cross, after, small)
    keep, send = pl.pallas_call(
        functools.partial(projection_kernel, steps, tuple(pieces)),
        out_shape=[struct((2 * count, lanes), F32)] * 2,
        in_specs=[whole()] * (2 + len(weights)),
        out_specs=[whole()] * 2,
        scratch_shapes=[pltpu.VMEM((2, 2 * count, lanes), F32)],
        compiler_params=vmem(6),
    )(mixed, hop(mixed, 1), *weights)
    shard = pl.pallas_call(
        state_kernel,
        out_shape=struct((2 * count + TILE, lanes), BF16),
        in_specs=[whole()] * 6,
        out_specs=whole(),
        compiler_params=vmem(6),
    )(keep, swap(send), near, cross, ids, small)

    units = gate_up_weight.shape[3]
    *loaded, done = pl.pallas_call(
        functools.partial(load_kernel, local),
        out_shape=[struct((2, 2, units, width), BF16)] * local
        + [struct((2, *down_weight.shape[1:]), BF16)] * local
        + [struct((8, 128), F32)],
        in_specs=[pl.BlockSpec(memory_space=pl.ANY)] * 3,
        out_specs=[whole()] * (2 * local + 1),
        scratch_shapes=[pltpu.SemaphoreType.DMA((2 * local,))],
        compiler_params=vmem(14),
    )(gate_up_weight.swapaxes(2, 3), down_weight, shard)

    slots = local * SLOTS
    state = None
    picked, backs = [], []
    column = {0: shard}
    for flip in range(1, steps):
        low = flip & -flip
        column[flip] = hop(column[flip - low], 2 * low)
    across = hop(shard, 1)
    column[1] = tie(column[1], across, done)
    for flip in range(steps):
        block = column[flip]
        crossed = hop(block, 1) if flip else across
        own = flip == 0
        later = steps - 1 if flip == steps - 3 else None
        out_shape = [
            struct((local, 2 * SLOTS, width), BF16),
            struct((2, count, slots), BF16),
        ]
        out_specs = [whole()] * 2
        if own:
            out_shape.append(struct((count, 2 * lanes), BF16))
            out_specs.append(whole())
        inputs = [block, crossed, swap(block), swap(crossed), small, router]
        in_specs = [whole()] * 6
        aliases = {}
        if later is not None:
            inputs.append(column[later])
            in_specs.append(pl.BlockSpec(memory_space=pl.ANY))
            aliases = {6: len(out_shape)}
            out_shape.append(struct(shard.shape, BF16))
            out_specs.append(pl.BlockSpec(memory_space=pl.ANY))
        results = pl.pallas_call(
            functools.partial(select_kernel, local, topk, own, later is not None),
            out_shape=out_shape,
            in_specs=in_specs,
            out_specs=out_specs,
            scratch_shapes=[pltpu.VMEM((count, width), BF16), pltpu.VMEM((experts, count), F32)],
            input_output_aliases=aliases,
            compiler_params=vmem(6),
        )(*inputs)
        picked.append(results[0])
        backs.append(results[1])
        if own:
            state = results[2]
        if later is not None:
            column[later] = results[-1]

    sources = 2 * steps
    room = sources * SLOTS
    hidden = pl.pallas_call(
        functools.partial(hidden_kernel, steps),
        out_shape=struct((local, room, 2 * units), BF16),
        in_specs=[whole()] * (steps + local),
        out_specs=whole(),
        compiler_params=vmem(6),
    )(*picked, *loaded[:local])
    share = pl.pallas_call(
        functools.partial(output_kernel, steps, local),
        out_shape=[struct((count, 2 * lanes), BF16)] * sources,
        in_specs=[whole()] * (2 + local + steps),
        out_specs=[whole()] * sources,
        scratch_shapes=[pltpu.VMEM((sources, slots, 2 * lanes), BF16)],
        compiler_params=vmem(8),
    )(hidden, swap(hidden), *loaded[local:], *backs)

    terms = [share[0]]
    for flip in range(steps - 1, -1, -1):
        crossed = hop(share[2 * flip + 1], 1)
        if flip:
            crossed = (share[2 * flip].astype(F32) + crossed.astype(F32)).astype(BF16)
            crossed = hop(crossed, 2 * flip)
        terms.append(crossed)
    return pl.pallas_call(
        final_kernel,
        out_shape=struct((count, 2 * lanes), BF16),
        in_specs=[whole()] * (2 + len(terms)),
        out_specs=whole(),
        compiler_params=vmem(8),
    )(state, small, *terms)


def extended(cells, sides, width):
    for axis, dim in sides:
        count = lax.axis_size(axis)
        ends = count - 1
        head = lax.slice_in_dim(cells, 0, width, axis=dim)
        tail = lax.slice_in_dim(cells, cells.shape[dim] - width, cells.shape[dim], axis=dim)
        cells = jnp.concatenate(
            [
                lax.ppermute(tail, axis, [(i, (i + 1) % count) for i in range(ends)]),
                cells,
                lax.ppermute(head, axis, [((i + 1) % count, i) for i in range(ends)]),
            ],
            axis=dim,
        )
    return cells


def window_attention(query, keys, values, index, total):
    count = query.shape[0]
    rows = jnp.arange(count, dtype=jnp.int32)[:, None]
    cols = jnp.arange(3 * count, dtype=jnp.int32)[None, :] - count
    place = index * count + cols
    allowed = (jnp.abs(cols - rows) <= count) & (place >= 0) & (place < total)
    scores = jnp.einsum(
        "qhd,khd->hqk", query, keys, preferred_element_type=jnp.float32
    ) / math.sqrt(query.shape[2])
    scores = jnp.where(allowed[None], scores, NEG)
    top = jnp.max(scores, -1, keepdims=True)
    weight = jnp.exp(scores - top)
    weight = (weight / jnp.sum(weight, -1, keepdims=True)).astype(jnp.bfloat16)
    mixed = jnp.einsum("hqk,khd->qhd", weight, values, preferred_element_type=jnp.float32)
    return mixed.astype(jnp.bfloat16)


def normalize(state, modulation):
    scale = lax.rsqrt(jnp.mean(state * state, -1, keepdims=True) + EPS)
    return (state * scale * (1.0 + modulation[2]) + modulation[1]).astype(jnp.bfloat16)


def route(normed, router_weight, expert_ids):
    logits = jnp.dot(normed, router_weight, preferred_element_type=jnp.float32)
    experts = router_weight.shape[1]
    match = expert_ids[:, :, None] == jnp.arange(experts, dtype=jnp.int32)[None, None, :]
    picked = jnp.sum(jnp.where(match, logits[:, None, :], 0.0), -1)
    lifted = jax.nn.sigmoid(picked)
    return lifted / jnp.sum(lifted, -1, keepdims=True)


def exchanged_body(
    tokens,
    query_key_value,
    out_weight,
    modulation,
    router_weight,
    expert_ids,
    gate_up_weight,
    down_weight,
):
    count = tokens.shape[0]
    width = tokens.shape[1]
    parts = lax.axis_size("sub")
    part = lax.axis_index("sub")
    position = lax.axis_index("dev")
    devices = lax.axis_size("dev")
    total = count * devices
    local_width = query_key_value.shape[2]
    heads_here = local_width // HEAD
    query = query_key_value[:, 0].reshape(count, heads_here, HEAD)
    pair = query_key_value[:, 1:]
    near = extended(pair, (("dev", 0),), count)
    keys = near[:, 0].reshape(3 * count, heads_here, HEAD)
    values = near[:, 1].reshape(3 * count, heads_here, HEAD)
    mixed = window_attention(query, keys, values, position, total).reshape(count, local_width)
    partial_proj = lax.dot_general(
        mixed,
        lax.all_gather(out_weight, "dev", axis=0, tiled=True),
        (((1,), (1,)), ((), ())),
        preferred_element_type=jnp.float32,
    )
    proj = lax.psum(partial_proj, "sub")
    state = tokens.astype(jnp.float32) + (1.0 + modulation[0]) * proj
    normed = normalize(state, modulation)
    gates = route(normed, router_weight, expert_ids)
    experts = router_weight.shape[1]
    topk = expert_ids.shape[1]
    flat = expert_ids.reshape(-1)
    picks = flat.shape[0]
    onehot = (flat[:, None] == jnp.arange(experts, dtype=jnp.int32)[None, :]).astype(BF16)
    order = jnp.arange(picks, dtype=jnp.int32)
    earlier = (order[None, :] < order[:, None]).astype(BF16)
    ahead = jnp.dot(earlier, onehot, preferred_element_type=F32)
    rank = jnp.sum(ahead * onehot.astype(F32), 1).astype(jnp.int32)
    target = flat * CAP + rank
    hit = target[None, :] == jnp.arange(experts * CAP, dtype=jnp.int32)[:, None]
    owner = jnp.any(hit.reshape(experts * CAP, count, topk), 2).astype(BF16)
    slice_width = width // parts
    sent = lax.dynamic_slice_in_dim(normed, part * slice_width, slice_width, 1)
    sent_width = sent.shape[1]
    rows_out = jnp.dot(owner, sent, preferred_element_type=F32).astype(BF16)
    halves_here = gate_up_weight.shape[0]
    doubled = jnp.broadcast_to(
        rows_out.reshape(experts, 1, CAP, sent_width), (experts, 2, CAP, sent_width)
    )
    outgoing = doubled.reshape(devices, halves_here, CAP, sent_width)
    up_form = "sxcd,xgdf->sxcgf"
    down_form = "sxcf,xfd->sxcd"
    incoming = lax.all_to_all(outgoing, "dev", split_axis=0, concat_axis=0, tiled=True)
    both = jnp.einsum(
        up_form,
        lax.all_gather(incoming, "sub", axis=3, tiled=True),
        gate_up_weight,
        preferred_element_type=jnp.float32,
    )
    hidden = (jax.nn.silu(both[..., 0, :]) * both[..., 1, :]).astype(jnp.bfloat16)
    gathered = lax.all_gather(hidden, "sub", axis=hidden.ndim - 1, tiled=True)
    result = jnp.einsum(down_form, gathered, down_weight, preferred_element_type=jnp.float32)
    returned = lax.all_to_all(
        result.astype(jnp.bfloat16), "dev", split_axis=0, concat_axis=0, tiled=True
    )
    own_width = returned.shape[-1]
    arranged = returned.reshape(experts, 2, CAP, own_width)
    combined = arranged[:, 0].astype(F32) + arranged[:, 1].astype(F32)
    share = jnp.sum(
        jnp.where(hit.reshape(experts * CAP, count, topk), gates[None], 0.0), 2
    )
    routed = lax.dot_general(
        share,
        combined.reshape(experts * CAP, own_width),
        (((0,), (0,)), ((), ())),
        precision=lax.Precision.HIGHEST,
        preferred_element_type=F32,
    )
    own = lax.dynamic_slice_in_dim(state, part * slice_width, slice_width, 1)
    lift = lax.dynamic_slice_in_dim(modulation[3], part * slice_width, slice_width, 0)
    return (own + (1.0 + lift) * routed).astype(jnp.bfloat16)


def body(*arrays):
    tokens, router_weight, expert_ids, gate_up_weight = arrays[0], arrays[4], arrays[5], arrays[6]
    devices = lax.axis_size("dev")
    count, width = tokens.shape
    local = gate_up_weight.shape[0] // 2
    fits = (
        lax.axis_size("sub") == 2
        and devices >= 4
        and devices & (devices - 1) == 0
        and gate_up_weight.shape[0] % 2 == 0
        and width % (devices * 128) == 0
        and arrays[1].shape[2] * 2 == width
        and count % HEAD == 0
        and expert_ids.shape[1] * count <= width // 4
        and router_weight.shape[1] <= 256
    )
    if fits and count * devices <= 2 * local * devices * CAP:
        return gathered_body(*arrays)
    return exchanged_body(*arrays)


def solution(mesh):
    return jax.shard_map(
        body,
        mesh=mesh,
        in_specs=(
            P(("groups", "dev"), None),
            P(("groups", "dev"), None, "sub"),
            P("dev", "sub"),
            P("groups", None),
            P(),
            P(("groups", "dev"), None),
            P("dev", None, None, "sub"),
            P("dev", None, "sub"),
        ),
        out_specs=P(("groups", "dev"), "sub"),
        check_vma=False,
    )
```

```python
import functools
import math

import jax
import jax.numpy as jnp
from jax import lax
from jax.experimental import pallas as pl
from jax.experimental.pallas import tpu as pltpu
from jax.sharding import PartitionSpec as P

HEAD = 128
CAP = 12
SLOTS = 16
TILE = 16

EPS = 1e-06
NEG = -1e30
F32 = jnp.float32
BF16 = jnp.bfloat16

NT = (((1,), (1,)), ((), ()))


def vmem(mib):
    return pltpu.CompilerParams(vmem_limit_bytes=mib * 2**20)


def whole():
    return pl.BlockSpec(memory_space=pltpu.VMEM)


def cut_kernel(split, tokens_ref, qkv_ref, weight_ref, *refs):
    query_ref, pair_ref, near_ref, cross_ref, sent_ref, own_ref, sem_ref = refs
    count, lanes = near_ref.shape
    chunk = tokens_ref.shape[1] // lax.axis_size("dev")
    side = lax.axis_index("dev") % 2
    part = lax.axis_index("sub")
    half = count // 2
    moves = [
        (qkv_ref.at[1], pair_ref.at[:count]),
        (qkv_ref.at[2], pair_ref.at[count:]),
        (qkv_ref.at[1], cross_ref.at[:count]),
        (qkv_ref.at[2], cross_ref.at[count : 2 * count]),
    ]
    for i in range(lanes // chunk):
        at = pl.multiple_of(part * 2 * lanes + (2 * i + 1 - side) * chunk, 128)
        for j in range(2):
            left = j * lanes + i * chunk
            moves.append(
                (
                    tokens_ref.at[j * half : (j + 1) * half, pl.ds(at, chunk)],
                    cross_ref.at[2 * count :, left : left + chunk],
                )
            )
        at = pl.multiple_of(part * 2 * lanes + (2 * i + side) * chunk, 128)
        moves.append(
            (tokens_ref.at[:, pl.ds(at, chunk)], near_ref.at[:, i * chunk : (i + 1) * chunk])
        )
    rows = sent_ref.shape[0]
    at = pl.multiple_of(lax.axis_index("groups") * rows if split else 0, TILE)
    moves += [
        (weight_ref.at[pl.ds(at, rows)], sent_ref),
        (qkv_ref.at[0], query_ref),
        (weight_ref, own_ref),
    ]
    copies = [pltpu.make_async_copy(*move, sem_ref.at[n]) for n, move in enumerate(moves)]
    for copy in copies:
        copy.start()
    for copy in copies:
        copy.wait()


def small_kernel(ids_ref, mod_ref, router_ref, _, row_ref, mod_to_ref, router_to_ref):
    topk, count = ids_ref.shape
    row_ref[...] = jnp.zeros(row_ref.shape, BF16)
    for k in range(topk):
        named = jnp.broadcast_to(ids_ref[k : k + 1, :], (TILE, count))
        row_ref[:, k * count : (k + 1) * count] = named.astype(F32).astype(BF16)
    mod_to_ref[...] = mod_ref[...]
    router_to_ref[...] = router_ref[...]


def attention_kernel(query_ref, own_ref, cross_ref, next_ref, *refs):
    mixed_ref = refs[-1]
    count, width = mixed_ref.shape
    place = lax.axis_index("dev")
    even = place % 2 == 0
    row = lax.broadcasted_iota(jnp.int32, (count, count), 0)
    col = lax.broadcasted_iota(jnp.int32, (count, count), 1)
    alone = (place == 0) | (place == lax.axis_size("dev") - 1)
    see_cross = jnp.where(even, col - row, row - col) <= 0
    see_next = (jnp.where(even, row - col, col - row) <= 0) & jnp.logical_not(alone)
    scale = 1.0 / math.sqrt(HEAD)

    def scored(q, k):
        return lax.dot_general(q, k, NT, preferred_element_type=F32) * scale

    for head in range(width // HEAD):
        lanes = slice(head * HEAD, (head + 1) * HEAD)
        q = query_ref[:, lanes]
        sc = jnp.where(see_cross, scored(q, cross_ref[:count, lanes]), NEG)
        so = scored(q, own_ref[:count, lanes])
        sn = jnp.where(see_next, scored(q, next_ref[:count, lanes]), NEG)
        top = jnp.max(jnp.maximum(jnp.maximum(sc, so), sn), 1, keepdims=True)
        wc, wo, wn = jnp.exp(sc - top), jnp.exp(so - top), jnp.exp(sn - top)
        inv = 1.0 / jnp.sum(wc + wo + wn, 1, keepdims=True)
        out = 0.0
        for weight, value in (
            (wo, own_ref[count:, lanes]),
            (wc, cross_ref[count : 2 * count, lanes]),
            (wn, next_ref[count:, lanes]),
        ):
            out += jnp.dot((weight * inv).astype(BF16), value, preferred_element_type=F32)
        mixed_ref[:, lanes] = out.astype(BF16)


def projection_kernel(steps, pieces, *refs):
    mixed_ref, other_ref = refs[0], refs[1]
    weight_refs = refs[2 : 2 + len(pieces)]
    keep_ref, send_ref, both_ref = refs[2 + len(pieces) :]
    count = mixed_ref.shape[0]
    half = steps // 2
    chunk = keep_ref.shape[1] // half
    z = lax.axis_index("dev") // 2
    part = lax.axis_index("sub")
    group = lax.axis_index("groups")
    for (hop, side), w_ref in zip(pieces, weight_refs):
        rows = w_ref.shape[0]
        target = jnp.bitwise_xor(z, hop)
        away = jnp.where(target // half == part, 0, 1)
        lane = (target % half) * chunk
        if side is not None:
            lane += (group if side == 0 else 1 - group) * rows
        lane = pl.multiple_of(lane, 128)
        for block, ref in enumerate((mixed_ref, other_ref)):
            both_ref[away, block * count : (block + 1) * count, pl.ds(lane, rows)] = (
                lax.dot_general(ref[...], w_ref[...], NT, preferred_element_type=F32)
            )
    keep_ref[...] = both_ref[0]
    send_ref[...] = both_ref[1]


def state_kernel(keep_ref, got_ref, near_ref, cross_ref, ids_ref, mod_ref, out_ref):
    count, lanes = near_ref.shape
    half = count // 2
    chunk = mod_ref.shape[1] // lax.axis_size("dev")
    side = lax.axis_index("dev") % 2
    part = lax.axis_index("sub")
    for i in range(lanes // chunk):
        at = pl.multiple_of(part * 2 * lanes + (2 * i + side) * chunk, 128)
        lift = 1.0 + mod_ref[0:1, pl.ds(at, chunk)]
        cols = slice(i * chunk, (i + 1) * chunk)
        for j in range(4):
            rows = slice(j * half, (j + 1) * half)
            if j < 2:
                token = near_ref[rows, cols]
            else:
                left = (j - 2) * lanes + i * chunk
                token = cross_ref[2 * count :, left : left + chunk]
            proj = keep_ref[rows, cols] + got_ref[rows, cols]
            out_ref[rows, cols] = (token.astype(F32) + lift * proj).astype(BF16)
    out_ref[2 * count :, :] = ids_ref[...]


def tie_kernel(*refs):
    pass


def tie(array, *others):
    anywhere = pl.BlockSpec(memory_space=pl.ANY)
    return pl.pallas_call(
        tie_kernel,
        out_shape=jax.ShapeDtypeStruct(array.shape, array.dtype),
        in_specs=[anywhere] * (1 + len(others)),
        out_specs=anywhere,
        input_output_aliases={0: 0},
        compiler_params=vmem(1),
    )(array, *others)


def select_kernel(local, topk, own, *refs):
    shard_refs, (mod_ref, router_ref) = refs[:4], refs[4:6]
    rows_ref, back_ref = refs[6:8]
    state_ref = refs[8] if own else None
    full_ref, gate_ref = refs[-2:]
    count, width = full_ref.shape
    lanes = shard_refs[0].shape[1]
    device = lax.axis_index("dev")
    side = device % 2
    part = lax.axis_index("sub")
    chunk = width // lax.axis_size("dev")
    experts = router_ref.shape[0]
    slots = local * SLOTS
    before = lax.broadcasted_iota(jnp.int32, (count, count), 0)
    after = lax.broadcasted_iota(jnp.int32, (count, count), 1)
    earlier = (before < after).astype(F32).astype(BF16)
    slot = lax.broadcasted_iota(jnp.int32, (slots, count), 0) % SLOTS
    mine = lax.broadcasted_iota(jnp.int32, (local, count), 0) + device * local
    every = lax.broadcasted_iota(jnp.int32, (experts, count), 0)
    for cross in range(2):
        for far_half in range(2):
            for far_side in range(2):
                ref = shard_refs[2 * far_half + far_side]
                top = (cross ^ far_side) * count
                half = part if far_half == 0 else 1 - part
                parity = side if far_side == 0 else 1 - side
                for i in range(lanes // chunk):
                    block = ref[top : top + count, i * chunk : (i + 1) * chunk]
                    at = (2 * i + parity) * chunk
                    full_ref[:, pl.ds(pl.multiple_of(half * 2 * lanes + at, 128), chunk)] = block
                    if own and cross == 0 and far_half == 0:
                        state_ref[:, pl.ds(pl.multiple_of(at, 128), chunk)] = block
        state = full_ref[...].astype(F32)
        scale = lax.rsqrt(jnp.mean(state * state, 1, keepdims=True) + EPS)
        normed = state * scale * (1.0 + mod_ref[2:3, :]) + mod_ref[1:2, :]
        normed = normed.astype(BF16)
        ids = shard_refs[cross][2 * count : 2 * count + TILE, :]
        ids = ids.astype(F32)[0:1, :].astype(jnp.int32)
        named = [ids[:, k * count : (k + 1) * count] for k in range(topk)]
        hot = sum((mine == n).astype(F32) for n in named)
        rank = jnp.dot(hot.astype(BF16), earlier, preferred_element_type=F32)
        rank = jnp.where(hot > 0.0, rank, -1.0)
        rank = jnp.concatenate(
            [jnp.broadcast_to(rank[e : e + 1], (SLOTS, count)) for e in range(local)]
        )
        pick = rank == slot.astype(F32)
        chosen = jnp.dot(
            jnp.where(pick, 1.0, 0.0).astype(BF16), normed, preferred_element_type=F32
        ).astype(BF16)
        for e in range(local):
            rows_ref[e, cross * SLOTS : (cross + 1) * SLOTS, :] = chosen[
                e * SLOTS : (e + 1) * SLOTS
            ]
        logits = lax.dot_general(router_ref[...], normed, NT, preferred_element_type=F32)
        lifted = sum(jnp.where(every == n, 1.0, 0.0) for n in named) * jax.nn.sigmoid(logits)
        gate_ref[...] = lifted / jnp.sum(lifted, 0, keepdims=True)
        here = gate_ref[pl.ds(pl.multiple_of(device * local, local), local), :]
        here = jnp.concatenate(
            [jnp.broadcast_to(here[e : e + 1], (SLOTS, count)) for e in range(local)]
        )
        back_ref[cross] = jnp.where(pick, here, 0.0).T.astype(BF16)


def load_kernel(local, up_ref, down_ref, _, *refs):
    to_refs, done_ref, sem_ref = refs[: 2 * local], refs[2 * local], refs[2 * local + 1]
    copies = []
    for n, ref in enumerate(to_refs):
        e = n % local
        whole_ref = up_ref if n < local else down_ref
        copies.append(
            pltpu.make_async_copy(whole_ref.at[2 * e : 2 * e + 2], ref, sem_ref.at[n])
        )
    for copy in copies:
        copy.start()
    done_ref[...] = jnp.zeros(done_ref.shape, F32)
    for copy in copies:
        copy.wait()


def hidden_kernel(steps, *refs):
    rows_refs, w_refs, hidden_ref = refs[:steps], refs[steps:-1], refs[-1]
    for e, w_ref in enumerate(w_refs):
        rows = jnp.concatenate([ref[e] for ref in rows_refs])
        halves = []
        for b in range(2):
            gate = lax.dot_general(w_ref[b, 0], rows, NT, preferred_element_type=F32)
            up = lax.dot_general(w_ref[b, 1], rows, NT, preferred_element_type=F32)
            halves.append(jax.nn.silu(gate) * up)
        hidden_ref[e] = jnp.concatenate(halves).T.astype(BF16)


def output_kernel(steps, local, near_ref, far_ref, *refs):
    w_refs, back_refs = refs[:local], refs[local : local + steps]
    out_refs, held_ref = refs[local + steps : local + 3 * steps], refs[-1]
    part = lax.axis_index("sub")
    units = near_ref.shape[2] // 2
    for e, w_ref in enumerate(w_refs):
        total = 0.0
        for ref, who in ((near_ref, part), (far_ref, 1 - part)):
            at = pl.multiple_of(who * units, 64)
            weight = jnp.concatenate([w_ref[b, pl.ds(at, units), :] for b in range(2)])
            total += jnp.dot(ref[e], weight, preferred_element_type=F32)
        total = total.astype(BF16)
        for source in range(2 * steps):
            held_ref[source, e * SLOTS : (e + 1) * SLOTS, :] = total[
                source * SLOTS : (source + 1) * SLOTS
            ]
    for source in range(2 * steps):
        out_refs[source][...] = jnp.dot(
            back_refs[source // 2][source % 2], held_ref[source], preferred_element_type=F32
        ).astype(BF16)


def final_kernel(state_ref, mod_ref, *refs):
    routed = sum(ref[...].astype(F32) for ref in refs[:-1])
    lanes = state_ref.shape[1]
    at = pl.multiple_of(lax.axis_index("sub") * lanes, 128)
    lift = 1.0 + mod_ref[3:4, pl.ds(at, lanes)]
    refs[-1][...] = (state_ref[...].astype(F32) + lift * routed).astype(BF16)


def gathered_body(
    tokens,
    query_key_value,
    out_weight,
    modulation,
    router_weight,
    expert_ids,
    gate_up_weight,
    down_weight,
):
    count, width = tokens.shape
    devices = lax.axis_size("dev")
    groups = lax.axis_size("groups")
    steps = devices // 2
    local_width = query_key_value.shape[2]
    chunk = width // devices
    lanes = width // 4
    halves_here = gate_up_weight.shape[0]
    local = halves_here // 2
    experts = router_weight.shape[1]
    topk = expert_ids.shape[1]
    struct = jax.ShapeDtypeStruct

    def hop(x, flip):
        return lax.ppermute(x, "dev", [(i, i ^ flip) for i in range(devices)])

    def swap(x):
        return lax.ppermute(x, "sub", [(0, 1), (1, 0)])

    split = groups == 2
    held = out_weight.shape[0] // (2 if split else 1)
    query, pair, near, cross, sent, own_weight = pl.pallas_call(
        functools.partial(cut_kernel, split),
        out_shape=[
            struct((count, local_width), BF16),
            struct((2 * count, local_width), BF16),
            struct((count, lanes), BF16),
            struct((2 * count + count // 2, local_width), BF16),
            struct((held, local_width), BF16),
            struct(out_weight.shape, BF16),
        ],
        in_specs=[pl.BlockSpec(memory_space=pl.ANY)] * 3,
        out_specs=[whole()] * 6,
        scratch_shapes=[pltpu.SemaphoreType.DMA((7 + 3 * (lanes // chunk),))],
        compiler_params=vmem(52),
    )(tokens, query_key_value.transpose(1, 0, 2), out_weight)
    ids, small, router = pl.pallas_call(
        small_kernel,
        out_shape=[
            struct((TILE, lanes), BF16),
            struct(modulation.shape, F32),
            struct((experts, width), BF16),
        ],
        in_specs=[whole()] * 3 + [pl.BlockSpec(memory_space=pl.ANY)],
        out_specs=[whole()] * 3,
        compiler_params=vmem(4),
    )(expert_ids.T, modulation, router_weight.T, query)
    odd = [(i, i + 1) for i in range(1, devices - 1, 2)]
    after = lax.ppermute(pair, "dev", odd + [(j, i) for i, j in odd])
    cross = hop(cross, 1)

    units = gate_up_weight.shape[3]
    *loaded, done = pl.pallas_call(
        functools.partial(load_kernel, local),
        out_shape=[struct((2, 2, units, width), BF16)] * local
        + [struct((2, *down_weight.shape[1:]), BF16)] * local
        + [struct((8, 128), F32)],
        in_specs=[pl.BlockSpec(memory_space=pl.ANY)] * 3,
        out_specs=[whole()] * (2 * local + 1),
        scratch_shapes=[pltpu.SemaphoreType.DMA((2 * local,))],
        compiler_params=vmem(14),
    )(gate_up_weight.swapaxes(2, 3), down_weight, query)

    pieces, weights = [(0, None), (1, None)], [own_weight, hop(own_weight, 2)]
    mine = {0: sent}
    for flip in range(2, steps):
        low = flip & -flip
        if flip > 2 and flip - low > 0:
            mine[flip] = hop(mine[flip - low], 2 * low)
        else:
            mine[flip] = tie(hop(sent, 2 * flip), done)

    mixed = pl.pallas_call(
        attention_kernel,
        out_shape=struct((count, local_width), BF16),
        in_specs=[whole()] * 4 + [pl.BlockSpec(memory_space=pl.ANY)] * 2,
        out_specs=whole(),
        compiler_params=vmem(6),
    )(query, pair, cross, after, small, weights[1])
    for flip in range(2, steps):
        if split:
            if flip == steps - 1:
                mine[flip] = tie(mine[flip], mixed)
            theirs = lax.ppermute(mine[flip], "groups", [(0, 1), (1, 0)])
            pieces += [(flip, 0), (flip, 1)]
            weights += [mine[flip], theirs]
        else:
            pieces.append((flip, None))
            weights.append(mine[flip])
    keep, send = pl.pallas_call(
        functools.partial(projection_kernel, steps, tuple(pieces)),
        out_shape=[struct((2 * count, lanes), F32)] * 2,
        in_specs=[whole()] * (2 + len(weights)),
        out_specs=[whole()] * 2,
        scratch_shapes=[pltpu.VMEM((2, 2 * count, lanes), F32)],
        compiler_params=vmem(6),
    )(mixed, hop(mixed, 1), *weights)
    shard = pl.pallas_call(
        state_kernel,
        out_shape=struct((2 * count + TILE, lanes), BF16),
        in_specs=[whole()] * 6,
        out_specs=whole(),
        compiler_params=vmem(6),
    )(keep, swap(send), near, cross, ids, small)

    slots = local * SLOTS
    state = None
    picked, backs = [], []
    column = {0: shard}
    for flip in range(1, steps):
        low = flip & -flip
        column[flip] = hop(column[flip - low], 2 * low)
    across = hop(shard, 1)
    column[1] = tie(column[1], across)
    for flip in range(steps):
        if flip == steps - 1:
            column[flip] = tie(column[flip], picked[0])
        block = column[flip]
        crossed = hop(block, 1) if flip else across
        if flip == steps - 1:
            crossed = tie(crossed, *picked[1:])
        own = flip == 0
        results = pl.pallas_call(
            functools.partial(select_kernel, local, topk, own),
            out_shape=[
                struct((local, 2 * SLOTS, width), BF16),
                struct((2, count, slots), BF16),
            ]
            + ([struct((count, 2 * lanes), BF16)] if own else []),
            in_specs=[whole()] * 6,
            out_specs=[whole()] * (3 if own else 2),
            scratch_shapes=[pltpu.VMEM((count, width), BF16), pltpu.VMEM((experts, count), F32)],
            compiler_params=vmem(6),
        )(block, crossed, swap(block), swap(crossed), small, router)
        picked.append(results[0])
        backs.append(results[1])
        if own:
            state = results[2]

    sources = 2 * steps
    room = sources * SLOTS
    hidden = pl.pallas_call(
        functools.partial(hidden_kernel, steps),
        out_shape=struct((local, room, 2 * units), BF16),
        in_specs=[whole()] * (steps + local),
        out_specs=whole(),
        compiler_params=vmem(6),
    )(*picked, *loaded[:local])
    share = pl.pallas_call(
        functools.partial(output_kernel, steps, local),
        out_shape=[struct((count, 2 * lanes), BF16)] * sources,
        in_specs=[whole()] * (2 + local + steps),
        out_specs=[whole()] * sources,
        scratch_shapes=[pltpu.VMEM((sources, slots, 2 * lanes), BF16)],
        compiler_params=vmem(8),
    )(hidden, swap(hidden), *loaded[local:], *backs)

    terms = [share[0]]
    for flip in range(steps - 1, -1, -1):
        crossed = hop(share[2 * flip + 1], 1)
        if flip:
            crossed = (share[2 * flip].astype(F32) + crossed.astype(F32)).astype(BF16)
            crossed = hop(crossed, 2 * flip)
        terms.append(crossed)
    return pl.pallas_call(
        final_kernel,
        out_shape=struct((count, 2 * lanes), BF16),
        in_specs=[whole()] * (2 + len(terms)),
        out_specs=whole(),
        compiler_params=vmem(8),
    )(state, small, *terms)


def extended(cells, sides, width):
    for axis, dim in sides:
        count = lax.axis_size(axis)
        ends = count - 1
        head = lax.slice_in_dim(cells, 0, width, axis=dim)
        tail = lax.slice_in_dim(cells, cells.shape[dim] - width, cells.shape[dim], axis=dim)
        cells = jnp.concatenate(
            [
                lax.ppermute(tail, axis, [(i, (i + 1) % count) for i in range(ends)]),
                cells,
                lax.ppermute(head, axis, [((i + 1) % count, i) for i in range(ends)]),
            ],
            axis=dim,
        )
    return cells


def window_attention(query, keys, values, index, total):
    count = query.shape[0]
    rows = jnp.arange(count, dtype=jnp.int32)[:, None]
    cols = jnp.arange(3 * count, dtype=jnp.int32)[None, :] - count
    place = index * count + cols
    allowed = (jnp.abs(cols - rows) <= count) & (place >= 0) & (place < total)
    scores = jnp.einsum(
        "qhd,khd->hqk", query, keys, preferred_element_type=jnp.float32
    ) / math.sqrt(query.shape[2])
    scores = jnp.where(allowed[None], scores, NEG)
    top = jnp.max(scores, -1, keepdims=True)
    weight = jnp.exp(scores - top)
    weight = (weight / jnp.sum(weight, -1, keepdims=True)).astype(jnp.bfloat16)
    mixed = jnp.einsum("hqk,khd->qhd", weight, values, preferred_element_type=jnp.float32)
    return mixed.astype(jnp.bfloat16)


def normalize(state, modulation):
    scale = lax.rsqrt(jnp.mean(state * state, -1, keepdims=True) + EPS)
    return (state * scale * (1.0 + modulation[2]) + modulation[1]).astype(jnp.bfloat16)


def route(normed, router_weight, expert_ids):
    logits = jnp.dot(normed, router_weight, preferred_element_type=jnp.float32)
    experts = router_weight.shape[1]
    match = expert_ids[:, :, None] == jnp.arange(experts, dtype=jnp.int32)[None, None, :]
    picked = jnp.sum(jnp.where(match, logits[:, None, :], 0.0), -1)
    lifted = jax.nn.sigmoid(picked)
    return lifted / jnp.sum(lifted, -1, keepdims=True)


def exchanged_body(
    tokens,
    query_key_value,
    out_weight,
    modulation,
    router_weight,
    expert_ids,
    gate_up_weight,
    down_weight,
):
    count = tokens.shape[0]
    width = tokens.shape[1]
    parts = lax.axis_size("sub")
    part = lax.axis_index("sub")
    position = lax.axis_index("dev")
    devices = lax.axis_size("dev")
    total = count * devices
    local_width = query_key_value.shape[2]
    heads_here = local_width // HEAD
    query = query_key_value[:, 0].reshape(count, heads_here, HEAD)
    pair = query_key_value[:, 1:]
    near = extended(pair, (("dev", 0),), count)
    keys = near[:, 0].reshape(3 * count, heads_here, HEAD)
    values = near[:, 1].reshape(3 * count, heads_here, HEAD)
    mixed = window_attention(query, keys, values, position, total).reshape(count, local_width)
    partial_proj = lax.dot_general(
        mixed,
        lax.all_gather(out_weight, "dev", axis=0, tiled=True),
        (((1,), (1,)), ((), ())),
        preferred_element_type=jnp.float32,
    )
    proj = lax.psum(partial_proj, "sub")
    state = tokens.astype(jnp.float32) + (1.0 + modulation[0]) * proj
    normed = normalize(state, modulation)
    gates = route(normed, router_weight, expert_ids)
    experts = router_weight.shape[1]
    topk = expert_ids.shape[1]
    flat = expert_ids.reshape(-1)
    picks = flat.shape[0]
    onehot = (flat[:, None] == jnp.arange(experts, dtype=jnp.int32)[None, :]).astype(BF16)
    order = jnp.arange(picks, dtype=jnp.int32)
    earlier = (order[None, :] < order[:, None]).astype(BF16)
    ahead = jnp.dot(earlier, onehot, preferred_element_type=F32)
    rank = jnp.sum(ahead * onehot.astype(F32), 1).astype(jnp.int32)
    target = flat * CAP + rank
    hit = target[None, :] == jnp.arange(experts * CAP, dtype=jnp.int32)[:, None]
    owner = jnp.any(hit.reshape(experts * CAP, count, topk), 2).astype(BF16)
    slice_width = width // parts
    sent = lax.dynamic_slice_in_dim(normed, part * slice_width, slice_width, 1)
    sent_width = sent.shape[1]
    rows_out = jnp.dot(owner, sent, preferred_element_type=F32).astype(BF16)
    halves_here = gate_up_weight.shape[0]
    doubled = jnp.broadcast_to(
        rows_out.reshape(experts, 1, CAP, sent_width), (experts, 2, CAP, sent_width)
    )
    outgoing = doubled.reshape(devices, halves_here, CAP, sent_width)
    up_form = "sxcd,xgdf->sxcgf"
    down_form = "sxcf,xfd->sxcd"
    incoming = lax.all_to_all(outgoing, "dev", split_axis=0, concat_axis=0, tiled=True)
    both = jnp.einsum(
        up_form,
        lax.all_gather(incoming, "sub", axis=3, tiled=True),
        gate_up_weight,
        preferred_element_type=jnp.float32,
    )
    hidden = (jax.nn.silu(both[..., 0, :]) * both[..., 1, :]).astype(jnp.bfloat16)
    gathered = lax.all_gather(hidden, "sub", axis=hidden.ndim - 1, tiled=True)
    result = jnp.einsum(down_form, gathered, down_weight, preferred_element_type=jnp.float32)
    returned = lax.all_to_all(
        result.astype(jnp.bfloat16), "dev", split_axis=0, concat_axis=0, tiled=True
    )
    own_width = returned.shape[-1]
    arranged = returned.reshape(experts, 2, CAP, own_width)
    combined = arranged[:, 0].astype(F32) + arranged[:, 1].astype(F32)
    share = jnp.sum(
        jnp.where(hit.reshape(experts * CAP, count, topk), gates[None], 0.0), 2
    )
    routed = lax.dot_general(
        share,
        combined.reshape(experts * CAP, own_width),
        (((0,), (0,)), ((), ())),
        precision=lax.Precision.HIGHEST,
        preferred_element_type=F32,
    )
    own = lax.dynamic_slice_in_dim(state, part * slice_width, slice_width, 1)
    lift = lax.dynamic_slice_in_dim(modulation[3], part * slice_width, slice_width, 0)
    return (own + (1.0 + lift) * routed).astype(jnp.bfloat16)


def body(*arrays):
    tokens, router_weight, expert_ids, gate_up_weight = arrays[0], arrays[4], arrays[5], arrays[6]
    devices = lax.axis_size("dev")
    count, width = tokens.shape
    local = gate_up_weight.shape[0] // 2
    fits = (
        lax.axis_size("sub") == 2
        and devices >= 4
        and devices & (devices - 1) == 0
        and gate_up_weight.shape[0] % 2 == 0
        and width % (devices * 128) == 0
        and arrays[1].shape[2] * 2 == width
        and count % HEAD == 0
        and expert_ids.shape[1] * count <= width // 4
        and router_weight.shape[1] <= 256
    )
    if fits and count * devices <= 2 * local * devices * CAP:
        return gathered_body(*arrays)
    return exchanged_body(*arrays)


def solution(mesh):
    return jax.shard_map(
        body,
        mesh=mesh,
        in_specs=(
            P(("groups", "dev"), None),
            P(("groups", "dev"), None, "sub"),
            P("dev", "sub"),
            P("groups", None),
            P(),
            P(("groups", "dev"), None),
            P("dev", None, None, "sub"),
            P("dev", None, "sub"),
        ),
        out_specs=P(("groups", "dev"), "sub"),
        check_vma=False,
    )
```

```python
import functools
import math

import jax
import jax.numpy as jnp
from jax import lax
from jax.experimental import pallas as pl
from jax.experimental.pallas import tpu as pltpu
from jax.sharding import PartitionSpec as P

HEAD = 128
CAP = 12
SLOTS = 16
TILE = 16

EPS = 1e-06
NEG = -1e30
F32 = jnp.float32
BF16 = jnp.bfloat16

NT = (((1,), (1,)), ((), ()))


def vmem(mib):
    return pltpu.CompilerParams(vmem_limit_bytes=mib * 2**20)


def whole():
    return pl.BlockSpec(memory_space=pltpu.VMEM)


def cut_kernel(split, tokens_ref, qkv_ref, weight_ref, *refs):
    query_ref, pair_ref, near_ref, cross_ref, sent_ref, own_ref, sem_ref = refs
    count, lanes = near_ref.shape
    chunk = tokens_ref.shape[1] // lax.axis_size("dev")
    side = lax.axis_index("dev") % 2
    part = lax.axis_index("sub")
    half = count // 2
    moves = [
        (qkv_ref.at[1], pair_ref.at[:count]),
        (qkv_ref.at[2], pair_ref.at[count:]),
        (qkv_ref.at[1], cross_ref.at[:count]),
        (qkv_ref.at[2], cross_ref.at[count : 2 * count]),
    ]
    for i in range(lanes // chunk):
        at = pl.multiple_of(part * 2 * lanes + (2 * i + 1 - side) * chunk, 128)
        for j in range(2):
            left = j * lanes + i * chunk
            moves.append(
                (
                    tokens_ref.at[j * half : (j + 1) * half, pl.ds(at, chunk)],
                    cross_ref.at[2 * count :, left : left + chunk],
                )
            )
        at = pl.multiple_of(part * 2 * lanes + (2 * i + side) * chunk, 128)
        moves.append(
            (tokens_ref.at[:, pl.ds(at, chunk)], near_ref.at[:, i * chunk : (i + 1) * chunk])
        )
    rows = sent_ref.shape[0]
    at = pl.multiple_of(lax.axis_index("groups") * rows if split else 0, TILE)
    moves += [
        (weight_ref.at[pl.ds(at, rows)], sent_ref),
        (qkv_ref.at[0], query_ref),
        (weight_ref, own_ref),
    ]
    copies = [pltpu.make_async_copy(*move, sem_ref.at[n]) for n, move in enumerate(moves)]
    for copy in copies:
        copy.start()
    for copy in copies:
        copy.wait()


def small_kernel(ids_ref, mod_ref, router_ref, _, row_ref, mod_to_ref, router_to_ref):
    topk, count = ids_ref.shape
    row_ref[...] = jnp.zeros(row_ref.shape, BF16)
    for k in range(topk):
        named = jnp.broadcast_to(ids_ref[k : k + 1, :], (TILE, count))
        row_ref[:, k * count : (k + 1) * count] = named.astype(F32).astype(BF16)
    mod_to_ref[...] = mod_ref[...]
    router_to_ref[...] = router_ref[...]


def attention_kernel(query_ref, own_ref, cross_ref, next_ref, *refs):
    mixed_ref = refs[-1]
    count, width = mixed_ref.shape
    place = lax.axis_index("dev")
    even = place % 2 == 0
    row = lax.broadcasted_iota(jnp.int32, (count, count), 0)
    col = lax.broadcasted_iota(jnp.int32, (count, count), 1)
    alone = (place == 0) | (place == lax.axis_size("dev") - 1)
    see_cross = jnp.where(even, col - row, row - col) <= 0
    see_next = (jnp.where(even, row - col, col - row) <= 0) & jnp.logical_not(alone)
    scale = 1.0 / math.sqrt(HEAD)

    def scored(q, k):
        return lax.dot_general(q, k, NT, preferred_element_type=F32) * scale

    for head in range(width // HEAD):
        lanes = slice(head * HEAD, (head + 1) * HEAD)
        q = query_ref[:, lanes]
        sc = jnp.where(see_cross, scored(q, cross_ref[:count, lanes]), NEG)
        so = scored(q, own_ref[:count, lanes])
        sn = jnp.where(see_next, scored(q, next_ref[:count, lanes]), NEG)
        top = jnp.max(jnp.maximum(jnp.maximum(sc, so), sn), 1, keepdims=True)
        wc, wo, wn = jnp.exp(sc - top), jnp.exp(so - top), jnp.exp(sn - top)
        inv = 1.0 / jnp.sum(wc + wo + wn, 1, keepdims=True)
        out = 0.0
        for weight, value in (
            (wo, own_ref[count:, lanes]),
            (wc, cross_ref[count : 2 * count, lanes]),
            (wn, next_ref[count:, lanes]),
        ):
            out += jnp.dot((weight * inv).astype(BF16), value, preferred_element_type=F32)
        mixed_ref[:, lanes] = out.astype(BF16)


def projection_kernel(steps, pieces, *refs):
    mixed_ref, other_ref = refs[0], refs[1]
    weight_refs = refs[2 : 2 + len(pieces)]
    keep_ref, send_ref, both_ref = refs[2 + len(pieces) :]
    count = mixed_ref.shape[0]
    half = steps // 2
    chunk = keep_ref.shape[1] // half
    z = lax.axis_index("dev") // 2
    part = lax.axis_index("sub")
    group = lax.axis_index("groups")
    for (hop, side), w_ref in zip(pieces, weight_refs):
        rows = w_ref.shape[0]
        target = jnp.bitwise_xor(z, hop)
        away = jnp.where(target // half == part, 0, 1)
        lane = (target % half) * chunk
        if side is not None:
            lane += (group if side == 0 else 1 - group) * rows
        lane = pl.multiple_of(lane, 128)
        for block, ref in enumerate((mixed_ref, other_ref)):
            both_ref[away, block * count : (block + 1) * count, pl.ds(lane, rows)] = (
                lax.dot_general(ref[...], w_ref[...], NT, preferred_element_type=F32)
            )
    keep_ref[...] = both_ref[0]
    send_ref[...] = both_ref[1]


def state_kernel(keep_ref, got_ref, near_ref, cross_ref, ids_ref, mod_ref, out_ref):
    count, lanes = near_ref.shape
    half = count // 2
    chunk = mod_ref.shape[1] // lax.axis_size("dev")
    side = lax.axis_index("dev") % 2
    part = lax.axis_index("sub")
    for i in range(lanes // chunk):
        at = pl.multiple_of(part * 2 * lanes + (2 * i + side) * chunk, 128)
        lift = 1.0 + mod_ref[0:1, pl.ds(at, chunk)]
        cols = slice(i * chunk, (i + 1) * chunk)
        for j in range(4):
            rows = slice(j * half, (j + 1) * half)
            if j < 2:
                token = near_ref[rows, cols]
            else:
                left = (j - 2) * lanes + i * chunk
                token = cross_ref[2 * count :, left : left + chunk]
            proj = keep_ref[rows, cols] + got_ref[rows, cols]
            out_ref[rows, cols] = (token.astype(F32) + lift * proj).astype(BF16)
    out_ref[2 * count :, :] = ids_ref[...]


def tie_kernel(*refs):
    pass


def tie(array, *others):
    anywhere = pl.BlockSpec(memory_space=pl.ANY)
    return pl.pallas_call(
        tie_kernel,
        out_shape=jax.ShapeDtypeStruct(array.shape, array.dtype),
        in_specs=[anywhere] * (1 + len(others)),
        out_specs=anywhere,
        input_output_aliases={0: 0},
        compiler_params=vmem(1),
    )(array, *others)


def select_kernel(local, topk, own, *refs):
    shard_refs, (mod_ref, router_ref) = refs[:4], refs[4:6]
    rows_ref, back_ref = refs[6:8]
    state_ref = refs[8] if own else None
    full_ref, gate_ref = refs[-2:]
    count, width = full_ref.shape
    lanes = shard_refs[0].shape[1]
    device = lax.axis_index("dev")
    side = device % 2
    part = lax.axis_index("sub")
    chunk = width // lax.axis_size("dev")
    experts = router_ref.shape[0]
    slots = local * SLOTS
    before = lax.broadcasted_iota(jnp.int32, (count, count), 0)
    after = lax.broadcasted_iota(jnp.int32, (count, count), 1)
    earlier = (before < after).astype(F32).astype(BF16)
    slot = lax.broadcasted_iota(jnp.int32, (slots, count), 0) % SLOTS
    mine = lax.broadcasted_iota(jnp.int32, (local, count), 0) + device * local
    every = lax.broadcasted_iota(jnp.int32, (experts, count), 0)
    for cross in range(2):
        for far_half in range(2):
            for far_side in range(2):
                ref = shard_refs[2 * far_half + far_side]
                top = (cross ^ far_side) * count
                half = part if far_half == 0 else 1 - part
                parity = side if far_side == 0 else 1 - side
                for i in range(lanes // chunk):
                    block = ref[top : top + count, i * chunk : (i + 1) * chunk]
                    at = (2 * i + parity) * chunk
                    full_ref[:, pl.ds(pl.multiple_of(half * 2 * lanes + at, 128), chunk)] = block
                    if own and cross == 0 and far_half == 0:
                        state_ref[:, pl.ds(pl.multiple_of(at, 128), chunk)] = block
        state = full_ref[...].astype(F32)
        scale = lax.rsqrt(jnp.mean(state * state, 1, keepdims=True) + EPS)
        normed = state * scale * (1.0 + mod_ref[2:3, :]) + mod_ref[1:2, :]
        normed = normed.astype(BF16)
        ids = shard_refs[cross][2 * count : 2 * count + TILE, :]
        ids = ids.astype(F32)[0:1, :].astype(jnp.int32)
        named = [ids[:, k * count : (k + 1) * count] for k in range(topk)]
        hot = sum((mine == n).astype(F32) for n in named)
        rank = jnp.dot(hot.astype(BF16), earlier, preferred_element_type=F32)
        rank = jnp.where(hot > 0.0, rank, -1.0)
        rank = jnp.concatenate(
            [jnp.broadcast_to(rank[e : e + 1], (SLOTS, count)) for e in range(local)]
        )
        pick = rank == slot.astype(F32)
        chosen = jnp.dot(
            jnp.where(pick, 1.0, 0.0).astype(BF16), normed, preferred_element_type=F32
        ).astype(BF16)
        for e in range(local):
            rows_ref[e, cross * SLOTS : (cross + 1) * SLOTS, :] = chosen[
                e * SLOTS : (e + 1) * SLOTS
            ]
        logits = lax.dot_general(router_ref[...], normed, NT, preferred_element_type=F32)
        lifted = sum(jnp.where(every == n, 1.0, 0.0) for n in named) * jax.nn.sigmoid(logits)
        gate_ref[...] = lifted / jnp.sum(lifted, 0, keepdims=True)
        here = gate_ref[pl.ds(pl.multiple_of(device * local, local), local), :]
        here = jnp.concatenate(
            [jnp.broadcast_to(here[e : e + 1], (SLOTS, count)) for e in range(local)]
        )
        back_ref[cross] = jnp.where(pick, here, 0.0).T.astype(BF16)


def load_kernel(local, up_ref, down_ref, _, *refs):
    to_refs, done_ref, sem_ref = refs[: 2 * local], refs[2 * local], refs[2 * local + 1]
    copies = []
    for n, ref in enumerate(to_refs):
        e = n % local
        whole_ref = up_ref if n < local else down_ref
        copies.append(
            pltpu.make_async_copy(whole_ref.at[2 * e : 2 * e + 2], ref, sem_ref.at[n])
        )
    for copy in copies:
        copy.start()
    done_ref[...] = jnp.zeros(done_ref.shape, F32)
    for copy in copies:
        copy.wait()


def hidden_kernel(steps, *refs):
    rows_refs, w_refs, hidden_ref = refs[:steps], refs[steps:-1], refs[-1]
    for e, w_ref in enumerate(w_refs):
        rows = jnp.concatenate([ref[e] for ref in rows_refs])
        halves = []
        for b in range(2):
            gate = lax.dot_general(w_ref[b, 0], rows, NT, preferred_element_type=F32)
            up = lax.dot_general(w_ref[b, 1], rows, NT, preferred_element_type=F32)
            halves.append(jax.nn.silu(gate) * up)
        hidden_ref[e] = jnp.concatenate(halves).T.astype(BF16)


def output_kernel(steps, local, near_ref, far_ref, *refs):
    w_refs, back_refs = refs[:local], refs[local : local + steps]
    out_refs, held_ref = refs[local + steps : local + 3 * steps], refs[-1]
    part = lax.axis_index("sub")
    units = near_ref.shape[2] // 2
    for e, w_ref in enumerate(w_refs):
        total = 0.0
        for ref, who in ((near_ref, part), (far_ref, 1 - part)):
            at = pl.multiple_of(who * units, 64)
            weight = jnp.concatenate([w_ref[b, pl.ds(at, units), :] for b in range(2)])
            total += jnp.dot(ref[e], weight, preferred_element_type=F32)
        total = total.astype(BF16)
        for source in range(2 * steps):
            held_ref[source, e * SLOTS : (e + 1) * SLOTS, :] = total[
                source * SLOTS : (source + 1) * SLOTS
            ]
    for source in range(2 * steps):
        out_refs[source][...] = jnp.dot(
            back_refs[source // 2][source % 2], held_ref[source], preferred_element_type=F32
        ).astype(BF16)


def final_kernel(state_ref, mod_ref, *refs):
    routed = sum(ref[...].astype(F32) for ref in refs[:-1])
    lanes = state_ref.shape[1]
    at = pl.multiple_of(lax.axis_index("sub") * lanes, 128)
    lift = 1.0 + mod_ref[3:4, pl.ds(at, lanes)]
    refs[-1][...] = (state_ref[...].astype(F32) + lift * routed).astype(BF16)


def gathered_body(
    tokens,
    query_key_value,
    out_weight,
    modulation,
    router_weight,
    expert_ids,
    gate_up_weight,
    down_weight,
):
    count, width = tokens.shape
    devices = lax.axis_size("dev")
    groups = lax.axis_size("groups")
    steps = devices // 2
    local_width = query_key_value.shape[2]
    chunk = width // devices
    lanes = width // 4
    halves_here = gate_up_weight.shape[0]
    local = halves_here // 2
    experts = router_weight.shape[1]
    topk = expert_ids.shape[1]
    struct = jax.ShapeDtypeStruct

    def hop(x, flip):
        return lax.ppermute(x, "dev", [(i, i ^ flip) for i in range(devices)])

    def swap(x):
        return lax.ppermute(x, "sub", [(0, 1), (1, 0)])

    split = groups == 2
    held = out_weight.shape[0] // (2 if split else 1)
    query, pair, near, cross, sent, own_weight = pl.pallas_call(
        functools.partial(cut_kernel, split),
        out_shape=[
            struct((count, local_width), BF16),
            struct((2 * count, local_width), BF16),
            struct((count, lanes), BF16),
            struct((2 * count + count // 2, local_width), BF16),
            struct((held, local_width), BF16),
            struct(out_weight.shape, BF16),
        ],
        in_specs=[pl.BlockSpec(memory_space=pl.ANY)] * 3,
        out_specs=[whole()] * 6,
        scratch_shapes=[pltpu.SemaphoreType.DMA((7 + 3 * (lanes // chunk),))],
        compiler_params=vmem(52),
    )(tokens, query_key_value.transpose(1, 0, 2), out_weight)
    ids, small, router = pl.pallas_call(
        small_kernel,
        out_shape=[
            struct((TILE, lanes), BF16),
            struct(modulation.shape, F32),
            struct((experts, width), BF16),
        ],
        in_specs=[whole()] * 3 + [pl.BlockSpec(memory_space=pl.ANY)],
        out_specs=[whole()] * 3,
        compiler_params=vmem(4),
    )(expert_ids.T, modulation, router_weight.T, query)
    odd = [(i, i + 1) for i in range(1, devices - 1, 2)]
    after = lax.ppermute(pair, "dev", odd + [(j, i) for i, j in odd])
    cross = hop(cross, 1)

    units = gate_up_weight.shape[3]
    *loaded, done = pl.pallas_call(
        functools.partial(load_kernel, local),
        out_shape=[struct((2, 2, units, width), BF16)] * local
        + [struct((2, *down_weight.shape[1:]), BF16)] * local
        + [struct((8, 128), F32)],
        in_specs=[pl.BlockSpec(memory_space=pl.ANY)] * 3,
        out_specs=[whole()] * (2 * local + 1),
        scratch_shapes=[pltpu.SemaphoreType.DMA((2 * local,))],
        compiler_params=vmem(14),
    )(gate_up_weight.swapaxes(2, 3), down_weight, query)

    mine = {0: sent}
    for flip in range(2, steps):
        low = flip & -flip
        if flip > 2 and flip - low > 0:
            mine[flip] = hop(mine[flip - low], 2 * low)
        else:
            mine[flip] = tie(hop(sent, 2 * flip), done)
    own_weight = tie(own_weight, mine[2])
    pieces, weights = [(0, None), (1, None)], [own_weight, hop(own_weight, 2)]

    mixed = pl.pallas_call(
        attention_kernel,
        out_shape=struct((count, local_width), BF16),
        in_specs=[whole()] * 4 + [pl.BlockSpec(memory_space=pl.ANY)],
        out_specs=whole(),
        compiler_params=vmem(6),
    )(query, pair, cross, after, small)
    for flip in range(2, steps):
        if split:
            if flip == steps - 1:
                mine[flip] = tie(mine[flip], mixed)
            theirs = lax.ppermute(mine[flip], "groups", [(0, 1), (1, 0)])
            pieces += [(flip, 0), (flip, 1)]
            weights += [mine[flip], theirs]
        else:
            pieces.append((flip, None))
            weights.append(mine[flip])
    keep, send = pl.pallas_call(
        functools.partial(projection_kernel, steps, tuple(pieces)),
        out_shape=[struct((2 * count, lanes), F32)] * 2,
        in_specs=[whole()] * (2 + len(weights)),
        out_specs=[whole()] * 2,
        scratch_shapes=[pltpu.VMEM((2, 2 * count, lanes), F32)],
        compiler_params=vmem(6),
    )(mixed, hop(mixed, 1), *weights)
    shard = pl.pallas_call(
        state_kernel,
        out_shape=struct((2 * count + TILE, lanes), BF16),
        in_specs=[whole()] * 6,
        out_specs=whole(),
        compiler_params=vmem(6),
    )(keep, swap(send), near, cross, ids, small)

    slots = local * SLOTS
    state = None
    picked, backs = [], []
    column = {0: shard, 1: hop(shard, 2)}
    across = hop(shard, 1)
    column[1] = tie(column[1], across)
    crossing = {0: across, 1: hop(column[1], 1)}
    column[2] = tie(hop(shard, 4), crossing[1])
    for flip in range(3, steps):
        low = flip & -flip
        column[flip] = hop(column[flip - low] if flip > low else shard, 2 * low)
    for flip in range(steps):
        if flip == steps - 1:
            column[flip] = tie(column[flip], picked[0])
        block = column[flip]
        crossed = crossing[flip] if flip in crossing else hop(block, 1)
        if flip == steps - 1:
            crossed = tie(crossed, *picked[1:])
        own = flip == 0
        results = pl.pallas_call(
            functools.partial(select_kernel, local, topk, own),
            out_shape=[
                struct((local, 2 * SLOTS, width), BF16),
                struct((2, count, slots), BF16),
            ]
            + ([struct((count, 2 * lanes), BF16)] if own else []),
            in_specs=[whole()] * 6,
            out_specs=[whole()] * (3 if own else 2),
            scratch_shapes=[pltpu.VMEM((count, width), BF16), pltpu.VMEM((experts, count), F32)],
            compiler_params=vmem(6),
        )(block, crossed, swap(block), swap(crossed), small, router)
        picked.append(results[0])
        backs.append(results[1])
        if own:
            state = results[2]

    sources = 2 * steps
    room = sources * SLOTS
    hidden = pl.pallas_call(
        functools.partial(hidden_kernel, steps),
        out_shape=struct((local, room, 2 * units), BF16),
        in_specs=[whole()] * (steps + local),
        out_specs=whole(),
        compiler_params=vmem(6),
    )(*picked, *loaded[:local])
    share = pl.pallas_call(
        functools.partial(output_kernel, steps, local),
        out_shape=[struct((count, 2 * lanes), BF16)] * sources,
        in_specs=[whole()] * (2 + local + steps),
        out_specs=[whole()] * sources,
        scratch_shapes=[pltpu.VMEM((sources, slots, 2 * lanes), BF16)],
        compiler_params=vmem(8),
    )(hidden, swap(hidden), *loaded[local:], *backs)

    terms = [share[0]]
    for flip in range(steps - 1, -1, -1):
        crossed = hop(share[2 * flip + 1], 1)
        if flip:
            crossed = (share[2 * flip].astype(F32) + crossed.astype(F32)).astype(BF16)
            crossed = hop(crossed, 2 * flip)
        terms.append(crossed)
    return pl.pallas_call(
        final_kernel,
        out_shape=struct((count, 2 * lanes), BF16),
        in_specs=[whole()] * (2 + len(terms)),
        out_specs=whole(),
        compiler_params=vmem(8),
    )(state, small, *terms)


def extended(cells, sides, width):
    for axis, dim in sides:
        count = lax.axis_size(axis)
        ends = count - 1
        head = lax.slice_in_dim(cells, 0, width, axis=dim)
        tail = lax.slice_in_dim(cells, cells.shape[dim] - width, cells.shape[dim], axis=dim)
        cells = jnp.concatenate(
            [
                lax.ppermute(tail, axis, [(i, (i + 1) % count) for i in range(ends)]),
                cells,
                lax.ppermute(head, axis, [((i + 1) % count, i) for i in range(ends)]),
            ],
            axis=dim,
        )
    return cells


def window_attention(query, keys, values, index, total):
    count = query.shape[0]
    rows = jnp.arange(count, dtype=jnp.int32)[:, None]
    cols = jnp.arange(3 * count, dtype=jnp.int32)[None, :] - count
    place = index * count + cols
    allowed = (jnp.abs(cols - rows) <= count) & (place >= 0) & (place < total)
    scores = jnp.einsum(
        "qhd,khd->hqk", query, keys, preferred_element_type=jnp.float32
    ) / math.sqrt(query.shape[2])
    scores = jnp.where(allowed[None], scores, NEG)
    top = jnp.max(scores, -1, keepdims=True)
    weight = jnp.exp(scores - top)
    weight = (weight / jnp.sum(weight, -1, keepdims=True)).astype(jnp.bfloat16)
    mixed = jnp.einsum("hqk,khd->qhd", weight, values, preferred_element_type=jnp.float32)
    return mixed.astype(jnp.bfloat16)


def normalize(state, modulation):
    scale = lax.rsqrt(jnp.mean(state * state, -1, keepdims=True) + EPS)
    return (state * scale * (1.0 + modulation[2]) + modulation[1]).astype(jnp.bfloat16)


def route(normed, router_weight, expert_ids):
    logits = jnp.dot(normed, router_weight, preferred_element_type=jnp.float32)
    experts = router_weight.shape[1]
    match = expert_ids[:, :, None] == jnp.arange(experts, dtype=jnp.int32)[None, None, :]
    picked = jnp.sum(jnp.where(match, logits[:, None, :], 0.0), -1)
    lifted = jax.nn.sigmoid(picked)
    return lifted / jnp.sum(lifted, -1, keepdims=True)


def exchanged_body(
    tokens,
    query_key_value,
    out_weight,
    modulation,
    router_weight,
    expert_ids,
    gate_up_weight,
    down_weight,
):
    count = tokens.shape[0]
    width = tokens.shape[1]
    parts = lax.axis_size("sub")
    part = lax.axis_index("sub")
    position = lax.axis_index("dev")
    devices = lax.axis_size("dev")
    total = count * devices
    local_width = query_key_value.shape[2]
    heads_here = local_width // HEAD
    query = query_key_value[:, 0].reshape(count, heads_here, HEAD)
    pair = query_key_value[:, 1:]
    near = extended(pair, (("dev", 0),), count)
    keys = near[:, 0].reshape(3 * count, heads_here, HEAD)
    values = near[:, 1].reshape(3 * count, heads_here, HEAD)
    mixed = window_attention(query, keys, values, position, total).reshape(count, local_width)
    partial_proj = lax.dot_general(
        mixed,
        lax.all_gather(out_weight, "dev", axis=0, tiled=True),
        (((1,), (1,)), ((), ())),
        preferred_element_type=jnp.float32,
    )
    proj = lax.psum(partial_proj, "sub")
    state = tokens.astype(jnp.float32) + (1.0 + modulation[0]) * proj
    normed = normalize(state, modulation)
    gates = route(normed, router_weight, expert_ids)
    experts = router_weight.shape[1]
    topk = expert_ids.shape[1]
    flat = expert_ids.reshape(-1)
    picks = flat.shape[0]
    onehot = (flat[:, None] == jnp.arange(experts, dtype=jnp.int32)[None, :]).astype(BF16)
    order = jnp.arange(picks, dtype=jnp.int32)
    earlier = (order[None, :] < order[:, None]).astype(BF16)
    ahead = jnp.dot(earlier, onehot, preferred_element_type=F32)
    rank = jnp.sum(ahead * onehot.astype(F32), 1).astype(jnp.int32)
    target = flat * CAP + rank
    hit = target[None, :] == jnp.arange(experts * CAP, dtype=jnp.int32)[:, None]
    owner = jnp.any(hit.reshape(experts * CAP, count, topk), 2).astype(BF16)
    slice_width = width // parts
    sent = lax.dynamic_slice_in_dim(normed, part * slice_width, slice_width, 1)
    sent_width = sent.shape[1]
    rows_out = jnp.dot(owner, sent, preferred_element_type=F32).astype(BF16)
    halves_here = gate_up_weight.shape[0]
    doubled = jnp.broadcast_to(
        rows_out.reshape(experts, 1, CAP, sent_width), (experts, 2, CAP, sent_width)
    )
    outgoing = doubled.reshape(devices, halves_here, CAP, sent_width)
    up_form = "sxcd,xgdf->sxcgf"
    down_form = "sxcf,xfd->sxcd"
    incoming = lax.all_to_all(outgoing, "dev", split_axis=0, concat_axis=0, tiled=True)
    both = jnp.einsum(
        up_form,
        lax.all_gather(incoming, "sub", axis=3, tiled=True),
        gate_up_weight,
        preferred_element_type=jnp.float32,
    )
    hidden = (jax.nn.silu(both[..., 0, :]) * both[..., 1, :]).astype(jnp.bfloat16)
    gathered = lax.all_gather(hidden, "sub", axis=hidden.ndim - 1, tiled=True)
    result = jnp.einsum(down_form, gathered, down_weight, preferred_element_type=jnp.float32)
    returned = lax.all_to_all(
        result.astype(jnp.bfloat16), "dev", split_axis=0, concat_axis=0, tiled=True
    )
    own_width = returned.shape[-1]
    arranged = returned.reshape(experts, 2, CAP, own_width)
    combined = arranged[:, 0].astype(F32) + arranged[:, 1].astype(F32)
    share = jnp.sum(
        jnp.where(hit.reshape(experts * CAP, count, topk), gates[None], 0.0), 2
    )
    routed = lax.dot_general(
        share,
        combined.reshape(experts * CAP, own_width),
        (((0,), (0,)), ((), ())),
        precision=lax.Precision.HIGHEST,
        preferred_element_type=F32,
    )
    own = lax.dynamic_slice_in_dim(state, part * slice_width, slice_width, 1)
    lift = lax.dynamic_slice_in_dim(modulation[3], part * slice_width, slice_width, 0)
    return (own + (1.0 + lift) * routed).astype(jnp.bfloat16)


def body(*arrays):
    tokens, router_weight, expert_ids, gate_up_weight = arrays[0], arrays[4], arrays[5], arrays[6]
    devices = lax.axis_size("dev")
    count, width = tokens.shape
    local = gate_up_weight.shape[0] // 2
    fits = (
        lax.axis_size("sub") == 2
        and devices >= 8
        and devices & (devices - 1) == 0
        and gate_up_weight.shape[0] % 2 == 0
        and width % (devices * 128) == 0
        and arrays[1].shape[2] * 2 == width
        and count % HEAD == 0
        and expert_ids.shape[1] * count <= width // 4
        and router_weight.shape[1] <= 256
    )
    if fits and count * devices <= 2 * local * devices * CAP:
        return gathered_body(*arrays)
    return exchanged_body(*arrays)


def solution(mesh):
    return jax.shard_map(
        body,
        mesh=mesh,
        in_specs=(
            P(("groups", "dev"), None),
            P(("groups", "dev"), None, "sub"),
            P("dev", "sub"),
            P("groups", None),
            P(),
            P(("groups", "dev"), None),
            P("dev", None, None, "sub"),
            P("dev", None, "sub"),
        ),
        out_specs=P(("groups", "dev"), "sub"),
        check_vma=False,
    )
```

```python
import functools
import math

import jax
import jax.numpy as jnp
from jax import lax
from jax.experimental import pallas as pl
from jax.experimental.pallas import tpu as pltpu
from jax.sharding import PartitionSpec as P

HEAD = 128
CAP = 12
SLOTS = 16
TILE = 16

EPS = 1e-06
NEG = -1e30
F32 = jnp.float32
BF16 = jnp.bfloat16

NT = (((1,), (1,)), ((), ()))


def vmem(mib):
    return pltpu.CompilerParams(vmem_limit_bytes=mib * 2**20)


def whole():
    return pl.BlockSpec(memory_space=pltpu.VMEM)


def cut_kernel(split, tokens_ref, qkv_ref, weight_ref, *refs):
    query_ref, pair_ref, near_ref, cross_ref, sent_ref, own_ref, sem_ref = refs
    count, lanes = near_ref.shape
    chunk = tokens_ref.shape[1] // lax.axis_size("dev")
    side = lax.axis_index("dev") % 2
    part = lax.axis_index("sub")
    half = count // 2
    moves = [
        (qkv_ref.at[1], pair_ref.at[:count]),
        (qkv_ref.at[2], pair_ref.at[count:]),
        (qkv_ref.at[1], cross_ref.at[:count]),
        (qkv_ref.at[2], cross_ref.at[count : 2 * count]),
    ]
    for i in range(lanes // chunk):
        at = pl.multiple_of(part * 2 * lanes + (2 * i + 1 - side) * chunk, 128)
        for j in range(2):
            left = j * lanes + i * chunk
            moves.append(
                (
                    tokens_ref.at[j * half : (j + 1) * half, pl.ds(at, chunk)],
                    cross_ref.at[2 * count :, left : left + chunk],
                )
            )
        at = pl.multiple_of(part * 2 * lanes + (2 * i + side) * chunk, 128)
        moves.append(
            (tokens_ref.at[:, pl.ds(at, chunk)], near_ref.at[:, i * chunk : (i + 1) * chunk])
        )
    rows = sent_ref.shape[0]
    at = pl.multiple_of(lax.axis_index("groups") * rows if split else 0, TILE)
    moves += [
        (weight_ref.at[pl.ds(at, rows)], sent_ref),
        (qkv_ref.at[0], query_ref),
        (weight_ref, own_ref),
    ]
    copies = [pltpu.make_async_copy(*move, sem_ref.at[n]) for n, move in enumerate(moves)]
    for copy in copies:
        copy.start()
    for copy in copies:
        copy.wait()


def small_kernel(ids_ref, mod_ref, router_ref, _, row_ref, mod_to_ref, router_to_ref):
    topk, count = ids_ref.shape
    row_ref[...] = jnp.zeros(row_ref.shape, BF16)
    for k in range(topk):
        named = jnp.broadcast_to(ids_ref[k : k + 1, :], (TILE, count))
        row_ref[:, k * count : (k + 1) * count] = named.astype(F32).astype(BF16)
    mod_to_ref[...] = mod_ref[...]
    router_to_ref[...] = router_ref[...]


def attention_kernel(query_ref, own_ref, cross_ref, next_ref, *refs):
    mixed_ref = refs[-1]
    count, width = mixed_ref.shape
    place = lax.axis_index("dev")
    even = place % 2 == 0
    row = lax.broadcasted_iota(jnp.int32, (count, count), 0)
    col = lax.broadcasted_iota(jnp.int32, (count, count), 1)
    alone = (place == 0) | (place == lax.axis_size("dev") - 1)
    see_cross = jnp.where(even, col - row, row - col) <= 0
    see_next = (jnp.where(even, row - col, col - row) <= 0) & jnp.logical_not(alone)
    scale = 1.0 / math.sqrt(HEAD)

    def scored(q, k):
        return lax.dot_general(q, k, NT, preferred_element_type=F32) * scale

    for head in range(width // HEAD):
        lanes = slice(head * HEAD, (head + 1) * HEAD)
        q = query_ref[:, lanes]
        sc = jnp.where(see_cross, scored(q, cross_ref[:count, lanes]), NEG)
        so = scored(q, own_ref[:count, lanes])
        sn = jnp.where(see_next, scored(q, next_ref[:count, lanes]), NEG)
        top = jnp.max(jnp.maximum(jnp.maximum(sc, so), sn), 1, keepdims=True)
        wc, wo, wn = jnp.exp(sc - top), jnp.exp(so - top), jnp.exp(sn - top)
        inv = 1.0 / jnp.sum(wc + wo + wn, 1, keepdims=True)
        out = 0.0
        for weight, value in (
            (wo, own_ref[count:, lanes]),
            (wc, cross_ref[count : 2 * count, lanes]),
            (wn, next_ref[count:, lanes]),
        ):
            out += jnp.dot((weight * inv).astype(BF16), value, preferred_element_type=F32)
        mixed_ref[:, lanes] = out.astype(BF16)


def projection_kernel(steps, pieces, *refs):
    mixed_ref, other_ref = refs[0], refs[1]
    weight_refs = refs[2 : 2 + len(pieces)]
    keep_ref, send_ref, both_ref = refs[-3:]
    count = mixed_ref.shape[0]
    half = steps // 2
    chunk = keep_ref.shape[1] // half
    z = lax.axis_index("dev") // 2
    part = lax.axis_index("sub")
    group = lax.axis_index("groups")
    for (hop, side), w_ref in zip(pieces, weight_refs):
        rows = w_ref.shape[0]
        target = jnp.bitwise_xor(z, hop)
        away = jnp.where(target // half == part, 0, 1)
        lane = (target % half) * chunk
        if side is not None:
            lane += (group if side == 0 else 1 - group) * rows
        lane = pl.multiple_of(lane, 128)
        for block, ref in enumerate((mixed_ref, other_ref)):
            both_ref[away, block * count : (block + 1) * count, pl.ds(lane, rows)] = (
                lax.dot_general(ref[...], w_ref[...], NT, preferred_element_type=F32)
            )
    keep_ref[...] = both_ref[0]
    send_ref[...] = both_ref[1]


def state_kernel(keep_ref, got_ref, near_ref, cross_ref, ids_ref, mod_ref, out_ref):
    count, lanes = near_ref.shape
    half = count // 2
    chunk = mod_ref.shape[1] // lax.axis_size("dev")
    side = lax.axis_index("dev") % 2
    part = lax.axis_index("sub")
    for i in range(lanes // chunk):
        at = pl.multiple_of(part * 2 * lanes + (2 * i + side) * chunk, 128)
        lift = 1.0 + mod_ref[0:1, pl.ds(at, chunk)]
        cols = slice(i * chunk, (i + 1) * chunk)
        for j in range(4):
            rows = slice(j * half, (j + 1) * half)
            if j < 2:
                token = near_ref[rows, cols]
            else:
                left = (j - 2) * lanes + i * chunk
                token = cross_ref[2 * count :, left : left + chunk]
            proj = keep_ref[rows, cols] + got_ref[rows, cols]
            out_ref[rows, cols] = (token.astype(F32) + lift * proj).astype(BF16)
    out_ref[2 * count :, :] = ids_ref[...]


def tie_kernel(*refs):
    pass


def tie(array, *others):
    anywhere = pl.BlockSpec(memory_space=pl.ANY)
    return pl.pallas_call(
        tie_kernel,
        out_shape=jax.ShapeDtypeStruct(array.shape, array.dtype),
        in_specs=[anywhere] * (1 + len(others)),
        out_specs=anywhere,
        input_output_aliases={0: 0},
        compiler_params=vmem(1),
    )(array, *others)


def select_kernel(local, topk, own, *refs):
    shard_refs, (mod_ref, router_ref) = refs[:4], refs[4:6]
    rows_ref, back_ref = refs[6:8]
    state_ref = refs[8] if own else None
    full_ref, gate_ref = refs[-2:]
    count, width = full_ref.shape
    lanes = shard_refs[0].shape[1]
    device = lax.axis_index("dev")
    side = device % 2
    part = lax.axis_index("sub")
    chunk = width // lax.axis_size("dev")
    experts = router_ref.shape[0]
    slots = local * SLOTS
    before = lax.broadcasted_iota(jnp.int32, (count, count), 0)
    after = lax.broadcasted_iota(jnp.int32, (count, count), 1)
    earlier = (before < after).astype(F32).astype(BF16)
    slot = lax.broadcasted_iota(jnp.int32, (slots, count), 0) % SLOTS
    mine = lax.broadcasted_iota(jnp.int32, (local, count), 0) + device * local
    every = lax.broadcasted_iota(jnp.int32, (experts, count), 0)
    for cross in range(2):
        for far_half in range(2):
            for far_side in range(2):
                ref = shard_refs[2 * far_half + far_side]
                top = (cross ^ far_side) * count
                half = part if far_half == 0 else 1 - part
                parity = side if far_side == 0 else 1 - side
                for i in range(lanes // chunk):
                    block = ref[top : top + count, i * chunk : (i + 1) * chunk]
                    at = (2 * i + parity) * chunk
                    full_ref[:, pl.ds(pl.multiple_of(half * 2 * lanes + at, 128), chunk)] = block
                    if own and cross == 0 and far_half == 0:
                        state_ref[:, pl.ds(pl.multiple_of(at, 128), chunk)] = block
        state = full_ref[...].astype(F32)
        scale = lax.rsqrt(jnp.mean(state * state, 1, keepdims=True) + EPS)
        normed = state * scale * (1.0 + mod_ref[2:3, :]) + mod_ref[1:2, :]
        normed = normed.astype(BF16)
        ids = shard_refs[cross][2 * count : 2 * count + TILE, :]
        ids = ids.astype(F32)[0:1, :].astype(jnp.int32)
        named = [ids[:, k * count : (k + 1) * count] for k in range(topk)]
        hot = sum((mine == n).astype(F32) for n in named)
        rank = jnp.dot(hot.astype(BF16), earlier, preferred_element_type=F32)
        rank = jnp.where(hot > 0.0, rank, -1.0)
        rank = jnp.concatenate(
            [jnp.broadcast_to(rank[e : e + 1], (SLOTS, count)) for e in range(local)]
        )
        pick = rank == slot.astype(F32)
        chosen = jnp.dot(
            jnp.where(pick, 1.0, 0.0).astype(BF16), normed, preferred_element_type=F32
        ).astype(BF16)
        for e in range(local):
            rows_ref[e, cross * SLOTS : (cross + 1) * SLOTS, :] = chosen[
                e * SLOTS : (e + 1) * SLOTS
            ]
        logits = lax.dot_general(router_ref[...], normed, NT, preferred_element_type=F32)
        lifted = sum(jnp.where(every == n, 1.0, 0.0) for n in named) * jax.nn.sigmoid(logits)
        gate_ref[...] = lifted / jnp.sum(lifted, 0, keepdims=True)
        here = gate_ref[pl.ds(pl.multiple_of(device * local, local), local), :]
        here = jnp.concatenate(
            [jnp.broadcast_to(here[e : e + 1], (SLOTS, count)) for e in range(local)]
        )
        back_ref[cross] = jnp.where(pick, here, 0.0).T.astype(BF16)


def load_kernel(from_ref, _, *refs):
    to_refs, done_ref, sem_ref = refs[:-2], refs[-2], refs[-1]
    copies = [
        pltpu.make_async_copy(from_ref.at[2 * e : 2 * e + 2], ref, sem_ref.at[e])
        for e, ref in enumerate(to_refs)
    ]
    for copy in copies:
        copy.start()
    done_ref[...] = jnp.zeros(done_ref.shape, F32)
    for copy in copies:
        copy.wait()


def load(weight, after_this, limit):
    local = weight.shape[0] // 2
    piece = jax.ShapeDtypeStruct((2, *weight.shape[1:]), BF16)
    return pl.pallas_call(
        load_kernel,
        out_shape=[piece] * local + [jax.ShapeDtypeStruct((8, 128), F32)],
        in_specs=[pl.BlockSpec(memory_space=pl.ANY)] * 2,
        out_specs=[whole()] * (local + 1),
        scratch_shapes=[pltpu.SemaphoreType.DMA((local,))],
        compiler_params=vmem(limit),
    )(weight, after_this)


def hidden_kernel(steps, *refs):
    rows_refs, w_refs, hidden_ref = refs[:steps], refs[steps:-1], refs[-1]
    for e, w_ref in enumerate(w_refs):
        rows = jnp.concatenate([ref[e] for ref in rows_refs])
        halves = []
        for b in range(2):
            gate = lax.dot_general(w_ref[b, 0], rows, NT, preferred_element_type=F32)
            up = lax.dot_general(w_ref[b, 1], rows, NT, preferred_element_type=F32)
            halves.append(jax.nn.silu(gate) * up)
        hidden_ref[e] = jnp.concatenate(halves).T.astype(BF16)


def output_kernel(steps, near_ref, far_ref, w_ref, *refs):
    back_refs, out_refs, held_ref = refs[:steps], refs[steps : 3 * steps], refs[-1]
    part = lax.axis_index("sub")
    units = near_ref.shape[2] // 2
    for e in range(near_ref.shape[0]):
        total = 0.0
        for ref, who in ((near_ref, part), (far_ref, 1 - part)):
            at = pl.multiple_of(who * units, 64)
            weight = jnp.concatenate([w_ref[2 * e + b, pl.ds(at, units), :] for b in range(2)])
            total += jnp.dot(ref[e], weight, preferred_element_type=F32)
        total = total.astype(BF16)
        for source in range(2 * steps):
            held_ref[source, e * SLOTS : (e + 1) * SLOTS, :] = total[
                source * SLOTS : (source + 1) * SLOTS
            ]
    for source in range(2 * steps):
        out_refs[source][...] = jnp.dot(
            back_refs[source // 2][source % 2], held_ref[source], preferred_element_type=F32
        ).astype(BF16)


def final_kernel(state_ref, mod_ref, *refs):
    routed = sum(ref[...].astype(F32) for ref in refs[:-1])
    lanes = state_ref.shape[1]
    at = pl.multiple_of(lax.axis_index("sub") * lanes, 128)
    lift = 1.0 + mod_ref[3:4, pl.ds(at, lanes)]
    refs[-1][...] = (state_ref[...].astype(F32) + lift * routed).astype(BF16)


def gathered_body(
    tokens,
    query_key_value,
    out_weight,
    modulation,
    router_weight,
    expert_ids,
    gate_up_weight,
    down_weight,
):
    count, width = tokens.shape
    devices = lax.axis_size("dev")
    groups = lax.axis_size("groups")
    steps = devices // 2
    local_width = query_key_value.shape[2]
    chunk = width // devices
    lanes = width // 4
    halves_here = gate_up_weight.shape[0]
    local = halves_here // 2
    experts = router_weight.shape[1]
    topk = expert_ids.shape[1]
    struct = jax.ShapeDtypeStruct

    def hop(x, flip):
        return lax.ppermute(x, "dev", [(i, i ^ flip) for i in range(devices)])

    def swap(x):
        return lax.ppermute(x, "sub", [(0, 1), (1, 0)])

    split = groups == 2
    held = out_weight.shape[0] // (2 if split else 1)
    query, pair, near, cross, sent, own_weight = pl.pallas_call(
        functools.partial(cut_kernel, split),
        out_shape=[
            struct((count, local_width), BF16),
            struct((2 * count, local_width), BF16),
            struct((count, lanes), BF16),
            struct((2 * count + count // 2, local_width), BF16),
            struct((held, local_width), BF16),
            struct(out_weight.shape, BF16),
        ],
        in_specs=[pl.BlockSpec(memory_space=pl.ANY)] * 3,
        out_specs=[whole()] * 6,
        scratch_shapes=[pltpu.SemaphoreType.DMA((7 + 3 * (lanes // chunk),))],
        compiler_params=vmem(52),
    )(tokens, query_key_value.transpose(1, 0, 2), out_weight)
    ids, small, router = pl.pallas_call(
        small_kernel,
        out_shape=[
            struct((TILE, lanes), BF16),
            struct(modulation.shape, F32),
            struct((experts, width), BF16),
        ],
        in_specs=[whole()] * 3 + [pl.BlockSpec(memory_space=pl.ANY)],
        out_specs=[whole()] * 3,
        compiler_params=vmem(4),
    )(expert_ids.T, modulation, router_weight.T, query)
    odd = [(i, i + 1) for i in range(1, devices - 1, 2)]
    after = lax.ppermute(pair, "dev", odd + [(j, i) for i, j in odd])
    cross = hop(cross, 1)

    units = gate_up_weight.shape[3]
    *ups, done = load(gate_up_weight.swapaxes(2, 3), query, 16)

    mine = {0: sent}
    for flip in range(2, steps):
        low = flip & -flip
        if flip > 2 and flip - low > 0:
            mine[flip] = hop(mine[flip - low], 2 * low)
        else:
            mine[flip] = tie(hop(sent, 2 * flip), done)
    own_weight = tie(own_weight, mine[2])
    pieces, weights = [(0, None), (1, None)], [own_weight, hop(own_weight, 2)]

    mixed = pl.pallas_call(
        attention_kernel,
        out_shape=struct((count, local_width), BF16),
        in_specs=[whole()] * 4 + [pl.BlockSpec(memory_space=pl.ANY)],
        out_specs=whole(),
        compiler_params=vmem(6),
    )(query, pair, cross, after, small)
    for flip in range(2, steps):
        if split:
            if flip == steps - 1:
                mine[flip] = tie(mine[flip], mixed)
            theirs = lax.ppermute(mine[flip], "groups", [(0, 1), (1, 0)])
            pieces += [(flip, 0), (flip, 1)]
            weights += [mine[flip], theirs]
        else:
            pieces.append((flip, None))
            weights.append(mine[flip])
    keep, send = pl.pallas_call(
        functools.partial(projection_kernel, steps, tuple(pieces)),
        out_shape=[struct((2 * count, lanes), F32)] * 2,
        in_specs=[whole()] * (2 + len(weights)),
        out_specs=[whole()] * 2,
        scratch_shapes=[pltpu.VMEM((2, 2 * count, lanes), F32)],
        compiler_params=vmem(6),
    )(mixed, hop(mixed, 1), *weights)
    shard = pl.pallas_call(
        state_kernel,
        out_shape=struct((2 * count + TILE, lanes), BF16),
        in_specs=[whole()] * 6,
        out_specs=whole(),
        compiler_params=vmem(6),
    )(keep, swap(send), near, cross, ids, small)

    slots = local * SLOTS
    state = None
    picked, backs = [], []
    column = {0: shard, 1: hop(shard, 2)}
    across = hop(shard, 1)
    column[1] = tie(column[1], across)
    crossing = {0: across, 1: hop(column[1], 1)}
    beside = swap(column[1])
    column[2] = tie(hop(shard, 4), beside)
    for flip in range(3, steps):
        low = flip & -flip
        column[flip] = hop(column[flip - low] if flip > low else shard, 2 * low)
    for flip in range(steps):
        if flip == steps - 1:
            column[flip] = tie(column[flip], picked[0])
        block = column[flip]
        crossed = crossing[flip] if flip in crossing else hop(block, 1)
        if flip == steps - 1:
            crossed = tie(crossed, *picked[1:])
        own = flip == 0
        results = pl.pallas_call(
            functools.partial(select_kernel, local, topk, own),
            out_shape=[
                struct((local, 2 * SLOTS, width), BF16),
                struct((2, count, slots), BF16),
            ]
            + ([struct((count, 2 * lanes), BF16)] if own else []),
            in_specs=[whole()] * 6,
            out_specs=[whole()] * (3 if own else 2),
            scratch_shapes=[pltpu.VMEM((count, width), BF16), pltpu.VMEM((experts, count), F32)],
            compiler_params=vmem(6),
        )(block, crossed, beside if flip == 1 else swap(block), swap(crossed), small, router)
        picked.append(results[0])
        backs.append(results[1])
        if own:
            state = results[2]

    sources = 2 * steps
    room = sources * SLOTS
    hidden = pl.pallas_call(
        functools.partial(hidden_kernel, steps),
        out_shape=struct((local, room, 2 * units), BF16),
        in_specs=[whole()] * (steps + local),
        out_specs=whole(),
        compiler_params=vmem(6),
    )(*picked, *ups)
    share = pl.pallas_call(
        functools.partial(output_kernel, steps),
        out_shape=[struct((count, 2 * lanes), BF16)] * sources,
        in_specs=[whole()] * (3 + steps),
        out_specs=[whole()] * sources,
        scratch_shapes=[pltpu.VMEM((sources, slots, 2 * lanes), BF16)],
        compiler_params=vmem(8),
    )(hidden, swap(hidden), down_weight, *backs)

    terms = [share[0]]
    for flip in range(steps - 1, -1, -1):
        crossed = hop(share[2 * flip + 1], 1)
        if flip:
            crossed = (share[2 * flip].astype(F32) + crossed.astype(F32)).astype(BF16)
            crossed = hop(crossed, 2 * flip)
        terms.append(crossed)
    return pl.pallas_call(
        final_kernel,
        out_shape=struct((count, 2 * lanes), BF16),
        in_specs=[whole()] * (2 + len(terms)),
        out_specs=whole(),
        compiler_params=vmem(8),
    )(state, small, *terms)


def extended(cells, sides, width):
    for axis, dim in sides:
        count = lax.axis_size(axis)
        ends = count - 1
        head = lax.slice_in_dim(cells, 0, width, axis=dim)
        tail = lax.slice_in_dim(cells, cells.shape[dim] - width, cells.shape[dim], axis=dim)
        cells = jnp.concatenate(
            [
                lax.ppermute(tail, axis, [(i, (i + 1) % count) for i in range(ends)]),
                cells,
                lax.ppermute(head, axis, [((i + 1) % count, i) for i in range(ends)]),
            ],
            axis=dim,
        )
    return cells


def window_attention(query, keys, values, index, total):
    count = query.shape[0]
    rows = jnp.arange(count, dtype=jnp.int32)[:, None]
    cols = jnp.arange(3 * count, dtype=jnp.int32)[None, :] - count
    place = index * count + cols
    allowed = (jnp.abs(cols - rows) <= count) & (place >= 0) & (place < total)
    scores = jnp.einsum(
        "qhd,khd->hqk", query, keys, preferred_element_type=jnp.float32
    ) / math.sqrt(query.shape[2])
    scores = jnp.where(allowed[None], scores, NEG)
    top = jnp.max(scores, -1, keepdims=True)
    weight = jnp.exp(scores - top)
    weight = (weight / jnp.sum(weight, -1, keepdims=True)).astype(jnp.bfloat16)
    mixed = jnp.einsum("hqk,khd->qhd", weight, values, preferred_element_type=jnp.float32)
    return mixed.astype(jnp.bfloat16)


def normalize(state, modulation):
    scale = lax.rsqrt(jnp.mean(state * state, -1, keepdims=True) + EPS)
    return (state * scale * (1.0 + modulation[2]) + modulation[1]).astype(jnp.bfloat16)


def route(normed, router_weight, expert_ids):
    logits = jnp.dot(normed, router_weight, preferred_element_type=jnp.float32)
    experts = router_weight.shape[1]
    match = expert_ids[:, :, None] == jnp.arange(experts, dtype=jnp.int32)[None, None, :]
    picked = jnp.sum(jnp.where(match, logits[:, None, :], 0.0), -1)
    lifted = jax.nn.sigmoid(picked)
    return lifted / jnp.sum(lifted, -1, keepdims=True)


def exchanged_body(
    tokens,
    query_key_value,
    out_weight,
    modulation,
    router_weight,
    expert_ids,
    gate_up_weight,
    down_weight,
):
    count = tokens.shape[0]
    width = tokens.shape[1]
    parts = lax.axis_size("sub")
    part = lax.axis_index("sub")
    position = lax.axis_index("dev")
    devices = lax.axis_size("dev")
    total = count * devices
    local_width = query_key_value.shape[2]
    heads_here = local_width // HEAD
    query = query_key_value[:, 0].reshape(count, heads_here, HEAD)
    pair = query_key_value[:, 1:]
    near = extended(pair, (("dev", 0),), count)
    keys = near[:, 0].reshape(3 * count, heads_here, HEAD)
    values = near[:, 1].reshape(3 * count, heads_here, HEAD)
    mixed = window_attention(query, keys, values, position, total).reshape(count, local_width)
    partial_proj = lax.dot_general(
        mixed,
        lax.all_gather(out_weight, "dev", axis=0, tiled=True),
        (((1,), (1,)), ((), ())),
        preferred_element_type=jnp.float32,
    )
    proj = lax.psum(partial_proj, "sub")
    state = tokens.astype(jnp.float32) + (1.0 + modulation[0]) * proj
    normed = normalize(state, modulation)
    gates = route(normed, router_weight, expert_ids)
    experts = router_weight.shape[1]
    topk = expert_ids.shape[1]
    flat = expert_ids.reshape(-1)
    picks = flat.shape[0]
    onehot = (flat[:, None] == jnp.arange(experts, dtype=jnp.int32)[None, :]).astype(BF16)
    order = jnp.arange(picks, dtype=jnp.int32)
    earlier = (order[None, :] < order[:, None]).astype(BF16)
    ahead = jnp.dot(earlier, onehot, preferred_element_type=F32)
    rank = jnp.sum(ahead * onehot.astype(F32), 1).astype(jnp.int32)
    target = flat * CAP + rank
    hit = target[None, :] == jnp.arange(experts * CAP, dtype=jnp.int32)[:, None]
    owner = jnp.any(hit.reshape(experts * CAP, count, topk), 2).astype(BF16)
    slice_width = width // parts
    sent = lax.dynamic_slice_in_dim(normed, part * slice_width, slice_width, 1)
    sent_width = sent.shape[1]
    rows_out = jnp.dot(owner, sent, preferred_element_type=F32).astype(BF16)
    halves_here = gate_up_weight.shape[0]
    doubled = jnp.broadcast_to(
        rows_out.reshape(experts, 1, CAP, sent_width), (experts, 2, CAP, sent_width)
    )
    outgoing = doubled.reshape(devices, halves_here, CAP, sent_width)
    up_form = "sxcd,xgdf->sxcgf"
    down_form = "sxcf,xfd->sxcd"
    incoming = lax.all_to_all(outgoing, "dev", split_axis=0, concat_axis=0, tiled=True)
    both = jnp.einsum(
        up_form,
        lax.all_gather(incoming, "sub", axis=3, tiled=True),
        gate_up_weight,
        preferred_element_type=jnp.float32,
    )
    hidden = (jax.nn.silu(both[..., 0, :]) * both[..., 1, :]).astype(jnp.bfloat16)
    gathered = lax.all_gather(hidden, "sub", axis=hidden.ndim - 1, tiled=True)
    result = jnp.einsum(down_form, gathered, down_weight, preferred_element_type=jnp.float32)
    returned = lax.all_to_all(
        result.astype(jnp.bfloat16), "dev", split_axis=0, concat_axis=0, tiled=True
    )
    own_width = returned.shape[-1]
    arranged = returned.reshape(experts, 2, CAP, own_width)
    combined = arranged[:, 0].astype(F32) + arranged[:, 1].astype(F32)
    share = jnp.sum(
        jnp.where(hit.reshape(experts * CAP, count, topk), gates[None], 0.0), 2
    )
    routed = lax.dot_general(
        share,
        combined.reshape(experts * CAP, own_width),
        (((0,), (0,)), ((), ())),
        precision=lax.Precision.HIGHEST,
        preferred_element_type=F32,
    )
    own = lax.dynamic_slice_in_dim(state, part * slice_width, slice_width, 1)
    lift = lax.dynamic_slice_in_dim(modulation[3], part * slice_width, slice_width, 0)
    return (own + (1.0 + lift) * routed).astype(jnp.bfloat16)


def body(*arrays):
    tokens, router_weight, expert_ids, gate_up_weight = arrays[0], arrays[4], arrays[5], arrays[6]
    devices = lax.axis_size("dev")
    count, width = tokens.shape
    local = gate_up_weight.shape[0] // 2
    fits = (
        lax.axis_size("sub") == 2
        and devices >= 8
        and devices & (devices - 1) == 0
        and gate_up_weight.shape[0] % 2 == 0
        and width % (devices * 128) == 0
        and arrays[1].shape[2] * 2 == width
        and count % HEAD == 0
        and expert_ids.shape[1] * count <= width // 4
        and router_weight.shape[1] <= 256
    )
    if fits and count * devices <= 2 * local * devices * CAP:
        return gathered_body(*arrays)
    return exchanged_body(*arrays)


def solution(mesh):
    return jax.shard_map(
        body,
        mesh=mesh,
        in_specs=(
            P(("groups", "dev"), None),
            P(("groups", "dev"), None, "sub"),
            P("dev", "sub"),
            P("groups", None),
            P(),
            P(("groups", "dev"), None),
            P("dev", None, None, "sub"),
            P("dev", None, "sub"),
        ),
        out_specs=P(("groups", "dev"), "sub"),
        check_vma=False,
    )
```

```python
import functools
import math

import jax
import jax.numpy as jnp
from jax import lax
from jax.experimental import pallas as pl
from jax.experimental.pallas import tpu as pltpu
from jax.sharding import PartitionSpec as P

HEAD = 128
CAP = 12
SLOTS = 16
TILE = 16

EPS = 1e-06
NEG = -1e30
F32 = jnp.float32
BF16 = jnp.bfloat16

NT = (((1,), (1,)), ((), ()))


def vmem(mib):
    return pltpu.CompilerParams(vmem_limit_bytes=mib * 2**20)


def whole():
    return pl.BlockSpec(memory_space=pltpu.VMEM)


def cut_kernel(split, tokens_ref, qkv_ref, weight_ref, *refs):
    query_ref, pair_ref, near_ref, cross_ref, sent_ref, own_ref, sem_ref = refs
    count, lanes = near_ref.shape
    chunk = tokens_ref.shape[1] // lax.axis_size("dev")
    side = lax.axis_index("dev") % 2
    part = lax.axis_index("sub")
    half = count // 2
    moves = [
        (qkv_ref.at[1], pair_ref.at[:count]),
        (qkv_ref.at[2], pair_ref.at[count:]),
        (qkv_ref.at[1], cross_ref.at[:count]),
        (qkv_ref.at[2], cross_ref.at[count : 2 * count]),
    ]
    for i in range(lanes // chunk):
        at = pl.multiple_of(part * 2 * lanes + (2 * i + 1 - side) * chunk, 128)
        for j in range(2):
            left = j * lanes + i * chunk
            moves.append(
                (
                    tokens_ref.at[j * half : (j + 1) * half, pl.ds(at, chunk)],
                    cross_ref.at[2 * count :, left : left + chunk],
                )
            )
        at = pl.multiple_of(part * 2 * lanes + (2 * i + side) * chunk, 128)
        moves.append(
            (tokens_ref.at[:, pl.ds(at, chunk)], near_ref.at[:, i * chunk : (i + 1) * chunk])
        )
    rows = sent_ref.shape[0]
    at = pl.multiple_of(lax.axis_index("groups") * rows if split else 0, TILE)
    moves += [
        (weight_ref.at[pl.ds(at, rows)], sent_ref),
        (qkv_ref.at[0], query_ref),
        (weight_ref, own_ref),
    ]
    copies = [pltpu.make_async_copy(*move, sem_ref.at[n]) for n, move in enumerate(moves)]
    for copy in copies:
        copy.start()
    for copy in copies:
        copy.wait()


def small_kernel(ids_ref, mod_ref, router_ref, _, row_ref, mod_to_ref, router_to_ref):
    topk, count = ids_ref.shape
    row_ref[...] = jnp.zeros(row_ref.shape, BF16)
    for k in range(topk):
        named = jnp.broadcast_to(ids_ref[k : k + 1, :], (TILE, count))
        row_ref[:, k * count : (k + 1) * count] = named.astype(F32).astype(BF16)
    mod_to_ref[...] = mod_ref[...]
    router_to_ref[...] = router_ref[...]


def attention_kernel(query_ref, own_ref, cross_ref, next_ref, *refs):
    mixed_ref = refs[-1]
    count, width = mixed_ref.shape
    place = lax.axis_index("dev")
    even = place % 2 == 0
    row = lax.broadcasted_iota(jnp.int32, (count, count), 0)
    col = lax.broadcasted_iota(jnp.int32, (count, count), 1)
    alone = (place == 0) | (place == lax.axis_size("dev") - 1)
    see_cross = jnp.where(even, col - row, row - col) <= 0
    see_next = (jnp.where(even, row - col, col - row) <= 0) & jnp.logical_not(alone)
    scale = 1.0 / math.sqrt(HEAD)

    def scored(q, k):
        return lax.dot_general(q, k, NT, preferred_element_type=F32) * scale

    for head in range(width // HEAD):
        lanes = slice(head * HEAD, (head + 1) * HEAD)
        q = query_ref[:, lanes]
        sc = jnp.where(see_cross, scored(q, cross_ref[:count, lanes]), NEG)
        so = scored(q, own_ref[:count, lanes])
        sn = jnp.where(see_next, scored(q, next_ref[:count, lanes]), NEG)
        top = jnp.max(jnp.maximum(jnp.maximum(sc, so), sn), 1, keepdims=True)
        wc, wo, wn = jnp.exp(sc - top), jnp.exp(so - top), jnp.exp(sn - top)
        inv = 1.0 / jnp.sum(wc + wo + wn, 1, keepdims=True)
        out = 0.0
        for weight, value in (
            (wo, own_ref[count:, lanes]),
            (wc, cross_ref[count : 2 * count, lanes]),
            (wn, next_ref[count:, lanes]),
        ):
            out += jnp.dot((weight * inv).astype(BF16), value, preferred_element_type=F32)
        mixed_ref[:, lanes] = out.astype(BF16)


def projection_kernel(steps, pieces, *refs):
    mixed_ref, other_ref = refs[0], refs[1]
    weight_refs = refs[2 : 2 + len(pieces)]
    keep_ref, send_ref, both_ref = refs[-3:]
    count = mixed_ref.shape[0]
    half = steps // 2
    chunk = keep_ref.shape[1] // half
    z = lax.axis_index("dev") // 2
    part = lax.axis_index("sub")
    group = lax.axis_index("groups")
    for (hop, side), w_ref in zip(pieces, weight_refs):
        rows = w_ref.shape[0]
        target = jnp.bitwise_xor(z, hop)
        away = jnp.where(target // half == part, 0, 1)
        lane = (target % half) * chunk
        if side is not None:
            lane += (group if side == 0 else 1 - group) * rows
        lane = pl.multiple_of(lane, 128)
        for block, ref in enumerate((mixed_ref, other_ref)):
            both_ref[away, block * count : (block + 1) * count, pl.ds(lane, rows)] = (
                lax.dot_general(ref[...], w_ref[...], NT, preferred_element_type=F32)
            )
    keep_ref[...] = both_ref[0]
    send_ref[...] = both_ref[1]


def state_kernel(keep_ref, got_ref, near_ref, cross_ref, ids_ref, mod_ref, out_ref):
    count, lanes = near_ref.shape
    half = count // 2
    chunk = mod_ref.shape[1] // lax.axis_size("dev")
    side = lax.axis_index("dev") % 2
    part = lax.axis_index("sub")
    for i in range(lanes // chunk):
        at = pl.multiple_of(part * 2 * lanes + (2 * i + side) * chunk, 128)
        lift = 1.0 + mod_ref[0:1, pl.ds(at, chunk)]
        cols = slice(i * chunk, (i + 1) * chunk)
        for j in range(4):
            rows = slice(j * half, (j + 1) * half)
            if j < 2:
                token = near_ref[rows, cols]
            else:
                left = (j - 2) * lanes + i * chunk
                token = cross_ref[2 * count :, left : left + chunk]
            proj = keep_ref[rows, cols] + got_ref[rows, cols]
            out_ref[rows, cols] = (token.astype(F32) + lift * proj).astype(BF16)
    out_ref[2 * count :, :] = ids_ref[...]


def tie_kernel(*refs):
    pass


def tie(array, *others):
    anywhere = pl.BlockSpec(memory_space=pl.ANY)
    return pl.pallas_call(
        tie_kernel,
        out_shape=jax.ShapeDtypeStruct(array.shape, array.dtype),
        in_specs=[anywhere] * (1 + len(others)),
        out_specs=anywhere,
        input_output_aliases={0: 0},
        compiler_params=vmem(1),
    )(array, *others)


def select_kernel(local, topk, own, *refs):
    shard_refs, (mod_ref, router_ref) = refs[:4], refs[4:6]
    rows_ref, back_ref = refs[6:8]
    state_ref = refs[8] if own else None
    full_ref, gate_ref = refs[-2:]
    count, width = full_ref.shape
    lanes = shard_refs[0].shape[1]
    device = lax.axis_index("dev")
    side = device % 2
    part = lax.axis_index("sub")
    chunk = width // lax.axis_size("dev")
    experts = router_ref.shape[0]
    slots = local * SLOTS
    before = lax.broadcasted_iota(jnp.int32, (count, count), 0)
    after = lax.broadcasted_iota(jnp.int32, (count, count), 1)
    earlier = (before < after).astype(F32).astype(BF16)
    slot = lax.broadcasted_iota(jnp.int32, (slots, count), 0) % SLOTS
    mine = lax.broadcasted_iota(jnp.int32, (local, count), 0) + device * local
    every = lax.broadcasted_iota(jnp.int32, (experts, count), 0)
    for cross in range(2):
        for far_half in range(2):
            for far_side in range(2):
                ref = shard_refs[2 * far_half + far_side]
                top = (cross ^ far_side) * count
                half = part if far_half == 0 else 1 - part
                parity = side if far_side == 0 else 1 - side
                for i in range(lanes // chunk):
                    block = ref[top : top + count, i * chunk : (i + 1) * chunk]
                    at = (2 * i + parity) * chunk
                    full_ref[:, pl.ds(pl.multiple_of(half * 2 * lanes + at, 128), chunk)] = block
                    if own and cross == 0 and far_half == 0:
                        state_ref[:, pl.ds(pl.multiple_of(at, 128), chunk)] = block
        state = full_ref[...].astype(F32)
        scale = lax.rsqrt(jnp.mean(state * state, 1, keepdims=True) + EPS)
        normed = state * scale * (1.0 + mod_ref[2:3, :]) + mod_ref[1:2, :]
        normed = normed.astype(BF16)
        ids = shard_refs[cross][2 * count : 2 * count + TILE, :]
        ids = ids.astype(F32)[0:1, :].astype(jnp.int32)
        named = [ids[:, k * count : (k + 1) * count] for k in range(topk)]
        hot = sum((mine == n).astype(F32) for n in named)
        rank = jnp.dot(hot.astype(BF16), earlier, preferred_element_type=F32)
        rank = jnp.where(hot > 0.0, rank, -1.0)
        rank = jnp.concatenate(
            [jnp.broadcast_to(rank[e : e + 1], (SLOTS, count)) for e in range(local)]
        )
        pick = rank == slot.astype(F32)
        chosen = jnp.dot(
            jnp.where(pick, 1.0, 0.0).astype(BF16), normed, preferred_element_type=F32
        ).astype(BF16)
        for e in range(local):
            rows_ref[e, cross * SLOTS : (cross + 1) * SLOTS, :] = chosen[
                e * SLOTS : (e + 1) * SLOTS
            ]
        logits = lax.dot_general(router_ref[...], normed, NT, preferred_element_type=F32)
        lifted = sum(jnp.where(every == n, 1.0, 0.0) for n in named) * jax.nn.sigmoid(logits)
        gate_ref[...] = lifted / jnp.sum(lifted, 0, keepdims=True)
        here = gate_ref[pl.ds(pl.multiple_of(device * local, local), local), :]
        here = jnp.concatenate(
            [jnp.broadcast_to(here[e : e + 1], (SLOTS, count)) for e in range(local)]
        )
        back_ref[cross] = jnp.where(pick, here, 0.0).T.astype(BF16)


def load_kernel(from_ref, _, *refs):
    to_refs, done_ref, sem_ref = refs[:-2], refs[-2], refs[-1]
    copies = [
        pltpu.make_async_copy(from_ref.at[2 * e : 2 * e + 2], ref, sem_ref.at[e])
        for e, ref in enumerate(to_refs)
    ]
    for copy in copies:
        copy.start()
    done_ref[...] = jnp.zeros(done_ref.shape, F32)
    for copy in copies:
        copy.wait()


def load(weight, after_this, limit):
    local = weight.shape[0] // 2
    piece = jax.ShapeDtypeStruct((2, *weight.shape[1:]), BF16)
    return pl.pallas_call(
        load_kernel,
        out_shape=[piece] * local + [jax.ShapeDtypeStruct((8, 128), F32)],
        in_specs=[pl.BlockSpec(memory_space=pl.ANY)] * 2,
        out_specs=[whole()] * (local + 1),
        scratch_shapes=[pltpu.SemaphoreType.DMA((local,))],
        compiler_params=vmem(limit),
    )(weight, after_this)


def hidden_kernel(steps, *refs):
    rows_refs, w_refs, hidden_ref = refs[:steps], refs[steps:-1], refs[-1]
    for e, w_ref in enumerate(w_refs):
        rows = jnp.concatenate([ref[e] for ref in rows_refs])
        halves = []
        for b in range(2):
            gate = lax.dot_general(w_ref[b, 0], rows, NT, preferred_element_type=F32)
            up = lax.dot_general(w_ref[b, 1], rows, NT, preferred_element_type=F32)
            halves.append(jax.nn.silu(gate) * up)
        hidden_ref[e] = jnp.concatenate(halves).T.astype(BF16)


def output_kernel(steps, near_ref, far_ref, w_ref, *refs):
    back_refs, out_refs, held_ref = refs[:steps], refs[steps:-1], refs[-1]
    part = lax.axis_index("sub")
    units = near_ref.shape[2] // 2
    for e in range(near_ref.shape[0]):
        total = 0.0
        for ref, who in ((near_ref, part), (far_ref, 1 - part)):
            at = pl.multiple_of(who * units, 64)
            weight = jnp.concatenate([w_ref[2 * e + b, pl.ds(at, units), :] for b in range(2)])
            total += jnp.dot(ref[e], weight, preferred_element_type=F32)
        total = total.astype(BF16)
        for source in range(2 * steps):
            held_ref[source, e * SLOTS : (e + 1) * SLOTS, :] = total[
                source * SLOTS : (source + 1) * SLOTS
            ]
    for source in range(2 * steps):
        routed = jnp.dot(
            back_refs[source // 2][source % 2], held_ref[source], preferred_element_type=F32
        ).astype(BF16)
        if source < 2:
            out_refs[source][...] = routed
        else:
            half = routed.shape[0] // 2
            out_refs[2 * source - 2][...] = routed[:half]
            out_refs[2 * source - 1][...] = routed[half:]


def final_kernel(tops, state_ref, mod_ref, *refs):
    out_ref = refs[-1]
    count, lanes = state_ref.shape
    at = pl.multiple_of(lax.axis_index("sub") * lanes, 128)
    lift = 1.0 + mod_ref[3:4, pl.ds(at, lanes)]
    for h, terms in enumerate((refs[2 : 2 + tops], refs[2 + tops : -1])):
        rows = slice(h * count // 2, (h + 1) * count // 2)
        routed = refs[0][rows].astype(F32) + refs[1][rows].astype(F32)
        for ref in terms:
            routed += ref[...].astype(F32)
        out_ref[rows] = (state_ref[rows].astype(F32) + lift * routed).astype(BF16)


def gathered_body(
    tokens,
    query_key_value,
    out_weight,
    modulation,
    router_weight,
    expert_ids,
    gate_up_weight,
    down_weight,
):
    count, width = tokens.shape
    devices = lax.axis_size("dev")
    groups = lax.axis_size("groups")
    steps = devices // 2
    local_width = query_key_value.shape[2]
    chunk = width // devices
    lanes = width // 4
    halves_here = gate_up_weight.shape[0]
    local = halves_here // 2
    experts = router_weight.shape[1]
    topk = expert_ids.shape[1]
    struct = jax.ShapeDtypeStruct

    def hop(x, flip):
        return lax.ppermute(x, "dev", [(i, i ^ flip) for i in range(devices)])

    def swap(x):
        return lax.ppermute(x, "sub", [(0, 1), (1, 0)])

    split = groups == 2
    held = out_weight.shape[0] // (2 if split else 1)
    query, pair, near, cross, sent, own_weight = pl.pallas_call(
        functools.partial(cut_kernel, split),
        out_shape=[
            struct((count, local_width), BF16),
            struct((2 * count, local_width), BF16),
            struct((count, lanes), BF16),
            struct((2 * count + count // 2, local_width), BF16),
            struct((held, local_width), BF16),
            struct(out_weight.shape, BF16),
        ],
        in_specs=[pl.BlockSpec(memory_space=pl.ANY)] * 3,
        out_specs=[whole()] * 6,
        scratch_shapes=[pltpu.SemaphoreType.DMA((7 + 3 * (lanes // chunk),))],
        compiler_params=vmem(52),
    )(tokens, query_key_value.transpose(1, 0, 2), out_weight)
    ids, small, router = pl.pallas_call(
        small_kernel,
        out_shape=[
            struct((TILE, lanes), BF16),
            struct(modulation.shape, F32),
            struct((experts, width), BF16),
        ],
        in_specs=[whole()] * 3 + [pl.BlockSpec(memory_space=pl.ANY)],
        out_specs=[whole()] * 3,
        compiler_params=vmem(4),
    )(expert_ids.T, modulation, router_weight.T, query)
    odd = [(i, i + 1) for i in range(1, devices - 1, 2)]
    after = lax.ppermute(pair, "dev", odd + [(j, i) for i, j in odd])
    cross = hop(cross, 1)

    units = gate_up_weight.shape[3]
    *ups, done = load(gate_up_weight.swapaxes(2, 3), query, 16)

    mine = {0: sent}
    for flip in range(2, steps):
        low = flip & -flip
        if flip > 2 and flip - low > 0:
            mine[flip] = hop(mine[flip - low], 2 * low)
        else:
            mine[flip] = tie(hop(sent, 2 * flip), done)
    own_weight = tie(own_weight, mine[2])
    pieces, weights = [(0, None), (1, None)], [own_weight, hop(own_weight, 2)]

    mixed = pl.pallas_call(
        attention_kernel,
        out_shape=struct((count, local_width), BF16),
        in_specs=[whole()] * 4 + [pl.BlockSpec(memory_space=pl.ANY)],
        out_specs=whole(),
        compiler_params=vmem(6),
    )(query, pair, cross, after, small)
    for flip in range(2, steps):
        if split:
            if flip == steps - 1:
                mine[flip] = tie(mine[flip], mixed)
            theirs = lax.ppermute(mine[flip], "groups", [(0, 1), (1, 0)])
            pieces += [(flip, 0), (flip, 1)]
            weights += [mine[flip], theirs]
        else:
            pieces.append((flip, None))
            weights.append(mine[flip])
    keep, send = pl.pallas_call(
        functools.partial(projection_kernel, steps, tuple(pieces)),
        out_shape=[struct((2 * count, lanes), F32)] * 2,
        in_specs=[whole()] * (2 + len(weights)),
        out_specs=[whole()] * 2,
        scratch_shapes=[pltpu.VMEM((2, 2 * count, lanes), F32)],
        compiler_params=vmem(6),
    )(mixed, hop(mixed, 1), *weights)
    shard = pl.pallas_call(
        state_kernel,
        out_shape=struct((2 * count + TILE, lanes), BF16),
        in_specs=[whole()] * 6,
        out_specs=whole(),
        compiler_params=vmem(6),
    )(keep, swap(send), near, cross, ids, small)

    slots = local * SLOTS
    state = None
    picked, backs = [], []
    column = {0: shard, 1: hop(shard, 2)}
    across = hop(shard, 1)
    column[1] = tie(column[1], across)
    crossing = {0: across, 1: hop(column[1], 1)}
    beside = swap(column[1])
    column[2] = tie(hop(shard, 4), beside)
    for flip in range(3, steps):
        low = flip & -flip
        column[flip] = hop(column[flip - low] if flip > low else shard, 2 * low)
    for flip in range(steps):
        if flip == steps - 1:
            column[flip] = tie(column[flip], picked[0])
        block = column[flip]
        crossed = crossing[flip] if flip in crossing else hop(block, 1)
        if flip == steps - 1:
            crossed = tie(crossed, *picked[1:])
        own = flip == 0
        results = pl.pallas_call(
            functools.partial(select_kernel, local, topk, own),
            out_shape=[
                struct((local, 2 * SLOTS, width), BF16),
                struct((2, count, slots), BF16),
            ]
            + ([struct((count, 2 * lanes), BF16)] if own else []),
            in_specs=[whole()] * 6,
            out_specs=[whole()] * (3 if own else 2),
            scratch_shapes=[pltpu.VMEM((count, width), BF16), pltpu.VMEM((experts, count), F32)],
            compiler_params=vmem(6),
        )(block, crossed, beside if flip == 1 else swap(block), swap(crossed), small, router)
        picked.append(results[0])
        backs.append(results[1])
        if own:
            state = results[2]

    sources = 2 * steps
    room = sources * SLOTS
    hidden = pl.pallas_call(
        functools.partial(hidden_kernel, steps),
        out_shape=struct((local, room, 2 * units), BF16),
        in_specs=[whole()] * (steps + local),
        out_specs=whole(),
        compiler_params=vmem(6),
    )(*picked, *ups)
    share = pl.pallas_call(
        functools.partial(output_kernel, steps),
        out_shape=[struct((count, 2 * lanes), BF16)] * 2
        + [struct((count // 2, 2 * lanes), BF16)] * (2 * sources - 4),
        in_specs=[whole()] * (3 + steps),
        out_specs=[whole()] * (2 * sources - 2),
        scratch_shapes=[pltpu.VMEM((sources, slots, 2 * lanes), BF16)],
        compiler_params=vmem(8),
    )(hidden, swap(hidden), down_weight, *backs)

    def added(x, y):
        return (x.astype(F32) + y.astype(F32)).astype(BF16)

    parts = {j: list(share[4 * j - 2 : 4 * j + 2]) for j in range(1, steps)}
    crossed = {
        (j, h): hop(parts[j][2 + h], 1) for j in range(steps - 1, 0, -1) for h in range(2)
    }
    across = hop(share[1], 1)
    merged = {}
    tops, bottoms = [], []
    for j in range(steps - 1, 0, -1):
        tops.append(hop(added(parts[j][0], crossed[j, 0]), 2 * j))
        bottom = added(parts[j][1], crossed[j, 1])
        for extra in merged.get(j, []):
            bottom = added(bottom, extra)
        low = j & -j
        if j == low:
            bottoms.append(hop(bottom, 2 * j))
        else:
            merged.setdefault(j - low, []).append(hop(bottom, 2 * low))
    return pl.pallas_call(
        functools.partial(final_kernel, len(tops)),
        out_shape=struct((count, 2 * lanes), BF16),
        in_specs=[whole()] * (4 + len(tops) + len(bottoms)),
        out_specs=whole(),
        compiler_params=vmem(8),
    )(state, small, share[0], across, *tops, *bottoms)


def extended(cells, sides, width):
    for axis, dim in sides:
        count = lax.axis_size(axis)
        ends = count - 1
        head = lax.slice_in_dim(cells, 0, width, axis=dim)
        tail = lax.slice_in_dim(cells, cells.shape[dim] - width, cells.shape[dim], axis=dim)
        cells = jnp.concatenate(
            [
                lax.ppermute(tail, axis, [(i, (i + 1) % count) for i in range(ends)]),
                cells,
                lax.ppermute(head, axis, [((i + 1) % count, i) for i in range(ends)]),
            ],
            axis=dim,
        )
    return cells


def window_attention(query, keys, values, index, total):
    count = query.shape[0]
    rows = jnp.arange(count, dtype=jnp.int32)[:, None]
    cols = jnp.arange(3 * count, dtype=jnp.int32)[None, :] - count
    place = index * count + cols
    allowed = (jnp.abs(cols - rows) <= count) & (place >= 0) & (place < total)
    scores = jnp.einsum(
        "qhd,khd->hqk", query, keys, preferred_element_type=jnp.float32
    ) / math.sqrt(query.shape[2])
    scores = jnp.where(allowed[None], scores, NEG)
    top = jnp.max(scores, -1, keepdims=True)
    weight = jnp.exp(scores - top)
    weight = (weight / jnp.sum(weight, -1, keepdims=True)).astype(jnp.bfloat16)
    mixed = jnp.einsum("hqk,khd->qhd", weight, values, preferred_element_type=jnp.float32)
    return mixed.astype(jnp.bfloat16)


def normalize(state, modulation):
    scale = lax.rsqrt(jnp.mean(state * state, -1, keepdims=True) + EPS)
    return (state * scale * (1.0 + modulation[2]) + modulation[1]).astype(jnp.bfloat16)


def route(normed, router_weight, expert_ids):
    logits = jnp.dot(normed, router_weight, preferred_element_type=jnp.float32)
    experts = router_weight.shape[1]
    match = expert_ids[:, :, None] == jnp.arange(experts, dtype=jnp.int32)[None, None, :]
    picked = jnp.sum(jnp.where(match, logits[:, None, :], 0.0), -1)
    lifted = jax.nn.sigmoid(picked)
    return lifted / jnp.sum(lifted, -1, keepdims=True)


def exchanged_body(
    tokens,
    query_key_value,
    out_weight,
    modulation,
    router_weight,
    expert_ids,
    gate_up_weight,
    down_weight,
):
    count = tokens.shape[0]
    width = tokens.shape[1]
    parts = lax.axis_size("sub")
    part = lax.axis_index("sub")
    position = lax.axis_index("dev")
    devices = lax.axis_size("dev")
    total = count * devices
    local_width = query_key_value.shape[2]
    heads_here = local_width // HEAD
    query = query_key_value[:, 0].reshape(count, heads_here, HEAD)
    pair = query_key_value[:, 1:]
    near = extended(pair, (("dev", 0),), count)
    keys = near[:, 0].reshape(3 * count, heads_here, HEAD)
    values = near[:, 1].reshape(3 * count, heads_here, HEAD)
    mixed = window_attention(query, keys, values, position, total).reshape(count, local_width)
    partial_proj = lax.dot_general(
        mixed,
        lax.all_gather(out_weight, "dev", axis=0, tiled=True),
        (((1,), (1,)), ((), ())),
        preferred_element_type=jnp.float32,
    )
    proj = lax.psum(partial_proj, "sub")
    state = tokens.astype(jnp.float32) + (1.0 + modulation[0]) * proj
    normed = normalize(state, modulation)
    gates = route(normed, router_weight, expert_ids)
    experts = router_weight.shape[1]
    topk = expert_ids.shape[1]
    flat = expert_ids.reshape(-1)
    picks = flat.shape[0]
    onehot = (flat[:, None] == jnp.arange(experts, dtype=jnp.int32)[None, :]).astype(BF16)
    order = jnp.arange(picks, dtype=jnp.int32)
    earlier = (order[None, :] < order[:, None]).astype(BF16)
    ahead = jnp.dot(earlier, onehot, preferred_element_type=F32)
    rank = jnp.sum(ahead * onehot.astype(F32), 1).astype(jnp.int32)
    target = flat * CAP + rank
    hit = target[None, :] == jnp.arange(experts * CAP, dtype=jnp.int32)[:, None]
    owner = jnp.any(hit.reshape(experts * CAP, count, topk), 2).astype(BF16)
    slice_width = width // parts
    sent = lax.dynamic_slice_in_dim(normed, part * slice_width, slice_width, 1)
    sent_width = sent.shape[1]
    rows_out = jnp.dot(owner, sent, preferred_element_type=F32).astype(BF16)
    halves_here = gate_up_weight.shape[0]
    doubled = jnp.broadcast_to(
        rows_out.reshape(experts, 1, CAP, sent_width), (experts, 2, CAP, sent_width)
    )
    outgoing = doubled.reshape(devices, halves_here, CAP, sent_width)
    up_form = "sxcd,xgdf->sxcgf"
    down_form = "sxcf,xfd->sxcd"
    incoming = lax.all_to_all(outgoing, "dev", split_axis=0, concat_axis=0, tiled=True)
    both = jnp.einsum(
        up_form,
        lax.all_gather(incoming, "sub", axis=3, tiled=True),
        gate_up_weight,
        preferred_element_type=jnp.float32,
    )
    hidden = (jax.nn.silu(both[..., 0, :]) * both[..., 1, :]).astype(jnp.bfloat16)
    gathered = lax.all_gather(hidden, "sub", axis=hidden.ndim - 1, tiled=True)
    result = jnp.einsum(down_form, gathered, down_weight, preferred_element_type=jnp.float32)
    returned = lax.all_to_all(
        result.astype(jnp.bfloat16), "dev", split_axis=0, concat_axis=0, tiled=True
    )
    own_width = returned.shape[-1]
    arranged = returned.reshape(experts, 2, CAP, own_width)
    combined = arranged[:, 0].astype(F32) + arranged[:, 1].astype(F32)
    share = jnp.sum(
        jnp.where(hit.reshape(experts * CAP, count, topk), gates[None], 0.0), 2
    )
    routed = lax.dot_general(
        share,
        combined.reshape(experts * CAP, own_width),
        (((0,), (0,)), ((), ())),
        precision=lax.Precision.HIGHEST,
        preferred_element_type=F32,
    )
    own = lax.dynamic_slice_in_dim(state, part * slice_width, slice_width, 1)
    lift = lax.dynamic_slice_in_dim(modulation[3], part * slice_width, slice_width, 0)
    return (own + (1.0 + lift) * routed).astype(jnp.bfloat16)


def body(*arrays):
    tokens, router_weight, expert_ids, gate_up_weight = arrays[0], arrays[4], arrays[5], arrays[6]
    devices = lax.axis_size("dev")
    count, width = tokens.shape
    local = gate_up_weight.shape[0] // 2
    fits = (
        lax.axis_size("sub") == 2
        and devices >= 8
        and devices & (devices - 1) == 0
        and gate_up_weight.shape[0] % 2 == 0
        and width % (devices * 128) == 0
        and arrays[1].shape[2] * 2 == width
        and count % HEAD == 0
        and expert_ids.shape[1] * count <= width // 4
        and router_weight.shape[1] <= 256
    )
    if fits and count * devices <= 2 * local * devices * CAP:
        return gathered_body(*arrays)
    return exchanged_body(*arrays)


def solution(mesh):
    return jax.shard_map(
        body,
        mesh=mesh,
        in_specs=(
            P(("groups", "dev"), None),
            P(("groups", "dev"), None, "sub"),
            P("dev", "sub"),
            P("groups", None),
            P(),
            P(("groups", "dev"), None),
            P("dev", None, None, "sub"),
            P("dev", None, "sub"),
        ),
        out_specs=P(("groups", "dev"), "sub"),
        check_vma=False,
    )
```

```python
import functools
import math

import jax
import jax.numpy as jnp
from jax import lax
from jax.experimental import pallas as pl
from jax.experimental.pallas import tpu as pltpu
from jax.sharding import PartitionSpec as P

HEAD = 128
CAP = 12
SLOTS = 16
TILE = 16

EPS = 1e-06
NEG = -1e30
F32 = jnp.float32
BF16 = jnp.bfloat16

NT = (((1,), (1,)), ((), ()))


def vmem(mib):
    return pltpu.CompilerParams(vmem_limit_bytes=mib * 2**20)


def whole():
    return pl.BlockSpec(memory_space=pltpu.VMEM)


def cut_kernel(split, tokens_ref, qkv_ref, weight_ref, *refs):
    pair_ref, cross_ref, sent_ref, sem_ref = refs
    count = pair_ref.shape[0] // 2
    lanes = tokens_ref.shape[1] // 4
    chunk = tokens_ref.shape[1] // lax.axis_size("dev")
    side = lax.axis_index("dev") % 2
    part = lax.axis_index("sub")
    half = count // 2
    moves = [
        (qkv_ref.at[1], pair_ref.at[:count]),
        (qkv_ref.at[2], pair_ref.at[count:]),
        (qkv_ref.at[1], cross_ref.at[:count]),
        (qkv_ref.at[2], cross_ref.at[count : 2 * count]),
    ]
    for i in range(lanes // chunk):
        at = pl.multiple_of(part * 2 * lanes + (2 * i + 1 - side) * chunk, 128)
        for j in range(2):
            left = j * lanes + i * chunk
            moves.append(
                (
                    tokens_ref.at[j * half : (j + 1) * half, pl.ds(at, chunk)],
                    cross_ref.at[2 * count :, left : left + chunk],
                )
            )
    rows = sent_ref.shape[0]
    at = pl.multiple_of(lax.axis_index("groups") * rows if split else 0, TILE)
    moves.append((weight_ref.at[pl.ds(at, rows)], sent_ref))
    copies = [pltpu.make_async_copy(*move, sem_ref.at[n]) for n, move in enumerate(moves)]
    for copy in copies:
        copy.start()
    for copy in copies:
        copy.wait()


def rest_kernel(tokens_ref, qkv_ref, weight_ref, _, query_ref, near_ref, own_ref, sem_ref):
    lanes = near_ref.shape[1]
    chunk = tokens_ref.shape[1] // lax.axis_size("dev")
    side = lax.axis_index("dev") % 2
    part = lax.axis_index("sub")
    moves = [(qkv_ref.at[0], query_ref), (weight_ref, own_ref)]
    for i in range(lanes // chunk):
        at = pl.multiple_of(part * 2 * lanes + (2 * i + side) * chunk, 128)
        moves.append(
            (tokens_ref.at[:, pl.ds(at, chunk)], near_ref.at[:, i * chunk : (i + 1) * chunk])
        )
    copies = [pltpu.make_async_copy(*move, sem_ref.at[n]) for n, move in enumerate(moves)]
    for copy in copies:
        copy.start()
    for copy in copies:
        copy.wait()


def small_kernel(ids_ref, mod_ref, router_ref, _, row_ref, mod_to_ref, router_to_ref):
    topk, count = ids_ref.shape
    row_ref[...] = jnp.zeros(row_ref.shape, BF16)
    for k in range(topk):
        named = jnp.broadcast_to(ids_ref[k : k + 1, :], (TILE, count))
        row_ref[:, k * count : (k + 1) * count] = named.astype(F32).astype(BF16)
    mod_to_ref[...] = mod_ref[...]
    router_to_ref[...] = router_ref[...]


def attention_kernel(query_ref, own_ref, cross_ref, next_ref, *refs):
    mixed_ref = refs[-1]
    count, width = mixed_ref.shape
    place = lax.axis_index("dev")
    even = place % 2 == 0
    row = lax.broadcasted_iota(jnp.int32, (count, count), 0)
    col = lax.broadcasted_iota(jnp.int32, (count, count), 1)
    alone = (place == 0) | (place == lax.axis_size("dev") - 1)
    see_cross = jnp.where(even, col - row, row - col) <= 0
    see_next = (jnp.where(even, row - col, col - row) <= 0) & jnp.logical_not(alone)
    scale = 1.0 / math.sqrt(HEAD)

    def scored(q, k):
        return lax.dot_general(q, k, NT, preferred_element_type=F32) * scale

    for head in range(width // HEAD):
        lanes = slice(head * HEAD, (head + 1) * HEAD)
        q = query_ref[:, lanes]
        sc = jnp.where(see_cross, scored(q, cross_ref[:count, lanes]), NEG)
        so = scored(q, own_ref[:count, lanes])
        sn = jnp.where(see_next, scored(q, next_ref[:count, lanes]), NEG)
        top = jnp.max(jnp.maximum(jnp.maximum(sc, so), sn), 1, keepdims=True)
        wc, wo, wn = jnp.exp(sc - top), jnp.exp(so - top), jnp.exp(sn - top)
        inv = 1.0 / jnp.sum(wc + wo + wn, 1, keepdims=True)
        out = 0.0
        for weight, value in (
            (wo, own_ref[count:, lanes]),
            (wc, cross_ref[count : 2 * count, lanes]),
            (wn, next_ref[count:, lanes]),
        ):
            out += jnp.dot((weight * inv).astype(BF16), value, preferred_element_type=F32)
        mixed_ref[:, lanes] = out.astype(BF16)


def projection_kernel(steps, pieces, wanted, *refs):
    mixed_ref, other_ref = refs[0], refs[1]
    weight_refs = refs[2 : 2 + len(pieces)]
    out_ref = refs[2 + len(pieces)]
    count = mixed_ref.shape[0]
    half = steps // 2
    chunk = out_ref.shape[1] // half
    z = lax.axis_index("dev") // 2
    part = lax.axis_index("sub")
    group = lax.axis_index("groups")
    for (hop, side), w_ref in zip(pieces, weight_refs):
        rows = w_ref.shape[0]
        target = jnp.bitwise_xor(z, hop)
        away = jnp.where(target // half == part, 0, 1)
        lane = (target % half) * chunk
        if side is not None:
            lane += (group if side == 0 else 1 - group) * rows

        @pl.when(away == wanted)
        def _(lane=pl.multiple_of(lane, 128), rows=rows, w_ref=w_ref):
            for block, ref in enumerate((mixed_ref, other_ref)):
                out_ref[block * count : (block + 1) * count, pl.ds(lane, rows)] = (
                    lax.dot_general(ref[...], w_ref[...], NT, preferred_element_type=F32)
                )


def state_kernel(keep_ref, got_ref, near_ref, cross_ref, ids_ref, mod_ref, out_ref, again_ref):
    count, lanes = near_ref.shape
    half = count // 2
    chunk = mod_ref.shape[1] // lax.axis_size("dev")
    side = lax.axis_index("dev") % 2
    part = lax.axis_index("sub")
    for i in range(lanes // chunk):
        at = pl.multiple_of(part * 2 * lanes + (2 * i + side) * chunk, 128)
        lift = 1.0 + mod_ref[0:1, pl.ds(at, chunk)]
        cols = slice(i * chunk, (i + 1) * chunk)
        for j in range(4):
            rows = slice(j * half, (j + 1) * half)
            if j < 2:
                token = near_ref[rows, cols]
            else:
                left = (j - 2) * lanes + i * chunk
                token = cross_ref[2 * count :, left : left + chunk]
            proj = keep_ref[rows, cols] + got_ref[rows, cols]
            out_ref[rows, cols] = (token.astype(F32) + lift * proj).astype(BF16)
    out_ref[2 * count :, :] = ids_ref[...]
    again_ref[...] = out_ref[...]


def tie_kernel(*refs):
    pass


def tie(array, *others):
    anywhere = pl.BlockSpec(memory_space=pl.ANY)
    return pl.pallas_call(
        tie_kernel,
        out_shape=jax.ShapeDtypeStruct(array.shape, array.dtype),
        in_specs=[anywhere] * (1 + len(others)),
        out_specs=anywhere,
        input_output_aliases={0: 0},
        compiler_params=vmem(1),
    )(array, *others)


def select_kernel(local, topk, own, *refs):
    shard_refs, (mod_ref, router_ref) = refs[:4], refs[4:6]
    rows_ref, back_ref = refs[6:8]
    state_ref = refs[8] if own else None
    full_ref, gate_ref = refs[-2:]
    count, width = full_ref.shape
    lanes = shard_refs[0].shape[1]
    device = lax.axis_index("dev")
    side = device % 2
    part = lax.axis_index("sub")
    chunk = width // lax.axis_size("dev")
    experts = router_ref.shape[0]
    slots = local * SLOTS
    before = lax.broadcasted_iota(jnp.int32, (count, count), 0)
    after = lax.broadcasted_iota(jnp.int32, (count, count), 1)
    earlier = (before < after).astype(F32).astype(BF16)
    slot = lax.broadcasted_iota(jnp.int32, (slots, count), 0) % SLOTS
    mine = lax.broadcasted_iota(jnp.int32, (local, count), 0) + device * local
    every = lax.broadcasted_iota(jnp.int32, (experts, count), 0)
    for cross in range(2):
        for far_half in range(2):
            for far_side in range(2):
                ref = shard_refs[2 * far_half + far_side]
                top = (cross ^ far_side) * count
                half = part if far_half == 0 else 1 - part
                parity = side if far_side == 0 else 1 - side
                for i in range(lanes // chunk):
                    block = ref[top : top + count, i * chunk : (i + 1) * chunk]
                    at = (2 * i + parity) * chunk
                    full_ref[:, pl.ds(pl.multiple_of(half * 2 * lanes + at, 128), chunk)] = block
                    if own and cross == 0 and far_half == 0:
                        state_ref[:, pl.ds(pl.multiple_of(at, 128), chunk)] = block
        state = full_ref[...].astype(F32)
        scale = lax.rsqrt(jnp.mean(state * state, 1, keepdims=True) + EPS)
        normed = state * scale * (1.0 + mod_ref[2:3, :]) + mod_ref[1:2, :]
        normed = normed.astype(BF16)
        ids = shard_refs[cross][2 * count : 2 * count + TILE, :]
        ids = ids.astype(F32)[0:1, :].astype(jnp.int32)
        named = [ids[:, k * count : (k + 1) * count] for k in range(topk)]
        hot = sum((mine == n).astype(F32) for n in named)
        rank = jnp.dot(hot.astype(BF16), earlier, preferred_element_type=F32)
        rank = jnp.where(hot > 0.0, rank, -1.0)
        rank = jnp.concatenate(
            [jnp.broadcast_to(rank[e : e + 1], (SLOTS, count)) for e in range(local)]
        )
        pick = rank == slot.astype(F32)
        chosen = jnp.dot(
            jnp.where(pick, 1.0, 0.0).astype(BF16), normed, preferred_element_type=F32
        ).astype(BF16)
        for e in range(local):
            rows_ref[e, cross * SLOTS : (cross + 1) * SLOTS, :] = chosen[
                e * SLOTS : (e + 1) * SLOTS
            ]
        logits = lax.dot_general(router_ref[...], normed, NT, preferred_element_type=F32)
        lifted = sum(jnp.where(every == n, 1.0, 0.0) for n in named) * jax.nn.sigmoid(logits)
        gate_ref[...] = lifted / jnp.sum(lifted, 0, keepdims=True)
        here = gate_ref[pl.ds(pl.multiple_of(device * local, local), local), :]
        here = jnp.concatenate(
            [jnp.broadcast_to(here[e : e + 1], (SLOTS, count)) for e in range(local)]
        )
        back_ref[cross] = jnp.where(pick, here, 0.0).T.astype(BF16)


def load_kernel(from_ref, _, *refs):
    to_refs, done_ref, sem_ref = refs[:-2], refs[-2], refs[-1]
    copies = [
        pltpu.make_async_copy(from_ref.at[2 * e : 2 * e + 2], ref, sem_ref.at[e])
        for e, ref in enumerate(to_refs)
    ]
    for copy in copies:
        copy.start()
    done_ref[...] = jnp.zeros(done_ref.shape, F32)
    for copy in copies:
        copy.wait()


def load(weight, after_this, limit):
    local = weight.shape[0] // 2
    piece = jax.ShapeDtypeStruct((2, *weight.shape[1:]), BF16)
    return pl.pallas_call(
        load_kernel,
        out_shape=[piece] * local + [jax.ShapeDtypeStruct((8, 128), F32)],
        in_specs=[pl.BlockSpec(memory_space=pl.ANY)] * 2,
        out_specs=[whole()] * (local + 1),
        scratch_shapes=[pltpu.SemaphoreType.DMA((local,))],
        compiler_params=vmem(limit),
    )(weight, after_this)


def hidden_kernel(steps, low, *refs):
    rows_refs, w_refs, hidden_ref = refs[:steps], refs[steps:-1], refs[-1]
    for e, w_ref in enumerate(w_refs):
        rows = jnp.concatenate([ref[low + e] for ref in rows_refs])
        halves = []
        for b in range(2):
            gate = lax.dot_general(w_ref[b, 0], rows, NT, preferred_element_type=F32)
            up = lax.dot_general(w_ref[b, 1], rows, NT, preferred_element_type=F32)
            halves.append(jax.nn.silu(gate) * up)
        hidden_ref[e] = jnp.concatenate(halves).T.astype(BF16)


def output_kernel(low, near_ref, far_ref, w_ref, held_ref):
    part = lax.axis_index("sub")
    units = near_ref.shape[2] // 2
    for e in range(near_ref.shape[0]):
        total = 0.0
        for ref, who in ((near_ref, part), (far_ref, 1 - part)):
            at = pl.multiple_of(who * units, 64)
            weight = jnp.concatenate(
                [w_ref[2 * (low + e) + b, pl.ds(at, units), :] for b in range(2)]
            )
            total += jnp.dot(ref[e], weight, preferred_element_type=F32)
        total = total.astype(BF16)
        for source in range(held_ref.shape[0]):
            held_ref[source, e * SLOTS : (e + 1) * SLOTS, :] = total[
                source * SLOTS : (source + 1) * SLOTS
            ]


def share_kernel(steps, low, before, near_ref, far_ref, w_ref, *refs):
    held_refs, back_refs = refs[:before], refs[before : before + steps]
    out_refs, held_ref = refs[before + steps : -1], refs[-1]
    output_kernel(low, near_ref, far_ref, w_ref, held_ref)
    for source in range(2 * steps):
        back = back_refs[source // 2][source % 2]
        rows = jnp.concatenate([ref[source] for ref in (*held_refs, held_ref)])
        out_refs[source][...] = jnp.dot(back, rows, preferred_element_type=F32).astype(BF16)


def final_kernel(state_ref, mod_ref, *refs):
    routed = sum(ref[...].astype(F32) for ref in refs[:-1])
    lanes = state_ref.shape[1]
    at = pl.multiple_of(lax.axis_index("sub") * lanes, 128)
    lift = 1.0 + mod_ref[3:4, pl.ds(at, lanes)]
    refs[-1][...] = (state_ref[...].astype(F32) + lift * routed).astype(BF16)


def gathered_body(
    tokens,
    query_key_value,
    out_weight,
    modulation,
    router_weight,
    expert_ids,
    gate_up_weight,
    down_weight,
):
    count, width = tokens.shape
    devices = lax.axis_size("dev")
    groups = lax.axis_size("groups")
    steps = devices // 2
    local_width = query_key_value.shape[2]
    chunk = width // devices
    lanes = width // 4
    halves_here = gate_up_weight.shape[0]
    local = halves_here // 2
    experts = router_weight.shape[1]
    topk = expert_ids.shape[1]
    struct = jax.ShapeDtypeStruct

    def hop(x, flip):
        return lax.ppermute(x, "dev", [(i, i ^ flip) for i in range(devices)])

    def swap(x):
        return lax.ppermute(x, "sub", [(0, 1), (1, 0)])

    split = groups == 2
    held = out_weight.shape[0] // (2 if split else 1)
    anywhere = pl.BlockSpec(memory_space=pl.ANY)
    stacked = query_key_value.transpose(1, 0, 2)
    pair, cross, sent = pl.pallas_call(
        functools.partial(cut_kernel, split),
        out_shape=[
            struct((2 * count, local_width), BF16),
            struct((2 * count + count // 2, local_width), BF16),
            struct((held, local_width), BF16),
        ],
        in_specs=[anywhere] * 3,
        out_specs=[whole()] * 3,
        scratch_shapes=[pltpu.SemaphoreType.DMA((5 + 2 * (lanes // chunk),))],
        compiler_params=vmem(53),
    )(tokens, stacked, out_weight)
    query, near, own_weight = pl.pallas_call(
        rest_kernel,
        out_shape=[
            struct((count, local_width), BF16),
            struct((count, lanes), BF16),
            struct(out_weight.shape, BF16),
        ],
        in_specs=[anywhere] * 4,
        out_specs=[whole()] * 3,
        scratch_shapes=[pltpu.SemaphoreType.DMA((2 + lanes // chunk,))],
        compiler_params=vmem(53),
    )(tokens, stacked, out_weight, sent)
    ids, small, router = pl.pallas_call(
        small_kernel,
        out_shape=[
            struct((TILE, lanes), BF16),
            struct(modulation.shape, F32),
            struct((experts, width), BF16),
        ],
        in_specs=[whole()] * 3 + [pl.BlockSpec(memory_space=pl.ANY)],
        out_specs=[whole()] * 3,
        compiler_params=vmem(4),
    )(expert_ids.T, modulation, router_weight.T, query)
    odd = [(i, i + 1) for i in range(1, devices - 1, 2)]
    after = lax.ppermute(pair, "dev", odd + [(j, i) for i, j in odd])
    cross = hop(cross, 1)

    units = gate_up_weight.shape[3]
    *ups, done = load(gate_up_weight.swapaxes(2, 3), query, 16)

    mine = {0: sent}
    for flip in range(2, steps):
        low = flip & -flip
        if flip > 2 and flip - low > 0:
            mine[flip] = hop(mine[flip - low], 2 * low)
        else:
            mine[flip] = tie(hop(sent, 2 * flip), done)
    own_weight = tie(own_weight, mine[2])
    pieces, weights = [(0, None), (1, None)], [own_weight, hop(own_weight, 2)]

    mixed = pl.pallas_call(
        attention_kernel,
        out_shape=struct((count, local_width), BF16),
        in_specs=[whole()] * 4 + [pl.BlockSpec(memory_space=pl.ANY)],
        out_specs=whole(),
        compiler_params=vmem(6),
    )(query, pair, cross, after, small)
    for flip in range(2, steps):
        if split:
            if flip == steps - 1:
                mine[flip] = tie(mine[flip], mixed)
            theirs = lax.ppermute(mine[flip], "groups", [(0, 1), (1, 0)])
            pieces += [(flip, 0), (flip, 1)]
            weights += [mine[flip], theirs]
        else:
            pieces.append((flip, None))
            weights.append(mine[flip])
    other = hop(mixed, 1)
    send, keep = (
        pl.pallas_call(
            functools.partial(projection_kernel, steps, tuple(pieces), wanted),
            out_shape=struct((2 * count, lanes), F32),
            in_specs=[whole()] * (2 + len(weights)),
            out_specs=whole(),
            compiler_params=vmem(6),
        )(mixed, other, *weights)
        for wanted in (1, 0)
    )
    shard, again = pl.pallas_call(
        state_kernel,
        out_shape=[struct((2 * count + TILE, lanes), BF16)] * 2,
        in_specs=[whole()] * 6,
        out_specs=[whole()] * 2,
        compiler_params=vmem(6),
    )(keep, swap(send), near, cross, ids, small)

    slots = local * SLOTS
    state = None
    picked, backs = [], []
    column = {0: shard, 1: hop(shard, 2)}
    across = hop(shard, 1)
    column[1] = tie(column[1], across)
    crossing = {0: across, 1: hop(column[1], 1)}
    beside = swap(column[1])
    swapped = swap(shard)
    column[2] = tie(hop(tie(again, swapped), 4), beside)
    for flip in range(3, steps):
        low = flip & -flip
        column[flip] = hop(column[flip - low] if flip > low else shard, 2 * low)
    for flip in range(steps):
        if flip == steps - 1:
            column[flip] = tie(column[flip], picked[0])
        block = column[flip]
        crossed = crossing[flip] if flip in crossing else hop(block, 1)
        if flip == steps - 1:
            crossed = tie(crossed, *picked[1:])
        own = flip == 0
        results = pl.pallas_call(
            functools.partial(select_kernel, local, topk, own),
            out_shape=[
                struct((local, 2 * SLOTS, width), BF16),
                struct((2, count, slots), BF16),
            ]
            + ([struct((count, 2 * lanes), BF16)] if own else []),
            in_specs=[whole()] * 6,
            out_specs=[whole()] * (3 if own else 2),
            scratch_shapes=[pltpu.VMEM((count, width), BF16), pltpu.VMEM((experts, count), F32)],
            compiler_params=vmem(6),
        )(block, crossed, beside if flip == 1 else swapped if own else swap(block), swap(crossed), small, router)
        picked.append(results[0])
        backs.append(results[1])
        if own:
            state = results[2]

    sources = 2 * steps
    room = sources * SLOTS
    first = local // 2
    groups_of = [(0, first), (first, local)] if first else [(0, local)]
    hidden = []
    for low, high in groups_of:
        own = pl.pallas_call(
            functools.partial(hidden_kernel, steps, low),
            out_shape=struct((high - low, room, 2 * units), BF16),
            in_specs=[whole()] * (steps + high - low),
            out_specs=whole(),
            compiler_params=vmem(6),
        )(*picked, *ups[low:high])
        hidden.append((own, swap(own)))
    held = []
    for (low, high), (own, other) in zip(groups_of[:-1], hidden[:-1]):
        held.append(
            pl.pallas_call(
                functools.partial(output_kernel, low),
                out_shape=struct((sources, (high - low) * SLOTS, 2 * lanes), BF16),
                in_specs=[whole()] * 3,
                out_specs=whole(),
                compiler_params=vmem(6),
            )(own, other, down_weight)
        )
    low, high = groups_of[-1]
    share = pl.pallas_call(
        functools.partial(share_kernel, steps, low, len(held)),
        out_shape=[struct((count, 2 * lanes), BF16)] * sources,
        in_specs=[whole()] * (3 + len(held) + steps),
        out_specs=[whole()] * sources,
        scratch_shapes=[pltpu.VMEM((sources, (high - low) * SLOTS, 2 * lanes), BF16)],
        compiler_params=vmem(8),
    )(*hidden[-1], down_weight, *held, *backs)

    terms = [share[0]]
    for flip in range(steps - 1, -1, -1):
        crossed = hop(share[2 * flip + 1], 1)
        if flip:
            crossed = (share[2 * flip].astype(F32) + crossed.astype(F32)).astype(BF16)
            crossed = hop(crossed, 2 * flip)
        terms.append(crossed)
    return pl.pallas_call(
        final_kernel,
        out_shape=struct((count, 2 * lanes), BF16),
        in_specs=[whole()] * (2 + len(terms)),
        out_specs=whole(),
        compiler_params=vmem(8),
    )(state, small, *terms)


def extended(cells, sides, width):
    for axis, dim in sides:
        count = lax.axis_size(axis)
        ends = count - 1
        head = lax.slice_in_dim(cells, 0, width, axis=dim)
        tail = lax.slice_in_dim(cells, cells.shape[dim] - width, cells.shape[dim], axis=dim)
        cells = jnp.concatenate(
            [
                lax.ppermute(tail, axis, [(i, (i + 1) % count) for i in range(ends)]),
                cells,
                lax.ppermute(head, axis, [((i + 1) % count, i) for i in range(ends)]),
            ],
            axis=dim,
        )
    return cells


def window_attention(query, keys, values, index, total):
    count = query.shape[0]
    rows = jnp.arange(count, dtype=jnp.int32)[:, None]
    cols = jnp.arange(3 * count, dtype=jnp.int32)[None, :] - count
    place = index * count + cols
    allowed = (jnp.abs(cols - rows) <= count) & (place >= 0) & (place < total)
    scores = jnp.einsum(
        "qhd,khd->hqk", query, keys, preferred_element_type=jnp.float32
    ) / math.sqrt(query.shape[2])
    scores = jnp.where(allowed[None], scores, NEG)
    top = jnp.max(scores, -1, keepdims=True)
    weight = jnp.exp(scores - top)
    weight = (weight / jnp.sum(weight, -1, keepdims=True)).astype(jnp.bfloat16)
    mixed = jnp.einsum("hqk,khd->qhd", weight, values, preferred_element_type=jnp.float32)
    return mixed.astype(jnp.bfloat16)


def normalize(state, modulation):
    scale = lax.rsqrt(jnp.mean(state * state, -1, keepdims=True) + EPS)
    return (state * scale * (1.0 + modulation[2]) + modulation[1]).astype(jnp.bfloat16)


def route(normed, router_weight, expert_ids):
    logits = jnp.dot(normed, router_weight, preferred_element_type=jnp.float32)
    experts = router_weight.shape[1]
    match = expert_ids[:, :, None] == jnp.arange(experts, dtype=jnp.int32)[None, None, :]
    picked = jnp.sum(jnp.where(match, logits[:, None, :], 0.0), -1)
    lifted = jax.nn.sigmoid(picked)
    return lifted / jnp.sum(lifted, -1, keepdims=True)


def exchanged_body(
    tokens,
    query_key_value,
    out_weight,
    modulation,
    router_weight,
    expert_ids,
    gate_up_weight,
    down_weight,
):
    count = tokens.shape[0]
    width = tokens.shape[1]
    parts = lax.axis_size("sub")
    part = lax.axis_index("sub")
    position = lax.axis_index("dev")
    devices = lax.axis_size("dev")
    total = count * devices
    local_width = query_key_value.shape[2]
    heads_here = local_width // HEAD
    query = query_key_value[:, 0].reshape(count, heads_here, HEAD)
    pair = query_key_value[:, 1:]
    near = extended(pair, (("dev", 0),), count)
    keys = near[:, 0].reshape(3 * count, heads_here, HEAD)
    values = near[:, 1].reshape(3 * count, heads_here, HEAD)
    mixed = window_attention(query, keys, values, position, total).reshape(count, local_width)
    partial_proj = lax.dot_general(
        mixed,
        lax.all_gather(out_weight, "dev", axis=0, tiled=True),
        (((1,), (1,)), ((), ())),
        preferred_element_type=jnp.float32,
    )
    proj = lax.psum(partial_proj, "sub")
    state = tokens.astype(jnp.float32) + (1.0 + modulation[0]) * proj
    normed = normalize(state, modulation)
    gates = route(normed, router_weight, expert_ids)
    experts = router_weight.shape[1]
    topk = expert_ids.shape[1]
    flat = expert_ids.reshape(-1)
    picks = flat.shape[0]
    onehot = (flat[:, None] == jnp.arange(experts, dtype=jnp.int32)[None, :]).astype(BF16)
    order = jnp.arange(picks, dtype=jnp.int32)
    earlier = (order[None, :] < order[:, None]).astype(BF16)
    ahead = jnp.dot(earlier, onehot, preferred_element_type=F32)
    rank = jnp.sum(ahead * onehot.astype(F32), 1).astype(jnp.int32)
    target = flat * CAP + rank
    hit = target[None, :] == jnp.arange(experts * CAP, dtype=jnp.int32)[:, None]
    owner = jnp.any(hit.reshape(experts * CAP, count, topk), 2).astype(BF16)
    slice_width = width // parts
    sent = lax.dynamic_slice_in_dim(normed, part * slice_width, slice_width, 1)
    sent_width = sent.shape[1]
    rows_out = jnp.dot(owner, sent, preferred_element_type=F32).astype(BF16)
    halves_here = gate_up_weight.shape[0]
    doubled = jnp.broadcast_to(
        rows_out.reshape(experts, 1, CAP, sent_width), (experts, 2, CAP, sent_width)
    )
    outgoing = doubled.reshape(devices, halves_here, CAP, sent_width)
    up_form = "sxcd,xgdf->sxcgf"
    down_form = "sxcf,xfd->sxcd"
    incoming = lax.all_to_all(outgoing, "dev", split_axis=0, concat_axis=0, tiled=True)
    both = jnp.einsum(
        up_form,
        lax.all_gather(incoming, "sub", axis=3, tiled=True),
        gate_up_weight,
        preferred_element_type=jnp.float32,
    )
    hidden = (jax.nn.silu(both[..., 0, :]) * both[..., 1, :]).astype(jnp.bfloat16)
    gathered = lax.all_gather(hidden, "sub", axis=hidden.ndim - 1, tiled=True)
    result = jnp.einsum(down_form, gathered, down_weight, preferred_element_type=jnp.float32)
    returned = lax.all_to_all(
        result.astype(jnp.bfloat16), "dev", split_axis=0, concat_axis=0, tiled=True
    )
    own_width = returned.shape[-1]
    arranged = returned.reshape(experts, 2, CAP, own_width)
    combined = arranged[:, 0].astype(F32) + arranged[:, 1].astype(F32)
    share = jnp.sum(
        jnp.where(hit.reshape(experts * CAP, count, topk), gates[None], 0.0), 2
    )
    routed = lax.dot_general(
        share,
        combined.reshape(experts * CAP, own_width),
        (((0,), (0,)), ((), ())),
        precision=lax.Precision.HIGHEST,
        preferred_element_type=F32,
    )
    own = lax.dynamic_slice_in_dim(state, part * slice_width, slice_width, 1)
    lift = lax.dynamic_slice_in_dim(modulation[3], part * slice_width, slice_width, 0)
    return (own + (1.0 + lift) * routed).astype(jnp.bfloat16)


def body(*arrays):
    tokens, router_weight, expert_ids, gate_up_weight = arrays[0], arrays[4], arrays[5], arrays[6]
    devices = lax.axis_size("dev")
    count, width = tokens.shape
    local = gate_up_weight.shape[0] // 2
    fits = (
        lax.axis_size("sub") == 2
        and devices >= 8
        and devices & (devices - 1) == 0
        and gate_up_weight.shape[0] % 2 == 0
        and width % (devices * 128) == 0
        and arrays[1].shape[2] * 2 == width
        and count % HEAD == 0
        and expert_ids.shape[1] * count <= width // 4
        and router_weight.shape[1] <= 256
    )
    if fits and count * devices <= 2 * local * devices * CAP:
        return gathered_body(*arrays)
    return exchanged_body(*arrays)


def solution(mesh):
    return jax.shard_map(
        body,
        mesh=mesh,
        in_specs=(
            P(("groups", "dev"), None),
            P(("groups", "dev"), None, "sub"),
            P("dev", "sub"),
            P("groups", None),
            P(),
            P(("groups", "dev"), None),
            P("dev", None, None, "sub"),
            P("dev", None, "sub"),
        ),
        out_specs=P(("groups", "dev"), "sub"),
        check_vma=False,
    )
```

```python
import functools
import math

import jax
import jax.numpy as jnp
from jax import lax
from jax.experimental import pallas as pl
from jax.experimental.pallas import tpu as pltpu
from jax.sharding import PartitionSpec as P

HEAD = 128
CAP = 12
SLOTS = 16
TILE = 16

EPS = 1e-06
NEG = -1e30
F32 = jnp.float32
BF16 = jnp.bfloat16

NT = (((1,), (1,)), ((), ()))


def vmem(mib):
    return pltpu.CompilerParams(vmem_limit_bytes=mib * 2**20)


def whole():
    return pl.BlockSpec(memory_space=pltpu.VMEM)


def cut_kernel(split, tokens_ref, qkv_ref, weight_ref, *refs):
    pair_ref, cross_ref, sent_ref, sem_ref = refs
    count = pair_ref.shape[0] // 2
    lanes = tokens_ref.shape[1] // 4
    chunk = tokens_ref.shape[1] // lax.axis_size("dev")
    side = lax.axis_index("dev") % 2
    part = lax.axis_index("sub")
    half = count // 2
    moves = [
        (qkv_ref.at[1], pair_ref.at[:count]),
        (qkv_ref.at[2], pair_ref.at[count:]),
        (qkv_ref.at[1], cross_ref.at[:count]),
        (qkv_ref.at[2], cross_ref.at[count : 2 * count]),
    ]
    for i in range(lanes // chunk):
        at = pl.multiple_of(part * 2 * lanes + (2 * i + 1 - side) * chunk, 128)
        for j in range(2):
            left = j * lanes + i * chunk
            moves.append(
                (
                    tokens_ref.at[j * half : (j + 1) * half, pl.ds(at, chunk)],
                    cross_ref.at[2 * count :, left : left + chunk],
                )
            )
    rows = sent_ref.shape[0]
    at = pl.multiple_of(lax.axis_index("groups") * rows if split else 0, TILE)
    moves.append((weight_ref.at[pl.ds(at, rows)], sent_ref))
    copies = [pltpu.make_async_copy(*move, sem_ref.at[n]) for n, move in enumerate(moves)]
    for copy in copies:
        copy.start()
    for copy in copies:
        copy.wait()


def rest_kernel(tokens_ref, qkv_ref, weight_ref, _, query_ref, near_ref, own_ref, sem_ref):
    lanes = near_ref.shape[1]
    chunk = tokens_ref.shape[1] // lax.axis_size("dev")
    side = lax.axis_index("dev") % 2
    part = lax.axis_index("sub")
    moves = [(qkv_ref.at[0], query_ref), (weight_ref, own_ref)]
    for i in range(lanes // chunk):
        at = pl.multiple_of(part * 2 * lanes + (2 * i + side) * chunk, 128)
        moves.append(
            (tokens_ref.at[:, pl.ds(at, chunk)], near_ref.at[:, i * chunk : (i + 1) * chunk])
        )
    copies = [pltpu.make_async_copy(*move, sem_ref.at[n]) for n, move in enumerate(moves)]
    for copy in copies:
        copy.start()
    for copy in copies:
        copy.wait()


def small_kernel(ids_ref, mod_ref, router_ref, _, row_ref, mod_to_ref, router_to_ref):
    topk, count = ids_ref.shape
    row_ref[...] = jnp.zeros(row_ref.shape, BF16)
    for k in range(topk):
        named = jnp.broadcast_to(ids_ref[k : k + 1, :], (TILE, count))
        row_ref[:, k * count : (k + 1) * count] = named.astype(F32).astype(BF16)
    mod_to_ref[...] = mod_ref[...]
    router_to_ref[...] = router_ref[...]


def attention_kernel(query_ref, own_ref, cross_ref, next_ref, *refs):
    mixed_ref = refs[-1]
    count, width = mixed_ref.shape
    place = lax.axis_index("dev")
    even = place % 2 == 0
    row = lax.broadcasted_iota(jnp.int32, (count, count), 0)
    col = lax.broadcasted_iota(jnp.int32, (count, count), 1)
    alone = (place == 0) | (place == lax.axis_size("dev") - 1)
    see_cross = jnp.where(even, col - row, row - col) <= 0
    see_next = (jnp.where(even, row - col, col - row) <= 0) & jnp.logical_not(alone)
    scale = 1.0 / math.sqrt(HEAD)

    def scored(q, k):
        return lax.dot_general(q, k, NT, preferred_element_type=F32) * scale

    for head in range(width // HEAD):
        lanes = slice(head * HEAD, (head + 1) * HEAD)
        q = query_ref[:, lanes]
        sc = jnp.where(see_cross, scored(q, cross_ref[:count, lanes]), NEG)
        so = scored(q, own_ref[:count, lanes])
        sn = jnp.where(see_next, scored(q, next_ref[:count, lanes]), NEG)
        top = jnp.max(jnp.maximum(jnp.maximum(sc, so), sn), 1, keepdims=True)
        wc, wo, wn = jnp.exp(sc - top), jnp.exp(so - top), jnp.exp(sn - top)
        inv = 1.0 / jnp.sum(wc + wo + wn, 1, keepdims=True)
        out = 0.0
        for weight, value in (
            (wo, own_ref[count:, lanes]),
            (wc, cross_ref[count : 2 * count, lanes]),
            (wn, next_ref[count:, lanes]),
        ):
            out += jnp.dot((weight * inv).astype(BF16), value, preferred_element_type=F32)
        mixed_ref[:, lanes] = out.astype(BF16)


def projection_kernel(steps, pieces, wanted, *refs):
    mixed_ref, other_ref = refs[0], refs[1]
    weight_refs = refs[2 : 2 + len(pieces)]
    out_ref = refs[2 + len(pieces)]
    count = mixed_ref.shape[0]
    half = steps // 2
    chunk = out_ref.shape[1] // half
    z = lax.axis_index("dev") // 2
    part = lax.axis_index("sub")
    group = lax.axis_index("groups")
    for (hop, side), w_ref in zip(pieces, weight_refs):
        rows = w_ref.shape[0]
        target = jnp.bitwise_xor(z, hop)
        away = jnp.where(target // half == part, 0, 1)
        lane = (target % half) * chunk
        if side is not None:
            lane += (group if side == 0 else 1 - group) * rows

        @pl.when(away == wanted)
        def _(lane=pl.multiple_of(lane, 128), rows=rows, w_ref=w_ref):
            for block, ref in enumerate((mixed_ref, other_ref)):
                out_ref[block * count : (block + 1) * count, pl.ds(lane, rows)] = (
                    lax.dot_general(ref[...], w_ref[...], NT, preferred_element_type=F32)
                )


def state_kernel(keep_ref, got_ref, near_ref, cross_ref, ids_ref, mod_ref, out_ref, again_ref):
    count, lanes = near_ref.shape
    half = count // 2
    chunk = mod_ref.shape[1] // lax.axis_size("dev")
    side = lax.axis_index("dev") % 2
    part = lax.axis_index("sub")
    for i in range(lanes // chunk):
        at = pl.multiple_of(part * 2 * lanes + (2 * i + side) * chunk, 128)
        lift = 1.0 + mod_ref[0:1, pl.ds(at, chunk)]
        cols = slice(i * chunk, (i + 1) * chunk)
        for j in range(4):
            rows = slice(j * half, (j + 1) * half)
            if j < 2:
                token = near_ref[rows, cols]
            else:
                left = (j - 2) * lanes + i * chunk
                token = cross_ref[2 * count :, left : left + chunk]
            proj = keep_ref[rows, cols] + got_ref[rows, cols]
            out_ref[rows, cols] = (token.astype(F32) + lift * proj).astype(BF16)
    out_ref[2 * count :, :] = ids_ref[...]
    again_ref[...] = out_ref[...]


def tie_kernel(*refs):
    pass


def tie(array, *others):
    anywhere = pl.BlockSpec(memory_space=pl.ANY)
    return pl.pallas_call(
        tie_kernel,
        out_shape=jax.ShapeDtypeStruct(array.shape, array.dtype),
        in_specs=[anywhere] * (1 + len(others)),
        out_specs=anywhere,
        input_output_aliases={0: 0},
        compiler_params=vmem(1),
    )(array, *others)


def select_kernel(local, topk, own, *refs):
    shard_refs, (mod_ref, router_ref) = refs[:4], refs[4:6]
    rows_ref, back_ref = refs[6:8]
    state_ref = refs[8] if own else None
    full_ref, gate_ref = refs[-2:]
    count, width = full_ref.shape
    lanes = shard_refs[0].shape[1]
    device = lax.axis_index("dev")
    side = device % 2
    part = lax.axis_index("sub")
    chunk = width // lax.axis_size("dev")
    experts = router_ref.shape[0]
    slots = local * SLOTS
    before = lax.broadcasted_iota(jnp.int32, (count, count), 0)
    after = lax.broadcasted_iota(jnp.int32, (count, count), 1)
    earlier = (before < after).astype(F32).astype(BF16)
    slot = lax.broadcasted_iota(jnp.int32, (slots, count), 0) % SLOTS
    mine = lax.broadcasted_iota(jnp.int32, (local, count), 0) + device * local
    every = lax.broadcasted_iota(jnp.int32, (experts, count), 0)
    for cross in range(2):
        for far_half in range(2):
            for far_side in range(2):
                ref = shard_refs[2 * far_half + far_side]
                top = (cross ^ far_side) * count
                half = part if far_half == 0 else 1 - part
                parity = side if far_side == 0 else 1 - side
                for i in range(lanes // chunk):
                    block = ref[top : top + count, i * chunk : (i + 1) * chunk]
                    at = (2 * i + parity) * chunk
                    full_ref[:, pl.ds(pl.multiple_of(half * 2 * lanes + at, 128), chunk)] = block
                    if own and cross == 0 and far_half == 0:
                        state_ref[:, pl.ds(pl.multiple_of(at, 128), chunk)] = block
        state = full_ref[...].astype(F32)
        scale = lax.rsqrt(jnp.mean(state * state, 1, keepdims=True) + EPS)
        normed = state * scale * (1.0 + mod_ref[2:3, :]) + mod_ref[1:2, :]
        normed = normed.astype(BF16)
        ids = shard_refs[cross][2 * count : 2 * count + TILE, :]
        ids = ids.astype(F32)[0:1, :].astype(jnp.int32)
        named = [ids[:, k * count : (k + 1) * count] for k in range(topk)]
        hot = sum((mine == n).astype(F32) for n in named)
        rank = jnp.dot(hot.astype(BF16), earlier, preferred_element_type=F32)
        rank = jnp.where(hot > 0.0, rank, -1.0)
        rank = jnp.concatenate(
            [jnp.broadcast_to(rank[e : e + 1], (SLOTS, count)) for e in range(local)]
        )
        pick = rank == slot.astype(F32)
        chosen = jnp.dot(
            jnp.where(pick, 1.0, 0.0).astype(BF16), normed, preferred_element_type=F32
        ).astype(BF16)
        for e in range(local):
            rows_ref[e, cross * SLOTS : (cross + 1) * SLOTS, :] = chosen[
                e * SLOTS : (e + 1) * SLOTS
            ]
        logits = lax.dot_general(router_ref[...], normed, NT, preferred_element_type=F32)
        lifted = sum(jnp.where(every == n, 1.0, 0.0) for n in named) * jax.nn.sigmoid(logits)
        gate_ref[...] = lifted / jnp.sum(lifted, 0, keepdims=True)
        here = gate_ref[pl.ds(pl.multiple_of(device * local, local), local), :]
        here = jnp.concatenate(
            [jnp.broadcast_to(here[e : e + 1], (SLOTS, count)) for e in range(local)]
        )
        back_ref[cross] = jnp.where(pick, here, 0.0).T.astype(BF16)


def load_kernel(from_ref, _, *refs):
    to_refs, done_ref, sem_ref = refs[:-2], refs[-2], refs[-1]
    copies = [
        pltpu.make_async_copy(from_ref.at[2 * e : 2 * e + 2], ref, sem_ref.at[e])
        for e, ref in enumerate(to_refs)
    ]
    for copy in copies:
        copy.start()
    done_ref[...] = jnp.zeros(done_ref.shape, F32)
    for copy in copies:
        copy.wait()


def load(weight, after_this, limit):
    local = weight.shape[0] // 2
    piece = jax.ShapeDtypeStruct((2, *weight.shape[1:]), BF16)
    return pl.pallas_call(
        load_kernel,
        out_shape=[piece] * local + [jax.ShapeDtypeStruct((8, 128), F32)],
        in_specs=[pl.BlockSpec(memory_space=pl.ANY)] * 2,
        out_specs=[whole()] * (local + 1),
        scratch_shapes=[pltpu.SemaphoreType.DMA((local,))],
        compiler_params=vmem(limit),
    )(weight, after_this)


def hidden_kernel(steps, low, *refs):
    rows_refs, w_refs, hidden_ref = refs[:steps], refs[steps:-1], refs[-1]
    for e, w_ref in enumerate(w_refs):
        rows = jnp.concatenate([ref[low + e] for ref in rows_refs])
        halves = []
        for b in range(2):
            gate = lax.dot_general(w_ref[b, 0], rows, NT, preferred_element_type=F32)
            up = lax.dot_general(w_ref[b, 1], rows, NT, preferred_element_type=F32)
            halves.append(jax.nn.silu(gate) * up)
        hidden_ref[e] = jnp.concatenate(halves).T.astype(BF16)


def output_kernel(low, near_ref, far_ref, w_ref, held_ref):
    part = lax.axis_index("sub")
    units = near_ref.shape[2] // 2
    for e in range(near_ref.shape[0]):
        total = 0.0
        for ref, who in ((near_ref, part), (far_ref, 1 - part)):
            at = pl.multiple_of(who * units, 64)
            weight = jnp.concatenate(
                [w_ref[2 * (low + e) + b, pl.ds(at, units), :] for b in range(2)]
            )
            total += jnp.dot(ref[e], weight, preferred_element_type=F32)
        total = total.astype(BF16)
        for source in range(held_ref.shape[0]):
            held_ref[source, e * SLOTS : (e + 1) * SLOTS, :] = total[
                source * SLOTS : (source + 1) * SLOTS
            ]


def share_kernel(steps, low, before, near_ref, far_ref, w_ref, *refs):
    held_refs, back_refs = refs[:before], refs[before : before + steps]
    out_refs, held_ref = refs[before + steps : -1], refs[-1]
    output_kernel(low, near_ref, far_ref, w_ref, held_ref)
    for source in range(2 * steps):
        back = back_refs[source // 2][source % 2]
        rows = jnp.concatenate([ref[source] for ref in (*held_refs, held_ref)])
        routed = jnp.dot(back, rows, preferred_element_type=F32).astype(BF16)
        if source < 2 * steps - 2:
            out_refs[source][...] = routed
        else:
            half = routed.shape[0] // 2
            at = 2 * source - (2 * steps - 2)
            out_refs[at][...] = routed[:half]
            out_refs[at + 1][...] = routed[half:]


def final_kernel(state_ref, mod_ref, top_ref, bottom_ref, *refs):
    out_ref = refs[-1]
    count, lanes = state_ref.shape
    at = pl.multiple_of(lax.axis_index("sub") * lanes, 128)
    lift = 1.0 + mod_ref[3:4, pl.ds(at, lanes)]
    for h, last_ref in enumerate((top_ref, bottom_ref)):
        rows = slice(h * count // 2, (h + 1) * count // 2)
        routed = last_ref[...].astype(F32)
        for ref in refs[:-1]:
            routed += ref[rows].astype(F32)
        out_ref[rows] = (state_ref[rows].astype(F32) + lift * routed).astype(BF16)


def gathered_body(
    tokens,
    query_key_value,
    out_weight,
    modulation,
    router_weight,
    expert_ids,
    gate_up_weight,
    down_weight,
):
    count, width = tokens.shape
    devices = lax.axis_size("dev")
    groups = lax.axis_size("groups")
    steps = devices // 2
    local_width = query_key_value.shape[2]
    chunk = width // devices
    lanes = width // 4
    halves_here = gate_up_weight.shape[0]
    local = halves_here // 2
    experts = router_weight.shape[1]
    topk = expert_ids.shape[1]
    struct = jax.ShapeDtypeStruct

    def hop(x, flip):
        return lax.ppermute(x, "dev", [(i, i ^ flip) for i in range(devices)])

    def swap(x):
        return lax.ppermute(x, "sub", [(0, 1), (1, 0)])

    split = groups == 2
    held = out_weight.shape[0] // (2 if split else 1)
    anywhere = pl.BlockSpec(memory_space=pl.ANY)
    stacked = query_key_value.transpose(1, 0, 2)
    pair, cross, sent = pl.pallas_call(
        functools.partial(cut_kernel, split),
        out_shape=[
            struct((2 * count, local_width), BF16),
            struct((2 * count + count // 2, local_width), BF16),
            struct((held, local_width), BF16),
        ],
        in_specs=[anywhere] * 3,
        out_specs=[whole()] * 3,
        scratch_shapes=[pltpu.SemaphoreType.DMA((5 + 2 * (lanes // chunk),))],
        compiler_params=vmem(53),
    )(tokens, stacked, out_weight)
    query, near, own_weight = pl.pallas_call(
        rest_kernel,
        out_shape=[
            struct((count, local_width), BF16),
            struct((count, lanes), BF16),
            struct(out_weight.shape, BF16),
        ],
        in_specs=[anywhere] * 4,
        out_specs=[whole()] * 3,
        scratch_shapes=[pltpu.SemaphoreType.DMA((2 + lanes // chunk,))],
        compiler_params=vmem(53),
    )(tokens, stacked, out_weight, sent)
    ids, small, router = pl.pallas_call(
        small_kernel,
        out_shape=[
            struct((TILE, lanes), BF16),
            struct(modulation.shape, F32),
            struct((experts, width), BF16),
        ],
        in_specs=[whole()] * 3 + [pl.BlockSpec(memory_space=pl.ANY)],
        out_specs=[whole()] * 3,
        compiler_params=vmem(4),
    )(expert_ids.T, modulation, router_weight.T, query)
    odd = [(i, i + 1) for i in range(1, devices - 1, 2)]
    after = lax.ppermute(pair, "dev", odd + [(j, i) for i, j in odd])
    cross = hop(cross, 1)

    units = gate_up_weight.shape[3]
    *ups, done = load(gate_up_weight.swapaxes(2, 3), query, 16)

    mine = {0: sent}
    for flip in range(2, steps):
        low = flip & -flip
        if flip > 2 and flip - low > 0:
            mine[flip] = hop(mine[flip - low], 2 * low)
        else:
            mine[flip] = tie(hop(sent, 2 * flip), done)
    own_weight = tie(own_weight, mine[2])
    pieces, weights = [(0, None), (1, None)], [own_weight, hop(own_weight, 2)]

    mixed = pl.pallas_call(
        attention_kernel,
        out_shape=struct((count, local_width), BF16),
        in_specs=[whole()] * 4 + [pl.BlockSpec(memory_space=pl.ANY)],
        out_specs=whole(),
        compiler_params=vmem(6),
    )(query, pair, cross, after, small)
    for flip in range(2, steps):
        if split:
            if flip == steps - 1:
                mine[flip] = tie(mine[flip], mixed)
            theirs = lax.ppermute(mine[flip], "groups", [(0, 1), (1, 0)])
            pieces += [(flip, 0), (flip, 1)]
            weights += [mine[flip], theirs]
        else:
            pieces.append((flip, None))
            weights.append(mine[flip])
    other = hop(mixed, 1)
    send, keep = (
        pl.pallas_call(
            functools.partial(projection_kernel, steps, tuple(pieces), wanted),
            out_shape=struct((2 * count, lanes), F32),
            in_specs=[whole()] * (2 + len(weights)),
            out_specs=whole(),
            compiler_params=vmem(6),
        )(mixed, other, *weights)
        for wanted in (1, 0)
    )
    shard, again = pl.pallas_call(
        state_kernel,
        out_shape=[struct((2 * count + TILE, lanes), BF16)] * 2,
        in_specs=[whole()] * 6,
        out_specs=[whole()] * 2,
        compiler_params=vmem(6),
    )(keep, swap(send), near, cross, ids, small)

    slots = local * SLOTS
    state = None
    picked, backs = [], []
    column = {0: shard, 1: hop(shard, 2)}
    across = hop(shard, 1)
    column[1] = tie(column[1], across)
    crossing = {0: across, 1: hop(column[1], 1)}
    beside = swap(column[1])
    swapped = swap(shard)
    column[2] = tie(hop(tie(again, swapped), 4), beside)
    for flip in range(3, steps):
        low = flip & -flip
        column[flip] = hop(column[flip - low] if flip > low else shard, 2 * low)
    for flip in range(steps):
        if flip == steps - 1:
            column[flip] = tie(column[flip], picked[0])
        block = column[flip]
        crossed = crossing[flip] if flip in crossing else hop(block, 1)
        if flip == steps - 1:
            crossed = tie(crossed, *picked[1:])
        own = flip == 0
        results = pl.pallas_call(
            functools.partial(select_kernel, local, topk, own),
            out_shape=[
                struct((local, 2 * SLOTS, width), BF16),
                struct((2, count, slots), BF16),
            ]
            + ([struct((count, 2 * lanes), BF16)] if own else []),
            in_specs=[whole()] * 6,
            out_specs=[whole()] * (3 if own else 2),
            scratch_shapes=[pltpu.VMEM((count, width), BF16), pltpu.VMEM((experts, count), F32)],
            compiler_params=vmem(6),
        )(block, crossed, beside if flip == 1 else swapped if own else swap(block), swap(crossed), small, router)
        picked.append(results[0])
        backs.append(results[1])
        if own:
            state = results[2]

    sources = 2 * steps
    room = sources * SLOTS
    first = local // 2
    groups_of = [(0, first), (first, local)] if first else [(0, local)]
    hidden = []
    for low, high in groups_of:
        own = pl.pallas_call(
            functools.partial(hidden_kernel, steps, low),
            out_shape=struct((high - low, room, 2 * units), BF16),
            in_specs=[whole()] * (steps + high - low),
            out_specs=whole(),
            compiler_params=vmem(6),
        )(*picked, *ups[low:high])
        hidden.append((own, swap(own)))
    held = []
    for (low, high), (own, other) in zip(groups_of[:-1], hidden[:-1]):
        held.append(
            pl.pallas_call(
                functools.partial(output_kernel, low),
                out_shape=struct((sources, (high - low) * SLOTS, 2 * lanes), BF16),
                in_specs=[whole()] * 3,
                out_specs=whole(),
                compiler_params=vmem(6),
            )(own, other, down_weight)
        )
    low, high = groups_of[-1]
    share = pl.pallas_call(
        functools.partial(share_kernel, steps, low, len(held)),
        out_shape=[struct((count, 2 * lanes), BF16)] * (sources - 2)
        + [struct((count // 2, 2 * lanes), BF16)] * 4,
        in_specs=[whole()] * (3 + len(held) + steps),
        out_specs=[whole()] * (sources + 2),
        scratch_shapes=[pltpu.VMEM((sources, (high - low) * SLOTS, 2 * lanes), BF16)],
        compiler_params=vmem(8),
    )(*hidden[-1], down_weight, *held, *backs)

    def forwarded(mine, theirs, flip):
        total = mine.astype(F32) + hop(theirs, 1).astype(F32)
        return hop(total.astype(BF16), 2 * flip)

    ends = share[-4:]
    halves = [forwarded(ends[h], ends[2 + h], steps - 1) for h in range(2)]
    terms = [
        forwarded(share[2 * flip], share[2 * flip + 1], flip)
        for flip in range(steps - 2, 0, -1)
    ]
    terms += [share[0], hop(share[1], 1)]
    return pl.pallas_call(
        final_kernel,
        out_shape=struct((count, 2 * lanes), BF16),
        in_specs=[whole()] * (4 + len(terms)),
        out_specs=whole(),
        compiler_params=vmem(8),
    )(state, small, *halves, *terms)


def extended(cells, sides, width):
    for axis, dim in sides:
        count = lax.axis_size(axis)
        ends = count - 1
        head = lax.slice_in_dim(cells, 0, width, axis=dim)
        tail = lax.slice_in_dim(cells, cells.shape[dim] - width, cells.shape[dim], axis=dim)
        cells = jnp.concatenate(
            [
                lax.ppermute(tail, axis, [(i, (i + 1) % count) for i in range(ends)]),
                cells,
                lax.ppermute(head, axis, [((i + 1) % count, i) for i in range(ends)]),
            ],
            axis=dim,
        )
    return cells


def window_attention(query, keys, values, index, total):
    count = query.shape[0]
    rows = jnp.arange(count, dtype=jnp.int32)[:, None]
    cols = jnp.arange(3 * count, dtype=jnp.int32)[None, :] - count
    place = index * count + cols
    allowed = (jnp.abs(cols - rows) <= count) & (place >= 0) & (place < total)
    scores = jnp.einsum(
        "qhd,khd->hqk", query, keys, preferred_element_type=jnp.float32
    ) / math.sqrt(query.shape[2])
    scores = jnp.where(allowed[None], scores, NEG)
    top = jnp.max(scores, -1, keepdims=True)
    weight = jnp.exp(scores - top)
    weight = (weight / jnp.sum(weight, -1, keepdims=True)).astype(jnp.bfloat16)
    mixed = jnp.einsum("hqk,khd->qhd", weight, values, preferred_element_type=jnp.float32)
    return mixed.astype(jnp.bfloat16)


def normalize(state, modulation):
    scale = lax.rsqrt(jnp.mean(state * state, -1, keepdims=True) + EPS)
    return (state * scale * (1.0 + modulation[2]) + modulation[1]).astype(jnp.bfloat16)


def route(normed, router_weight, expert_ids):
    logits = jnp.dot(normed, router_weight, preferred_element_type=jnp.float32)
    experts = router_weight.shape[1]
    match = expert_ids[:, :, None] == jnp.arange(experts, dtype=jnp.int32)[None, None, :]
    picked = jnp.sum(jnp.where(match, logits[:, None, :], 0.0), -1)
    lifted = jax.nn.sigmoid(picked)
    return lifted / jnp.sum(lifted, -1, keepdims=True)


def exchanged_body(
    tokens,
    query_key_value,
    out_weight,
    modulation,
    router_weight,
    expert_ids,
    gate_up_weight,
    down_weight,
):
    count = tokens.shape[0]
    width = tokens.shape[1]
    parts = lax.axis_size("sub")
    part = lax.axis_index("sub")
    position = lax.axis_index("dev")
    devices = lax.axis_size("dev")
    total = count * devices
    local_width = query_key_value.shape[2]
    heads_here = local_width // HEAD
    query = query_key_value[:, 0].reshape(count, heads_here, HEAD)
    pair = query_key_value[:, 1:]
    near = extended(pair, (("dev", 0),), count)
    keys = near[:, 0].reshape(3 * count, heads_here, HEAD)
    values = near[:, 1].reshape(3 * count, heads_here, HEAD)
    mixed = window_attention(query, keys, values, position, total).reshape(count, local_width)
    partial_proj = lax.dot_general(
        mixed,
        lax.all_gather(out_weight, "dev", axis=0, tiled=True),
        (((1,), (1,)), ((), ())),
        preferred_element_type=jnp.float32,
    )
    proj = lax.psum(partial_proj, "sub")
    state = tokens.astype(jnp.float32) + (1.0 + modulation[0]) * proj
    normed = normalize(state, modulation)
    gates = route(normed, router_weight, expert_ids)
    experts = router_weight.shape[1]
    topk = expert_ids.shape[1]
    flat = expert_ids.reshape(-1)
    picks = flat.shape[0]
    onehot = (flat[:, None] == jnp.arange(experts, dtype=jnp.int32)[None, :]).astype(BF16)
    order = jnp.arange(picks, dtype=jnp.int32)
    earlier = (order[None, :] < order[:, None]).astype(BF16)
    ahead = jnp.dot(earlier, onehot, preferred_element_type=F32)
    rank = jnp.sum(ahead * onehot.astype(F32), 1).astype(jnp.int32)
    target = flat * CAP + rank
    hit = target[None, :] == jnp.arange(experts * CAP, dtype=jnp.int32)[:, None]
    owner = jnp.any(hit.reshape(experts * CAP, count, topk), 2).astype(BF16)
    slice_width = width // parts
    sent = lax.dynamic_slice_in_dim(normed, part * slice_width, slice_width, 1)
    sent_width = sent.shape[1]
    rows_out = jnp.dot(owner, sent, preferred_element_type=F32).astype(BF16)
    halves_here = gate_up_weight.shape[0]
    doubled = jnp.broadcast_to(
        rows_out.reshape(experts, 1, CAP, sent_width), (experts, 2, CAP, sent_width)
    )
    outgoing = doubled.reshape(devices, halves_here, CAP, sent_width)
    up_form = "sxcd,xgdf->sxcgf"
    down_form = "sxcf,xfd->sxcd"
    incoming = lax.all_to_all(outgoing, "dev", split_axis=0, concat_axis=0, tiled=True)
    both = jnp.einsum(
        up_form,
        lax.all_gather(incoming, "sub", axis=3, tiled=True),
        gate_up_weight,
        preferred_element_type=jnp.float32,
    )
    hidden = (jax.nn.silu(both[..., 0, :]) * both[..., 1, :]).astype(jnp.bfloat16)
    gathered = lax.all_gather(hidden, "sub", axis=hidden.ndim - 1, tiled=True)
    result = jnp.einsum(down_form, gathered, down_weight, preferred_element_type=jnp.float32)
    returned = lax.all_to_all(
        result.astype(jnp.bfloat16), "dev", split_axis=0, concat_axis=0, tiled=True
    )
    own_width = returned.shape[-1]
    arranged = returned.reshape(experts, 2, CAP, own_width)
    combined = arranged[:, 0].astype(F32) + arranged[:, 1].astype(F32)
    share = jnp.sum(
        jnp.where(hit.reshape(experts * CAP, count, topk), gates[None], 0.0), 2
    )
    routed = lax.dot_general(
        share,
        combined.reshape(experts * CAP, own_width),
        (((0,), (0,)), ((), ())),
        precision=lax.Precision.HIGHEST,
        preferred_element_type=F32,
    )
    own = lax.dynamic_slice_in_dim(state, part * slice_width, slice_width, 1)
    lift = lax.dynamic_slice_in_dim(modulation[3], part * slice_width, slice_width, 0)
    return (own + (1.0 + lift) * routed).astype(jnp.bfloat16)


def body(*arrays):
    tokens, router_weight, expert_ids, gate_up_weight = arrays[0], arrays[4], arrays[5], arrays[6]
    devices = lax.axis_size("dev")
    count, width = tokens.shape
    local = gate_up_weight.shape[0] // 2
    fits = (
        lax.axis_size("sub") == 2
        and devices >= 8
        and devices & (devices - 1) == 0
        and gate_up_weight.shape[0] % 2 == 0
        and width % (devices * 128) == 0
        and arrays[1].shape[2] * 2 == width
        and count % HEAD == 0
        and expert_ids.shape[1] * count <= width // 4
        and router_weight.shape[1] <= 256
    )
    if fits and count * devices <= 2 * local * devices * CAP:
        return gathered_body(*arrays)
    return exchanged_body(*arrays)


def solution(mesh):
    return jax.shard_map(
        body,
        mesh=mesh,
        in_specs=(
            P(("groups", "dev"), None),
            P(("groups", "dev"), None, "sub"),
            P("dev", "sub"),
            P("groups", None),
            P(),
            P(("groups", "dev"), None),
            P("dev", None, None, "sub"),
            P("dev", None, "sub"),
        ),
        out_specs=P(("groups", "dev"), "sub"),
        check_vma=False,
    )
```

```python
import functools
import math

import jax
import jax.numpy as jnp
from jax import lax
from jax.experimental import pallas as pl
from jax.experimental.pallas import tpu as pltpu
from jax.sharding import PartitionSpec as P

HEAD = 128
CAP = 12
SLOTS = 16
TILE = 16

EPS = 1e-06
NEG = -1e30
F32 = jnp.float32
BF16 = jnp.bfloat16

NT = (((1,), (1,)), ((), ()))


def vmem(mib):
    return pltpu.CompilerParams(vmem_limit_bytes=mib * 2**20)


def whole():
    return pl.BlockSpec(memory_space=pltpu.VMEM)


def cut_kernel(split, tokens_ref, qkv_ref, weight_ref, *refs):
    pair_ref, cross_ref, sent_ref, sem_ref = refs
    count = pair_ref.shape[0] // 2
    lanes = tokens_ref.shape[1] // 4
    chunk = tokens_ref.shape[1] // lax.axis_size("dev")
    side = lax.axis_index("dev") % 2
    part = lax.axis_index("sub")
    half = count // 2
    moves = [
        (qkv_ref.at[1], pair_ref.at[:count]),
        (qkv_ref.at[2], pair_ref.at[count:]),
        (qkv_ref.at[1], cross_ref.at[:count]),
        (qkv_ref.at[2], cross_ref.at[count : 2 * count]),
    ]
    for i in range(lanes // chunk):
        at = pl.multiple_of(part * 2 * lanes + (2 * i + 1 - side) * chunk, 128)
        for j in range(2):
            left = j * lanes + i * chunk
            moves.append(
                (
                    tokens_ref.at[j * half : (j + 1) * half, pl.ds(at, chunk)],
                    cross_ref.at[2 * count :, left : left + chunk],
                )
            )
    rows = sent_ref.shape[0]
    at = pl.multiple_of(lax.axis_index("groups") * rows if split else 0, TILE)
    moves.append((weight_ref.at[pl.ds(at, rows)], sent_ref))
    copies = [pltpu.make_async_copy(*move, sem_ref.at[n]) for n, move in enumerate(moves)]
    for copy in copies:
        copy.start()
    for copy in copies:
        copy.wait()


def rest_kernel(tokens_ref, qkv_ref, weight_ref, _, query_ref, near_ref, own_ref, sem_ref):
    lanes = near_ref.shape[1]
    chunk = tokens_ref.shape[1] // lax.axis_size("dev")
    side = lax.axis_index("dev") % 2
    part = lax.axis_index("sub")
    moves = [(qkv_ref.at[0], query_ref), (weight_ref, own_ref)]
    for i in range(lanes // chunk):
        at = pl.multiple_of(part * 2 * lanes + (2 * i + side) * chunk, 128)
        moves.append(
            (tokens_ref.at[:, pl.ds(at, chunk)], near_ref.at[:, i * chunk : (i + 1) * chunk])
        )
    copies = [pltpu.make_async_copy(*move, sem_ref.at[n]) for n, move in enumerate(moves)]
    for copy in copies:
        copy.start()
    for copy in copies:
        copy.wait()


def small_kernel(ids_ref, mod_ref, router_ref, _, row_ref, mod_to_ref, router_to_ref):
    topk, count = ids_ref.shape
    row_ref[...] = jnp.zeros(row_ref.shape, BF16)
    for k in range(topk):
        named = jnp.broadcast_to(ids_ref[k : k + 1, :], (TILE, count))
        row_ref[:, k * count : (k + 1) * count] = named.astype(F32).astype(BF16)
    mod_to_ref[...] = mod_ref[...]
    router_to_ref[...] = router_ref[...]


def attention_kernel(query_ref, own_ref, cross_ref, next_ref, *refs):
    mixed_ref = refs[-1]
    count, width = mixed_ref.shape
    place = lax.axis_index("dev")
    even = place % 2 == 0
    row = lax.broadcasted_iota(jnp.int32, (count, count), 0)
    col = lax.broadcasted_iota(jnp.int32, (count, count), 1)
    alone = (place == 0) | (place == lax.axis_size("dev") - 1)
    see_cross = jnp.where(even, col - row, row - col) <= 0
    see_next = (jnp.where(even, row - col, col - row) <= 0) & jnp.logical_not(alone)
    scale = 1.0 / math.sqrt(HEAD)

    def scored(q, k):
        return lax.dot_general(q, k, NT, preferred_element_type=F32) * scale

    for head in range(width // HEAD):
        lanes = slice(head * HEAD, (head + 1) * HEAD)
        q = query_ref[:, lanes]
        sc = jnp.where(see_cross, scored(q, cross_ref[:count, lanes]), NEG)
        so = scored(q, own_ref[:count, lanes])
        sn = jnp.where(see_next, scored(q, next_ref[:count, lanes]), NEG)
        top = jnp.max(jnp.maximum(jnp.maximum(sc, so), sn), 1, keepdims=True)
        wc, wo, wn = jnp.exp(sc - top), jnp.exp(so - top), jnp.exp(sn - top)
        inv = 1.0 / jnp.sum(wc + wo + wn, 1, keepdims=True)
        out = 0.0
        for weight, value in (
            (wo, own_ref[count:, lanes]),
            (wc, cross_ref[count : 2 * count, lanes]),
            (wn, next_ref[count:, lanes]),
        ):
            out += jnp.dot((weight * inv).astype(BF16), value, preferred_element_type=F32)
        mixed_ref[:, lanes] = out.astype(BF16)


def projection_kernel(steps, pieces, wanted, *refs):
    mixed_ref, other_ref = refs[0], refs[1]
    weight_refs = refs[2 : 2 + len(pieces)]
    out_ref = refs[2 + len(pieces)]
    count = mixed_ref.shape[0]
    half = steps // 2
    chunk = out_ref.shape[1] // half
    z = lax.axis_index("dev") // 2
    part = lax.axis_index("sub")
    group = lax.axis_index("groups")
    for (hop, side), w_ref in zip(pieces, weight_refs):
        rows = w_ref.shape[0]
        target = jnp.bitwise_xor(z, hop)
        away = jnp.where(target // half == part, 0, 1)
        lane = (target % half) * chunk
        if side is not None:
            lane += (group if side == 0 else 1 - group) * rows

        @pl.when(away == wanted)
        def _(lane=pl.multiple_of(lane, 128), rows=rows, w_ref=w_ref):
            for block, ref in enumerate((mixed_ref, other_ref)):
                out_ref[block * count : (block + 1) * count, pl.ds(lane, rows)] = (
                    lax.dot_general(ref[...], w_ref[...], NT, preferred_element_type=F32)
                )


def state_kernel(keep_ref, got_ref, near_ref, cross_ref, ids_ref, mod_ref, out_ref, again_ref):
    count, lanes = near_ref.shape
    half = count // 2
    chunk = mod_ref.shape[1] // lax.axis_size("dev")
    side = lax.axis_index("dev") % 2
    part = lax.axis_index("sub")
    for i in range(lanes // chunk):
        at = pl.multiple_of(part * 2 * lanes + (2 * i + side) * chunk, 128)
        lift = 1.0 + mod_ref[0:1, pl.ds(at, chunk)]
        cols = slice(i * chunk, (i + 1) * chunk)
        for j in range(4):
            rows = slice(j * half, (j + 1) * half)
            if j < 2:
                token = near_ref[rows, cols]
            else:
                left = (j - 2) * lanes + i * chunk
                token = cross_ref[2 * count :, left : left + chunk]
            proj = keep_ref[rows, cols] + got_ref[rows, cols]
            out_ref[rows, cols] = (token.astype(F32) + lift * proj).astype(BF16)
    out_ref[2 * count :, :] = ids_ref[...]
    again_ref[...] = out_ref[...]


def tie_kernel(*refs):
    pass


def tie(array, *others):
    anywhere = pl.BlockSpec(memory_space=pl.ANY)
    return pl.pallas_call(
        tie_kernel,
        out_shape=jax.ShapeDtypeStruct(array.shape, array.dtype),
        in_specs=[anywhere] * (1 + len(others)),
        out_specs=anywhere,
        input_output_aliases={0: 0},
        compiler_params=vmem(1),
    )(array, *others)


def select_kernel(local, topk, own, *refs):
    shard_refs, (mod_ref, router_ref) = refs[:4], refs[4:6]
    rows_ref, back_ref = refs[6:8]
    state_ref = refs[8] if own else None
    full_ref, gate_ref = refs[-2:]
    count, width = full_ref.shape
    lanes = shard_refs[0].shape[1]
    device = lax.axis_index("dev")
    side = device % 2
    part = lax.axis_index("sub")
    chunk = width // lax.axis_size("dev")
    experts = router_ref.shape[0]
    slots = local * SLOTS
    before = lax.broadcasted_iota(jnp.int32, (count, count), 0)
    after = lax.broadcasted_iota(jnp.int32, (count, count), 1)
    earlier = (before < after).astype(F32).astype(BF16)
    slot = lax.broadcasted_iota(jnp.int32, (slots, count), 0) % SLOTS
    mine = lax.broadcasted_iota(jnp.int32, (local, count), 0) + device * local
    every = lax.broadcasted_iota(jnp.int32, (experts, count), 0)
    for cross in range(2):
        for far_half in range(2):
            for far_side in range(2):
                ref = shard_refs[2 * far_half + far_side]
                top = (cross ^ far_side) * count
                half = part if far_half == 0 else 1 - part
                parity = side if far_side == 0 else 1 - side
                for i in range(lanes // chunk):
                    block = ref[top : top + count, i * chunk : (i + 1) * chunk]
                    at = (2 * i + parity) * chunk
                    full_ref[:, pl.ds(pl.multiple_of(half * 2 * lanes + at, 128), chunk)] = block
                    if own and cross == 0 and far_half == 0:
                        state_ref[:, pl.ds(pl.multiple_of(at, 128), chunk)] = block
        state = full_ref[...].astype(F32)
        scale = lax.rsqrt(jnp.mean(state * state, 1, keepdims=True) + EPS)
        normed = state * scale * (1.0 + mod_ref[2:3, :]) + mod_ref[1:2, :]
        normed = normed.astype(BF16)
        ids = shard_refs[cross][2 * count : 2 * count + TILE, :]
        ids = ids.astype(F32)[0:1, :].astype(jnp.int32)
        named = [ids[:, k * count : (k + 1) * count] for k in range(topk)]
        hot = sum((mine == n).astype(F32) for n in named)
        rank = jnp.dot(hot.astype(BF16), earlier, preferred_element_type=F32)
        rank = jnp.where(hot > 0.0, rank, -1.0)
        rank = jnp.concatenate(
            [jnp.broadcast_to(rank[e : e + 1], (SLOTS, count)) for e in range(local)]
        )
        pick = rank == slot.astype(F32)
        chosen = jnp.dot(
            jnp.where(pick, 1.0, 0.0).astype(BF16), normed, preferred_element_type=F32
        ).astype(BF16)
        for e in range(local):
            rows_ref[e, cross * SLOTS : (cross + 1) * SLOTS, :] = chosen[
                e * SLOTS : (e + 1) * SLOTS
            ]
        logits = lax.dot_general(router_ref[...], normed, NT, preferred_element_type=F32)
        lifted = sum(jnp.where(every == n, 1.0, 0.0) for n in named) * jax.nn.sigmoid(logits)
        gate_ref[...] = lifted / jnp.sum(lifted, 0, keepdims=True)
        here = gate_ref[pl.ds(pl.multiple_of(device * local, local), local), :]
        here = jnp.concatenate(
            [jnp.broadcast_to(here[e : e + 1], (SLOTS, count)) for e in range(local)]
        )
        back_ref[cross] = jnp.where(pick, here, 0.0).T.astype(BF16)


def load_kernel(from_ref, _, *refs):
    to_refs, done_ref, sem_ref = refs[:-2], refs[-2], refs[-1]
    copies = [
        pltpu.make_async_copy(from_ref.at[2 * e : 2 * e + 2], ref, sem_ref.at[e])
        for e, ref in enumerate(to_refs)
    ]
    for copy in copies:
        copy.start()
    done_ref[...] = jnp.zeros(done_ref.shape, F32)
    for copy in copies:
        copy.wait()


def load(weight, after_this, limit):
    local = weight.shape[0] // 2
    piece = jax.ShapeDtypeStruct((2, *weight.shape[1:]), BF16)
    return pl.pallas_call(
        load_kernel,
        out_shape=[piece] * local + [jax.ShapeDtypeStruct((8, 128), F32)],
        in_specs=[pl.BlockSpec(memory_space=pl.ANY)] * 2,
        out_specs=[whole()] * (local + 1),
        scratch_shapes=[pltpu.SemaphoreType.DMA((local,))],
        compiler_params=vmem(limit),
    )(weight, after_this)


def hidden_kernel(steps, low, *refs):
    rows_refs, w_refs, hidden_ref = refs[:steps], refs[steps:-1], refs[-1]
    for e, w_ref in enumerate(w_refs):
        rows = jnp.concatenate([ref[low + e] for ref in rows_refs])
        halves = []
        for b in range(2):
            gate = lax.dot_general(w_ref[b, 0], rows, NT, preferred_element_type=F32)
            up = lax.dot_general(w_ref[b, 1], rows, NT, preferred_element_type=F32)
            halves.append(jax.nn.silu(gate) * up)
        hidden_ref[e] = jnp.concatenate(halves).T.astype(BF16)


def output_kernel(low, near_ref, far_ref, w_ref, held_ref):
    part = lax.axis_index("sub")
    units = near_ref.shape[2] // 2
    for e in range(near_ref.shape[0]):
        total = 0.0
        for ref, who in ((near_ref, part), (far_ref, 1 - part)):
            at = pl.multiple_of(who * units, 64)
            weight = jnp.concatenate(
                [w_ref[2 * (low + e) + b, pl.ds(at, units), :] for b in range(2)]
            )
            total += jnp.dot(ref[e], weight, preferred_element_type=F32)
        total = total.astype(BF16)
        for source in range(held_ref.shape[0]):
            held_ref[source, e * SLOTS : (e + 1) * SLOTS, :] = total[
                source * SLOTS : (source + 1) * SLOTS
            ]


def share_kernel(steps, low, before, near_ref, far_ref, w_ref, *refs):
    held_refs, back_refs = refs[:before], refs[before : before + steps]
    out_refs, held_ref = refs[before + steps : -1], refs[-1]
    output_kernel(low, near_ref, far_ref, w_ref, held_ref)
    for source in range(2 * steps):
        back = back_refs[source // 2][source % 2]
        rows = jnp.concatenate([ref[source] for ref in (*held_refs, held_ref)])
        routed = jnp.dot(back, rows, preferred_element_type=F32).astype(BF16)
        if source < 2 * steps - 2:
            out_refs[source][...] = routed
        else:
            half = routed.shape[0] // 2
            at = 2 * source - (2 * steps - 2)
            out_refs[at][...] = routed[:half]
            out_refs[at + 1][...] = routed[half:]


def final_kernel(state_ref, mod_ref, top_ref, bottom_ref, *refs):
    out_ref = refs[-1]
    count, lanes = state_ref.shape
    at = pl.multiple_of(lax.axis_index("sub") * lanes, 128)
    lift = 1.0 + mod_ref[3:4, pl.ds(at, lanes)]
    for h, last_ref in enumerate((top_ref, bottom_ref)):
        rows = slice(h * count // 2, (h + 1) * count // 2)
        routed = last_ref[...].astype(F32)
        for ref in refs[:-1]:
            routed += ref[rows].astype(F32)
        out_ref[rows] = (state_ref[rows].astype(F32) + lift * routed).astype(BF16)


def gathered_body(
    tokens,
    query_key_value,
    out_weight,
    modulation,
    router_weight,
    expert_ids,
    gate_up_weight,
    down_weight,
):
    count, width = tokens.shape
    devices = lax.axis_size("dev")
    groups = lax.axis_size("groups")
    steps = devices // 2
    local_width = query_key_value.shape[2]
    chunk = width // devices
    lanes = width // 4
    halves_here = gate_up_weight.shape[0]
    local = halves_here // 2
    experts = router_weight.shape[1]
    topk = expert_ids.shape[1]
    struct = jax.ShapeDtypeStruct

    def hop(x, flip):
        return lax.ppermute(x, "dev", [(i, i ^ flip) for i in range(devices)])

    def swap(x):
        return lax.ppermute(x, "sub", [(0, 1), (1, 0)])

    split = groups == 2
    held = out_weight.shape[0] // (2 if split else 1)
    anywhere = pl.BlockSpec(memory_space=pl.ANY)
    stacked = query_key_value.transpose(1, 0, 2)
    pair, cross, sent = pl.pallas_call(
        functools.partial(cut_kernel, split),
        out_shape=[
            struct((2 * count, local_width), BF16),
            struct((2 * count + count // 2, local_width), BF16),
            struct((held, local_width), BF16),
        ],
        in_specs=[anywhere] * 3,
        out_specs=[whole()] * 3,
        scratch_shapes=[pltpu.SemaphoreType.DMA((5 + 2 * (lanes // chunk),))],
        compiler_params=vmem(53),
    )(tokens, stacked, out_weight)
    query, near, own_weight = pl.pallas_call(
        rest_kernel,
        out_shape=[
            struct((count, local_width), BF16),
            struct((count, lanes), BF16),
            struct(out_weight.shape, BF16),
        ],
        in_specs=[anywhere] * 4,
        out_specs=[whole()] * 3,
        scratch_shapes=[pltpu.SemaphoreType.DMA((2 + lanes // chunk,))],
        compiler_params=vmem(53),
    )(tokens, stacked, out_weight, sent)
    ids, small, router = pl.pallas_call(
        small_kernel,
        out_shape=[
            struct((TILE, lanes), BF16),
            struct(modulation.shape, F32),
            struct((experts, width), BF16),
        ],
        in_specs=[whole()] * 3 + [pl.BlockSpec(memory_space=pl.ANY)],
        out_specs=[whole()] * 3,
        compiler_params=vmem(4),
    )(expert_ids.T, modulation, router_weight.T, query)
    odd = [(i, i + 1) for i in range(1, devices - 1, 2)]
    after = lax.ppermute(pair, "dev", odd + [(j, i) for i, j in odd])
    cross = hop(cross, 1)

    units = gate_up_weight.shape[3]
    *ups, done = load(gate_up_weight.swapaxes(2, 3), query, 16)

    mine = {0: sent}
    for flip in range(2, steps):
        low = flip & -flip
        if flip > 2 and flip - low > 0:
            mine[flip] = hop(mine[flip - low], 2 * low)
        else:
            mine[flip] = tie(hop(sent, 2 * flip), done)
    own_weight = tie(own_weight, mine[2])
    pieces, weights = [(0, None), (1, None)], [own_weight, hop(own_weight, 2)]

    mixed = pl.pallas_call(
        attention_kernel,
        out_shape=struct((count, local_width), BF16),
        in_specs=[whole()] * 4 + [pl.BlockSpec(memory_space=pl.ANY)],
        out_specs=whole(),
        compiler_params=vmem(6),
    )(query, pair, cross, after, small)
    for flip in range(2, steps):
        if split:
            if flip == steps - 1:
                mine[flip] = tie(mine[flip], mixed)
            theirs = lax.ppermute(mine[flip], "groups", [(0, 1), (1, 0)])
            pieces += [(flip, 0), (flip, 1)]
            weights += [mine[flip], theirs]
        else:
            pieces.append((flip, None))
            weights.append(mine[flip])
    other = hop(mixed, 1)
    send, keep = (
        pl.pallas_call(
            functools.partial(projection_kernel, steps, tuple(pieces), wanted),
            out_shape=struct((2 * count, lanes), F32),
            in_specs=[whole()] * (2 + len(weights)),
            out_specs=whole(),
            compiler_params=vmem(6),
        )(mixed, other, *weights)
        for wanted in (1, 0)
    )
    shard, again = pl.pallas_call(
        state_kernel,
        out_shape=[struct((2 * count + TILE, lanes), BF16)] * 2,
        in_specs=[whole()] * 6,
        out_specs=[whole()] * 2,
        compiler_params=vmem(6),
    )(keep, swap(send), near, cross, ids, small)

    slots = local * SLOTS
    state = None
    picked, backs = [], []
    column = {0: shard, 1: hop(shard, 2)}
    across = hop(shard, 1)
    column[1] = tie(column[1], across)
    crossing = {0: across, 1: hop(column[1], 1)}
    beside = swap(column[1])
    swapped = swap(shard)
    column[2] = tie(hop(tie(again, swapped), 4), beside)
    for flip in range(3, steps):
        low = flip & -flip
        column[flip] = hop(column[flip - low] if flip > low else shard, 2 * low)
    for flip in range(steps):
        if flip == steps - 1:
            column[flip] = tie(column[flip], picked[0])
        block = column[flip]
        crossed = crossing[flip] if flip in crossing else hop(block, 1)
        if flip == steps - 1:
            crossed = tie(crossed, *picked[1:])
        own = flip == 0
        results = pl.pallas_call(
            functools.partial(select_kernel, local, topk, own),
            out_shape=[
                struct((local, 2 * SLOTS, width), BF16),
                struct((2, count, slots), BF16),
            ]
            + ([struct((count, 2 * lanes), BF16)] if own else []),
            in_specs=[whole()] * 6,
            out_specs=[whole()] * (3 if own else 2),
            scratch_shapes=[pltpu.VMEM((count, width), BF16), pltpu.VMEM((experts, count), F32)],
            compiler_params=vmem(6),
        )(block, crossed, beside if flip == 1 else swapped if own else swap(block), swap(crossed), small, router)
        picked.append(results[0])
        backs.append(results[1])
        if own:
            state = results[2]

    sources = 2 * steps
    room = sources * SLOTS
    first = local // 2
    groups_of = [(0, first), (first, local)] if first else [(0, local)]
    hidden = []
    for low, high in groups_of:
        own = pl.pallas_call(
            functools.partial(hidden_kernel, steps, low),
            out_shape=struct((high - low, room, 2 * units), BF16),
            in_specs=[whole()] * (steps + high - low),
            out_specs=whole(),
            compiler_params=vmem(6),
        )(*picked, *ups[low:high])
        hidden.append((own, swap(own)))
    held = []
    for (low, high), (own, other) in zip(groups_of[:-1], hidden[:-1]):
        held.append(
            pl.pallas_call(
                functools.partial(output_kernel, low),
                out_shape=struct((sources, (high - low) * SLOTS, 2 * lanes), BF16),
                in_specs=[whole()] * 3,
                out_specs=whole(),
                compiler_params=vmem(6),
            )(own, other, down_weight)
        )
    low, high = groups_of[-1]
    share = pl.pallas_call(
        functools.partial(share_kernel, steps, low, len(held)),
        out_shape=[struct((count, 2 * lanes), BF16)] * (sources - 2)
        + [struct((count // 2, 2 * lanes), BF16)] * 4,
        in_specs=[whole()] * (3 + len(held) + steps),
        out_specs=[whole()] * (sources + 2),
        scratch_shapes=[pltpu.VMEM((sources, (high - low) * SLOTS, 2 * lanes), BF16)],
        compiler_params=vmem(8),
    )(*hidden[-1], down_weight, *held, *backs)

    def forwarded(mine, crossed, flip):
        total = mine.astype(F32) + crossed.astype(F32)
        return hop(total.astype(BF16), 2 * flip)

    ends = share[-4:]
    top = hop(ends[2], 1)
    crossed = {flip: hop(share[2 * flip + 1], 1) for flip in range(steps - 2, 0, -1)}
    bottom = hop(tie(ends[3], top), 1)
    halves = [forwarded(ends[0], top, steps - 1), forwarded(ends[1], bottom, steps - 1)]
    terms = [forwarded(share[2 * flip], crossed[flip], flip) for flip in crossed]
    terms += [share[0], hop(tie(share[1], crossed[steps - 2]), 1)]
    return pl.pallas_call(
        final_kernel,
        out_shape=struct((count, 2 * lanes), BF16),
        in_specs=[whole()] * (4 + len(terms)),
        out_specs=whole(),
        compiler_params=vmem(8),
    )(state, small, *halves, *terms)


def extended(cells, sides, width):
    for axis, dim in sides:
        count = lax.axis_size(axis)
        ends = count - 1
        head = lax.slice_in_dim(cells, 0, width, axis=dim)
        tail = lax.slice_in_dim(cells, cells.shape[dim] - width, cells.shape[dim], axis=dim)
        cells = jnp.concatenate(
            [
                lax.ppermute(tail, axis, [(i, (i + 1) % count) for i in range(ends)]),
                cells,
                lax.ppermute(head, axis, [((i + 1) % count, i) for i in range(ends)]),
            ],
            axis=dim,
        )
    return cells


def window_attention(query, keys, values, index, total):
    count = query.shape[0]
    rows = jnp.arange(count, dtype=jnp.int32)[:, None]
    cols = jnp.arange(3 * count, dtype=jnp.int32)[None, :] - count
    place = index * count + cols
    allowed = (jnp.abs(cols - rows) <= count) & (place >= 0) & (place < total)
    scores = jnp.einsum(
        "qhd,khd->hqk", query, keys, preferred_element_type=jnp.float32
    ) / math.sqrt(query.shape[2])
    scores = jnp.where(allowed[None], scores, NEG)
    top = jnp.max(scores, -1, keepdims=True)
    weight = jnp.exp(scores - top)
    weight = (weight / jnp.sum(weight, -1, keepdims=True)).astype(jnp.bfloat16)
    mixed = jnp.einsum("hqk,khd->qhd", weight, values, preferred_element_type=jnp.float32)
    return mixed.astype(jnp.bfloat16)


def normalize(state, modulation):
    scale = lax.rsqrt(jnp.mean(state * state, -1, keepdims=True) + EPS)
    return (state * scale * (1.0 + modulation[2]) + modulation[1]).astype(jnp.bfloat16)


def route(normed, router_weight, expert_ids):
    logits = jnp.dot(normed, router_weight, preferred_element_type=jnp.float32)
    experts = router_weight.shape[1]
    match = expert_ids[:, :, None] == jnp.arange(experts, dtype=jnp.int32)[None, None, :]
    picked = jnp.sum(jnp.where(match, logits[:, None, :], 0.0), -1)
    lifted = jax.nn.sigmoid(picked)
    return lifted / jnp.sum(lifted, -1, keepdims=True)


def exchanged_body(
    tokens,
    query_key_value,
    out_weight,
    modulation,
    router_weight,
    expert_ids,
    gate_up_weight,
    down_weight,
):
    count = tokens.shape[0]
    width = tokens.shape[1]
    parts = lax.axis_size("sub")
    part = lax.axis_index("sub")
    position = lax.axis_index("dev")
    devices = lax.axis_size("dev")
    total = count * devices
    local_width = query_key_value.shape[2]
    heads_here = local_width // HEAD
    query = query_key_value[:, 0].reshape(count, heads_here, HEAD)
    pair = query_key_value[:, 1:]
    near = extended(pair, (("dev", 0),), count)
    keys = near[:, 0].reshape(3 * count, heads_here, HEAD)
    values = near[:, 1].reshape(3 * count, heads_here, HEAD)
    mixed = window_attention(query, keys, values, position, total).reshape(count, local_width)
    partial_proj = lax.dot_general(
        mixed,
        lax.all_gather(out_weight, "dev", axis=0, tiled=True),
        (((1,), (1,)), ((), ())),
        preferred_element_type=jnp.float32,
    )
    proj = lax.psum(partial_proj, "sub")
    state = tokens.astype(jnp.float32) + (1.0 + modulation[0]) * proj
    normed = normalize(state, modulation)
    gates = route(normed, router_weight, expert_ids)
    experts = router_weight.shape[1]
    topk = expert_ids.shape[1]
    flat = expert_ids.reshape(-1)
    picks = flat.shape[0]
    onehot = (flat[:, None] == jnp.arange(experts, dtype=jnp.int32)[None, :]).astype(BF16)
    order = jnp.arange(picks, dtype=jnp.int32)
    earlier = (order[None, :] < order[:, None]).astype(BF16)
    ahead = jnp.dot(earlier, onehot, preferred_element_type=F32)
    rank = jnp.sum(ahead * onehot.astype(F32), 1).astype(jnp.int32)
    target = flat * CAP + rank
    hit = target[None, :] == jnp.arange(experts * CAP, dtype=jnp.int32)[:, None]
    owner = jnp.any(hit.reshape(experts * CAP, count, topk), 2).astype(BF16)
    slice_width = width // parts
    sent = lax.dynamic_slice_in_dim(normed, part * slice_width, slice_width, 1)
    sent_width = sent.shape[1]
    rows_out = jnp.dot(owner, sent, preferred_element_type=F32).astype(BF16)
    halves_here = gate_up_weight.shape[0]
    doubled = jnp.broadcast_to(
        rows_out.reshape(experts, 1, CAP, sent_width), (experts, 2, CAP, sent_width)
    )
    outgoing = doubled.reshape(devices, halves_here, CAP, sent_width)
    up_form = "sxcd,xgdf->sxcgf"
    down_form = "sxcf,xfd->sxcd"
    incoming = lax.all_to_all(outgoing, "dev", split_axis=0, concat_axis=0, tiled=True)
    both = jnp.einsum(
        up_form,
        lax.all_gather(incoming, "sub", axis=3, tiled=True),
        gate_up_weight,
        preferred_element_type=jnp.float32,
    )
    hidden = (jax.nn.silu(both[..., 0, :]) * both[..., 1, :]).astype(jnp.bfloat16)
    gathered = lax.all_gather(hidden, "sub", axis=hidden.ndim - 1, tiled=True)
    result = jnp.einsum(down_form, gathered, down_weight, preferred_element_type=jnp.float32)
    returned = lax.all_to_all(
        result.astype(jnp.bfloat16), "dev", split_axis=0, concat_axis=0, tiled=True
    )
    own_width = returned.shape[-1]
    arranged = returned.reshape(experts, 2, CAP, own_width)
    combined = arranged[:, 0].astype(F32) + arranged[:, 1].astype(F32)
    share = jnp.sum(
        jnp.where(hit.reshape(experts * CAP, count, topk), gates[None], 0.0), 2
    )
    routed = lax.dot_general(
        share,
        combined.reshape(experts * CAP, own_width),
        (((0,), (0,)), ((), ())),
        precision=lax.Precision.HIGHEST,
        preferred_element_type=F32,
    )
    own = lax.dynamic_slice_in_dim(state, part * slice_width, slice_width, 1)
    lift = lax.dynamic_slice_in_dim(modulation[3], part * slice_width, slice_width, 0)
    return (own + (1.0 + lift) * routed).astype(jnp.bfloat16)


def body(*arrays):
    tokens, router_weight, expert_ids, gate_up_weight = arrays[0], arrays[4], arrays[5], arrays[6]
    devices = lax.axis_size("dev")
    count, width = tokens.shape
    local = gate_up_weight.shape[0] // 2
    fits = (
        lax.axis_size("sub") == 2
        and devices >= 8
        and devices & (devices - 1) == 0
        and gate_up_weight.shape[0] % 2 == 0
        and width % (devices * 128) == 0
        and arrays[1].shape[2] * 2 == width
        and count % HEAD == 0
        and expert_ids.shape[1] * count <= width // 4
        and router_weight.shape[1] <= 256
    )
    if fits and count * devices <= 2 * local * devices * CAP:
        return gathered_body(*arrays)
    return exchanged_body(*arrays)


def solution(mesh):
    return jax.shard_map(
        body,
        mesh=mesh,
        in_specs=(
            P(("groups", "dev"), None),
            P(("groups", "dev"), None, "sub"),
            P("dev", "sub"),
            P("groups", None),
            P(),
            P(("groups", "dev"), None),
            P("dev", None, None, "sub"),
            P("dev", None, "sub"),
        ),
        out_specs=P(("groups", "dev"), "sub"),
        check_vma=False,
    )
```

```python
import functools
import math

import jax
import jax.numpy as jnp
from jax import lax
from jax.experimental import pallas as pl
from jax.experimental.pallas import tpu as pltpu
from jax.sharding import PartitionSpec as P

HEAD = 128
CAP = 12
SLOTS = 16
TILE = 16

EPS = 1e-06
NEG = -1e30
F32 = jnp.float32
BF16 = jnp.bfloat16

NT = (((1,), (1,)), ((), ()))


def vmem(mib):
    return pltpu.CompilerParams(vmem_limit_bytes=mib * 2**20)


def whole():
    return pl.BlockSpec(memory_space=pltpu.VMEM)


def cut_kernel(split, tokens_ref, qkv_ref, weight_ref, *refs):
    pair_ref, cross_ref, sent_ref, sem_ref = refs
    count = pair_ref.shape[0] // 2
    lanes = tokens_ref.shape[1] // 4
    chunk = tokens_ref.shape[1] // lax.axis_size("dev")
    side = lax.axis_index("dev") % 2
    part = lax.axis_index("sub")
    half = count // 2
    moves = [
        (qkv_ref.at[1], pair_ref.at[:count]),
        (qkv_ref.at[2], pair_ref.at[count:]),
        (qkv_ref.at[1], cross_ref.at[:count]),
        (qkv_ref.at[2], cross_ref.at[count : 2 * count]),
    ]
    for i in range(lanes // chunk):
        at = pl.multiple_of(part * 2 * lanes + (2 * i + 1 - side) * chunk, 128)
        for j in range(2):
            left = j * lanes + i * chunk
            moves.append(
                (
                    tokens_ref.at[j * half : (j + 1) * half, pl.ds(at, chunk)],
                    cross_ref.at[2 * count :, left : left + chunk],
                )
            )
    rows = sent_ref.shape[0]
    at = pl.multiple_of(lax.axis_index("groups") * rows if split else 0, TILE)
    moves.append((weight_ref.at[pl.ds(at, rows)], sent_ref))
    copies = [pltpu.make_async_copy(*move, sem_ref.at[n]) for n, move in enumerate(moves)]
    for copy in copies:
        copy.start()
    for copy in copies:
        copy.wait()


def rest_kernel(tokens_ref, qkv_ref, weight_ref, _, query_ref, near_ref, own_ref, sem_ref):
    lanes = near_ref.shape[1]
    chunk = tokens_ref.shape[1] // lax.axis_size("dev")
    side = lax.axis_index("dev") % 2
    part = lax.axis_index("sub")
    moves = [(qkv_ref.at[0], query_ref), (weight_ref, own_ref)]
    for i in range(lanes // chunk):
        at = pl.multiple_of(part * 2 * lanes + (2 * i + side) * chunk, 128)
        moves.append(
            (tokens_ref.at[:, pl.ds(at, chunk)], near_ref.at[:, i * chunk : (i + 1) * chunk])
        )
    copies = [pltpu.make_async_copy(*move, sem_ref.at[n]) for n, move in enumerate(moves)]
    for copy in copies:
        copy.start()
    for copy in copies:
        copy.wait()


def small_kernel(ids_ref, mod_ref, router_ref, _, row_ref, mod_to_ref, router_to_ref):
    topk, count = ids_ref.shape
    row_ref[...] = jnp.zeros(row_ref.shape, BF16)
    for k in range(topk):
        named = jnp.broadcast_to(ids_ref[k : k + 1, :], (TILE, count))
        row_ref[:, k * count : (k + 1) * count] = named.astype(F32).astype(BF16)
    mod_to_ref[...] = mod_ref[...]
    router_to_ref[...] = router_ref[...]


def attention_kernel(query_ref, own_ref, cross_ref, next_ref, *refs):
    mixed_ref = refs[-1]
    count, width = mixed_ref.shape
    place = lax.axis_index("dev")
    even = place % 2 == 0
    row = lax.broadcasted_iota(jnp.int32, (count, count), 0)
    col = lax.broadcasted_iota(jnp.int32, (count, count), 1)
    alone = (place == 0) | (place == lax.axis_size("dev") - 1)
    see_cross = jnp.where(even, col - row, row - col) <= 0
    see_next = (jnp.where(even, row - col, col - row) <= 0) & jnp.logical_not(alone)
    scale = 1.0 / math.sqrt(HEAD)

    def scored(q, k):
        return lax.dot_general(q, k, NT, preferred_element_type=F32) * scale

    for head in range(width // HEAD):
        lanes = slice(head * HEAD, (head + 1) * HEAD)
        q = query_ref[:, lanes]
        sc = jnp.where(see_cross, scored(q, cross_ref[:count, lanes]), NEG)
        so = scored(q, own_ref[:count, lanes])
        sn = jnp.where(see_next, scored(q, next_ref[:count, lanes]), NEG)
        top = jnp.max(jnp.maximum(jnp.maximum(sc, so), sn), 1, keepdims=True)
        wc, wo, wn = jnp.exp(sc - top), jnp.exp(so - top), jnp.exp(sn - top)
        inv = 1.0 / jnp.sum(wc + wo + wn, 1, keepdims=True)
        out = 0.0
        for weight, value in (
            (wo, own_ref[count:, lanes]),
            (wc, cross_ref[count : 2 * count, lanes]),
            (wn, next_ref[count:, lanes]),
        ):
            out += jnp.dot((weight * inv).astype(BF16), value, preferred_element_type=F32)
        mixed_ref[:, lanes] = out.astype(BF16)


def projection_kernel(steps, pieces, wanted, *refs):
    mixed_ref, other_ref = refs[0], refs[1]
    weight_refs = refs[2 : 2 + len(pieces)]
    out_ref = refs[2 + len(pieces)]
    count = mixed_ref.shape[0]
    half = steps // 2
    chunk = out_ref.shape[1] // half
    z = lax.axis_index("dev") // 2
    part = lax.axis_index("sub")
    group = lax.axis_index("groups")
    for (hop, side), w_ref in zip(pieces, weight_refs):
        rows = w_ref.shape[0]
        target = jnp.bitwise_xor(z, hop)
        away = jnp.where(target // half == part, 0, 1)
        lane = (target % half) * chunk
        if side is not None:
            lane += (group if side == 0 else 1 - group) * rows

        @pl.when(away == wanted)
        def _(lane=pl.multiple_of(lane, 128), rows=rows, w_ref=w_ref):
            for block, ref in enumerate((mixed_ref, other_ref)):
                out_ref[block * count : (block + 1) * count, pl.ds(lane, rows)] = (
                    lax.dot_general(ref[...], w_ref[...], NT, preferred_element_type=F32)
                )


def state_kernel(keep_ref, got_ref, near_ref, cross_ref, ids_ref, mod_ref, out_ref, again_ref):
    count, lanes = near_ref.shape
    half = count // 2
    chunk = mod_ref.shape[1] // lax.axis_size("dev")
    side = lax.axis_index("dev") % 2
    part = lax.axis_index("sub")
    for i in range(lanes // chunk):
        at = pl.multiple_of(part * 2 * lanes + (2 * i + side) * chunk, 128)
        lift = 1.0 + mod_ref[0:1, pl.ds(at, chunk)]
        cols = slice(i * chunk, (i + 1) * chunk)
        for j in range(4):
            rows = slice(j * half, (j + 1) * half)
            if j < 2:
                token = near_ref[rows, cols]
            else:
                left = (j - 2) * lanes + i * chunk
                token = cross_ref[2 * count :, left : left + chunk]
            proj = keep_ref[rows, cols] + got_ref[rows, cols]
            out_ref[rows, cols] = (token.astype(F32) + lift * proj).astype(BF16)
    out_ref[2 * count :, :] = ids_ref[...]
    again_ref[...] = out_ref[...]


def tie_kernel(*refs):
    pass


def tie(array, *others):
    anywhere = pl.BlockSpec(memory_space=pl.ANY)
    return pl.pallas_call(
        tie_kernel,
        out_shape=jax.ShapeDtypeStruct(array.shape, array.dtype),
        in_specs=[anywhere] * (1 + len(others)),
        out_specs=anywhere,
        input_output_aliases={0: 0},
        compiler_params=vmem(1),
    )(array, *others)


def select_kernel(local, topk, own, cut, *refs):
    shard_refs, refs = refs[: 4 * cut], refs[4 * cut :]
    mod_ref, router_ref, rows_ref, back_ref = refs[:4]
    state_ref = refs[4] if own else None
    full_ref, gate_ref = refs[-2:]
    count, width = full_ref.shape
    lanes = shard_refs[0].shape[1]
    tail = (3 - cut) * count
    device = lax.axis_index("dev")
    side = device % 2
    part = lax.axis_index("sub")
    chunk = width // lax.axis_size("dev")
    experts = router_ref.shape[0]
    slots = local * SLOTS
    before = lax.broadcasted_iota(jnp.int32, (count, count), 0)
    after = lax.broadcasted_iota(jnp.int32, (count, count), 1)
    earlier = (before < after).astype(F32).astype(BF16)
    slot = lax.broadcasted_iota(jnp.int32, (slots, count), 0) % SLOTS
    mine = lax.broadcasted_iota(jnp.int32, (local, count), 0) + device * local
    every = lax.broadcasted_iota(jnp.int32, (experts, count), 0)
    for cross in range(2):
        for far_half in range(2):
            for far_side in range(2):
                top = (cross ^ far_side) * count
                ref = shard_refs[cut * (2 * far_half + far_side) + (top if cut == 2 else 0) // count]
                top = 0 if cut == 2 else top
                half = part if far_half == 0 else 1 - part
                parity = side if far_side == 0 else 1 - side
                for i in range(lanes // chunk):
                    block = ref[top : top + count, i * chunk : (i + 1) * chunk]
                    at = (2 * i + parity) * chunk
                    full_ref[:, pl.ds(pl.multiple_of(half * 2 * lanes + at, 128), chunk)] = block
                    if own and cross == 0 and far_half == 0:
                        state_ref[:, pl.ds(pl.multiple_of(at, 128), chunk)] = block
        state = full_ref[...].astype(F32)
        scale = lax.rsqrt(jnp.mean(state * state, 1, keepdims=True) + EPS)
        normed = state * scale * (1.0 + mod_ref[2:3, :]) + mod_ref[1:2, :]
        normed = normed.astype(BF16)
        ids = shard_refs[cut * cross + cut - 1][tail : tail + TILE, :]
        ids = ids.astype(F32)[0:1, :].astype(jnp.int32)
        named = [ids[:, k * count : (k + 1) * count] for k in range(topk)]
        hot = sum((mine == n).astype(F32) for n in named)
        rank = jnp.dot(hot.astype(BF16), earlier, preferred_element_type=F32)
        rank = jnp.where(hot > 0.0, rank, -1.0)
        rank = jnp.concatenate(
            [jnp.broadcast_to(rank[e : e + 1], (SLOTS, count)) for e in range(local)]
        )
        pick = rank == slot.astype(F32)
        chosen = jnp.dot(
            jnp.where(pick, 1.0, 0.0).astype(BF16), normed, preferred_element_type=F32
        ).astype(BF16)
        for e in range(local):
            rows_ref[e, cross * SLOTS : (cross + 1) * SLOTS, :] = chosen[
                e * SLOTS : (e + 1) * SLOTS
            ]
        logits = lax.dot_general(router_ref[...], normed, NT, preferred_element_type=F32)
        lifted = sum(jnp.where(every == n, 1.0, 0.0) for n in named) * jax.nn.sigmoid(logits)
        gate_ref[...] = lifted / jnp.sum(lifted, 0, keepdims=True)
        here = gate_ref[pl.ds(pl.multiple_of(device * local, local), local), :]
        here = jnp.concatenate(
            [jnp.broadcast_to(here[e : e + 1], (SLOTS, count)) for e in range(local)]
        )
        back_ref[cross] = jnp.where(pick, here, 0.0).T.astype(BF16)


def load_kernel(from_ref, _, *refs):
    to_refs, done_ref, sem_ref = refs[:-2], refs[-2], refs[-1]
    copies = [
        pltpu.make_async_copy(from_ref.at[2 * e : 2 * e + 2], ref, sem_ref.at[e])
        for e, ref in enumerate(to_refs)
    ]
    for copy in copies:
        copy.start()
    done_ref[...] = jnp.zeros(done_ref.shape, F32)
    for copy in copies:
        copy.wait()


def load(weight, after_this, limit):
    local = weight.shape[0] // 2
    piece = jax.ShapeDtypeStruct((2, *weight.shape[1:]), BF16)
    return pl.pallas_call(
        load_kernel,
        out_shape=[piece] * local + [jax.ShapeDtypeStruct((8, 128), F32)],
        in_specs=[pl.BlockSpec(memory_space=pl.ANY)] * 2,
        out_specs=[whole()] * (local + 1),
        scratch_shapes=[pltpu.SemaphoreType.DMA((local,))],
        compiler_params=vmem(limit),
    )(weight, after_this)


def hidden_kernel(steps, low, *refs):
    rows_refs, w_refs, hidden_ref = refs[:steps], refs[steps:-1], refs[-1]
    for e, w_ref in enumerate(w_refs):
        rows = jnp.concatenate([ref[low + e] for ref in rows_refs])
        halves = []
        for b in range(2):
            gate = lax.dot_general(w_ref[b, 0], rows, NT, preferred_element_type=F32)
            up = lax.dot_general(w_ref[b, 1], rows, NT, preferred_element_type=F32)
            halves.append(jax.nn.silu(gate) * up)
        hidden_ref[e] = jnp.concatenate(halves).T.astype(BF16)


def output_kernel(low, near_ref, far_ref, w_ref, held_ref):
    part = lax.axis_index("sub")
    units = near_ref.shape[2] // 2
    for e in range(near_ref.shape[0]):
        total = 0.0
        for ref, who in ((near_ref, part), (far_ref, 1 - part)):
            at = pl.multiple_of(who * units, 64)
            weight = jnp.concatenate(
                [w_ref[2 * (low + e) + b, pl.ds(at, units), :] for b in range(2)]
            )
            total += jnp.dot(ref[e], weight, preferred_element_type=F32)
        total = total.astype(BF16)
        for source in range(held_ref.shape[0]):
            held_ref[source, e * SLOTS : (e + 1) * SLOTS, :] = total[
                source * SLOTS : (source + 1) * SLOTS
            ]


def share_kernel(steps, low, before, near_ref, far_ref, w_ref, *refs):
    held_refs, back_refs = refs[:before], refs[before : before + steps]
    out_refs, held_ref = refs[before + steps : -1], refs[-1]
    output_kernel(low, near_ref, far_ref, w_ref, held_ref)
    for source in range(2 * steps):
        back = back_refs[source // 2][source % 2]
        rows = jnp.concatenate([ref[source] for ref in (*held_refs, held_ref)])
        routed = jnp.dot(back, rows, preferred_element_type=F32).astype(BF16)
        if source < 2 * steps - 2:
            out_refs[source][...] = routed
        else:
            half = routed.shape[0] // 2
            at = 2 * source - (2 * steps - 2)
            out_refs[at][...] = routed[:half]
            out_refs[at + 1][...] = routed[half:]


def final_kernel(state_ref, mod_ref, top_ref, bottom_ref, *refs):
    out_ref = refs[-1]
    count, lanes = state_ref.shape
    at = pl.multiple_of(lax.axis_index("sub") * lanes, 128)
    lift = 1.0 + mod_ref[3:4, pl.ds(at, lanes)]
    for h, last_ref in enumerate((top_ref, bottom_ref)):
        rows = slice(h * count // 2, (h + 1) * count // 2)
        routed = last_ref[...].astype(F32)
        for ref in refs[:-1]:
            routed += ref[rows].astype(F32)
        out_ref[rows] = (state_ref[rows].astype(F32) + lift * routed).astype(BF16)


def gathered_body(
    tokens,
    query_key_value,
    out_weight,
    modulation,
    router_weight,
    expert_ids,
    gate_up_weight,
    down_weight,
):
    count, width = tokens.shape
    devices = lax.axis_size("dev")
    groups = lax.axis_size("groups")
    steps = devices // 2
    local_width = query_key_value.shape[2]
    chunk = width // devices
    lanes = width // 4
    halves_here = gate_up_weight.shape[0]
    local = halves_here // 2
    experts = router_weight.shape[1]
    topk = expert_ids.shape[1]
    struct = jax.ShapeDtypeStruct

    def hop(x, flip):
        return lax.ppermute(x, "dev", [(i, i ^ flip) for i in range(devices)])

    def swap(x):
        return lax.ppermute(x, "sub", [(0, 1), (1, 0)])

    split = groups == 2
    held = out_weight.shape[0] // (2 if split else 1)
    anywhere = pl.BlockSpec(memory_space=pl.ANY)
    stacked = query_key_value.transpose(1, 0, 2)
    pair, cross, sent = pl.pallas_call(
        functools.partial(cut_kernel, split),
        out_shape=[
            struct((2 * count, local_width), BF16),
            struct((2 * count + count // 2, local_width), BF16),
            struct((held, local_width), BF16),
        ],
        in_specs=[anywhere] * 3,
        out_specs=[whole()] * 3,
        scratch_shapes=[pltpu.SemaphoreType.DMA((5 + 2 * (lanes // chunk),))],
        compiler_params=vmem(53),
    )(tokens, stacked, out_weight)
    query, near, own_weight = pl.pallas_call(
        rest_kernel,
        out_shape=[
            struct((count, local_width), BF16),
            struct((count, lanes), BF16),
            struct(out_weight.shape, BF16),
        ],
        in_specs=[anywhere] * 4,
        out_specs=[whole()] * 3,
        scratch_shapes=[pltpu.SemaphoreType.DMA((2 + lanes // chunk,))],
        compiler_params=vmem(53),
    )(tokens, stacked, out_weight, sent)
    ids, small, router = pl.pallas_call(
        small_kernel,
        out_shape=[
            struct((TILE, lanes), BF16),
            struct(modulation.shape, F32),
            struct((experts, width), BF16),
        ],
        in_specs=[whole()] * 3 + [pl.BlockSpec(memory_space=pl.ANY)],
        out_specs=[whole()] * 3,
        compiler_params=vmem(4),
    )(expert_ids.T, modulation, router_weight.T, query)
    odd = [(i, i + 1) for i in range(1, devices - 1, 2)]
    after = lax.ppermute(pair, "dev", odd + [(j, i) for i, j in odd])
    cross = hop(cross, 1)

    units = gate_up_weight.shape[3]
    *ups, done = load(gate_up_weight.swapaxes(2, 3), query, 16)

    mine = {0: sent}
    for flip in range(2, steps):
        low = flip & -flip
        if flip > 2 and flip - low > 0:
            mine[flip] = hop(mine[flip - low], 2 * low)
        else:
            mine[flip] = tie(hop(sent, 2 * flip), done)
    own_weight = tie(own_weight, mine[2])
    pieces, weights = [(0, None), (1, None)], [own_weight, hop(own_weight, 2)]

    mixed = pl.pallas_call(
        attention_kernel,
        out_shape=struct((count, local_width), BF16),
        in_specs=[whole()] * 4 + [pl.BlockSpec(memory_space=pl.ANY)],
        out_specs=whole(),
        compiler_params=vmem(6),
    )(query, pair, cross, after, small)
    for flip in range(2, steps):
        if split:
            if flip == steps - 1:
                mine[flip] = tie(mine[flip], mixed)
            theirs = lax.ppermute(mine[flip], "groups", [(0, 1), (1, 0)])
            pieces += [(flip, 0), (flip, 1)]
            weights += [mine[flip], theirs]
        else:
            pieces.append((flip, None))
            weights.append(mine[flip])
    other = hop(mixed, 1)
    send, keep = (
        pl.pallas_call(
            functools.partial(projection_kernel, steps, tuple(pieces), wanted),
            out_shape=struct((2 * count, lanes), F32),
            in_specs=[whole()] * (2 + len(weights)),
            out_specs=whole(),
            compiler_params=vmem(6),
        )(mixed, other, *weights)
        for wanted in (1, 0)
    )
    shard, again = pl.pallas_call(
        state_kernel,
        out_shape=[struct((2 * count + TILE, lanes), BF16)] * 2,
        in_specs=[whole()] * 6,
        out_specs=[whole()] * 2,
        compiler_params=vmem(6),
    )(keep, swap(send), near, cross, ids, small)

    slots = local * SLOTS
    state = None
    picked, backs = [], []
    column = {0: shard, 1: hop(shard, 2)}
    across = hop(shard, 1)
    column[1] = tie(column[1], across)
    crossing = {0: across, 1: hop(column[1], 1)}
    beside = swap(column[1])
    swapped = swap(shard)
    column[2] = tie(hop(tie(again, swapped), 4), beside)
    for flip in range(3, steps):
        low = flip & -flip
        column[flip] = hop(column[flip - low] if flip > low else shard, 2 * low)
    for flip in range(steps):
        own = flip == 0
        if flip == steps - 1:
            low = flip & -flip
            before = column[flip - low]
            cut = [hop(before[:count], 2 * low), hop(before[count:], 2 * low)]
            cut[0] = tie(cut[0], picked[0])
            over = [hop(piece, 1) for piece in cut]
            over[1] = tie(over[1], *picked[1:])
            blocks = cut + over + [swap(piece) for piece in cut + over]
        else:
            block = column[flip]
            crossed = crossing[flip] if flip in crossing else hop(block, 1)
            near_half = beside if flip == 1 else swapped if own else swap(block)
            blocks = [block, crossed, near_half, swap(crossed)]
        results = pl.pallas_call(
            functools.partial(select_kernel, local, topk, own, len(blocks) // 4),
            out_shape=[
                struct((local, 2 * SLOTS, width), BF16),
                struct((2, count, slots), BF16),
            ]
            + ([struct((count, 2 * lanes), BF16)] if own else []),
            in_specs=[whole()] * (2 + len(blocks)),
            out_specs=[whole()] * (3 if own else 2),
            scratch_shapes=[pltpu.VMEM((count, width), BF16), pltpu.VMEM((experts, count), F32)],
            compiler_params=vmem(6),
        )(*blocks, small, router)
        picked.append(results[0])
        backs.append(results[1])
        if own:
            state = results[2]

    sources = 2 * steps
    room = sources * SLOTS
    first = local // 2
    groups_of = [(0, first), (first, local)] if first else [(0, local)]
    hidden = []
    for low, high in groups_of:
        own = pl.pallas_call(
            functools.partial(hidden_kernel, steps, low),
            out_shape=struct((high - low, room, 2 * units), BF16),
            in_specs=[whole()] * (steps + high - low),
            out_specs=whole(),
            compiler_params=vmem(6),
        )(*picked, *ups[low:high])
        hidden.append((own, swap(own)))
    held = []
    for (low, high), (own, other) in zip(groups_of[:-1], hidden[:-1]):
        held.append(
            pl.pallas_call(
                functools.partial(output_kernel, low),
                out_shape=struct((sources, (high - low) * SLOTS, 2 * lanes), BF16),
                in_specs=[whole()] * 3,
                out_specs=whole(),
                compiler_params=vmem(6),
            )(own, other, down_weight)
        )
    low, high = groups_of[-1]
    share = pl.pallas_call(
        functools.partial(share_kernel, steps, low, len(held)),
        out_shape=[struct((count, 2 * lanes), BF16)] * (sources - 2)
        + [struct((count // 2, 2 * lanes), BF16)] * 4,
        in_specs=[whole()] * (3 + len(held) + steps),
        out_specs=[whole()] * (sources + 2),
        scratch_shapes=[pltpu.VMEM((sources, (high - low) * SLOTS, 2 * lanes), BF16)],
        compiler_params=vmem(8),
    )(*hidden[-1], down_weight, *held, *backs)

    def forwarded(mine, crossed, flip):
        total = mine.astype(F32) + crossed.astype(F32)
        return hop(total.astype(BF16), 2 * flip)

    ends = share[-4:]
    top = hop(ends[2], 1)
    crossed = {flip: hop(share[2 * flip + 1], 1) for flip in range(steps - 2, 0, -1)}
    bottom = hop(tie(ends[3], top), 1)
    halves = [forwarded(ends[0], top, steps - 1), forwarded(ends[1], bottom, steps - 1)]
    terms = [forwarded(share[2 * flip], crossed[flip], flip) for flip in crossed]
    terms += [share[0], hop(tie(share[1], crossed[steps - 2]), 1)]
    return pl.pallas_call(
        final_kernel,
        out_shape=struct((count, 2 * lanes), BF16),
        in_specs=[whole()] * (4 + len(terms)),
        out_specs=whole(),
        compiler_params=vmem(8),
    )(state, small, *halves, *terms)


def extended(cells, sides, width):
    for axis, dim in sides:
        count = lax.axis_size(axis)
        ends = count - 1
        head = lax.slice_in_dim(cells, 0, width, axis=dim)
        tail = lax.slice_in_dim(cells, cells.shape[dim] - width, cells.shape[dim], axis=dim)
        cells = jnp.concatenate(
            [
                lax.ppermute(tail, axis, [(i, (i + 1) % count) for i in range(ends)]),
                cells,
                lax.ppermute(head, axis, [((i + 1) % count, i) for i in range(ends)]),
            ],
            axis=dim,
        )
    return cells


def window_attention(query, keys, values, index, total):
    count = query.shape[0]
    rows = jnp.arange(count, dtype=jnp.int32)[:, None]
    cols = jnp.arange(3 * count, dtype=jnp.int32)[None, :] - count
    place = index * count + cols
    allowed = (jnp.abs(cols - rows) <= count) & (place >= 0) & (place < total)
    scores = jnp.einsum(
        "qhd,khd->hqk", query, keys, preferred_element_type=jnp.float32
    ) / math.sqrt(query.shape[2])
    scores = jnp.where(allowed[None], scores, NEG)
    top = jnp.max(scores, -1, keepdims=True)
    weight = jnp.exp(scores - top)
    weight = (weight / jnp.sum(weight, -1, keepdims=True)).astype(jnp.bfloat16)
    mixed = jnp.einsum("hqk,khd->qhd", weight, values, preferred_element_type=jnp.float32)
    return mixed.astype(jnp.bfloat16)


def normalize(state, modulation):
    scale = lax.rsqrt(jnp.mean(state * state, -1, keepdims=True) + EPS)
    return (state * scale * (1.0 + modulation[2]) + modulation[1]).astype(jnp.bfloat16)


def route(normed, router_weight, expert_ids):
    logits = jnp.dot(normed, router_weight, preferred_element_type=jnp.float32)
    experts = router_weight.shape[1]
    match = expert_ids[:, :, None] == jnp.arange(experts, dtype=jnp.int32)[None, None, :]
    picked = jnp.sum(jnp.where(match, logits[:, None, :], 0.0), -1)
    lifted = jax.nn.sigmoid(picked)
    return lifted / jnp.sum(lifted, -1, keepdims=True)


def exchanged_body(
    tokens,
    query_key_value,
    out_weight,
    modulation,
    router_weight,
    expert_ids,
    gate_up_weight,
    down_weight,
):
    count = tokens.shape[0]
    width = tokens.shape[1]
    parts = lax.axis_size("sub")
    part = lax.axis_index("sub")
    position = lax.axis_index("dev")
    devices = lax.axis_size("dev")
    total = count * devices
    local_width = query_key_value.shape[2]
    heads_here = local_width // HEAD
    query = query_key_value[:, 0].reshape(count, heads_here, HEAD)
    pair = query_key_value[:, 1:]
    near = extended(pair, (("dev", 0),), count)
    keys = near[:, 0].reshape(3 * count, heads_here, HEAD)
    values = near[:, 1].reshape(3 * count, heads_here, HEAD)
    mixed = window_attention(query, keys, values, position, total).reshape(count, local_width)
    partial_proj = lax.dot_general(
        mixed,
        lax.all_gather(out_weight, "dev", axis=0, tiled=True),
        (((1,), (1,)), ((), ())),
        preferred_element_type=jnp.float32,
    )
    proj = lax.psum(partial_proj, "sub")
    state = tokens.astype(jnp.float32) + (1.0 + modulation[0]) * proj
    normed = normalize(state, modulation)
    gates = route(normed, router_weight, expert_ids)
    experts = router_weight.shape[1]
    topk = expert_ids.shape[1]
    flat = expert_ids.reshape(-1)
    picks = flat.shape[0]
    onehot = (flat[:, None] == jnp.arange(experts, dtype=jnp.int32)[None, :]).astype(BF16)
    order = jnp.arange(picks, dtype=jnp.int32)
    earlier = (order[None, :] < order[:, None]).astype(BF16)
    ahead = jnp.dot(earlier, onehot, preferred_element_type=F32)
    rank = jnp.sum(ahead * onehot.astype(F32), 1).astype(jnp.int32)
    target = flat * CAP + rank
    hit = target[None, :] == jnp.arange(experts * CAP, dtype=jnp.int32)[:, None]
    owner = jnp.any(hit.reshape(experts * CAP, count, topk), 2).astype(BF16)
    slice_width = width // parts
    sent = lax.dynamic_slice_in_dim(normed, part * slice_width, slice_width, 1)
    sent_width = sent.shape[1]
    rows_out = jnp.dot(owner, sent, preferred_element_type=F32).astype(BF16)
    halves_here = gate_up_weight.shape[0]
    doubled = jnp.broadcast_to(
        rows_out.reshape(experts, 1, CAP, sent_width), (experts, 2, CAP, sent_width)
    )
    outgoing = doubled.reshape(devices, halves_here, CAP, sent_width)
    up_form = "sxcd,xgdf->sxcgf"
    down_form = "sxcf,xfd->sxcd"
    incoming = lax.all_to_all(outgoing, "dev", split_axis=0, concat_axis=0, tiled=True)
    both = jnp.einsum(
        up_form,
        lax.all_gather(incoming, "sub", axis=3, tiled=True),
        gate_up_weight,
        preferred_element_type=jnp.float32,
    )
    hidden = (jax.nn.silu(both[..., 0, :]) * both[..., 1, :]).astype(jnp.bfloat16)
    gathered = lax.all_gather(hidden, "sub", axis=hidden.ndim - 1, tiled=True)
    result = jnp.einsum(down_form, gathered, down_weight, preferred_element_type=jnp.float32)
    returned = lax.all_to_all(
        result.astype(jnp.bfloat16), "dev", split_axis=0, concat_axis=0, tiled=True
    )
    own_width = returned.shape[-1]
    arranged = returned.reshape(experts, 2, CAP, own_width)
    combined = arranged[:, 0].astype(F32) + arranged[:, 1].astype(F32)
    share = jnp.sum(
        jnp.where(hit.reshape(experts * CAP, count, topk), gates[None], 0.0), 2
    )
    routed = lax.dot_general(
        share,
        combined.reshape(experts * CAP, own_width),
        (((0,), (0,)), ((), ())),
        precision=lax.Precision.HIGHEST,
        preferred_element_type=F32,
    )
    own = lax.dynamic_slice_in_dim(state, part * slice_width, slice_width, 1)
    lift = lax.dynamic_slice_in_dim(modulation[3], part * slice_width, slice_width, 0)
    return (own + (1.0 + lift) * routed).astype(jnp.bfloat16)


def body(*arrays):
    tokens, router_weight, expert_ids, gate_up_weight = arrays[0], arrays[4], arrays[5], arrays[6]
    devices = lax.axis_size("dev")
    count, width = tokens.shape
    local = gate_up_weight.shape[0] // 2
    fits = (
        lax.axis_size("sub") == 2
        and devices >= 8
        and devices & (devices - 1) == 0
        and gate_up_weight.shape[0] % 2 == 0
        and width % (devices * 128) == 0
        and arrays[1].shape[2] * 2 == width
        and count % HEAD == 0
        and expert_ids.shape[1] * count <= width // 4
        and router_weight.shape[1] <= 256
    )
    if fits and count * devices <= 2 * local * devices * CAP:
        return gathered_body(*arrays)
    return exchanged_body(*arrays)


def solution(mesh):
    return jax.shard_map(
        body,
        mesh=mesh,
        in_specs=(
            P(("groups", "dev"), None),
            P(("groups", "dev"), None, "sub"),
            P("dev", "sub"),
            P("groups", None),
            P(),
            P(("groups", "dev"), None),
            P("dev", None, None, "sub"),
            P("dev", None, "sub"),
        ),
        out_specs=P(("groups", "dev"), "sub"),
        check_vma=False,
    )
```

```python
import functools
import math

import jax
import jax.numpy as jnp
from jax import lax
from jax.experimental import pallas as pl
from jax.experimental.pallas import tpu as pltpu
from jax.sharding import PartitionSpec as P

HEAD = 128
CAP = 12
SLOTS = 16
TILE = 16

EPS = 1e-06
NEG = -1e30
F32 = jnp.float32
BF16 = jnp.bfloat16

NT = (((1,), (1,)), ((), ()))


def vmem(mib):
    return pltpu.CompilerParams(vmem_limit_bytes=mib * 2**20)


def whole():
    return pl.BlockSpec(memory_space=pltpu.VMEM)


def cut_kernel(split, tokens_ref, qkv_ref, weight_ref, *refs):
    pair_ref, cross_ref, sent_ref, sem_ref = refs
    count = pair_ref.shape[0] // 2
    lanes = tokens_ref.shape[1] // 4
    chunk = tokens_ref.shape[1] // lax.axis_size("dev")
    side = lax.axis_index("dev") % 2
    part = lax.axis_index("sub")
    half = count // 2
    moves = [
        (qkv_ref.at[1], pair_ref.at[:count]),
        (qkv_ref.at[2], pair_ref.at[count:]),
        (qkv_ref.at[1], cross_ref.at[:count]),
        (qkv_ref.at[2], cross_ref.at[count : 2 * count]),
    ]
    for i in range(lanes // chunk):
        at = pl.multiple_of(part * 2 * lanes + (2 * i + 1 - side) * chunk, 128)
        for j in range(2):
            left = j * lanes + i * chunk
            moves.append(
                (
                    tokens_ref.at[j * half : (j + 1) * half, pl.ds(at, chunk)],
                    cross_ref.at[2 * count :, left : left + chunk],
                )
            )
    rows = sent_ref.shape[0]
    at = pl.multiple_of(lax.axis_index("groups") * rows if split else 0, TILE)
    moves.append((weight_ref.at[pl.ds(at, rows)], sent_ref))
    copies = [pltpu.make_async_copy(*move, sem_ref.at[n]) for n, move in enumerate(moves)]
    for copy in copies:
        copy.start()
    for copy in copies:
        copy.wait()


def rest_kernel(tokens_ref, qkv_ref, weight_ref, _, query_ref, near_ref, own_ref, sem_ref):
    lanes = near_ref.shape[1]
    chunk = tokens_ref.shape[1] // lax.axis_size("dev")
    side = lax.axis_index("dev") % 2
    part = lax.axis_index("sub")
    moves = [(qkv_ref.at[0], query_ref), (weight_ref, own_ref)]
    for i in range(lanes // chunk):
        at = pl.multiple_of(part * 2 * lanes + (2 * i + side) * chunk, 128)
        moves.append(
            (tokens_ref.at[:, pl.ds(at, chunk)], near_ref.at[:, i * chunk : (i + 1) * chunk])
        )
    copies = [pltpu.make_async_copy(*move, sem_ref.at[n]) for n, move in enumerate(moves)]
    for copy in copies:
        copy.start()
    for copy in copies:
        copy.wait()


def small_kernel(ids_ref, mod_ref, router_ref, _, row_ref, mod_to_ref, router_to_ref):
    topk, count = ids_ref.shape
    row_ref[...] = jnp.zeros(row_ref.shape, BF16)
    for k in range(topk):
        named = jnp.broadcast_to(ids_ref[k : k + 1, :], (TILE, count))
        row_ref[:, k * count : (k + 1) * count] = named.astype(F32).astype(BF16)
    mod_to_ref[...] = mod_ref[...]
    router_to_ref[...] = router_ref[...]


def attention_kernel(query_ref, own_ref, cross_ref, next_ref, *refs):
    mixed_ref = refs[-1]
    count, width = mixed_ref.shape
    place = lax.axis_index("dev")
    even = place % 2 == 0
    row = lax.broadcasted_iota(jnp.int32, (count, count), 0)
    col = lax.broadcasted_iota(jnp.int32, (count, count), 1)
    alone = (place == 0) | (place == lax.axis_size("dev") - 1)
    see_cross = jnp.where(even, col - row, row - col) <= 0
    see_next = (jnp.where(even, row - col, col - row) <= 0) & jnp.logical_not(alone)
    scale = 1.0 / math.sqrt(HEAD)

    def scored(q, k):
        return lax.dot_general(q, k, NT, preferred_element_type=F32) * scale

    for head in range(width // HEAD):
        lanes = slice(head * HEAD, (head + 1) * HEAD)
        q = query_ref[:, lanes]
        sc = jnp.where(see_cross, scored(q, cross_ref[:count, lanes]), NEG)
        so = scored(q, own_ref[:count, lanes])
        sn = jnp.where(see_next, scored(q, next_ref[:count, lanes]), NEG)
        top = jnp.max(jnp.maximum(jnp.maximum(sc, so), sn), 1, keepdims=True)
        wc, wo, wn = jnp.exp(sc - top), jnp.exp(so - top), jnp.exp(sn - top)
        inv = 1.0 / jnp.sum(wc + wo + wn, 1, keepdims=True)
        out = 0.0
        for weight, value in (
            (wo, own_ref[count:, lanes]),
            (wc, cross_ref[count : 2 * count, lanes]),
            (wn, next_ref[count:, lanes]),
        ):
            out += jnp.dot((weight * inv).astype(BF16), value, preferred_element_type=F32)
        mixed_ref[:, lanes] = out.astype(BF16)


def projection_kernel(steps, pieces, wanted, *refs):
    mixed_ref, other_ref = refs[0], refs[1]
    weight_refs = refs[2 : 2 + len(pieces)]
    out_ref = refs[2 + len(pieces)]
    count = mixed_ref.shape[0]
    half = steps // 2
    chunk = out_ref.shape[1] // half
    z = lax.axis_index("dev") // 2
    part = lax.axis_index("sub")
    group = lax.axis_index("groups")
    for (hop, side), w_ref in zip(pieces, weight_refs):
        rows = w_ref.shape[0]
        target = jnp.bitwise_xor(z, hop)
        away = jnp.where(target // half == part, 0, 1)
        lane = (target % half) * chunk
        if side is not None:
            lane += (group if side == 0 else 1 - group) * rows

        @pl.when(away == wanted)
        def _(lane=pl.multiple_of(lane, 128), rows=rows, w_ref=w_ref):
            for block, ref in enumerate((mixed_ref, other_ref)):
                out_ref[block * count : (block + 1) * count, pl.ds(lane, rows)] = (
                    lax.dot_general(ref[...], w_ref[...], NT, preferred_element_type=F32)
                )


def state_kernel(keep_ref, got_ref, near_ref, cross_ref, ids_ref, mod_ref, out_ref, again_ref):
    count, lanes = near_ref.shape
    half = count // 2
    chunk = mod_ref.shape[1] // lax.axis_size("dev")
    side = lax.axis_index("dev") % 2
    part = lax.axis_index("sub")
    for i in range(lanes // chunk):
        at = pl.multiple_of(part * 2 * lanes + (2 * i + side) * chunk, 128)
        lift = 1.0 + mod_ref[0:1, pl.ds(at, chunk)]
        cols = slice(i * chunk, (i + 1) * chunk)
        for j in range(4):
            rows = slice(j * half, (j + 1) * half)
            if j < 2:
                token = near_ref[rows, cols]
            else:
                left = (j - 2) * lanes + i * chunk
                token = cross_ref[2 * count :, left : left + chunk]
            proj = keep_ref[rows, cols] + got_ref[rows, cols]
            out_ref[rows, cols] = (token.astype(F32) + lift * proj).astype(BF16)
    out_ref[2 * count :, :] = ids_ref[...]
    again_ref[...] = out_ref[...]


def tie_kernel(*refs):
    pass


def tie(array, *others):
    anywhere = pl.BlockSpec(memory_space=pl.ANY)
    return pl.pallas_call(
        tie_kernel,
        out_shape=jax.ShapeDtypeStruct(array.shape, array.dtype),
        in_specs=[anywhere] * (1 + len(others)),
        out_specs=anywhere,
        input_output_aliases={0: 0},
        compiler_params=vmem(1),
    )(array, *others)


def select_kernel(local, topk, own, *refs):
    shard_refs, (mod_ref, router_ref) = refs[:4], refs[4:6]
    rows_ref, back_ref = refs[6:8]
    state_ref = refs[8] if own else None
    full_ref, gate_ref = refs[-2:]
    count, width = full_ref.shape
    lanes = shard_refs[0].shape[1]
    device = lax.axis_index("dev")
    side = device % 2
    part = lax.axis_index("sub")
    chunk = width // lax.axis_size("dev")
    experts = router_ref.shape[0]
    slots = local * SLOTS
    before = lax.broadcasted_iota(jnp.int32, (count, count), 0)
    after = lax.broadcasted_iota(jnp.int32, (count, count), 1)
    earlier = (before < after).astype(F32).astype(BF16)
    slot = lax.broadcasted_iota(jnp.int32, (slots, count), 0) % SLOTS
    mine = lax.broadcasted_iota(jnp.int32, (local, count), 0) + device * local
    every = lax.broadcasted_iota(jnp.int32, (experts, count), 0)
    for cross in range(2):
        for far_half in range(2):
            for far_side in range(2):
                ref = shard_refs[2 * far_half + far_side]
                top = (cross ^ far_side) * count
                half = part if far_half == 0 else 1 - part
                parity = side if far_side == 0 else 1 - side
                for i in range(lanes // chunk):
                    block = ref[top : top + count, i * chunk : (i + 1) * chunk]
                    at = (2 * i + parity) * chunk
                    full_ref[:, pl.ds(pl.multiple_of(half * 2 * lanes + at, 128), chunk)] = block
                    if own and cross == 0 and far_half == 0:
                        state_ref[:, pl.ds(pl.multiple_of(at, 128), chunk)] = block
        state = full_ref[...].astype(F32)
        scale = lax.rsqrt(jnp.mean(state * state, 1, keepdims=True) + EPS)
        normed = state * scale * (1.0 + mod_ref[2:3, :]) + mod_ref[1:2, :]
        normed = normed.astype(BF16)
        ids = shard_refs[cross][2 * count : 2 * count + TILE, :]
        ids = ids.astype(F32)[0:1, :].astype(jnp.int32)
        named = [ids[:, k * count : (k + 1) * count] for k in range(topk)]
        hot = sum((mine == n).astype(F32) for n in named)
        rank = jnp.dot(hot.astype(BF16), earlier, preferred_element_type=F32)
        rank = jnp.where(hot > 0.0, rank, -1.0)
        rank = jnp.concatenate(
            [jnp.broadcast_to(rank[e : e + 1], (SLOTS, count)) for e in range(local)]
        )
        pick = rank == slot.astype(F32)
        chosen = jnp.dot(
            jnp.where(pick, 1.0, 0.0).astype(BF16), normed, preferred_element_type=F32
        ).astype(BF16)
        for e in range(local):
            rows_ref[e, cross * SLOTS : (cross + 1) * SLOTS, :] = chosen[
                e * SLOTS : (e + 1) * SLOTS
            ]
        logits = lax.dot_general(router_ref[...], normed, NT, preferred_element_type=F32)
        lifted = sum(jnp.where(every == n, 1.0, 0.0) for n in named) * jax.nn.sigmoid(logits)
        gate_ref[...] = lifted / jnp.sum(lifted, 0, keepdims=True)
        here = gate_ref[pl.ds(pl.multiple_of(device * local, local), local), :]
        here = jnp.concatenate(
            [jnp.broadcast_to(here[e : e + 1], (SLOTS, count)) for e in range(local)]
        )
        back_ref[cross] = jnp.where(pick, here, 0.0).T.astype(BF16)


def load_kernel(from_ref, _, *refs):
    to_refs, done_ref, sem_ref = refs[:-2], refs[-2], refs[-1]
    copies = [
        pltpu.make_async_copy(from_ref.at[2 * e : 2 * e + 2], ref, sem_ref.at[e])
        for e, ref in enumerate(to_refs)
    ]
    for copy in copies:
        copy.start()
    done_ref[...] = jnp.zeros(done_ref.shape, F32)
    for copy in copies:
        copy.wait()


def load(weight, after_this, limit):
    local = weight.shape[0] // 2
    piece = jax.ShapeDtypeStruct((2, *weight.shape[1:]), BF16)
    return pl.pallas_call(
        load_kernel,
        out_shape=[piece] * local + [jax.ShapeDtypeStruct((8, 128), F32)],
        in_specs=[pl.BlockSpec(memory_space=pl.ANY)] * 2,
        out_specs=[whole()] * (local + 1),
        scratch_shapes=[pltpu.SemaphoreType.DMA((local,))],
        compiler_params=vmem(limit),
    )(weight, after_this)


def hidden_kernel(steps, low, *refs):
    rows_refs, w_refs, hidden_ref = refs[:steps], refs[steps:-1], refs[-1]
    for e, w_ref in enumerate(w_refs):
        rows = jnp.concatenate([ref[low + e] for ref in rows_refs])
        halves = []
        for b in range(2):
            gate = lax.dot_general(w_ref[b, 0], rows, NT, preferred_element_type=F32)
            up = lax.dot_general(w_ref[b, 1], rows, NT, preferred_element_type=F32)
            halves.append(jax.nn.silu(gate) * up)
        hidden_ref[e] = jnp.concatenate(halves).T.astype(BF16)


def output_kernel(low, near_ref, far_ref, w_ref, held_ref):
    part = lax.axis_index("sub")
    units = near_ref.shape[2] // 2
    for e in range(near_ref.shape[0]):
        total = 0.0
        for ref, who in ((near_ref, part), (far_ref, 1 - part)):
            at = pl.multiple_of(who * units, 64)
            weight = jnp.concatenate(
                [w_ref[2 * (low + e) + b, pl.ds(at, units), :] for b in range(2)]
            )
            total += jnp.dot(ref[e], weight, preferred_element_type=F32)
        total = total.astype(BF16)
        for source in range(held_ref.shape[0]):
            held_ref[source, e * SLOTS : (e + 1) * SLOTS, :] = total[
                source * SLOTS : (source + 1) * SLOTS
            ]


def routed_rows(steps, which, back_refs, held_refs, out_refs):
    for flip in range(steps):
        source = 2 * flip + which
        rows = jnp.concatenate([ref[source] for ref in held_refs])
        routed = jnp.dot(back_refs[flip][which], rows, preferred_element_type=F32).astype(BF16)
        if flip < steps - 1:
            out_refs[flip][...] = routed
        else:
            half = routed.shape[0] // 2
            out_refs[flip][...] = routed[:half]
            out_refs[flip + 1][...] = routed[half:]


def crossing_kernel(steps, low, before, near_ref, far_ref, w_ref, *refs):
    held_refs, back_refs = refs[:before], refs[before : before + steps]
    out_refs, held_ref = refs[before + steps : -1], refs[-1]
    output_kernel(low, near_ref, far_ref, w_ref, held_ref)
    routed_rows(steps, 1, back_refs, (*held_refs, held_ref), out_refs)


def column_kernel(steps, before, *refs):
    routed_rows(steps, 0, refs[before : before + steps], refs[:before], refs[before + steps :])


def final_kernel(state_ref, mod_ref, top_ref, bottom_ref, *refs):
    out_ref = refs[-1]
    count, lanes = state_ref.shape
    at = pl.multiple_of(lax.axis_index("sub") * lanes, 128)
    lift = 1.0 + mod_ref[3:4, pl.ds(at, lanes)]
    for h, last_ref in enumerate((top_ref, bottom_ref)):
        rows = slice(h * count // 2, (h + 1) * count // 2)
        routed = last_ref[...].astype(F32)
        for ref in refs[:-1]:
            routed += ref[rows].astype(F32)
        out_ref[rows] = (state_ref[rows].astype(F32) + lift * routed).astype(BF16)


def gathered_body(
    tokens,
    query_key_value,
    out_weight,
    modulation,
    router_weight,
    expert_ids,
    gate_up_weight,
    down_weight,
):
    count, width = tokens.shape
    devices = lax.axis_size("dev")
    groups = lax.axis_size("groups")
    steps = devices // 2
    local_width = query_key_value.shape[2]
    chunk = width // devices
    lanes = width // 4
    halves_here = gate_up_weight.shape[0]
    local = halves_here // 2
    experts = router_weight.shape[1]
    topk = expert_ids.shape[1]
    struct = jax.ShapeDtypeStruct

    def hop(x, flip):
        return lax.ppermute(x, "dev", [(i, i ^ flip) for i in range(devices)])

    def swap(x):
        return lax.ppermute(x, "sub", [(0, 1), (1, 0)])

    split = groups == 2
    held = out_weight.shape[0] // (2 if split else 1)
    anywhere = pl.BlockSpec(memory_space=pl.ANY)
    stacked = query_key_value.transpose(1, 0, 2)
    pair, cross, sent = pl.pallas_call(
        functools.partial(cut_kernel, split),
        out_shape=[
            struct((2 * count, local_width), BF16),
            struct((2 * count + count // 2, local_width), BF16),
            struct((held, local_width), BF16),
        ],
        in_specs=[anywhere] * 3,
        out_specs=[whole()] * 3,
        scratch_shapes=[pltpu.SemaphoreType.DMA((5 + 2 * (lanes // chunk),))],
        compiler_params=vmem(53),
    )(tokens, stacked, out_weight)
    query, near, own_weight = pl.pallas_call(
        rest_kernel,
        out_shape=[
            struct((count, local_width), BF16),
            struct((count, lanes), BF16),
            struct(out_weight.shape, BF16),
        ],
        in_specs=[anywhere] * 4,
        out_specs=[whole()] * 3,
        scratch_shapes=[pltpu.SemaphoreType.DMA((2 + lanes // chunk,))],
        compiler_params=vmem(53),
    )(tokens, stacked, out_weight, sent)
    ids, small, router = pl.pallas_call(
        small_kernel,
        out_shape=[
            struct((TILE, lanes), BF16),
            struct(modulation.shape, F32),
            struct((experts, width), BF16),
        ],
        in_specs=[whole()] * 3 + [pl.BlockSpec(memory_space=pl.ANY)],
        out_specs=[whole()] * 3,
        compiler_params=vmem(4),
    )(expert_ids.T, modulation, router_weight.T, query)
    odd = [(i, i + 1) for i in range(1, devices - 1, 2)]
    after = lax.ppermute(pair, "dev", odd + [(j, i) for i, j in odd])
    cross = hop(cross, 1)

    units = gate_up_weight.shape[3]
    *ups, done = load(gate_up_weight.swapaxes(2, 3), query, 16)

    mine = {0: sent}
    for flip in range(2, steps):
        low = flip & -flip
        if flip > 2 and flip - low > 0:
            mine[flip] = hop(mine[flip - low], 2 * low)
        else:
            mine[flip] = tie(hop(sent, 2 * flip), done)
    own_weight = tie(own_weight, mine[2])
    pieces, weights = [(0, None), (1, None)], [own_weight, hop(own_weight, 2)]

    mixed = pl.pallas_call(
        attention_kernel,
        out_shape=struct((count, local_width), BF16),
        in_specs=[whole()] * 4 + [pl.BlockSpec(memory_space=pl.ANY)],
        out_specs=whole(),
        compiler_params=vmem(6),
    )(query, pair, cross, after, small)
    for flip in range(2, steps):
        if split:
            if flip == steps - 1:
                mine[flip] = tie(mine[flip], mixed)
            theirs = lax.ppermute(mine[flip], "groups", [(0, 1), (1, 0)])
            pieces += [(flip, 0), (flip, 1)]
            weights += [mine[flip], theirs]
        else:
            pieces.append((flip, None))
            weights.append(mine[flip])
    other = hop(mixed, 1)
    send, keep = (
        pl.pallas_call(
            functools.partial(projection_kernel, steps, tuple(pieces), wanted),
            out_shape=struct((2 * count, lanes), F32),
            in_specs=[whole()] * (2 + len(weights)),
            out_specs=whole(),
            compiler_params=vmem(6),
        )(mixed, other, *weights)
        for wanted in (1, 0)
    )
    shard, again = pl.pallas_call(
        state_kernel,
        out_shape=[struct((2 * count + TILE, lanes), BF16)] * 2,
        in_specs=[whole()] * 6,
        out_specs=[whole()] * 2,
        compiler_params=vmem(6),
    )(keep, swap(send), near, cross, ids, small)

    slots = local * SLOTS
    state = None
    picked, backs = [], []
    column = {0: shard, 1: hop(shard, 2)}
    across = hop(shard, 1)
    column[1] = tie(column[1], across)
    crossing = {0: across, 1: hop(column[1], 1)}
    beside = swap(column[1])
    swapped = swap(shard)
    column[2] = tie(hop(tie(again, swapped), 4), beside)
    for flip in range(3, steps):
        low = flip & -flip
        column[flip] = hop(column[flip - low] if flip > low else shard, 2 * low)
    for flip in range(steps):
        if flip == steps - 1:
            column[flip] = tie(column[flip], picked[0])
        block = column[flip]
        crossed = crossing[flip] if flip in crossing else hop(block, 1)
        if flip == steps - 1:
            crossed = tie(crossed, *picked[1:])
        own = flip == 0
        results = pl.pallas_call(
            functools.partial(select_kernel, local, topk, own),
            out_shape=[
                struct((local, 2 * SLOTS, width), BF16),
                struct((2, count, slots), BF16),
            ]
            + ([struct((count, 2 * lanes), BF16)] if own else []),
            in_specs=[whole()] * 6,
            out_specs=[whole()] * (3 if own else 2),
            scratch_shapes=[pltpu.VMEM((count, width), BF16), pltpu.VMEM((experts, count), F32)],
            compiler_params=vmem(6),
        )(block, crossed, beside if flip == 1 else swapped if own else swap(block), swap(crossed), small, router)
        picked.append(results[0])
        backs.append(results[1])
        if own:
            state = results[2]

    sources = 2 * steps
    room = sources * SLOTS
    first = local // 2
    groups_of = [(0, first), (first, local)] if first else [(0, local)]
    hidden = []
    for low, high in groups_of:
        own = pl.pallas_call(
            functools.partial(hidden_kernel, steps, low),
            out_shape=struct((high - low, room, 2 * units), BF16),
            in_specs=[whole()] * (steps + high - low),
            out_specs=whole(),
            compiler_params=vmem(6),
        )(*picked, *ups[low:high])
        hidden.append((own, swap(own)))
    held = []
    for (low, high), (own, other) in zip(groups_of[:-1], hidden[:-1]):
        held.append(
            pl.pallas_call(
                functools.partial(output_kernel, low),
                out_shape=struct((sources, (high - low) * SLOTS, 2 * lanes), BF16),
                in_specs=[whole()] * 3,
                out_specs=whole(),
                compiler_params=vmem(6),
            )(own, other, down_weight)
        )
    low, high = groups_of[-1]
    blocks_out = [struct((count, 2 * lanes), BF16)] * (steps - 1)
    blocks_out += [struct((count // 2, 2 * lanes), BF16)] * 2
    *crossing_out, last = pl.pallas_call(
        functools.partial(crossing_kernel, steps, low, len(held)),
        out_shape=blocks_out + [struct((sources, (high - low) * SLOTS, 2 * lanes), BF16)],
        in_specs=[whole()] * (3 + len(held) + steps),
        out_specs=[whole()] * (steps + 2),
        compiler_params=vmem(8),
    )(*hidden[-1], down_weight, *held, *backs)
    held.append(last)
    column_out = pl.pallas_call(
        functools.partial(column_kernel, steps, len(held)),
        out_shape=blocks_out,
        in_specs=[whole()] * (len(held) + steps),
        out_specs=[whole()] * (steps + 1),
        compiler_params=vmem(8),
    )(*held, *backs)

    def forwarded(mine, crossed, flip):
        total = mine.astype(F32) + crossed.astype(F32)
        return hop(total.astype(BF16), 2 * flip)

    top = hop(crossing_out[-2], 1)
    crossed = {flip: hop(crossing_out[flip], 1) for flip in range(steps - 2, 0, -1)}
    bottom = hop(tie(crossing_out[-1], top), 1)
    halves = [forwarded(column_out[h - 2], (top, bottom)[h], steps - 1) for h in range(2)]
    terms = [forwarded(column_out[flip], crossed[flip], flip) for flip in crossed]
    terms += [column_out[0], hop(tie(crossing_out[0], crossed[steps - 2]), 1)]
    return pl.pallas_call(
        final_kernel,
        out_shape=struct((count, 2 * lanes), BF16),
        in_specs=[whole()] * (4 + len(terms)),
        out_specs=whole(),
        compiler_params=vmem(8),
    )(state, small, *halves, *terms)


def extended(cells, sides, width):
    for axis, dim in sides:
        count = lax.axis_size(axis)
        ends = count - 1
        head = lax.slice_in_dim(cells, 0, width, axis=dim)
        tail = lax.slice_in_dim(cells, cells.shape[dim] - width, cells.shape[dim], axis=dim)
        cells = jnp.concatenate(
            [
                lax.ppermute(tail, axis, [(i, (i + 1) % count) for i in range(ends)]),
                cells,
                lax.ppermute(head, axis, [((i + 1) % count, i) for i in range(ends)]),
            ],
            axis=dim,
        )
    return cells


def window_attention(query, keys, values, index, total):
    count = query.shape[0]
    rows = jnp.arange(count, dtype=jnp.int32)[:, None]
    cols = jnp.arange(3 * count, dtype=jnp.int32)[None, :] - count
    place = index * count + cols
    allowed = (jnp.abs(cols - rows) <= count) & (place >= 0) & (place < total)
    scores = jnp.einsum(
        "qhd,khd->hqk", query, keys, preferred_element_type=jnp.float32
    ) / math.sqrt(query.shape[2])
    scores = jnp.where(allowed[None], scores, NEG)
    top = jnp.max(scores, -1, keepdims=True)
    weight = jnp.exp(scores - top)
    weight = (weight / jnp.sum(weight, -1, keepdims=True)).astype(jnp.bfloat16)
    mixed = jnp.einsum("hqk,khd->qhd", weight, values, preferred_element_type=jnp.float32)
    return mixed.astype(jnp.bfloat16)


def normalize(state, modulation):
    scale = lax.rsqrt(jnp.mean(state * state, -1, keepdims=True) + EPS)
    return (state * scale * (1.0 + modulation[2]) + modulation[1]).astype(jnp.bfloat16)


def route(normed, router_weight, expert_ids):
    logits = jnp.dot(normed, router_weight, preferred_element_type=jnp.float32)
    experts = router_weight.shape[1]
    match = expert_ids[:, :, None] == jnp.arange(experts, dtype=jnp.int32)[None, None, :]
    picked = jnp.sum(jnp.where(match, logits[:, None, :], 0.0), -1)
    lifted = jax.nn.sigmoid(picked)
    return lifted / jnp.sum(lifted, -1, keepdims=True)


def exchanged_body(
    tokens,
    query_key_value,
    out_weight,
    modulation,
    router_weight,
    expert_ids,
    gate_up_weight,
    down_weight,
):
    count = tokens.shape[0]
    width = tokens.shape[1]
    parts = lax.axis_size("sub")
    part = lax.axis_index("sub")
    position = lax.axis_index("dev")
    devices = lax.axis_size("dev")
    total = count * devices
    local_width = query_key_value.shape[2]
    heads_here = local_width // HEAD
    query = query_key_value[:, 0].reshape(count, heads_here, HEAD)
    pair = query_key_value[:, 1:]
    near = extended(pair, (("dev", 0),), count)
    keys = near[:, 0].reshape(3 * count, heads_here, HEAD)
    values = near[:, 1].reshape(3 * count, heads_here, HEAD)
    mixed = window_attention(query, keys, values, position, total).reshape(count, local_width)
    partial_proj = lax.dot_general(
        mixed,
        lax.all_gather(out_weight, "dev", axis=0, tiled=True),
        (((1,), (1,)), ((), ())),
        preferred_element_type=jnp.float32,
    )
    proj = lax.psum(partial_proj, "sub")
    state = tokens.astype(jnp.float32) + (1.0 + modulation[0]) * proj
    normed = normalize(state, modulation)
    gates = route(normed, router_weight, expert_ids)
    experts = router_weight.shape[1]
    topk = expert_ids.shape[1]
    flat = expert_ids.reshape(-1)
    picks = flat.shape[0]
    onehot = (flat[:, None] == jnp.arange(experts, dtype=jnp.int32)[None, :]).astype(BF16)
    order = jnp.arange(picks, dtype=jnp.int32)
    earlier = (order[None, :] < order[:, None]).astype(BF16)
    ahead = jnp.dot(earlier, onehot, preferred_element_type=F32)
    rank = jnp.sum(ahead * onehot.astype(F32), 1).astype(jnp.int32)
    target = flat * CAP + rank
    hit = target[None, :] == jnp.arange(experts * CAP, dtype=jnp.int32)[:, None]
    owner = jnp.any(hit.reshape(experts * CAP, count, topk), 2).astype(BF16)
    slice_width = width // parts
    sent = lax.dynamic_slice_in_dim(normed, part * slice_width, slice_width, 1)
    sent_width = sent.shape[1]
    rows_out = jnp.dot(owner, sent, preferred_element_type=F32).astype(BF16)
    halves_here = gate_up_weight.shape[0]
    doubled = jnp.broadcast_to(
        rows_out.reshape(experts, 1, CAP, sent_width), (experts, 2, CAP, sent_width)
    )
    outgoing = doubled.reshape(devices, halves_here, CAP, sent_width)
    up_form = "sxcd,xgdf->sxcgf"
    down_form = "sxcf,xfd->sxcd"
    incoming = lax.all_to_all(outgoing, "dev", split_axis=0, concat_axis=0, tiled=True)
    both = jnp.einsum(
        up_form,
        lax.all_gather(incoming, "sub", axis=3, tiled=True),
        gate_up_weight,
        preferred_element_type=jnp.float32,
    )
    hidden = (jax.nn.silu(both[..., 0, :]) * both[..., 1, :]).astype(jnp.bfloat16)
    gathered = lax.all_gather(hidden, "sub", axis=hidden.ndim - 1, tiled=True)
    result = jnp.einsum(down_form, gathered, down_weight, preferred_element_type=jnp.float32)
    returned = lax.all_to_all(
        result.astype(jnp.bfloat16), "dev", split_axis=0, concat_axis=0, tiled=True
    )
    own_width = returned.shape[-1]
    arranged = returned.reshape(experts, 2, CAP, own_width)
    combined = arranged[:, 0].astype(F32) + arranged[:, 1].astype(F32)
    share = jnp.sum(
        jnp.where(hit.reshape(experts * CAP, count, topk), gates[None], 0.0), 2
    )
    routed = lax.dot_general(
        share,
        combined.reshape(experts * CAP, own_width),
        (((0,), (0,)), ((), ())),
        precision=lax.Precision.HIGHEST,
        preferred_element_type=F32,
    )
    own = lax.dynamic_slice_in_dim(state, part * slice_width, slice_width, 1)
    lift = lax.dynamic_slice_in_dim(modulation[3], part * slice_width, slice_width, 0)
    return (own + (1.0 + lift) * routed).astype(jnp.bfloat16)


def body(*arrays):
    tokens, router_weight, expert_ids, gate_up_weight = arrays[0], arrays[4], arrays[5], arrays[6]
    devices = lax.axis_size("dev")
    count, width = tokens.shape
    local = gate_up_weight.shape[0] // 2
    fits = (
        lax.axis_size("sub") == 2
        and devices >= 8
        and devices & (devices - 1) == 0
        and gate_up_weight.shape[0] % 2 == 0
        and width % (devices * 128) == 0
        and arrays[1].shape[2] * 2 == width
        and count % HEAD == 0
        and expert_ids.shape[1] * count <= width // 4
        and router_weight.shape[1] <= 256
    )
    if fits and count * devices <= 2 * local * devices * CAP:
        return gathered_body(*arrays)
    return exchanged_body(*arrays)


def solution(mesh):
    return jax.shard_map(
        body,
        mesh=mesh,
        in_specs=(
            P(("groups", "dev"), None),
            P(("groups", "dev"), None, "sub"),
            P("dev", "sub"),
            P("groups", None),
            P(),
            P(("groups", "dev"), None),
            P("dev", None, None, "sub"),
            P("dev", None, "sub"),
        ),
        out_specs=P(("groups", "dev"), "sub"),
        check_vma=False,
    )
```

```python
import functools
import math

import jax
import jax.numpy as jnp
from jax import lax
from jax.experimental import pallas as pl
from jax.experimental.pallas import tpu as pltpu
from jax.sharding import PartitionSpec as P

HEAD = 128
CAP = 12
SLOTS = 16
TILE = 16

EPS = 1e-06
NEG = -1e30
F32 = jnp.float32
BF16 = jnp.bfloat16

NT = (((1,), (1,)), ((), ()))


def vmem(mib):
    return pltpu.CompilerParams(vmem_limit_bytes=mib * 2**20)


def whole():
    return pl.BlockSpec(memory_space=pltpu.VMEM)


def cut_kernel(split, tokens_ref, qkv_ref, weight_ref, *refs):
    pair_ref, cross_ref, sent_ref, sem_ref = refs
    count = pair_ref.shape[0] // 2
    lanes = tokens_ref.shape[1] // 4
    chunk = tokens_ref.shape[1] // lax.axis_size("dev")
    side = lax.axis_index("dev") % 2
    part = lax.axis_index("sub")
    half = count // 2
    moves = [
        (qkv_ref.at[1], pair_ref.at[:count]),
        (qkv_ref.at[2], pair_ref.at[count:]),
        (qkv_ref.at[1], cross_ref.at[:count]),
        (qkv_ref.at[2], cross_ref.at[count : 2 * count]),
    ]
    for i in range(lanes // chunk):
        at = pl.multiple_of(part * 2 * lanes + (2 * i + 1 - side) * chunk, 128)
        for j in range(2):
            left = j * lanes + i * chunk
            moves.append(
                (
                    tokens_ref.at[j * half : (j + 1) * half, pl.ds(at, chunk)],
                    cross_ref.at[2 * count :, left : left + chunk],
                )
            )
    rows = sent_ref.shape[0]
    at = pl.multiple_of(lax.axis_index("groups") * rows if split else 0, TILE)
    moves.append((weight_ref.at[pl.ds(at, rows)], sent_ref))
    copies = [pltpu.make_async_copy(*move, sem_ref.at[n]) for n, move in enumerate(moves)]
    for copy in copies:
        copy.start()
    for copy in copies:
        copy.wait()


def rest_kernel(tokens_ref, qkv_ref, weight_ref, _, query_ref, near_ref, own_ref, sem_ref):
    lanes = near_ref.shape[1]
    chunk = tokens_ref.shape[1] // lax.axis_size("dev")
    side = lax.axis_index("dev") % 2
    part = lax.axis_index("sub")
    moves = [(qkv_ref.at[0], query_ref), (weight_ref, own_ref)]
    for i in range(lanes // chunk):
        at = pl.multiple_of(part * 2 * lanes + (2 * i + side) * chunk, 128)
        moves.append(
            (tokens_ref.at[:, pl.ds(at, chunk)], near_ref.at[:, i * chunk : (i + 1) * chunk])
        )
    copies = [pltpu.make_async_copy(*move, sem_ref.at[n]) for n, move in enumerate(moves)]
    for copy in copies:
        copy.start()
    for copy in copies:
        copy.wait()


def small_kernel(ids_ref, mod_ref, router_ref, _, row_ref, mod_to_ref, router_to_ref):
    topk, count = ids_ref.shape
    row_ref[...] = jnp.zeros(row_ref.shape, BF16)
    for k in range(topk):
        named = jnp.broadcast_to(ids_ref[k : k + 1, :], (TILE, count))
        row_ref[:, k * count : (k + 1) * count] = named.astype(F32).astype(BF16)
    mod_to_ref[...] = mod_ref[...]
    router_to_ref[...] = router_ref[...]


def attention_kernel(query_ref, own_ref, cross_ref, next_ref, *refs):
    mixed_ref = refs[-1]
    count, width = mixed_ref.shape
    place = lax.axis_index("dev")
    even = place % 2 == 0
    row = lax.broadcasted_iota(jnp.int32, (count, count), 0)
    col = lax.broadcasted_iota(jnp.int32, (count, count), 1)
    alone = (place == 0) | (place == lax.axis_size("dev") - 1)
    see_cross = jnp.where(even, col - row, row - col) <= 0
    see_next = (jnp.where(even, row - col, col - row) <= 0) & jnp.logical_not(alone)
    scale = 1.0 / math.sqrt(HEAD)

    def scored(q, k):
        return lax.dot_general(q, k, NT, preferred_element_type=F32) * scale

    for head in range(width // HEAD):
        lanes = slice(head * HEAD, (head + 1) * HEAD)
        q = query_ref[:, lanes]
        sc = jnp.where(see_cross, scored(q, cross_ref[:count, lanes]), NEG)
        so = scored(q, own_ref[:count, lanes])
        sn = jnp.where(see_next, scored(q, next_ref[:count, lanes]), NEG)
        top = jnp.max(jnp.maximum(jnp.maximum(sc, so), sn), 1, keepdims=True)
        wc, wo, wn = jnp.exp(sc - top), jnp.exp(so - top), jnp.exp(sn - top)
        inv = 1.0 / jnp.sum(wc + wo + wn, 1, keepdims=True)
        out = 0.0
        for weight, value in (
            (wo, own_ref[count:, lanes]),
            (wc, cross_ref[count : 2 * count, lanes]),
            (wn, next_ref[count:, lanes]),
        ):
            out += jnp.dot((weight * inv).astype(BF16), value, preferred_element_type=F32)
        mixed_ref[:, lanes] = out.astype(BF16)


def projection_kernel(steps, pieces, wanted, *refs):
    mixed_ref, other_ref = refs[0], refs[1]
    weight_refs = refs[2 : 2 + len(pieces)]
    out_ref = refs[2 + len(pieces)]
    count = mixed_ref.shape[0]
    half = steps // 2
    chunk = out_ref.shape[1] // half
    z = lax.axis_index("dev") // 2
    part = lax.axis_index("sub")
    group = lax.axis_index("groups")
    for (hop, side), w_ref in zip(pieces, weight_refs):
        rows = w_ref.shape[0]
        target = jnp.bitwise_xor(z, hop)
        away = jnp.where(target // half == part, 0, 1)
        lane = (target % half) * chunk
        if side is not None:
            lane += (group if side == 0 else 1 - group) * rows

        @pl.when(away == wanted)
        def _(lane=pl.multiple_of(lane, 128), rows=rows, w_ref=w_ref):
            for block, ref in enumerate((mixed_ref, other_ref)):
                out_ref[block * count : (block + 1) * count, pl.ds(lane, rows)] = (
                    lax.dot_general(ref[...], w_ref[...], NT, preferred_element_type=F32)
                )


def state_kernel(keep_ref, got_ref, near_ref, cross_ref, ids_ref, mod_ref, out_ref, again_ref):
    count, lanes = near_ref.shape
    half = count // 2
    chunk = mod_ref.shape[1] // lax.axis_size("dev")
    side = lax.axis_index("dev") % 2
    part = lax.axis_index("sub")
    for i in range(lanes // chunk):
        at = pl.multiple_of(part * 2 * lanes + (2 * i + side) * chunk, 128)
        lift = 1.0 + mod_ref[0:1, pl.ds(at, chunk)]
        cols = slice(i * chunk, (i + 1) * chunk)
        for j in range(4):
            rows = slice(j * half, (j + 1) * half)
            if j < 2:
                token = near_ref[rows, cols]
            else:
                left = (j - 2) * lanes + i * chunk
                token = cross_ref[2 * count :, left : left + chunk]
            proj = keep_ref[rows, cols] + got_ref[rows, cols]
            out_ref[rows, cols] = (token.astype(F32) + lift * proj).astype(BF16)
    out_ref[2 * count :, :] = ids_ref[...]
    again_ref[...] = out_ref[...]


def tie_kernel(*refs):
    pass


def tie(array, *others):
    anywhere = pl.BlockSpec(memory_space=pl.ANY)
    return pl.pallas_call(
        tie_kernel,
        out_shape=jax.ShapeDtypeStruct(array.shape, array.dtype),
        in_specs=[anywhere] * (1 + len(others)),
        out_specs=anywhere,
        input_output_aliases={0: 0},
        compiler_params=vmem(1),
    )(array, *others)


def select_kernel(local, topk, own, *refs):
    shard_refs, (mod_ref, router_ref) = refs[:4], refs[4:6]
    rows_ref, back_ref = refs[6:8]
    state_ref = refs[8] if own else None
    full_ref, gate_ref = refs[-2:]
    count, width = full_ref.shape
    lanes = shard_refs[0].shape[1]
    device = lax.axis_index("dev")
    side = device % 2
    part = lax.axis_index("sub")
    chunk = width // lax.axis_size("dev")
    experts = router_ref.shape[0]
    slots = local * SLOTS
    before = lax.broadcasted_iota(jnp.int32, (count, count), 0)
    after = lax.broadcasted_iota(jnp.int32, (count, count), 1)
    earlier = (before < after).astype(F32).astype(BF16)
    slot = lax.broadcasted_iota(jnp.int32, (slots, count), 0) % SLOTS
    mine = lax.broadcasted_iota(jnp.int32, (local, count), 0) + device * local
    every = lax.broadcasted_iota(jnp.int32, (experts, count), 0)
    for cross in range(2):
        for far_half in range(2):
            for far_side in range(2):
                ref = shard_refs[2 * far_half + far_side]
                top = (cross ^ far_side) * count
                half = part if far_half == 0 else 1 - part
                parity = side if far_side == 0 else 1 - side
                for i in range(lanes // chunk):
                    block = ref[top : top + count, i * chunk : (i + 1) * chunk]
                    at = (2 * i + parity) * chunk
                    full_ref[:, pl.ds(pl.multiple_of(half * 2 * lanes + at, 128), chunk)] = block
                    if own and cross == 0 and far_half == 0:
                        state_ref[:, pl.ds(pl.multiple_of(at, 128), chunk)] = block
        state = full_ref[...].astype(F32)
        scale = lax.rsqrt(jnp.mean(state * state, 1, keepdims=True) + EPS)
        normed = state * scale * (1.0 + mod_ref[2:3, :]) + mod_ref[1:2, :]
        normed = normed.astype(BF16)
        ids = shard_refs[cross][2 * count : 2 * count + TILE, :]
        ids = ids.astype(F32)[0:1, :].astype(jnp.int32)
        named = [ids[:, k * count : (k + 1) * count] for k in range(topk)]
        hot = sum((mine == n).astype(F32) for n in named)
        rank = jnp.dot(hot.astype(BF16), earlier, preferred_element_type=F32)
        rank = jnp.where(hot > 0.0, rank, -1.0)
        rank = jnp.concatenate(
            [jnp.broadcast_to(rank[e : e + 1], (SLOTS, count)) for e in range(local)]
        )
        pick = rank == slot.astype(F32)
        chosen = jnp.dot(
            jnp.where(pick, 1.0, 0.0).astype(BF16), normed, preferred_element_type=F32
        ).astype(BF16)
        for e in range(local):
            rows_ref[e, cross * SLOTS : (cross + 1) * SLOTS, :] = chosen[
                e * SLOTS : (e + 1) * SLOTS
            ]
        logits = lax.dot_general(router_ref[...], normed, NT, preferred_element_type=F32)
        lifted = sum(jnp.where(every == n, 1.0, 0.0) for n in named) * jax.nn.sigmoid(logits)
        gate_ref[...] = lifted / jnp.sum(lifted, 0, keepdims=True)
        here = gate_ref[pl.ds(pl.multiple_of(device * local, local), local), :]
        here = jnp.concatenate(
            [jnp.broadcast_to(here[e : e + 1], (SLOTS, count)) for e in range(local)]
        )
        back_ref[cross] = jnp.where(pick, here, 0.0).T.astype(BF16)


def load_kernel(from_ref, _, *refs):
    to_refs, done_ref, sem_ref = refs[:-2], refs[-2], refs[-1]
    copies = [
        pltpu.make_async_copy(from_ref.at[2 * e : 2 * e + 2], ref, sem_ref.at[e])
        for e, ref in enumerate(to_refs)
    ]
    for copy in copies:
        copy.start()
    done_ref[...] = jnp.zeros(done_ref.shape, F32)
    for copy in copies:
        copy.wait()


def load(weight, after_this, limit):
    local = weight.shape[0] // 2
    piece = jax.ShapeDtypeStruct((2, *weight.shape[1:]), BF16)
    return pl.pallas_call(
        load_kernel,
        out_shape=[piece] * local + [jax.ShapeDtypeStruct((8, 128), F32)],
        in_specs=[pl.BlockSpec(memory_space=pl.ANY)] * 2,
        out_specs=[whole()] * (local + 1),
        scratch_shapes=[pltpu.SemaphoreType.DMA((local,))],
        compiler_params=vmem(limit),
    )(weight, after_this)


def hidden_kernel(steps, low, *refs):
    rows_refs, w_refs, hidden_ref = refs[:steps], refs[steps:-1], refs[-1]
    for e, w_ref in enumerate(w_refs):
        rows = jnp.concatenate([ref[low + e] for ref in rows_refs])
        halves = []
        for b in range(2):
            gate = lax.dot_general(w_ref[b, 0], rows, NT, preferred_element_type=F32)
            up = lax.dot_general(w_ref[b, 1], rows, NT, preferred_element_type=F32)
            halves.append(jax.nn.silu(gate) * up)
        hidden_ref[e] = jnp.concatenate(halves).T.astype(BF16)


def output_kernel(low, near_ref, far_ref, w_ref, held_ref):
    part = lax.axis_index("sub")
    units = near_ref.shape[2] // 2
    for e in range(near_ref.shape[0]):
        total = 0.0
        for ref, who in ((near_ref, part), (far_ref, 1 - part)):
            at = pl.multiple_of(who * units, 64)
            weight = jnp.concatenate(
                [w_ref[2 * (low + e) + b, pl.ds(at, units), :] for b in range(2)]
            )
            total += jnp.dot(ref[e], weight, preferred_element_type=F32)
        total = total.astype(BF16)
        for source in range(held_ref.shape[0]):
            held_ref[source, e * SLOTS : (e + 1) * SLOTS, :] = total[
                source * SLOTS : (source + 1) * SLOTS
            ]


def routed_rows(steps, which, back_refs, held_refs, out_refs):
    for flip in range(steps):
        source = 2 * flip + which
        rows = jnp.concatenate([ref[source] for ref in held_refs])
        routed = jnp.dot(back_refs[flip][which], rows, preferred_element_type=F32).astype(BF16)
        if flip < steps - 1:
            out_refs[flip][...] = routed
        else:
            half = routed.shape[0] // 2
            out_refs[flip][...] = routed[:half]
            out_refs[flip + 1][...] = routed[half:]


def crossing_kernel(steps, low, before, near_ref, far_ref, w_ref, *refs):
    held_refs, back_refs = refs[:before], refs[before : before + steps]
    out_refs, held_ref = refs[before + steps : -1], refs[-1]
    output_kernel(low, near_ref, far_ref, w_ref, held_ref)
    routed_rows(steps, 1, back_refs, (*held_refs, held_ref), out_refs)


def column_kernel(steps, before, *refs):
    routed_rows(steps, 0, refs[before : before + steps], refs[:before], refs[before + steps :])


def final_kernel(state_ref, mod_ref, top_ref, bottom_ref, *refs):
    out_ref = refs[-1]
    count, lanes = state_ref.shape
    at = pl.multiple_of(lax.axis_index("sub") * lanes, 128)
    lift = 1.0 + mod_ref[3:4, pl.ds(at, lanes)]
    for h, last_ref in enumerate((top_ref, bottom_ref)):
        rows = slice(h * count // 2, (h + 1) * count // 2)
        routed = last_ref[...].astype(F32)
        for ref in refs[:-1]:
            routed += ref[rows].astype(F32)
        out_ref[rows] = (state_ref[rows].astype(F32) + lift * routed).astype(BF16)


def gathered_body(
    tokens,
    query_key_value,
    out_weight,
    modulation,
    router_weight,
    expert_ids,
    gate_up_weight,
    down_weight,
):
    count, width = tokens.shape
    devices = lax.axis_size("dev")
    groups = lax.axis_size("groups")
    steps = devices // 2
    local_width = query_key_value.shape[2]
    chunk = width // devices
    lanes = width // 4
    halves_here = gate_up_weight.shape[0]
    local = halves_here // 2
    experts = router_weight.shape[1]
    topk = expert_ids.shape[1]
    struct = jax.ShapeDtypeStruct

    def hop(x, flip):
        return lax.ppermute(x, "dev", [(i, i ^ flip) for i in range(devices)])

    def swap(x):
        return lax.ppermute(x, "sub", [(0, 1), (1, 0)])

    split = groups == 2
    held = out_weight.shape[0] // (2 if split else 1)
    anywhere = pl.BlockSpec(memory_space=pl.ANY)
    stacked = query_key_value.transpose(1, 0, 2)
    pair, cross, sent = pl.pallas_call(
        functools.partial(cut_kernel, split),
        out_shape=[
            struct((2 * count, local_width), BF16),
            struct((2 * count + count // 2, local_width), BF16),
            struct((held, local_width), BF16),
        ],
        in_specs=[anywhere] * 3,
        out_specs=[whole()] * 3,
        scratch_shapes=[pltpu.SemaphoreType.DMA((5 + 2 * (lanes // chunk),))],
        compiler_params=vmem(53),
    )(tokens, stacked, out_weight)
    query, near, own_weight = pl.pallas_call(
        rest_kernel,
        out_shape=[
            struct((count, local_width), BF16),
            struct((count, lanes), BF16),
            struct(out_weight.shape, BF16),
        ],
        in_specs=[anywhere] * 4,
        out_specs=[whole()] * 3,
        scratch_shapes=[pltpu.SemaphoreType.DMA((2 + lanes // chunk,))],
        compiler_params=vmem(53),
    )(tokens, stacked, out_weight, sent)
    ids, small, router = pl.pallas_call(
        small_kernel,
        out_shape=[
            struct((TILE, lanes), BF16),
            struct(modulation.shape, F32),
            struct((experts, width), BF16),
        ],
        in_specs=[whole()] * 3 + [pl.BlockSpec(memory_space=pl.ANY)],
        out_specs=[whole()] * 3,
        compiler_params=vmem(4),
    )(expert_ids.T, modulation, router_weight.T, query)
    odd = [(i, i + 1) for i in range(1, devices - 1, 2)]
    after = lax.ppermute(pair, "dev", odd + [(j, i) for i, j in odd])
    cross = hop(cross, 1)

    units = gate_up_weight.shape[3]
    *ups, done = load(gate_up_weight.swapaxes(2, 3), query, 16)

    mine = {0: sent}
    for flip in range(2, steps):
        low = flip & -flip
        if flip > 2 and flip - low > 0:
            mine[flip] = hop(mine[flip - low], 2 * low)
        else:
            mine[flip] = tie(hop(sent, 2 * flip), done)
    own_weight = tie(own_weight, mine[2])
    pieces, weights = [(0, None), (1, None)], [own_weight, hop(own_weight, 2)]

    mixed = pl.pallas_call(
        attention_kernel,
        out_shape=struct((count, local_width), BF16),
        in_specs=[whole()] * 4 + [pl.BlockSpec(memory_space=pl.ANY)],
        out_specs=whole(),
        compiler_params=vmem(6),
    )(query, pair, cross, after, small)
    for flip in range(2, steps):
        if split:
            if flip == steps - 1:
                mine[flip] = tie(mine[flip], mixed)
            theirs = lax.ppermute(mine[flip], "groups", [(0, 1), (1, 0)])
            pieces += [(flip, 0), (flip, 1)]
            weights += [mine[flip], theirs]
        else:
            pieces.append((flip, None))
            weights.append(mine[flip])
    other = hop(mixed, 1)
    send, keep = (
        pl.pallas_call(
            functools.partial(projection_kernel, steps, tuple(pieces), wanted),
            out_shape=struct((2 * count, lanes), F32),
            in_specs=[whole()] * (2 + len(weights)),
            out_specs=whole(),
            compiler_params=vmem(6),
        )(mixed, other, *weights)
        for wanted in (1, 0)
    )
    shard, again = pl.pallas_call(
        state_kernel,
        out_shape=[struct((2 * count + TILE, lanes), BF16)] * 2,
        in_specs=[whole()] * 6,
        out_specs=[whole()] * 2,
        compiler_params=vmem(6),
    )(keep, swap(send), near, cross, ids, small)

    slots = local * SLOTS
    state = None
    picked, backs = [], []
    column = {0: shard, 1: hop(shard, 2)}
    across = hop(shard, 1)
    column[1] = tie(column[1], across)
    crossing = {0: across, 1: hop(column[1], 1)}
    beside = swap(column[1])
    swapped = swap(shard)
    column[2] = tie(hop(tie(again, swapped), 4), beside)
    for flip in range(3, steps):
        low = flip & -flip
        column[flip] = hop(column[flip - low] if flip > low else shard, 2 * low)
    for flip in range(steps):
        if flip == steps - 1:
            column[flip] = tie(column[flip], picked[0])
        block = column[flip]
        crossed = crossing[flip] if flip in crossing else hop(block, 1)
        if flip == steps - 1:
            crossed = tie(crossed, *picked[1:])
        own = flip == 0
        results = pl.pallas_call(
            functools.partial(select_kernel, local, topk, own),
            out_shape=[
                struct((local, 2 * SLOTS, width), BF16),
                struct((2, count, slots), BF16),
            ]
            + ([struct((count, 2 * lanes), BF16)] if own else []),
            in_specs=[whole()] * 6,
            out_specs=[whole()] * (3 if own else 2),
            scratch_shapes=[pltpu.VMEM((count, width), BF16), pltpu.VMEM((experts, count), F32)],
            compiler_params=vmem(6),
        )(block, crossed, beside if flip == 1 else swapped if own else swap(block), swap(crossed), small, router)
        picked.append(results[0])
        backs.append(results[1])
        if own:
            state = results[2]

    sources = 2 * steps
    room = sources * SLOTS
    first = 5 * local // 8
    groups_of = [(0, first), (first, local)] if first else [(0, local)]
    hidden = []
    for low, high in groups_of:
        own = pl.pallas_call(
            functools.partial(hidden_kernel, steps, low),
            out_shape=struct((high - low, room, 2 * units), BF16),
            in_specs=[whole()] * (steps + high - low),
            out_specs=whole(),
            compiler_params=vmem(6),
        )(*picked, *ups[low:high])
        hidden.append((own, swap(own)))
    held = []
    for (low, high), (own, other) in zip(groups_of[:-1], hidden[:-1]):
        held.append(
            pl.pallas_call(
                functools.partial(output_kernel, low),
                out_shape=struct((sources, (high - low) * SLOTS, 2 * lanes), BF16),
                in_specs=[whole()] * 3,
                out_specs=whole(),
                compiler_params=vmem(6),
            )(own, other, down_weight)
        )
    low, high = groups_of[-1]
    blocks_out = [struct((count, 2 * lanes), BF16)] * (steps - 1)
    blocks_out += [struct((count // 2, 2 * lanes), BF16)] * 2
    *crossing_out, last = pl.pallas_call(
        functools.partial(crossing_kernel, steps, low, len(held)),
        out_shape=blocks_out + [struct((sources, (high - low) * SLOTS, 2 * lanes), BF16)],
        in_specs=[whole()] * (3 + len(held) + steps),
        out_specs=[whole()] * (steps + 2),
        compiler_params=vmem(8),
    )(*hidden[-1], down_weight, *held, *backs)
    held.append(last)
    column_out = pl.pallas_call(
        functools.partial(column_kernel, steps, len(held)),
        out_shape=blocks_out,
        in_specs=[whole()] * (len(held) + steps),
        out_specs=[whole()] * (steps + 1),
        compiler_params=vmem(8),
    )(*held, *backs)

    def forwarded(mine, crossed, flip):
        total = mine.astype(F32) + crossed.astype(F32)
        return hop(total.astype(BF16), 2 * flip)

    top = hop(crossing_out[-2], 1)
    crossed = {flip: hop(crossing_out[flip], 1) for flip in range(steps - 2, 0, -1)}
    bottom = hop(tie(crossing_out[-1], top), 1)
    halves = [forwarded(column_out[h - 2], (top, bottom)[h], steps - 1) for h in range(2)]
    terms = [forwarded(column_out[flip], crossed[flip], flip) for flip in crossed]
    terms += [column_out[0], hop(tie(crossing_out[0], crossed[steps - 2]), 1)]
    return pl.pallas_call(
        final_kernel,
        out_shape=struct((count, 2 * lanes), BF16),
        in_specs=[whole()] * (4 + len(terms)),
        out_specs=whole(),
        compiler_params=vmem(8),
    )(state, small, *halves, *terms)


def extended(cells, sides, width):
    for axis, dim in sides:
        count = lax.axis_size(axis)
        ends = count - 1
        head = lax.slice_in_dim(cells, 0, width, axis=dim)
        tail = lax.slice_in_dim(cells, cells.shape[dim] - width, cells.shape[dim], axis=dim)
        cells = jnp.concatenate(
            [
                lax.ppermute(tail, axis, [(i, (i + 1) % count) for i in range(ends)]),
                cells,
                lax.ppermute(head, axis, [((i + 1) % count, i) for i in range(ends)]),
            ],
            axis=dim,
        )
    return cells


def window_attention(query, keys, values, index, total):
    count = query.shape[0]
    rows = jnp.arange(count, dtype=jnp.int32)[:, None]
    cols = jnp.arange(3 * count, dtype=jnp.int32)[None, :] - count
    place = index * count + cols
    allowed = (jnp.abs(cols - rows) <= count) & (place >= 0) & (place < total)
    scores = jnp.einsum(
        "qhd,khd->hqk", query, keys, preferred_element_type=jnp.float32
    ) / math.sqrt(query.shape[2])
    scores = jnp.where(allowed[None], scores, NEG)
    top = jnp.max(scores, -1, keepdims=True)
    weight = jnp.exp(scores - top)
    weight = (weight / jnp.sum(weight, -1, keepdims=True)).astype(jnp.bfloat16)
    mixed = jnp.einsum("hqk,khd->qhd", weight, values, preferred_element_type=jnp.float32)
    return mixed.astype(jnp.bfloat16)


def normalize(state, modulation):
    scale = lax.rsqrt(jnp.mean(state * state, -1, keepdims=True) + EPS)
    return (state * scale * (1.0 + modulation[2]) + modulation[1]).astype(jnp.bfloat16)


def route(normed, router_weight, expert_ids):
    logits = jnp.dot(normed, router_weight, preferred_element_type=jnp.float32)
    experts = router_weight.shape[1]
    match = expert_ids[:, :, None] == jnp.arange(experts, dtype=jnp.int32)[None, None, :]
    picked = jnp.sum(jnp.where(match, logits[:, None, :], 0.0), -1)
    lifted = jax.nn.sigmoid(picked)
    return lifted / jnp.sum(lifted, -1, keepdims=True)


def exchanged_body(
    tokens,
    query_key_value,
    out_weight,
    modulation,
    router_weight,
    expert_ids,
    gate_up_weight,
    down_weight,
):
    count = tokens.shape[0]
    width = tokens.shape[1]
    parts = lax.axis_size("sub")
    part = lax.axis_index("sub")
    position = lax.axis_index("dev")
    devices = lax.axis_size("dev")
    total = count * devices
    local_width = query_key_value.shape[2]
    heads_here = local_width // HEAD
    query = query_key_value[:, 0].reshape(count, heads_here, HEAD)
    pair = query_key_value[:, 1:]
    near = extended(pair, (("dev", 0),), count)
    keys = near[:, 0].reshape(3 * count, heads_here, HEAD)
    values = near[:, 1].reshape(3 * count, heads_here, HEAD)
    mixed = window_attention(query, keys, values, position, total).reshape(count, local_width)
    partial_proj = lax.dot_general(
        mixed,
        lax.all_gather(out_weight, "dev", axis=0, tiled=True),
        (((1,), (1,)), ((), ())),
        preferred_element_type=jnp.float32,
    )
    proj = lax.psum(partial_proj, "sub")
    state = tokens.astype(jnp.float32) + (1.0 + modulation[0]) * proj
    normed = normalize(state, modulation)
    gates = route(normed, router_weight, expert_ids)
    experts = router_weight.shape[1]
    topk = expert_ids.shape[1]
    flat = expert_ids.reshape(-1)
    picks = flat.shape[0]
    onehot = (flat[:, None] == jnp.arange(experts, dtype=jnp.int32)[None, :]).astype(BF16)
    order = jnp.arange(picks, dtype=jnp.int32)
    earlier = (order[None, :] < order[:, None]).astype(BF16)
    ahead = jnp.dot(earlier, onehot, preferred_element_type=F32)
    rank = jnp.sum(ahead * onehot.astype(F32), 1).astype(jnp.int32)
    target = flat * CAP + rank
    hit = target[None, :] == jnp.arange(experts * CAP, dtype=jnp.int32)[:, None]
    owner = jnp.any(hit.reshape(experts * CAP, count, topk), 2).astype(BF16)
    slice_width = width // parts
    sent = lax.dynamic_slice_in_dim(normed, part * slice_width, slice_width, 1)
    sent_width = sent.shape[1]
    rows_out = jnp.dot(owner, sent, preferred_element_type=F32).astype(BF16)
    halves_here = gate_up_weight.shape[0]
    doubled = jnp.broadcast_to(
        rows_out.reshape(experts, 1, CAP, sent_width), (experts, 2, CAP, sent_width)
    )
    outgoing = doubled.reshape(devices, halves_here, CAP, sent_width)
    up_form = "sxcd,xgdf->sxcgf"
    down_form = "sxcf,xfd->sxcd"
    incoming = lax.all_to_all(outgoing, "dev", split_axis=0, concat_axis=0, tiled=True)
    both = jnp.einsum(
        up_form,
        lax.all_gather(incoming, "sub", axis=3, tiled=True),
        gate_up_weight,
        preferred_element_type=jnp.float32,
    )
    hidden = (jax.nn.silu(both[..., 0, :]) * both[..., 1, :]).astype(jnp.bfloat16)
    gathered = lax.all_gather(hidden, "sub", axis=hidden.ndim - 1, tiled=True)
    result = jnp.einsum(down_form, gathered, down_weight, preferred_element_type=jnp.float32)
    returned = lax.all_to_all(
        result.astype(jnp.bfloat16), "dev", split_axis=0, concat_axis=0, tiled=True
    )
    own_width = returned.shape[-1]
    arranged = returned.reshape(experts, 2, CAP, own_width)
    combined = arranged[:, 0].astype(F32) + arranged[:, 1].astype(F32)
    share = jnp.sum(
        jnp.where(hit.reshape(experts * CAP, count, topk), gates[None], 0.0), 2
    )
    routed = lax.dot_general(
        share,
        combined.reshape(experts * CAP, own_width),
        (((0,), (0,)), ((), ())),
        precision=lax.Precision.HIGHEST,
        preferred_element_type=F32,
    )
    own = lax.dynamic_slice_in_dim(state, part * slice_width, slice_width, 1)
    lift = lax.dynamic_slice_in_dim(modulation[3], part * slice_width, slice_width, 0)
    return (own + (1.0 + lift) * routed).astype(jnp.bfloat16)


def body(*arrays):
    tokens, router_weight, expert_ids, gate_up_weight = arrays[0], arrays[4], arrays[5], arrays[6]
    devices = lax.axis_size("dev")
    count, width = tokens.shape
    local = gate_up_weight.shape[0] // 2
    fits = (
        lax.axis_size("sub") == 2
        and devices >= 8
        and devices & (devices - 1) == 0
        and gate_up_weight.shape[0] % 2 == 0
        and width % (devices * 128) == 0
        and arrays[1].shape[2] * 2 == width
        and count % HEAD == 0
        and expert_ids.shape[1] * count <= width // 4
        and router_weight.shape[1] <= 256
    )
    if fits and count * devices <= 2 * local * devices * CAP:
        return gathered_body(*arrays)
    return exchanged_body(*arrays)


def solution(mesh):
    return jax.shard_map(
        body,
        mesh=mesh,
        in_specs=(
            P(("groups", "dev"), None),
            P(("groups", "dev"), None, "sub"),
            P("dev", "sub"),
            P("groups", None),
            P(),
            P(("groups", "dev"), None),
            P("dev", None, None, "sub"),
            P("dev", None, "sub"),
        ),
        out_specs=P(("groups", "dev"), "sub"),
        check_vma=False,
    )
```
